32 devices in a mesh: section: 2 (over core), wide: 4 (over y, x), rows: 4 (over z).
Axes of the slice: x: 2, y: 2, z: 4, core: 2. Of those that a mesh axis runs over, the one named last changes fastest.
Arguments:
- enc_embed: bfloat16 [2, 16, 256, 1472], P(None, ('wide', 'rows')), may hold values from -6 to 6
- dec_embed: bfloat16 [2, 16, 64, 1472], P(None, ('wide', 'rows')), may hold values from -6 to 6
- out_cot: bfloat16 [2, 16, 64, 1472], P(None, ('wide', 'rows')), may hold values from -6 to 6
- enc_lengths: int32 [2, 16, 8], P(None, ('wide', 'rows')), may hold values from 1 to 128, 256 in all within a row
- dec_lengths: int32 [2, 16, 8], P(None, ('wide', 'rows')), may hold values from 1 to 32, 64 in all within a row
- norm_gains: float32 [2, 3, 1472], P('section'), may hold values from 0.5 to 1.5
- rel_bias: float32 [2, 32, 6], P('section'), may hold values from -3 to 3
- attn_in: bfloat16 [2, 1472, 1152], P('section', 'wide'), may hold values from -0.09375 to 0.09375
- attn_out: bfloat16 [2, 384, 1472], P('section', None, 'wide'), may hold values from -0.875 to 0.875
- ffn_in: bfloat16 [2, 1472, 7168], P('section', 'wide'), may hold values from -0.15625 to 0.15625
- ffn_out: bfloat16 [2, 3584, 1472], P('section', None, 'wide'), may hold values from -0.09375 to 0.09375
- cross_in: bfloat16 [2, 1472, 384], P('section', 'wide'), may hold values from -0.09375 to 0.09375
- cross_out: bfloat16 [2, 1472, 384], P('section', 'wide'), may hold values from -0.21875 to 0.21875
Outputs:
- dec_out: bfloat16 [2, 16, 64, 1472], P(None, ('wide', 'rows'), None, 'section')
- enc_grad: float32 [2, 16, 256, 1472], P(None, ('wide', 'rows'), None, 'section')
- dec_grad: float32 [2, 16, 64, 1472], P(None, ('wide', 'rows'), None, 'section')
- gain_grad: float32 [2, 3, 1472], P('section')
- bias_grad: float32 [2, 32, 6], P('section')
- attn_in_grad: float32 [2, 1472, 1152], P('section', 'wide', 'rows')
- attn_out_grad: float32 [2, 384, 1472], P('section', 'rows', 'wide')
- ffn_in_grad: float32 [2, 1472, 7168], P('section', 'wide', 'rows')
- ffn_out_grad: float32 [2, 3584, 1472], P('section', 'rows', 'wide')
- cross_in_grad: float32 [2, 1472, 384], P('section', 'wide', 'rows')
- cross_out_grad: float32 [2, 1472, 384], P('section', 'wide', 'rows')
The draws below stay inside these ranges and needn't reach their ends.
Inputs may be any that keep to these rules, and one draw needn't show every extreme that they name: `enc_lengths`: each row's 8 encoder item lengths sum to 256. `dec_lengths`: each row's 8 target item lengths sum to 64.
All inputs are finite; a program needn't handle non-finite values.
Results may differ from the reference program's by a relative error of at most 0.03.
The reference program's roundings to bfloat16 on the way (of `attend` and `memory_kv`) count: a program that leaves them out, or rounds other values in their place, can miss the bound.
Values may be sent and summed in bfloat16 or wider, within the bound.
A program may use at most 960 MiB of HBM per device.

```python
import math
import jax
import jax.numpy as jnp
import numpy as np
from jax import lax

D = 1472
H = 6
DH = 64
FF = 3584
NB = 32
MAXDIST = 128
MB = 2
LE = 256
LD = 64
C = 8
HD = 384
ROWS = 16


def block_levels(stream_key, dims, split, smallest, largest):
    gain, own = 1.0, jax.random.fold_in(stream_key, 6)
    for dim, shards_of in split:
        steps = jnp.exp(jax.random.uniform(jax.random.fold_in(own, dim), (shards_of,), jnp.float32, smallest / len(split), largest / len(split)))
        gain = gain * jnp.repeat(steps, dims[dim] // shards_of).reshape([-1 if axis == dim else 1 for axis in range(len(dims))])
    return gain


def split_up(count, total, most, lean):
    weights = [(1 << 20) // math.isqrt(standing ** lean) + 1 for standing in range(2, count + 1)]
    surplus, counts = total - most - (count - 1), [1] * (count - 1)
    while surplus > 0:
        free = [i for i in range(count - 1) if counts[i] < most]
        whole, budget = sum([weights[i] for i in free]), surplus
        for i in free:
            more = min(most - counts[i], max(1, budget * weights[i] // whole), surplus)
            counts[i] = counts[i] + more
            surplus = surplus - more
    return np.array([most] + counts)


def ragged(key, count, total, reach, skew):
    if count == 2:
        one = jax.random.randint(key, (), max(1, total - reach), min(reach, total - 1) + 1)
        return jnp.stack([one, total - one])
    sizes = jnp.asarray(split_up(count, total, reach, skew), jnp.int32)
    pairs = (count - 1) // 2
    donor, sink = sizes[1:1 + 2 * pairs:2], sizes[2:2 + 2 * pairs:2]
    margin = jnp.minimum(donor - 1, reach - sink)
    passed = jax.random.randint(jax.random.fold_in(key, 1), (pairs,), 0, 1 << 20) % (margin + 1)
    sizes = sizes.at[1:1 + 2 * pairs:2].set(donor - passed).at[2:2 + 2 * pairs:2].set(sink + passed)
    return sizes[jax.random.permutation(jax.random.fold_in(key, 2), count)]


def normal_values(rng, extent, spread, reach, pieces=(), kind=jnp.bfloat16):
    values = spread * jax.random.normal(rng, extent, jnp.float32)
    if pieces:
        values = values * block_levels(rng, extent, pieces, -0.22, 0.18)
    return jnp.clip(values, -reach, reach).astype(kind)


def setup_inputs(seed: int = 0) -> dict:
    arg_keys = jax.random.split(jax.random.key(seed), 14)
    return {
        "enc_embed": normal_values(arg_keys[0], (MB, ROWS, LE, D), 1.0, 6.0, ((1, 16),)),
        "dec_embed": normal_values(arg_keys[1], (MB, ROWS, LD, D), 1.0, 6.0, ((1, 16),)),
        "out_cot": normal_values(arg_keys[2], (MB, ROWS, LD, D), 1.0, 6.0, ((1, 16),)),
        "enc_lengths": jax.vmap(lambda own: ragged(own, C, LE, LE // 2, 2))(jax.random.split(arg_keys[3], MB * ROWS)).reshape((MB, ROWS, C)).astype(jnp.int32),
        "dec_lengths": jax.vmap(lambda own: ragged(own, C, LD, LD // 2, 2))(jax.random.split(arg_keys[4], MB * ROWS)).reshape((MB, ROWS, C)).astype(jnp.int32),
        "norm_gains": jnp.clip(1.0 + 0.1 * jax.random.normal(arg_keys[5], (2, 3, D), jnp.float32), 0.5, 1.5),
        "rel_bias": normal_values(arg_keys[6], (2, NB, H), 0.5, 3.0, ((0, 2),), jnp.float32),
        "attn_in": normal_values(arg_keys[7], (2, D, 3 * HD), (3 * D) ** -0.5, 0.09375, ((0, 2), (1, 4))),
        "attn_out": normal_values(arg_keys[8], (2, HD, D), (HD // 8) ** -0.5, 0.875, ((0, 2), (2, 4))),
        "ffn_in": normal_values(arg_keys[9], (2, D, 2 * FF), D ** -0.5, 0.15625, ((0, 2), (1, 4))),
        "ffn_out": normal_values(arg_keys[10], (2, FF, D), FF ** -0.5, 0.09375, ((0, 2), (2, 4))),
        "cross_in": normal_values(arg_keys[11], (2, D, HD), (3 * D) ** -0.5, 0.09375, ((0, 2), (1, 4))),
        "cross_out": normal_values(arg_keys[12], (2, D, HD), (D // 2) ** -0.5, 0.21875, ((0, 2), (1, 4))),
    }


@jax.custom_vjp
def low(v):
    return lax.optimization_barrier(v.astype(jnp.bfloat16)).astype(jnp.float32)

@jax.custom_vjp
def low_back(v):
    return v

def low_keep(v):
    return (low(v), None)

def low_pass(kept, grad):
    return (grad,)

def back_keep(v):
    return (v, None)

def back_low(kept, grad):
    return (low(grad),)
low.defvjp(low_keep, low_pass)
low_back.defvjp(back_keep, back_low)
EPSILON = 1e-06
NEGATIVE = -1000000000.0
HIGHEST = lax.Precision.HIGHEST

def bucket_table(length, both_ways):
    positions = np.arange(length)
    offsets = positions[None, :] - positions[:, None]
    buckets = NB
    result = np.zeros(offsets.shape, np.int64)
    if both_ways:
        buckets = buckets // 2
        result = result + (offsets > 0) * buckets
        distance = np.abs(offsets)
    else:
        distance = np.maximum(-offsets, 0)
    exact_count = buckets // 2
    log_ratio = np.log(np.maximum(distance, 1) / exact_count) / np.log(MAXDIST / exact_count)
    far_bucket = np.minimum(exact_count + np.floor(log_ratio * (buckets - exact_count)).astype(np.int64), buckets - 1)
    return result + np.where(distance < exact_count, distance, far_bucket)

def one_hot(length, both_ways):
    bucket_ids = jnp.asarray(bucket_table(length, both_ways), jnp.int32)
    return (bucket_ids[:, :, None] == jnp.arange(NB, dtype=jnp.int32)[None, None, :]).astype(jnp.float32)

def item_ids(lengths, length):
    item_ends = jnp.cumsum(lengths)
    positions = jnp.arange(length, dtype=jnp.int32)
    return lax.optimization_barrier(jnp.sum((positions[:, None] >= item_ends[None, :-1]).astype(jnp.int32), axis=1))

def rms_norm(residual, gain_row):
    return residual * lax.rsqrt(lax.optimization_barrier(jnp.mean(residual * residual, axis=-1, keepdims=True)) + EPSILON) * gain_row

def matmul(left_side, right_side):
    return jnp.dot(left_side, right_side, precision=HIGHEST)

def attend(queries, key_rows, value_rows, bias_full, allowed):
    query_count = queries.shape[0]
    heads_q = queries.reshape(query_count, H, DH)
    heads_k = key_rows.reshape(key_rows.shape[0], H, DH)
    heads_v = value_rows.reshape(value_rows.shape[0], H, DH)
    scores = low_back(jnp.einsum('qhd,khd->hqk', heads_q, heads_k, precision=HIGHEST) + bias_full)
    scores = jnp.where(allowed[None], scores, NEGATIVE)
    shifted = jnp.exp(scores - lax.optimization_barrier(jnp.max(scores, axis=-1, keepdims=True)))
    weights = shifted / lax.optimization_barrier(jnp.sum(shifted, axis=-1, keepdims=True))
    context = jnp.einsum('hqk,khd->qhd', low(weights), heads_v, precision=HIGHEST)
    return low(low_back(context.reshape(query_count, HD)))

def self_block(residual, gain_row, weight_in, weight_out, bias_full, allowed):
    normed = low(rms_norm(residual, gain_row))
    projected = low(low_back(matmul(normed, weight_in)))
    context = attend(projected[:, :HD], projected[:, HD:2 * HD], projected[:, 2 * HD:], bias_full, allowed)
    return residual + low_back(matmul(context, weight_out))

def feed_forward(residual, gain_row, weight_in, weight_out):
    normed = low(rms_norm(residual, gain_row))
    both_parts = low_back(matmul(normed, weight_in))
    hidden = low(jax.nn.gelu(both_parts[:, :FF], approximate=True) * both_parts[:, FF:])
    return residual + low_back(matmul(hidden, weight_out))

def one_row(params, row_inputs):
    gain_rows, biases, attn_w_in, attn_w_out, ffn_w_in, ffn_w_out, cross_w_in, cross_w_out = params
    enc_row, dec_row, enc_len, dec_len = row_inputs
    enc_items = item_ids(enc_len, LE)
    dec_items = item_ids(dec_len, LD)
    enc_bias = jnp.einsum('qkb,bh->hqk', one_hot(LE, True), biases[0], precision=HIGHEST)
    state = self_block(enc_row, gain_rows[0, 0], attn_w_in[0], attn_w_out[0], enc_bias, enc_items[:, None] == enc_items[None, :])
    state = feed_forward(state, gain_rows[0, 1], ffn_w_in[0], ffn_w_out[0])
    memory = low(rms_norm(state, gain_rows[0, 2]))
    memory_kv = low(low_back(matmul(memory, jnp.concatenate([cross_w_in[0], cross_w_out[0]], axis=1))))
    causal = jnp.arange(LD)[:, None] >= jnp.arange(LD)[None, :]
    dec_bias = jnp.einsum('qkb,bh->hqk', one_hot(LD, False), biases[1], precision=HIGHEST)
    target = self_block(dec_row, gain_rows[1, 0], attn_w_in[1], attn_w_out[1], dec_bias, (dec_items[:, None] == dec_items[None, :]) & causal)
    normed = low(rms_norm(target, gain_rows[1, 1]))
    queries = low(low_back(matmul(normed, cross_w_in[1])))
    context = attend(queries, memory_kv[:, :HD], memory_kv[:, HD:], 0.0, dec_items[:, None] == enc_items[None, :])
    target = target + low_back(matmul(context, cross_w_out[1].T))
    return feed_forward(target, gain_rows[1, 2], ffn_w_in[1], ffn_w_out[1])

def to_wide(tensor):
    return tensor.astype(jnp.float32)

def reference(enc_embed, dec_embed, out_cot, enc_lengths, dec_lengths, norm_gains, rel_bias, attn_in, attn_out, ffn_in, ffn_out, cross_in, cross_out):
    params = (to_wide(norm_gains), to_wide(rel_bias), to_wide(attn_in), to_wide(attn_out), to_wide(ffn_in), to_wide(ffn_out), to_wide(cross_in), to_wide(cross_out))
    enc_rows = to_wide(enc_embed).reshape(MB * ROWS, LE, D)
    dec_rows = to_wide(dec_embed).reshape(MB * ROWS, LD, D)
    enc_len = enc_lengths.reshape(MB * ROWS, C)
    dec_len = dec_lengths.reshape(MB * ROWS, C)

    def forward(weight_set, enc_part, dec_part):

        def row_step(row_inputs):
            return one_row(weight_set, row_inputs)
        return lax.map(jax.checkpoint(row_step), (enc_part, dec_part, enc_len, dec_len))
    outputs, pullback = jax.vjp(forward, params, enc_rows, dec_rows)
    weight_grads, enc_back, dec_back = pullback(to_wide(out_cot).reshape(MB * ROWS, LD, D))
    return (outputs.reshape(MB, ROWS, LD, D).astype(jnp.bfloat16), enc_back.reshape(MB, ROWS, LE, D), dec_back.reshape(MB, ROWS, LD, D), weight_grads[0], weight_grads[1], weight_grads[2], weight_grads[3], weight_grads[4], weight_grads[5], weight_grads[6], weight_grads[7])
```

```python
import jax
import jax.numpy as jnp
import numpy as np
from jax import lax
from jax.sharding import PartitionSpec as P

D = 1472
H = 6
DH = 64
FF = 3584
NB = 32
MAXDIST = 128
MB = 2
LE = 256
LD = 64
HD = 384


EPSILON = 1e-06
NEGATIVE = -1000000000.0
HIGHEST = lax.Precision.HIGHEST


def bucket_table(length, both_ways):
    positions = np.arange(length)
    offsets = positions[None, :] - positions[:, None]
    buckets = NB
    result = np.zeros(offsets.shape, np.int64)
    if both_ways:
        buckets = buckets // 2
        result = result + (offsets > 0) * buckets
        distance = np.abs(offsets)
    else:
        distance = np.maximum(-offsets, 0)
    exact_count = buckets // 2
    log_ratio = np.log(np.maximum(distance, 1) / exact_count) / np.log(MAXDIST / exact_count)
    far_bucket = np.minimum(
        exact_count + np.floor(log_ratio * (buckets - exact_count)).astype(np.int64), buckets - 1
    )
    return result + np.where(distance < exact_count, distance, far_bucket)


def one_hot(length, both_ways):
    bucket_ids = jnp.asarray(bucket_table(length, both_ways), jnp.int32)
    return (bucket_ids[:, :, None] == jnp.arange(NB, dtype=jnp.int32)[None, None, :]).astype(
        jnp.float32
    )


def item_ids(lengths, length):
    item_ends = jnp.cumsum(lengths)
    positions = jnp.arange(length, dtype=jnp.int32)
    return jnp.sum((positions[:, None] >= item_ends[None, :-1]).astype(jnp.int32), axis=1)


def rms_norm(residual, gain_row):
    return (
        residual
        * lax.rsqrt(jnp.mean(residual * residual, axis=-1, keepdims=True) + EPSILON)
        * gain_row
    )


def matmul(left_side, right_side):
    return jnp.dot(left_side, right_side, preferred_element_type=jnp.float32)


def to_low(tensor):
    return tensor.astype(jnp.bfloat16)


def gated(gate_part, up_part):
    return jax.nn.gelu(gate_part, approximate=True) * up_part


def attend_forward(queries, key_rows, value_rows, bias_full, allowed):
    query_count = queries.shape[0]
    heads_q = queries.reshape(query_count, H, DH)
    heads_k = key_rows.reshape(key_rows.shape[0], H, DH)
    heads_v = value_rows.reshape(value_rows.shape[0], H, DH)
    scores = (
        jnp.einsum("qhd,khd->hqk", heads_q, heads_k, preferred_element_type=jnp.float32) + bias_full
    )
    scores = jnp.where(allowed[None], scores, NEGATIVE)
    shifted = jnp.exp(scores - jnp.max(scores, axis=-1, keepdims=True))
    weights = shifted / jnp.sum(shifted, axis=-1, keepdims=True)
    low_weights = to_low(weights)
    context = jnp.einsum("hqk,khd->qhd", low_weights, heads_v, preferred_element_type=jnp.float32)
    return (to_low(context.reshape(query_count, H * DH)), weights, low_weights)


def attend_backward(queries, key_rows, value_rows, weights, low_weights, grad_context):
    query_count = queries.shape[0]
    key_count = key_rows.shape[0]
    heads_q = queries.reshape(query_count, H, DH)
    heads_k = key_rows.reshape(key_count, H, DH)
    heads_v = value_rows.reshape(key_count, H, DH)
    grad_heads = grad_context.reshape(query_count, H, DH)
    grad_weights = jnp.einsum(
        "qhd,khd->hqk", grad_heads, heads_v, preferred_element_type=jnp.float32
    )
    grad_values = jnp.einsum(
        "hqk,qhd->khd", low_weights, grad_heads, preferred_element_type=jnp.float32
    )
    grad_scores = weights * (grad_weights - jnp.sum(grad_weights * weights, axis=-1, keepdims=True))
    low_scores = to_low(grad_scores)
    grad_queries = jnp.einsum(
        "hqk,khd->qhd", low_scores, heads_k, preferred_element_type=jnp.float32
    )
    grad_keys = jnp.einsum("hqk,qhd->khd", low_scores, heads_q, preferred_element_type=jnp.float32)
    return (
        grad_queries.reshape(query_count, H * DH),
        grad_keys.reshape(key_count, H * DH),
        grad_values.reshape(key_count, H * DH),
        low_scores,
    )


def xor_permute(value, axis, distance):
    count = lax.axis_size(axis)
    return lax.ppermute(value, axis, [(i, i ^ distance) for i in range(count)])


def gather_wide(block):
    count = lax.axis_size("wide")
    if count != 4:
        return [block] + [xor_permute(block, "wide", v) for v in range(1, count)]
    half = block.shape[0] // 2
    first = xor_permute(block, "wide", 1)
    second = xor_permute(block, "wide", 2)
    third = jnp.concatenate(
        [xor_permute(first[:half], "wide", 2), xor_permute(second[half:], "wide", 1)], axis=0
    )
    return [block, first, second, third]


def scatter_wide(parts):
    count = lax.axis_size("wide")
    total = parts[0]
    if count != 4:
        for v in range(1, count):
            total = total + xor_permute(to_low(parts[v]), "wide", v).astype(jnp.float32)
        return total
    half = total.shape[0] // 2
    via_first = xor_permute(to_low(parts[3][:half]), "wide", 1).astype(jnp.float32)
    via_second = xor_permute(to_low(parts[3][half:]), "wide", 2).astype(jnp.float32)
    to_first = jnp.concatenate([parts[1][:half], parts[1][half:] + via_second], axis=0)
    to_second = jnp.concatenate([parts[2][:half] + via_first, parts[2][half:]], axis=0)
    total = total + xor_permute(to_low(to_first), "wide", 1).astype(jnp.float32)
    return total + xor_permute(to_low(to_second), "wide", 2).astype(jnp.float32)


def placed_rows(pieces, place):
    rows = pieces[0].shape[0]
    buffer = jnp.zeros((rows * len(pieces),) + pieces[0].shape[1:], pieces[0].dtype)
    for v, piece in enumerate(pieces):
        start = (place ^ v) * rows
        buffer = lax.dynamic_update_slice(buffer, piece, (start,) + (0,) * (piece.ndim - 1))
    return buffer


def both_sections(own, section):
    other = xor_permute(own, "section", 1)
    is_dec = section == 1
    return jnp.where(is_dec, other, own), jnp.where(is_dec, own, other)


def norm_backward(residual, gain_row, grad_normed):
    _, norm_pull = jax.vjp(rms_norm, residual, gain_row)
    return norm_pull(grad_normed)


def self_forward(residual, gain_row, weight, bias_full, allowed):
    normed = to_low(rms_norm(residual, gain_row))
    projected = to_low(matmul(normed, weight[:, : 3 * HD]))
    context, weights, low_weights = attend_forward(
        projected[:, :HD], projected[:, HD : 2 * HD], projected[:, 2 * HD :], bias_full, allowed
    )
    return (
        residual + matmul(context, weight[:, 3 * HD : 4 * HD].T),
        (residual, normed, projected, context, weights, low_weights),
    )


def self_backward(kept, gain_row, weight, hot, grad_out):
    residual, normed, projected, context, weights, low_weights = kept
    grad_low = to_low(grad_out)
    grad_wout = matmul(grad_low.T, context)
    grad_context = to_low(matmul(grad_low, weight[:, 3 * HD : 4 * HD]))
    grad_queries, grad_keys, grad_values, low_scores = attend_backward(
        projected[:, :HD],
        projected[:, HD : 2 * HD],
        projected[:, 2 * HD :],
        weights,
        low_weights,
        grad_context,
    )
    grad_projected = to_low(jnp.concatenate([grad_queries, grad_keys, grad_values], axis=1))
    grad_win = matmul(normed.T, grad_projected)
    grad_residual, grad_gain = norm_backward(
        residual, gain_row, matmul(grad_projected, weight[:, : 3 * HD].T)
    )
    grad_bias = jnp.einsum(
        "hqk,qkb->bh", low_scores, hot.astype(jnp.bfloat16), preferred_element_type=jnp.float32
    )
    return grad_out + grad_residual, grad_gain, grad_win, grad_wout, grad_bias


def hidden_columns(weight):
    width = weight.shape[1] * 2 // 3
    return weight[:, :width], weight[:, width:]


def ffn_hidden(blocks, weight):
    w_in, _ = hidden_columns(weight)
    both = [matmul(block, w_in) for block in blocks]
    units = w_in.shape[1] // 2
    return both, [to_low(gated(part[:, :units], part[:, units:])) for part in both]


def ffn_forward(residual, gain_row, weight):
    blocks = gather_wide(to_low(rms_norm(residual, gain_row)))
    both, hidden = ffn_hidden(blocks, weight)
    _, w_out = hidden_columns(weight)
    out = residual + scatter_wide([matmul(part, w_out.T) for part in hidden])
    return out, (residual, blocks, both, hidden)


def ffn_backward(kept, gain_row, weight, grad_out, grad_blocks):
    residual, blocks, both, hidden = kept
    w_in, w_out = hidden_columns(weight)
    units = w_out.shape[1]
    parts, grad_both = [], []
    for block, pre in zip(grad_blocks, both):
        _, pull = jax.vjp(gated, pre[:, :units], pre[:, units:])
        grad_gate, grad_up = pull(matmul(block, w_out))
        low = to_low(jnp.concatenate([grad_gate, grad_up], axis=1))
        grad_both.append(low)
        parts.append(matmul(low, w_in.T))
    grad_residual, grad_gain = norm_backward(residual, gain_row, scatter_wide(parts))
    joined = jnp.concatenate(grad_both, axis=0)
    grad_in = matmul(jnp.concatenate(blocks, axis=0).T, joined)
    grad_wout = matmul(jnp.concatenate(grad_blocks, axis=0).T, jnp.concatenate(hidden, axis=0))
    return grad_out + grad_residual, grad_gain, (grad_in, grad_wout)


def core_halves(grad, core, wide):
    depth, columns = grad.shape
    split = to_low(grad).reshape(wide, 2, depth // wide // 2, columns)
    mine = lax.dynamic_index_in_dim(split, core, 1, keepdims=False)
    sent = lax.dynamic_index_in_dim(split, 1 - core, 1, keepdims=False)
    return mine.astype(jnp.float32) + xor_permute(sent, "section", 1).astype(jnp.float32)


def reduce_ffn(grads, core, wide, rows):
    grad_in, grad_wout = grads
    depth = grad_in.shape[0]
    both = jnp.concatenate(
        [grad_in.reshape(depth, rows, -1), grad_wout.reshape(depth, rows, -1)], axis=2
    )
    columns = both.shape[2]
    halves = core_halves(both.reshape(depth, rows * columns), core, wide)
    halves = to_low(halves).reshape(wide * (depth // wide // 2), rows, columns).transpose(1, 0, 2)
    summed = lax.psum_scatter(halves, "rows", scatter_dimension=0, tiled=True)[0]
    blocks = summed.reshape(wide, depth // wide // 2, columns)
    place = lax.axis_index("wide")
    out = [lax.dynamic_index_in_dim(blocks, place, 0, keepdims=False)]
    for v in range(1, wide):
        block = lax.dynamic_index_in_dim(blocks, place ^ v, 0, keepdims=False)
        out.append(xor_permute(block, "wide", v))
    return placed_rows([piece[None] for piece in out], place)


def reduce_attn(grad, core, wide, rows):
    depth, columns = grad.shape
    halves = core_halves(grad, core, wide)
    place = lax.axis_index("wide")
    parts = [
        lax.dynamic_index_in_dim(halves, place ^ v, 0, keepdims=False) for v in range(wide)
    ]
    mine = to_low(scatter_wide(parts))
    pieces, start = [], 0
    for width in (3 * HD, HD, HD, HD):
        pieces.append(mine[:, start : start + width].reshape(mine.shape[0], rows, width // rows))
        start += width
    stacked = jnp.concatenate(pieces, axis=2).transpose(1, 0, 2)
    return lax.psum_scatter(stacked, "rows", scatter_dimension=0, tiled=True)[0]


def to_section(enc_half, dec_half, core):
    is_dec = core == 1
    own = jnp.where(is_dec, dec_half, enc_half)
    got = xor_permute(jnp.where(is_dec, enc_half, dec_half), "section", 1)
    low, high = jnp.where(is_dec, got, own), jnp.where(is_dec, own, got)
    return jnp.concatenate([low, high], axis=-2).astype(jnp.float32)


def shards(
    enc_embed,
    dec_embed,
    out_cot,
    enc_lengths,
    dec_lengths,
    norm_gains,
    rel_bias,
    attn_in,
    attn_out,
    ffn_in,
    ffn_out,
    cross_in,
    cross_out,
):
    core = lax.axis_index("section")
    place = lax.axis_index("wide")
    wide, rows = lax.axis_size("wide"), lax.axis_size("rows")
    depth = attn_in.shape[1]
    unit = FF // (wide * rows)

    small = jnp.concatenate([norm_gains[0].reshape(-1), rel_bias[0].reshape(-1)])
    enc_small, dec_small = both_sections(small, core)
    gains = [each[: 3 * D].reshape(3, D) for each in (enc_small, dec_small)]
    biases = [each[3 * D :].reshape(NB, H) for each in (enc_small, dec_small)]

    attn_shard = jnp.concatenate([attn_in[0], attn_out[0].T, cross_in[0], cross_out[0]], axis=1)
    attn_own = placed_rows(gather_wide(attn_shard), place)
    ffn_blocks = jnp.concatenate(
        [
            ffn_in[0].reshape(depth, 2 * rows, wide, unit).transpose(2, 0, 1, 3).reshape(wide, depth, -1),
            ffn_out[0].T.reshape(depth, rows, wide, unit).transpose(2, 0, 1, 3).reshape(wide, depth, -1),
        ],
        axis=2,
    )
    ffn_got = [lax.dynamic_index_in_dim(ffn_blocks, place, 0, keepdims=False)]
    for v in range(1, wide):
        block = lax.dynamic_index_in_dim(ffn_blocks, place ^ v, 0, keepdims=False)
        ffn_got.append(xor_permute(block, "wide", v))
    ffn_own = placed_rows(ffn_got, place)
    attn_enc, attn_dec = both_sections(attn_own, core)
    ffn_enc, ffn_dec = both_sections(ffn_own, core)
    memory_weight = attn_enc[:, 4 * HD :]
    cross_w_in, cross_w_out = attn_dec[:, 4 * HD : 5 * HD], attn_dec[:, 5 * HD :]

    def own_row(array):
        return lax.dynamic_index_in_dim(array[:, 0], core, 0, keepdims=False)

    enc_row = own_row(enc_embed).astype(jnp.float32)
    dec_row = own_row(dec_embed).astype(jnp.float32)
    cot_row = own_row(out_cot)
    enc_items = item_ids(own_row(enc_lengths), LE)
    dec_items = item_ids(own_row(dec_lengths), LD)
    enc_hot, dec_hot = one_hot(LE, True), one_hot(LD, False)
    enc_bias = jnp.einsum("qkb,bh->hqk", enc_hot, biases[0], precision=HIGHEST)
    dec_bias = jnp.einsum("qkb,bh->hqk", dec_hot, biases[1], precision=HIGHEST)
    causal = jnp.arange(LD)[:, None] >= jnp.arange(LD)[None, :]

    cot_blocks = gather_wide(cot_row)
    x1, enc_self = self_forward(
        enc_row, gains[0][0], attn_enc, enc_bias, enc_items[:, None] == enc_items[None, :]
    )
    y1, dec_self = self_forward(
        dec_row,
        gains[1][0],
        attn_dec,
        dec_bias,
        (dec_items[:, None] == dec_items[None, :]) & causal,
    )
    x2, enc_ffn = ffn_forward(x1, gains[0][1], ffn_enc)
    memory = to_low(rms_norm(x2, gains[0][2]))
    memory_kv = to_low(matmul(memory, memory_weight))
    cross_normed = to_low(rms_norm(y1, gains[1][1]))
    queries = to_low(matmul(cross_normed, cross_w_in))
    context, weights, low_weights = attend_forward(
        queries,
        memory_kv[:, :HD],
        memory_kv[:, HD:],
        0.0,
        dec_items[:, None] == enc_items[None, :],
    )
    y2 = y1 + matmul(context, cross_w_out.T)
    y3, dec_ffn = ffn_forward(y2, gains[1][2], ffn_dec)

    g2, dec_ffn_gain, dec_ffn_grads = ffn_backward(
        dec_ffn, gains[1][2], ffn_dec, cot_row.astype(jnp.float32), cot_blocks
    )
    dec_ffn_share = reduce_ffn(dec_ffn_grads, core, wide, rows)
    g2_low = to_low(g2)
    grad_cross_out = matmul(g2_low.T, context)
    grad_context = to_low(matmul(g2_low, cross_w_out))
    grad_queries, grad_keys, grad_values, _ = attend_backward(
        queries, memory_kv[:, :HD], memory_kv[:, HD:], weights, low_weights, grad_context
    )
    grad_query_low = to_low(grad_queries)
    grad_kv = to_low(jnp.concatenate([grad_keys, grad_values], axis=1))
    grad_x2, enc_final_gain = norm_backward(x2, gains[0][2], matmul(grad_kv, memory_weight.T))
    grad_x1, enc_ffn_gain, enc_ffn_grads = ffn_backward(
        enc_ffn, gains[0][1], ffn_enc, grad_x2, gather_wide(to_low(grad_x2))
    )
    enc_ffn_share = reduce_ffn(enc_ffn_grads, core, wide, rows)

    grad_cross_in = matmul(cross_normed.T, grad_query_low)
    grad_memory = matmul(memory.T, grad_kv)
    from_cross, dec_cross_gain = norm_backward(
        y1, gains[1][1], matmul(grad_query_low, cross_w_in.T)
    )
    grad_y, dec_self_gain, dec_win, dec_wout, dec_bias_grad = self_backward(
        dec_self, gains[1][0], attn_dec, dec_hot, g2 + from_cross
    )
    dec_attn_share = reduce_attn(
        jnp.concatenate([dec_win, dec_wout, grad_cross_in, grad_cross_out], axis=1),
        core,
        wide,
        rows,
    )
    grad_x, enc_self_gain, enc_win, enc_wout, enc_bias_grad = self_backward(
        enc_self, gains[0][0], attn_enc, enc_hot, grad_x1
    )
    enc_attn_share = reduce_attn(
        jnp.concatenate([enc_win, enc_wout, grad_memory], axis=1), core, wide, rows
    )

    small_grads = jnp.stack(
        [
            jnp.concatenate(
                [enc_self_gain, enc_ffn_gain, enc_final_gain, enc_bias_grad.reshape(-1)]
            ),
            jnp.concatenate(
                [dec_self_gain, dec_cross_gain, dec_ffn_gain, dec_bias_grad.reshape(-1)]
            ),
        ]
    )
    small_total = lax.psum(small_grads, ("section", "wide", "rows"))
    small_own = jnp.where(core == 1, small_total[1], small_total[0])

    attn_share = to_section(enc_attn_share, dec_attn_share, core)
    ffn_share = to_section(enc_ffn_share, dec_ffn_share, core)
    in_width = 2 * FF // rows // wide
    ffn_in_grad = (
        ffn_share[:, :, :in_width]
        .reshape(wide, depth, 2, unit)
        .transpose(1, 2, 0, 3)
        .reshape(depth, 2 * FF // rows)
    )
    ffn_out_grad = ffn_share[:, :, in_width:].transpose(0, 2, 1).reshape(FF // rows, depth)
    widths = [3 * HD // rows, HD // rows, HD // rows]
    edges = np.cumsum([0] + widths + [HD // rows])
    win, wout, cin, cout = [attn_share[:, a:b] for a, b in zip(edges[:-1], edges[1:])]

    half = D // 2

    def by_half(own):
        halves = jnp.stack([own[:, :half], own[:, half:]])
        keep = lax.dynamic_index_in_dim(halves, core, 0, keepdims=False)
        send = lax.dynamic_index_in_dim(halves, 1 - core, 0, keepdims=False)
        got = xor_permute(send, "section", 1)
        is_dec = core == 1
        return jnp.stack([jnp.where(is_dec, got, keep), jnp.where(is_dec, keep, got)])[:, None]

    return (
        by_half(to_low(y3)),
        by_half(grad_x),
        by_half(grad_y),
        small_own[: 3 * D].reshape(1, 3, D),
        small_own[3 * D :].reshape(1, NB, H),
        win[None],
        wout.T[None],
        ffn_in_grad[None],
        ffn_out_grad[None],
        cin[None],
        cout[None],
    )


def solution(mesh):
    placed = (
        P(None, ("wide", "rows"), None, None),
        P(None, ("wide", "rows"), None, None),
        P(None, ("wide", "rows"), None, None),
        P(None, ("wide", "rows"), None),
        P(None, ("wide", "rows"), None),
        P("section", None, None),
        P("section", None, None),
        P("section", "wide", None),
        P("section", None, "wide"),
        P("section", "wide", None),
        P("section", None, "wide"),
        P("section", "wide", None),
        P("section", "wide", None),
    )
    return jax.shard_map(
        shards,
        mesh=mesh,
        in_specs=placed,
        out_specs=(
            P(None, ("wide", "rows"), None, "section"),
            P(None, ("wide", "rows"), None, "section"),
            P(None, ("wide", "rows"), None, "section"),
            P("section", None, None),
            P("section", None, None),
            P("section", "wide", "rows"),
            P("section", "rows", "wide"),
            P("section", "wide", "rows"),
            P("section", "rows", "wide"),
            P("section", "wide", "rows"),
            P("section", "wide", "rows"),
        ),
        check_vma=False,
    )
```

```python
import jax
import jax.numpy as jnp
import numpy as np
from jax import lax
from jax.experimental import pallas as pl
from jax.experimental.pallas import tpu as pltpu
from jax.sharding import PartitionSpec as P

D = 1472
H = 6
DH = 64
FF = 3584
NB = 32
MAXDIST = 128
MB = 2
LE = 256
LD = 64
HD = 384


EPSILON = 1e-06
NEGATIVE = -1000000000.0
HIGHEST = lax.Precision.HIGHEST


def bucket_table(length, both_ways):
    positions = np.arange(length)
    offsets = positions[None, :] - positions[:, None]
    buckets = NB
    result = np.zeros(offsets.shape, np.int64)
    if both_ways:
        buckets = buckets // 2
        result = result + (offsets > 0) * buckets
        distance = np.abs(offsets)
    else:
        distance = np.maximum(-offsets, 0)
    exact_count = buckets // 2
    log_ratio = np.log(np.maximum(distance, 1) / exact_count) / np.log(MAXDIST / exact_count)
    far_bucket = np.minimum(
        exact_count + np.floor(log_ratio * (buckets - exact_count)).astype(np.int64), buckets - 1
    )
    return result + np.where(distance < exact_count, distance, far_bucket)


def one_hot(length, both_ways):
    bucket_ids = jnp.asarray(bucket_table(length, both_ways), jnp.int32)
    return (bucket_ids[:, :, None] == jnp.arange(NB, dtype=jnp.int32)[None, None, :]).astype(
        jnp.float32
    )


def item_ids(lengths, length):
    item_ends = jnp.cumsum(lengths)
    positions = jnp.arange(length, dtype=jnp.int32)
    return jnp.sum((positions[:, None] >= item_ends[None, :-1]).astype(jnp.int32), axis=1)


def rms_norm(residual, gain_row):
    return (
        residual
        * lax.rsqrt(jnp.mean(residual * residual, axis=-1, keepdims=True) + EPSILON)
        * gain_row
    )


def matmul(left_side, right_side):
    return jnp.dot(left_side, right_side, preferred_element_type=jnp.float32)


def to_low(tensor):
    return tensor.astype(jnp.bfloat16)


def gated(gate_part, up_part):
    return jax.nn.gelu(gate_part, approximate=True) * up_part


def attend_forward(queries, key_rows, value_rows, bias_full, allowed):
    query_count = queries.shape[0]
    heads_q = queries.reshape(query_count, H, DH)
    heads_k = key_rows.reshape(key_rows.shape[0], H, DH)
    heads_v = value_rows.reshape(value_rows.shape[0], H, DH)
    scores = (
        jnp.einsum("qhd,khd->hqk", heads_q, heads_k, preferred_element_type=jnp.float32) + bias_full
    )
    scores = jnp.where(allowed[None], scores, NEGATIVE)
    shifted = jnp.exp(scores - jnp.max(scores, axis=-1, keepdims=True))
    weights = shifted / jnp.sum(shifted, axis=-1, keepdims=True)
    low_weights = to_low(weights)
    context = jnp.einsum("hqk,khd->qhd", low_weights, heads_v, preferred_element_type=jnp.float32)
    return (to_low(context.reshape(query_count, H * DH)), weights, low_weights)


def attend_backward(queries, key_rows, value_rows, weights, low_weights, grad_context):
    query_count = queries.shape[0]
    key_count = key_rows.shape[0]
    heads_q = queries.reshape(query_count, H, DH)
    heads_k = key_rows.reshape(key_count, H, DH)
    heads_v = value_rows.reshape(key_count, H, DH)
    grad_heads = grad_context.reshape(query_count, H, DH)
    grad_weights = jnp.einsum(
        "qhd,khd->hqk", grad_heads, heads_v, preferred_element_type=jnp.float32
    )
    grad_values = jnp.einsum(
        "hqk,qhd->khd", low_weights, grad_heads, preferred_element_type=jnp.float32
    )
    grad_scores = weights * (grad_weights - jnp.sum(grad_weights * weights, axis=-1, keepdims=True))
    low_scores = to_low(grad_scores)
    grad_queries = jnp.einsum(
        "hqk,khd->qhd", low_scores, heads_k, preferred_element_type=jnp.float32
    )
    grad_keys = jnp.einsum("hqk,qhd->khd", low_scores, heads_q, preferred_element_type=jnp.float32)
    return (
        grad_queries.reshape(query_count, H * DH),
        grad_keys.reshape(key_count, H * DH),
        grad_values.reshape(key_count, H * DH),
        low_scores,
    )


def xor_permute(value, axis, distance):
    count = lax.axis_size(axis)
    return lax.ppermute(value, axis, [(i, i ^ distance) for i in range(count)])


def gather_wide(block):
    count = lax.axis_size("wide")
    if count != 4:
        return [block] + [xor_permute(block, "wide", v) for v in range(1, count)]
    half = block.shape[0] // 2
    first = xor_permute(block, "wide", 1)
    second = xor_permute(block, "wide", 2)
    third = jnp.concatenate(
        [xor_permute(first[:half], "wide", 2), xor_permute(second[half:], "wide", 1)], axis=0
    )
    return [block, first, second, third]


def scatter_wide(parts):
    count = lax.axis_size("wide")
    total = parts[0]
    if count != 4:
        for v in range(1, count):
            total = total + xor_permute(to_low(parts[v]), "wide", v).astype(jnp.float32)
        return total
    half = total.shape[0] // 2
    via_first = xor_permute(to_low(parts[3][:half]), "wide", 1).astype(jnp.float32)
    via_second = xor_permute(to_low(parts[3][half:]), "wide", 2).astype(jnp.float32)
    to_first = jnp.concatenate([parts[1][:half], parts[1][half:] + via_second], axis=0)
    to_second = jnp.concatenate([parts[2][:half] + via_first, parts[2][half:]], axis=0)
    total = total + xor_permute(to_low(to_first), "wide", 1).astype(jnp.float32)
    return total + xor_permute(to_low(to_second), "wide", 2).astype(jnp.float32)


def placed_rows(pieces, place):
    rows = pieces[0].shape[0]
    buffer = jnp.zeros((rows * len(pieces),) + pieces[0].shape[1:], pieces[0].dtype)
    for v, piece in enumerate(pieces):
        start = (place ^ v) * rows
        buffer = lax.dynamic_update_slice(buffer, piece, (start,) + (0,) * (piece.ndim - 1))
    return buffer


def both_sections(own, section):
    other = xor_permute(own, "section", 1)
    is_dec = section == 1
    return jnp.where(is_dec, other, own), jnp.where(is_dec, own, other)


def norm_backward(residual, gain_row, grad_normed):
    _, norm_pull = jax.vjp(rms_norm, residual, gain_row)
    return norm_pull(grad_normed)


def self_forward(residual, gain_row, weight, bias_full, allowed):
    normed = to_low(rms_norm(residual, gain_row))
    projected = to_low(matmul(normed, weight[:, : 3 * HD]))
    context, weights, low_weights = attend_forward(
        projected[:, :HD], projected[:, HD : 2 * HD], projected[:, 2 * HD :], bias_full, allowed
    )
    return (
        residual + matmul(context, weight[:, 3 * HD : 4 * HD].T),
        (residual, normed, projected, context, weights, low_weights),
    )


def self_backward(kept, gain_row, weight, hot, grad_out):
    residual, normed, projected, context, weights, low_weights = kept
    grad_low = to_low(grad_out)
    grad_wout = matmul(grad_low.T, context)
    grad_context = to_low(matmul(grad_low, weight[:, 3 * HD : 4 * HD]))
    grad_queries, grad_keys, grad_values, low_scores = attend_backward(
        projected[:, :HD],
        projected[:, HD : 2 * HD],
        projected[:, 2 * HD :],
        weights,
        low_weights,
        grad_context,
    )
    grad_projected = to_low(jnp.concatenate([grad_queries, grad_keys, grad_values], axis=1))
    grad_win = matmul(normed.T, grad_projected)
    grad_residual, grad_gain = norm_backward(
        residual, gain_row, matmul(grad_projected, weight[:, : 3 * HD].T)
    )
    grad_bias = jnp.einsum(
        "hqk,qkb->bh", low_scores, hot.astype(jnp.bfloat16), preferred_element_type=jnp.float32
    )
    return grad_out + grad_residual, grad_gain, grad_win, grad_wout, grad_bias


def core_halves(grad, core, wide):
    depth, columns = grad.shape
    split = to_low(grad).reshape(wide, 2, depth // wide // 2, columns)
    mine = lax.dynamic_index_in_dim(split, core, 1, keepdims=False)
    sent = lax.dynamic_index_in_dim(split, 1 - core, 1, keepdims=False)
    return mine.astype(jnp.float32) + xor_permute(sent, "section", 1).astype(jnp.float32)


def to_owners(value, axis, wide):
    place = lax.axis_index("wide")
    size = value.shape[axis] // wide

    def piece(owner):
        return lax.dynamic_slice_in_dim(value, owner * size, size, axis)

    got = [piece(place)] + [xor_permute(piece(place ^ v), "wide", v) for v in range(1, wide)]
    return placed_rows([each[None] for each in got], place)


def reduce_ffn(share_in, share_out, wide):
    summed_in = lax.psum_scatter(share_in, "rows", scatter_dimension=0, tiled=True)[0]
    summed_out = lax.psum_scatter(share_out, "rows", scatter_dimension=0, tiled=True)[0]
    return to_owners(summed_in, 0, wide), to_owners(summed_out, 1, wide)


def reduce_attn(grad, core, wide, rows):
    depth, columns = grad.shape
    halves = core_halves(grad, core, wide)
    place = lax.axis_index("wide")
    parts = [
        lax.dynamic_index_in_dim(halves, place ^ v, 0, keepdims=False) for v in range(wide)
    ]
    mine = to_low(scatter_wide(parts))
    pieces, start = [], 0
    for width in (3 * HD, HD, HD, HD):
        pieces.append(mine[:, start : start + width].reshape(mine.shape[0], rows, width // rows))
        start += width
    stacked = jnp.concatenate(pieces, axis=2).transpose(1, 0, 2)
    return lax.psum_scatter(stacked, "rows", scatter_dimension=0, tiled=True)[0]


def to_section(enc_half, dec_half, core):
    is_dec = core == 1
    own = jnp.where(is_dec, dec_half, enc_half)
    got = xor_permute(jnp.where(is_dec, enc_half, dec_half), "section", 1)
    return jnp.stack([jnp.where(is_dec, got, own), jnp.where(is_dec, own, got)])


MESH = pl.DeviceIdType.MESH
HBM = pl.BlockSpec(memory_space=pl.ANY)
VM = pl.BlockSpec(memory_space=pltpu.VMEM)
TILE = 128
VMEM_LIMIT = 60 * 1024 * 1024


def peers_of(count):
    place, core = lax.axis_index("wide"), lax.axis_index("section")
    return [{"wide": place ^ v} for v in range(1, count)] + [{"section": 1 - core}]


def greet(peers):
    barrier = pltpu.get_barrier_semaphore()
    for peer in peers:
        pl.semaphore_signal(barrier, inc=1, device_id=peer, device_id_type=MESH)
    pl.semaphore_wait(barrier, len(peers))


def remote(source, target, sems, index, peer):
    return pltpu.make_async_remote_copy(
        src_ref=source,
        dst_ref=target,
        send_sem=sems[0].at[index],
        recv_sem=sems[1].at[index],
        device_id=peer,
        device_id_type=MESH,
    )


def nt(left, right):
    return lax.dot_general(left, right, (((1,), (1,)), ((), ())), preferred_element_type=jnp.float32)


def tn(left, right):
    return lax.dot_general(left, right, (((0,), (0,)), ((), ())), preferred_element_type=jnp.float32)


class GatherPlane:
    def __init__(self, blocks, sems, base, peers, rows):
        half = rows // 2
        first, second = peers[0], peers[1]
        self.direct = [
            remote(blocks.at[0], blocks.at[1], sems, base, first),
            remote(blocks.at[0], blocks.at[2], sems, base + 1, second),
        ]
        self.passed = [
            remote(
                blocks.at[1, pl.ds(0, half)], blocks.at[3, pl.ds(0, half)], sems, base + 2, second
            ),
            remote(
                blocks.at[2, pl.ds(half, half)],
                blocks.at[3, pl.ds(half, half)],
                sems,
                base + 3,
                first,
            ),
        ]

    def start(self):
        for copy in self.direct:
            copy.start()

    def arrive(self, index):
        if index < 2:
            self.direct[index].wait_recv()
            self.passed[index].start()
        else:
            for copy in self.passed:
                copy.wait_recv()

    def finish(self):
        for copy in self.direct + self.passed:
            copy.wait_send()


class ScatterPlane:
    def __init__(self, parts, landing, sems, base, peers, rows):
        half = rows // 2
        first, second = peers[0], peers[1]
        low, high = pl.ds(0, half), pl.ds(half, half)
        self.parts, self.landing, self.half = parts, landing, half
        self.far = [
            remote(parts.at[3, low], landing.at[0, low], sems, base, first),
            remote(parts.at[3, high], landing.at[0, high], sems, base + 1, second),
        ]
        self.early = [
            remote(parts.at[1, low], landing.at[1, low], sems, base + 2, first),
            remote(parts.at[2, high], landing.at[2, high], sems, base + 3, second),
        ]
        self.late = [
            remote(parts.at[1, high], landing.at[1, high], sems, base + 4, first),
            remote(parts.at[2, low], landing.at[2, low], sems, base + 5, second),
        ]

    def send_early(self, index):
        self.early[index].start()

    def send_far(self):
        for copy in self.far:
            copy.start()

    def pass_on(self):
        low, high = pl.ds(0, self.half), pl.ds(self.half, self.half)
        self.far[0].wait_recv()
        self.parts[2, low] = (
            self.parts[2, low].astype(jnp.float32) + self.landing[0, low].astype(jnp.float32)
        ).astype(jnp.bfloat16)
        self.late[1].start()
        self.far[1].wait_recv()
        self.parts[1, high] = (
            self.parts[1, high].astype(jnp.float32) + self.landing[0, high].astype(jnp.float32)
        ).astype(jnp.bfloat16)
        self.late[0].start()

    def total(self):
        for copy in self.early + self.late:
            copy.wait_recv()
        return self.landing[1].astype(jnp.float32) + self.landing[2].astype(jnp.float32)

    def finish(self):
        for copy in self.far + self.early + self.late:
            copy.wait_send()


def rms_rows(residual):
    return lax.rsqrt(jnp.mean(residual * residual, axis=-1, keepdims=True) + EPSILON)


def norm_pull(residual, gain_row, grad_normed):
    scale = rms_rows(residual)
    unit = residual * scale
    inner = grad_normed * gain_row
    grad_residual = scale * (inner - unit * jnp.mean(inner * unit, axis=-1, keepdims=True))
    return grad_residual, jnp.sum(grad_normed * unit, axis=0, keepdims=True)


def prepare_weights_kernel(wide, rows, in_ref, out_ref, *refs):
    enc, dec = refs[:wide], refs[wide : 2 * wide]
    blocks, send_sem, recv_sem, local_sem = refs[2 * wide :]
    core, place = lax.axis_index("section"), lax.axis_index("wide")
    sibling = {"section": 1 - core}
    greet([sibling])
    units = FF // (wide * rows * 2)
    per_row = FF // rows
    row_ids = lax.broadcasted_iota(jnp.int32, (2 * TILE, TILE), 0)
    lane_ids = lax.broadcasted_iota(jnp.int32, (2 * TILE, TILE), 1)
    straight = (
        lax.broadcasted_iota(jnp.int32, (units, TILE), 0)
        == lax.broadcasted_iota(jnp.int32, (units, TILE), 1)
    ).astype(jnp.bfloat16)
    for index in range(2 * wide):
        target, half = index // 2, index % 2
        offset = index * units
        start, shift = offset // TILE * TILE, offset % TILE
        picks = ((row_ids == lane_ids + shift) & (lane_ids < units)).astype(jnp.bfloat16)
        window = min(2 * TILE, per_row - start)
        picks = picks[:window]
        for part in range(3):
            for row in range(rows):
                column = (part * rows + row) * TILE
                if part < 2:
                    source = in_ref[0, :, pl.ds(part * FF + row * per_row + start, window)]
                    tile = matmul(source, picks)
                else:
                    source = out_ref[0, pl.ds(row * per_row + offset, units), :]
                    tile = tn(source, straight)
                blocks[half, target ^ place, :, pl.ds(column, TILE)] = tile.astype(jnp.bfloat16)
    def move(outs):
        copies = []
        for v in range(wide):
            keep = pltpu.make_async_copy(blocks.at[core, v], outs[v], local_sem.at[v])
            give = remote(blocks.at[1 - core, v], outs[v], (send_sem, recv_sem), v, sibling)
            keep.start()
            give.start()
            copies += [keep]
            copies += [give]
        for keep in copies[::2]:
            keep.wait()
        for give in copies[1::2]:
            give.wait_send()

    def receive(outs):
        for v in range(wide):
            remote(blocks.at[0, v], outs[v], (send_sem, recv_sem), v, sibling).wait_recv()

    @pl.when(core == 0)
    def _():
        move(enc)
        receive(dec)

    @pl.when(core == 1)
    def _():
        move(dec)
        receive(enc)


def prepare_weights(wide, rows, ffn_in, ffn_out):
    depth = ffn_in.shape[1]
    block = jax.ShapeDtypeStruct((depth, 3 * rows * TILE), jnp.bfloat16)
    outs = pl.pallas_call(
        lambda *refs: prepare_weights_kernel(wide, rows, *refs),
        out_shape=[block] * (2 * wide),
        in_specs=[VM, VM],
        out_specs=[HBM] * (2 * wide),
        scratch_shapes=[
            pltpu.VMEM((2, wide) + block.shape, jnp.bfloat16),
            pltpu.SemaphoreType.DMA((wide,)),
            pltpu.SemaphoreType.DMA((wide,)),
            pltpu.SemaphoreType.DMA((wide,)),
        ],
        compiler_params=pltpu.CompilerParams(
            collective_id=1, has_side_effects=True, vmem_limit_bytes=VMEM_LIMIT
        ),
        name="prepare_weights",
    )(ffn_in, ffn_out)
    return outs[:wide], outs[wide:]


def ffn_forward_kernel(wide, x_ref, gain_ref, *refs):
    pieces = refs[:wide]
    y_ref, at_out, pre_out, hidden_out, weight_out = refs[wide : wide + 5]
    blocks, at, pre, hidden, weight, parts, landing, acc, send_sem, recv_sem, local_sem = refs[
        wide + 5 :
    ]
    rows = x_ref.shape[0]
    depth = pieces[0].shape[0]
    span = weight.shape[2] // 3
    core, place = lax.axis_index("section"), lax.axis_index("wide")
    peers = peers_of(wide)
    sems = (send_sem, recv_sem)
    greet(peers)
    residual = x_ref[...]
    blocks[0] = (residual * rms_rows(residual) * gain_ref[...]).astype(jnp.bfloat16)
    gather = GatherPlane(blocks, sems, 0, peers, rows)
    gather.start()
    loads, swaps = [], []
    for v in range(wide):
        place_rows = pl.ds(pl.multiple_of((place ^ v) * depth, 16), depth)
        load = pltpu.make_async_copy(pieces[v], weight.at[core, place_rows], local_sem.at[v])
        swap = remote(pieces[v], weight.at[core, place_rows], sems, 10 + v, peers[-1])
        load.start()
        swap.start()
        loads.append(load)
        swaps.append(swap)
    scatter = ScatterPlane(parts, landing, sems, 4, peers, rows)
    for v in range(wide):
        if v == 0:
            for load in loads:
                load.wait()
        else:
            gather.arrive(v - 1)
        block = blocks[v]
        for step in range(2):
            if v == 0 and step == 1:
                for swap in swaps:
                    swap.wait_recv()
            half = core if step == 0 else 1 - core
            token_rows = pl.ds(v * rows, rows)
            gate = matmul(block, weight[half, :, pl.ds(0, span)])
            up = matmul(block, weight[half, :, pl.ds(span, span)])
            pre[half, token_rows, pl.ds(0, span)] = gate.astype(jnp.bfloat16)
            pre[half, token_rows, pl.ds(span, span)] = up.astype(jnp.bfloat16)
            low = gated(gate, up).astype(jnp.bfloat16)
            hidden[half, token_rows, :] = low
            out = nt(low, weight[half, :, pl.ds(2 * span, span)])
            if step == 0:
                acc[...] = out
            elif v == 0:
                y_ref[...] = residual + acc[...] + out
            else:
                parts[v] = (acc[...] + out).astype(jnp.bfloat16)
        if v in (1, 2):
            scatter.send_early(v - 1)
        if v == 3:
            scatter.send_far()
    copies = [
        pltpu.make_async_copy(pre, pre_out, local_sem.at[4]),
        pltpu.make_async_copy(weight, weight_out, local_sem.at[5]),
    ]
    for copy in copies:
        copy.start()
    scatter.pass_on()
    at[...] = jnp.concatenate([blocks[v] for v in range(wide)], axis=0).T
    last = pltpu.make_async_copy(at, at_out, local_sem.at[6])
    last.start()
    copies.append(last)
    for half in range(2):
        hidden_out[half] = hidden[half].T
    y_ref[...] += scatter.total()
    for copy in copies:
        copy.wait()
    gather.finish()
    scatter.finish()
    for swap in swaps:
        swap.wait_send()


def ffn_forward_call(wide, residual, gain_row, pieces, call_id):
    rows = residual.shape[0]
    total = rows * wide
    columns = pieces[0].shape[1]
    span = columns // 3
    low = jnp.bfloat16
    return pl.pallas_call(
        lambda *refs: ffn_forward_kernel(wide, *refs),
        out_shape=[
            jax.ShapeDtypeStruct((rows, D), jnp.float32),
            jax.ShapeDtypeStruct((D, total), low),
            jax.ShapeDtypeStruct((2, total, 2 * span), low),
            jax.ShapeDtypeStruct((2, span, total), low),
            jax.ShapeDtypeStruct((2, D, columns), low),
        ],
        in_specs=[VM, VM] + [HBM] * wide,
        out_specs=[VM, HBM, HBM, VM, HBM],
        scratch_shapes=[
            pltpu.VMEM((wide, rows, D), low),
            pltpu.VMEM((D, total), low),
            pltpu.VMEM((2, total, 2 * span), low),
            pltpu.VMEM((2, total, span), low),
            pltpu.VMEM((2, D, columns), low),
            pltpu.VMEM((wide, rows, D), low),
            pltpu.VMEM((3, rows, D), low),
            pltpu.VMEM((rows, D), jnp.float32),
            pltpu.SemaphoreType.DMA((14,)),
            pltpu.SemaphoreType.DMA((14,)),
            pltpu.SemaphoreType.DMA((7,)),
        ],
        compiler_params=pltpu.CompilerParams(
            collective_id=call_id, has_side_effects=True, vmem_limit_bytes=VMEM_LIMIT
        ),
        name="ffn_forward_%d" % rows,
    )(residual, gain_row, *pieces)


def ffn_backward_kernel(wide, rows_axis, g_ref, x_ref, gain_ref, at_in, pre_in, hidden_in, weight_in, *refs):
    gx_ref, gain_out, grad_in, grad_out = refs[:4]
    (
        blocks,
        at,
        pre,
        hidden,
        weight,
        parts,
        landing,
        acc,
        give_in,
        give_out,
        got_in,
        got_out,
        send_sem,
        recv_sem,
        local_sem,
    ) = refs[4:]
    rows = x_ref.shape[0]
    span = weight.shape[2] // 3
    units = FF // (wide * rows_axis * 2)
    core = lax.axis_index("section")
    peers = peers_of(wide)
    sems = (send_sem, recv_sem)
    greet(peers)
    loads = [
        pltpu.make_async_copy(weight_in, weight, local_sem.at[0]),
        pltpu.make_async_copy(pre_in, pre, local_sem.at[1]),
        pltpu.make_async_copy(hidden_in, hidden, local_sem.at[2]),
        pltpu.make_async_copy(at_in, at, local_sem.at[3]),
    ]
    for load in loads:
        load.start()
    blocks[0] = g_ref[...].astype(jnp.bfloat16)
    gather = GatherPlane(blocks, sems, 0, peers, rows)
    gather.start()
    scatter = ScatterPlane(parts, landing, sems, 4, peers, rows)
    loads[0].wait()
    loads[1].wait()
    for v in range(wide):
        if v > 0:
            gather.arrive(v - 1)
        block = blocks[v]
        token_rows = pl.ds(v * rows, rows)
        for half in range(2):
            grad_hidden = matmul(block, weight[half, :, pl.ds(2 * span, span)])
            gate = pre[half, token_rows, pl.ds(0, span)].astype(jnp.float32)
            up = pre[half, token_rows, pl.ds(span, span)].astype(jnp.float32)
            inner = GELU_A * (gate + GELU_B * gate * gate * gate)
            tanh = jnp.tanh(inner)
            slope = 0.5 * (1.0 + tanh) + 0.5 * gate * (1.0 - tanh * tanh) * GELU_A * (
                1.0 + 3.0 * GELU_B * gate * gate
            )
            value = 0.5 * gate * (1.0 + tanh)
            low_gate = (grad_hidden * up * slope).astype(jnp.bfloat16)
            low_up = (grad_hidden * value).astype(jnp.bfloat16)
            pre[half, token_rows, pl.ds(0, span)] = low_gate
            pre[half, token_rows, pl.ds(span, span)] = low_up
            out = nt(low_gate, weight[half, :, pl.ds(0, span)]) + nt(
                low_up, weight[half, :, pl.ds(span, span)]
            )
            if half == 0:
                acc[...] = out
            elif v == 0:
                acc[...] += out
                gx_ref[...] = acc[...]
            else:
                parts[v] = (acc[...] + out).astype(jnp.bfloat16)
        if v in (1, 2):
            scatter.send_early(v - 1)
        if v == 3:
            scatter.send_far()
    scatter.pass_on()
    loads[2].wait()
    loads[3].wait()
    chunk = 2 * TILE

    def input_chunk(half, index):
        columns = pl.ds(pl.multiple_of(index * chunk, chunk), chunk)
        return matmul(at[...], pre[half, :, columns])

    def output_rows(half):
        return matmul(hidden[half], blocks[...].reshape(wide * rows, D))

    @pl.loop(0, rows_axis)
    def _(index):
        give_in[index] = input_chunk(1 - core, index).astype(jnp.bfloat16)

    swap_in = remote(give_in, got_in, sems, 10, peers[-1])
    swap_in.start()
    out_rows = output_rows(1 - core)
    for row in range(rows_axis):
        give_out[row] = out_rows[row * TILE : row * TILE + units].astype(jnp.bfloat16)
    swap_out = remote(give_out, got_out, sems, 11, peers[-1])
    swap_out.start()
    total = gx_ref[...] + scatter.total()
    grad_residual, grad_gain = norm_pull(x_ref[...], gain_ref[...], total)
    gx_ref[...] = g_ref[...] + grad_residual
    gain_out[...] = grad_gain
    out_rows = output_rows(core)
    swap_in.wait_recv()

    @pl.loop(0, rows_axis)
    def _(index):
        got_in[index] = (
            input_chunk(core, index) + got_in[index].astype(jnp.float32)
        ).astype(jnp.bfloat16)

    store_in = pltpu.make_async_copy(got_in, grad_in, local_sem.at[4])
    store_in.start()
    swap_out.wait_recv()
    for row in range(rows_axis):
        got_out[row] = (
            out_rows[row * TILE : row * TILE + units] + got_out[row].astype(jnp.float32)
        ).astype(jnp.bfloat16)
    store_out = pltpu.make_async_copy(got_out, grad_out, local_sem.at[5])
    store_out.start()
    store_in.wait()
    store_out.wait()
    swap_in.wait_send()
    swap_out.wait_send()
    gather.finish()
    scatter.finish()


GELU_A = float(np.sqrt(2.0 / np.pi))
GELU_B = 0.044715


def ffn_backward_call(wide, rows_axis, grad, residual, gain_row, kept, call_id):
    at, pre, hidden, weight = kept
    rows = residual.shape[0]
    low = jnp.bfloat16
    units = FF // (wide * rows_axis * 2)
    share_in = (rows_axis, D, 2 * TILE)
    share_out = (rows_axis, units, D)
    return pl.pallas_call(
        lambda *refs: ffn_backward_kernel(wide, rows_axis, *refs),
        out_shape=[
            jax.ShapeDtypeStruct((rows, D), jnp.float32),
            jax.ShapeDtypeStruct((1, D), jnp.float32),
            jax.ShapeDtypeStruct(share_in, low),
            jax.ShapeDtypeStruct(share_out, low),
        ],
        in_specs=[VM, VM, VM, HBM, HBM, HBM, HBM],
        out_specs=[VM, VM, HBM, HBM],
        scratch_shapes=[
            pltpu.VMEM((wide, rows, D), low),
            pltpu.VMEM(at.shape, low),
            pltpu.VMEM(pre.shape, low),
            pltpu.VMEM(hidden.shape, low),
            pltpu.VMEM(weight.shape, low),
            pltpu.VMEM((wide, rows, D), low),
            pltpu.VMEM((3, rows, D), low),
            pltpu.VMEM((rows, D), jnp.float32),
            pltpu.VMEM(share_in, low),
            pltpu.VMEM(share_out, low),
            pltpu.VMEM(share_in, low),
            pltpu.VMEM(share_out, low),
            pltpu.SemaphoreType.DMA((12,)),
            pltpu.SemaphoreType.DMA((12,)),
            pltpu.SemaphoreType.DMA((6,)),
        ],
        compiler_params=pltpu.CompilerParams(
            collective_id=call_id, has_side_effects=True, vmem_limit_bytes=VMEM_LIMIT
        ),
        name="ffn_backward_%d" % rows,
    )(grad, residual, gain_row, at, pre, hidden, weight)


def plain_hidden_columns(weight):
    width = weight.shape[1] * 2 // 3
    return weight[:, :width], weight[:, width:]


def plain_ffn_hidden(blocks, weight):
    w_in, _ = plain_hidden_columns(weight)
    both = [matmul(block, w_in) for block in blocks]
    units = w_in.shape[1] // 2
    return both, [to_low(gated(part[:, :units], part[:, units:])) for part in both]


def plain_ffn_forward(residual, gain_row, weight):
    blocks = gather_wide(to_low(rms_norm(residual, gain_row)))
    both, hidden = plain_ffn_hidden(blocks, weight)
    _, w_out = plain_hidden_columns(weight)
    out = residual + scatter_wide([matmul(part, w_out.T) for part in hidden])
    return out, (residual, blocks, both, hidden)


def plain_ffn_backward(kept, gain_row, weight, grad_out, grad_blocks):
    residual, blocks, both, hidden = kept
    w_in, w_out = plain_hidden_columns(weight)
    units = w_out.shape[1]
    parts, grad_both = [], []
    for block, pre in zip(grad_blocks, both):
        _, pull = jax.vjp(gated, pre[:, :units], pre[:, units:])
        grad_gate, grad_up = pull(matmul(block, w_out))
        low = to_low(jnp.concatenate([grad_gate, grad_up], axis=1))
        grad_both.append(low)
        parts.append(matmul(low, w_in.T))
    grad_residual, grad_gain = norm_backward(residual, gain_row, scatter_wide(parts))
    joined = jnp.concatenate(grad_both, axis=0)
    grad_in = matmul(jnp.concatenate(blocks, axis=0).T, joined)
    grad_wout = matmul(jnp.concatenate(grad_blocks, axis=0).T, jnp.concatenate(hidden, axis=0))
    return grad_out + grad_residual, grad_gain, (grad_in, grad_wout)


def plain_reduce_ffn(grads, core, wide, rows):
    grad_in, grad_wout = grads
    depth = grad_in.shape[0]
    both = jnp.concatenate(
        [grad_in.reshape(depth, rows, -1), grad_wout.reshape(depth, rows, -1)], axis=2
    )
    columns = both.shape[2]
    halves = core_halves(both.reshape(depth, rows * columns), core, wide)
    halves = to_low(halves).reshape(wide * (depth // wide // 2), rows, columns).transpose(1, 0, 2)
    summed = lax.psum_scatter(halves, "rows", scatter_dimension=0, tiled=True)[0]
    blocks = summed.reshape(wide, depth // wide // 2, columns)
    place = lax.axis_index("wide")
    out = [lax.dynamic_index_in_dim(blocks, place, 0, keepdims=False)]
    for v in range(1, wide):
        block = lax.dynamic_index_in_dim(blocks, place ^ v, 0, keepdims=False)
        out.append(xor_permute(block, "wide", v))
    return placed_rows([piece[None] for piece in out], place)


def plain_to_section(enc_half, dec_half, core):
    is_dec = core == 1
    own = jnp.where(is_dec, dec_half, enc_half)
    got = xor_permute(jnp.where(is_dec, enc_half, dec_half), "section", 1)
    low, high = jnp.where(is_dec, got, own), jnp.where(is_dec, own, got)
    return jnp.concatenate([low, high], axis=-2).astype(jnp.float32)


def plain_shards(
    enc_embed,
    dec_embed,
    out_cot,
    enc_lengths,
    dec_lengths,
    norm_gains,
    rel_bias,
    attn_in,
    attn_out,
    ffn_in,
    ffn_out,
    cross_in,
    cross_out,
):
    core = lax.axis_index("section")
    place = lax.axis_index("wide")
    wide, rows = lax.axis_size("wide"), lax.axis_size("rows")
    depth = attn_in.shape[1]
    unit = FF // (wide * rows)

    small = jnp.concatenate([norm_gains[0].reshape(-1), rel_bias[0].reshape(-1)])
    enc_small, dec_small = both_sections(small, core)
    gains = [each[: 3 * D].reshape(3, D) for each in (enc_small, dec_small)]
    biases = [each[3 * D :].reshape(NB, H) for each in (enc_small, dec_small)]

    attn_shard = jnp.concatenate([attn_in[0], attn_out[0].T, cross_in[0], cross_out[0]], axis=1)
    attn_own = placed_rows(gather_wide(attn_shard), place)
    ffn_blocks = jnp.concatenate(
        [
            ffn_in[0].reshape(depth, 2 * rows, wide, unit).transpose(2, 0, 1, 3).reshape(wide, depth, -1),
            ffn_out[0].T.reshape(depth, rows, wide, unit).transpose(2, 0, 1, 3).reshape(wide, depth, -1),
        ],
        axis=2,
    )
    ffn_got = [lax.dynamic_index_in_dim(ffn_blocks, place, 0, keepdims=False)]
    for v in range(1, wide):
        block = lax.dynamic_index_in_dim(ffn_blocks, place ^ v, 0, keepdims=False)
        ffn_got.append(xor_permute(block, "wide", v))
    ffn_own = placed_rows(ffn_got, place)
    attn_enc, attn_dec = both_sections(attn_own, core)
    ffn_enc, ffn_dec = both_sections(ffn_own, core)
    memory_weight = attn_enc[:, 4 * HD :]
    cross_w_in, cross_w_out = attn_dec[:, 4 * HD : 5 * HD], attn_dec[:, 5 * HD :]

    def own_row(array):
        return lax.dynamic_index_in_dim(array[:, 0], core, 0, keepdims=False)

    enc_row = own_row(enc_embed).astype(jnp.float32)
    dec_row = own_row(dec_embed).astype(jnp.float32)
    cot_row = own_row(out_cot)
    enc_items = item_ids(own_row(enc_lengths), LE)
    dec_items = item_ids(own_row(dec_lengths), LD)
    enc_hot, dec_hot = one_hot(LE, True), one_hot(LD, False)
    enc_bias = jnp.einsum("qkb,bh->hqk", enc_hot, biases[0], precision=HIGHEST)
    dec_bias = jnp.einsum("qkb,bh->hqk", dec_hot, biases[1], precision=HIGHEST)
    causal = jnp.arange(LD)[:, None] >= jnp.arange(LD)[None, :]

    cot_blocks = gather_wide(cot_row)
    x1, enc_self = self_forward(
        enc_row, gains[0][0], attn_enc, enc_bias, enc_items[:, None] == enc_items[None, :]
    )
    y1, dec_self = self_forward(
        dec_row,
        gains[1][0],
        attn_dec,
        dec_bias,
        (dec_items[:, None] == dec_items[None, :]) & causal,
    )
    x2, enc_ffn = plain_ffn_forward(x1, gains[0][1], ffn_enc)
    memory = to_low(rms_norm(x2, gains[0][2]))
    memory_kv = to_low(matmul(memory, memory_weight))
    cross_normed = to_low(rms_norm(y1, gains[1][1]))
    queries = to_low(matmul(cross_normed, cross_w_in))
    context, weights, low_weights = attend_forward(
        queries,
        memory_kv[:, :HD],
        memory_kv[:, HD:],
        0.0,
        dec_items[:, None] == enc_items[None, :],
    )
    y2 = y1 + matmul(context, cross_w_out.T)
    y3, dec_ffn = plain_ffn_forward(y2, gains[1][2], ffn_dec)

    g2, dec_ffn_gain, dec_ffn_grads = plain_ffn_backward(
        dec_ffn, gains[1][2], ffn_dec, cot_row.astype(jnp.float32), cot_blocks
    )
    dec_ffn_share = plain_reduce_ffn(dec_ffn_grads, core, wide, rows)
    g2_low = to_low(g2)
    grad_cross_out = matmul(g2_low.T, context)
    grad_context = to_low(matmul(g2_low, cross_w_out))
    grad_queries, grad_keys, grad_values, _ = attend_backward(
        queries, memory_kv[:, :HD], memory_kv[:, HD:], weights, low_weights, grad_context
    )
    grad_query_low = to_low(grad_queries)
    grad_kv = to_low(jnp.concatenate([grad_keys, grad_values], axis=1))
    grad_x2, enc_final_gain = norm_backward(x2, gains[0][2], matmul(grad_kv, memory_weight.T))
    grad_x1, enc_ffn_gain, enc_ffn_grads = plain_ffn_backward(
        enc_ffn, gains[0][1], ffn_enc, grad_x2, gather_wide(to_low(grad_x2))
    )
    enc_ffn_share = plain_reduce_ffn(enc_ffn_grads, core, wide, rows)

    grad_cross_in = matmul(cross_normed.T, grad_query_low)
    grad_memory = matmul(memory.T, grad_kv)
    from_cross, dec_cross_gain = norm_backward(
        y1, gains[1][1], matmul(grad_query_low, cross_w_in.T)
    )
    grad_y, dec_self_gain, dec_win, dec_wout, dec_bias_grad = self_backward(
        dec_self, gains[1][0], attn_dec, dec_hot, g2 + from_cross
    )
    dec_attn_share = reduce_attn(
        jnp.concatenate([dec_win, dec_wout, grad_cross_in, grad_cross_out], axis=1),
        core,
        wide,
        rows,
    )
    grad_x, enc_self_gain, enc_win, enc_wout, enc_bias_grad = self_backward(
        enc_self, gains[0][0], attn_enc, enc_hot, grad_x1
    )
    enc_attn_share = reduce_attn(
        jnp.concatenate([enc_win, enc_wout, grad_memory], axis=1), core, wide, rows
    )

    small_grads = jnp.stack(
        [
            jnp.concatenate(
                [enc_self_gain, enc_ffn_gain, enc_final_gain, enc_bias_grad.reshape(-1)]
            ),
            jnp.concatenate(
                [dec_self_gain, dec_cross_gain, dec_ffn_gain, dec_bias_grad.reshape(-1)]
            ),
        ]
    )
    small_total = lax.psum(small_grads, ("section", "wide", "rows"))
    small_own = jnp.where(core == 1, small_total[1], small_total[0])

    attn_share = plain_to_section(enc_attn_share, dec_attn_share, core)
    ffn_share = plain_to_section(enc_ffn_share, dec_ffn_share, core)
    in_width = 2 * FF // rows // wide
    ffn_in_grad = (
        ffn_share[:, :, :in_width]
        .reshape(wide, depth, 2, unit)
        .transpose(1, 2, 0, 3)
        .reshape(depth, 2 * FF // rows)
    )
    ffn_out_grad = ffn_share[:, :, in_width:].transpose(0, 2, 1).reshape(FF // rows, depth)
    widths = [3 * HD // rows, HD // rows, HD // rows]
    edges = np.cumsum([0] + widths + [HD // rows])
    win, wout, cin, cout = [attn_share[:, a:b] for a, b in zip(edges[:-1], edges[1:])]

    half = D // 2

    def by_half(own):
        halves = jnp.stack([own[:, :half], own[:, half:]])
        keep = lax.dynamic_index_in_dim(halves, core, 0, keepdims=False)
        send = lax.dynamic_index_in_dim(halves, 1 - core, 0, keepdims=False)
        got = xor_permute(send, "section", 1)
        is_dec = core == 1
        return jnp.stack([jnp.where(is_dec, got, keep), jnp.where(is_dec, keep, got)])[:, None]

    return (
        by_half(to_low(y3)),
        by_half(grad_x),
        by_half(grad_y),
        small_own[: 3 * D].reshape(1, 3, D),
        small_own[3 * D :].reshape(1, NB, H),
        win[None],
        wout.T[None],
        ffn_in_grad[None],
        ffn_out_grad[None],
        cin[None],
        cout[None],
    )


def shards(
    enc_embed,
    dec_embed,
    out_cot,
    enc_lengths,
    dec_lengths,
    norm_gains,
    rel_bias,
    attn_in,
    attn_out,
    ffn_in,
    ffn_out,
    cross_in,
    cross_out,
):
    core = lax.axis_index("section")
    place = lax.axis_index("wide")
    wide, rows = lax.axis_size("wide"), lax.axis_size("rows")
    depth = attn_in.shape[1]
    unit = FF // (wide * rows)

    small = jnp.concatenate([norm_gains[0].reshape(-1), rel_bias[0].reshape(-1)])
    enc_small, dec_small = both_sections(small, core)
    gains = [each[: 3 * D].reshape(3, D) for each in (enc_small, dec_small)]
    biases = [each[3 * D :].reshape(NB, H) for each in (enc_small, dec_small)]

    attn_shard = jnp.concatenate([attn_in[0], attn_out[0].T, cross_in[0], cross_out[0]], axis=1)
    attn_own = placed_rows(gather_wide(attn_shard), place)
    enc_blocks, dec_blocks = prepare_weights(wide, rows, ffn_in, ffn_out)
    enc_pieces = [enc_blocks[0]] + [xor_permute(enc_blocks[v], "wide", v) for v in range(1, wide)]
    dec_pieces = [dec_blocks[0]] + [xor_permute(dec_blocks[v], "wide", v) for v in range(1, wide)]
    attn_enc, attn_dec = both_sections(attn_own, core)
    memory_weight = attn_enc[:, 4 * HD :]
    cross_w_in, cross_w_out = attn_dec[:, 4 * HD : 5 * HD], attn_dec[:, 5 * HD :]

    def own_row(array):
        return lax.dynamic_index_in_dim(array[:, 0], core, 0, keepdims=False)

    enc_row = own_row(enc_embed).astype(jnp.float32)
    dec_row = own_row(dec_embed).astype(jnp.float32)
    cot_row = own_row(out_cot)
    enc_items = item_ids(own_row(enc_lengths), LE)
    dec_items = item_ids(own_row(dec_lengths), LD)
    enc_hot, dec_hot = one_hot(LE, True), one_hot(LD, False)
    enc_bias = jnp.einsum("qkb,bh->hqk", enc_hot, biases[0], precision=HIGHEST)
    dec_bias = jnp.einsum("qkb,bh->hqk", dec_hot, biases[1], precision=HIGHEST)
    causal = jnp.arange(LD)[:, None] >= jnp.arange(LD)[None, :]

    x1, enc_self = self_forward(
        enc_row, gains[0][0], attn_enc, enc_bias, enc_items[:, None] == enc_items[None, :]
    )
    y1, dec_self = self_forward(
        dec_row,
        gains[1][0],
        attn_dec,
        dec_bias,
        (dec_items[:, None] == dec_items[None, :]) & causal,
    )
    x2, *enc_ffn = ffn_forward_call(wide, x1, gains[0][1:2], enc_pieces, 2)
    memory = to_low(rms_norm(x2, gains[0][2]))
    memory_kv = to_low(matmul(memory, memory_weight))
    cross_normed = to_low(rms_norm(y1, gains[1][1]))
    queries = to_low(matmul(cross_normed, cross_w_in))
    context, weights, low_weights = attend_forward(
        queries,
        memory_kv[:, :HD],
        memory_kv[:, HD:],
        0.0,
        dec_items[:, None] == enc_items[None, :],
    )
    y2 = y1 + matmul(context, cross_w_out.T)
    y3, *dec_ffn = ffn_forward_call(wide, y2, gains[1][2:3], dec_pieces, 3)

    g2, dec_ffn_gain, *dec_ffn_grads = ffn_backward_call(
        wide, rows, cot_row.astype(jnp.float32), y2, gains[1][2:3], dec_ffn, 4
    )
    dec_ffn_share = reduce_ffn(*dec_ffn_grads, wide)
    g2_low = to_low(g2)
    grad_cross_out = matmul(g2_low.T, context)
    grad_context = to_low(matmul(g2_low, cross_w_out))
    grad_queries, grad_keys, grad_values, _ = attend_backward(
        queries, memory_kv[:, :HD], memory_kv[:, HD:], weights, low_weights, grad_context
    )
    grad_query_low = to_low(grad_queries)
    grad_kv = to_low(jnp.concatenate([grad_keys, grad_values], axis=1))
    grad_x2, enc_final_gain = norm_backward(x2, gains[0][2], matmul(grad_kv, memory_weight.T))
    grad_x1, enc_ffn_gain, *enc_ffn_grads = ffn_backward_call(
        wide, rows, grad_x2, x1, gains[0][1:2], enc_ffn, 5
    )
    enc_ffn_share = reduce_ffn(*enc_ffn_grads, wide)
    grad_cross_in = matmul(cross_normed.T, grad_query_low)
    grad_memory = matmul(memory.T, grad_kv)
    from_cross, dec_cross_gain = norm_backward(
        y1, gains[1][1], matmul(grad_query_low, cross_w_in.T)
    )
    grad_y, dec_self_gain, dec_win, dec_wout, dec_bias_grad = self_backward(
        dec_self, gains[1][0], attn_dec, dec_hot, g2 + from_cross
    )
    dec_attn_share = reduce_attn(
        jnp.concatenate([dec_win, dec_wout, grad_cross_in, grad_cross_out], axis=1),
        core,
        wide,
        rows,
    )
    grad_x, enc_self_gain, enc_win, enc_wout, enc_bias_grad = self_backward(
        enc_self, gains[0][0], attn_enc, enc_hot, grad_x1
    )
    enc_attn_share = reduce_attn(
        jnp.concatenate([enc_win, enc_wout, grad_memory], axis=1), core, wide, rows
    )

    small_grads = jnp.stack(
        [
            jnp.concatenate(
                [enc_self_gain, enc_ffn_gain[0], enc_final_gain, enc_bias_grad.reshape(-1)]
            ),
            jnp.concatenate(
                [dec_self_gain, dec_cross_gain, dec_ffn_gain[0], dec_bias_grad.reshape(-1)]
            ),
        ]
    )
    small_total = lax.psum(small_grads, ("section", "wide", "rows"))
    small_own = jnp.where(core == 1, small_total[1], small_total[0])

    attn_share = to_section(enc_attn_share, dec_attn_share, core).astype(jnp.float32)
    attn_share = attn_share.reshape(depth, attn_share.shape[2])
    in_share = to_section(enc_ffn_share[0], dec_ffn_share[0], core)
    out_share = to_section(enc_ffn_share[1], dec_ffn_share[1], core)
    units = unit // 2
    ffn_in_grad = (
        in_share.reshape(2, wide, depth, 2, TILE)[..., :units]
        .transpose(2, 3, 1, 0, 4)
        .reshape(depth, 2 * FF // rows)
        .astype(jnp.float32)
    )
    ffn_out_grad = out_share.transpose(1, 0, 2, 3).reshape(FF // rows, depth).astype(jnp.float32)
    widths = [3 * HD // rows, HD // rows, HD // rows]
    edges = np.cumsum([0] + widths + [HD // rows])
    win, wout, cin, cout = [attn_share[:, a:b] for a, b in zip(edges[:-1], edges[1:])]

    half = D // 2

    def by_half(own):
        halves = jnp.stack([own[:, :half], own[:, half:]])
        keep = lax.dynamic_index_in_dim(halves, core, 0, keepdims=False)
        send = lax.dynamic_index_in_dim(halves, 1 - core, 0, keepdims=False)
        got = xor_permute(send, "section", 1)
        is_dec = core == 1
        return jnp.stack([jnp.where(is_dec, got, keep), jnp.where(is_dec, keep, got)])[:, None]

    return (
        by_half(to_low(y3)),
        by_half(grad_x),
        by_half(grad_y),
        small_own[: 3 * D].reshape(1, 3, D),
        small_own[3 * D :].reshape(1, NB, H),
        win[None],
        wout.T[None],
        ffn_in_grad[None],
        ffn_out_grad[None],
        cin[None],
        cout[None],
    )


def solution(mesh):
    placed = (
        P(None, ("wide", "rows"), None, None),
        P(None, ("wide", "rows"), None, None),
        P(None, ("wide", "rows"), None, None),
        P(None, ("wide", "rows"), None),
        P(None, ("wide", "rows"), None),
        P("section", None, None),
        P("section", None, None),
        P("section", "wide", None),
        P("section", None, "wide"),
        P("section", "wide", None),
        P("section", None, "wide"),
        P("section", "wide", None),
        P("section", "wide", None),
    )
    wide, rows = mesh.shape["wide"], mesh.shape["rows"]
    in_tiles = D // wide % 16 == 0 and FF // (wide * rows) % 32 == 0
    return jax.shard_map(
        shards if wide == 4 and rows == 4 and in_tiles else plain_shards,
        mesh=mesh,
        in_specs=placed,
        out_specs=(
            P(None, ("wide", "rows"), None, "section"),
            P(None, ("wide", "rows"), None, "section"),
            P(None, ("wide", "rows"), None, "section"),
            P("section", None, None),
            P("section", None, None),
            P("section", "wide", "rows"),
            P("section", "rows", "wide"),
            P("section", "wide", "rows"),
            P("section", "rows", "wide"),
            P("section", "wide", "rows"),
            P("section", "wide", "rows"),
        ),
        check_vma=False,
    )
```

```python
import jax
import jax.numpy as jnp
import numpy as np
from jax import lax
from jax.experimental import pallas as pl
from jax.experimental.pallas import tpu as pltpu
from jax.sharding import PartitionSpec as P

D = 1472
H = 6
DH = 64
FF = 3584
NB = 32
MAXDIST = 128
MB = 2
LE = 256
LD = 64
HD = 384


EPSILON = 1e-06
NEGATIVE = -1000000000.0
HIGHEST = lax.Precision.HIGHEST


def bucket_table(length, both_ways):
    positions = np.arange(length)
    offsets = positions[None, :] - positions[:, None]
    buckets = NB
    result = np.zeros(offsets.shape, np.int64)
    if both_ways:
        buckets = buckets // 2
        result = result + (offsets > 0) * buckets
        distance = np.abs(offsets)
    else:
        distance = np.maximum(-offsets, 0)
    exact_count = buckets // 2
    log_ratio = np.log(np.maximum(distance, 1) / exact_count) / np.log(MAXDIST / exact_count)
    far_bucket = np.minimum(
        exact_count + np.floor(log_ratio * (buckets - exact_count)).astype(np.int64), buckets - 1
    )
    return result + np.where(distance < exact_count, distance, far_bucket)


def one_hot(length, both_ways):
    bucket_ids = jnp.asarray(bucket_table(length, both_ways), jnp.int32)
    return (bucket_ids[:, :, None] == jnp.arange(NB, dtype=jnp.int32)[None, None, :]).astype(
        jnp.float32
    )


def item_ids(lengths, length):
    item_ends = jnp.cumsum(lengths)
    positions = jnp.arange(length, dtype=jnp.int32)
    return jnp.sum((positions[:, None] >= item_ends[None, :-1]).astype(jnp.int32), axis=1)


def rms_norm(residual, gain_row):
    return (
        residual
        * lax.rsqrt(jnp.mean(residual * residual, axis=-1, keepdims=True) + EPSILON)
        * gain_row
    )


def matmul(left_side, right_side):
    return jnp.dot(left_side, right_side, preferred_element_type=jnp.float32)


def matmul_exact(left_side, right_side):
    return jnp.dot(left_side, right_side, precision=HIGHEST)


def to_low(tensor):
    return tensor.astype(jnp.bfloat16)


def gated(gate_part, up_part):
    return jax.nn.gelu(gate_part, approximate=True) * up_part


def attend_forward(queries, key_rows, value_rows, bias_full, allowed):
    query_count = queries.shape[0]
    heads_q = queries.reshape(query_count, H, DH)
    heads_k = key_rows.reshape(key_rows.shape[0], H, DH)
    heads_v = value_rows.reshape(value_rows.shape[0], H, DH)
    scores = (
        jnp.einsum("qhd,khd->hqk", heads_q, heads_k, preferred_element_type=jnp.float32) + bias_full
    )
    scores = jnp.where(allowed[None], scores, NEGATIVE)
    shifted = jnp.exp(scores - jnp.max(scores, axis=-1, keepdims=True))
    weights = shifted / jnp.sum(shifted, axis=-1, keepdims=True)
    low_weights = to_low(weights)
    context = jnp.einsum("hqk,khd->qhd", low_weights, heads_v, preferred_element_type=jnp.float32)
    return (to_low(context.reshape(query_count, H * DH)), weights, low_weights)


def attend_backward(queries, key_rows, value_rows, weights, low_weights, grad_context):
    query_count = queries.shape[0]
    key_count = key_rows.shape[0]
    heads_q = queries.reshape(query_count, H, DH)
    heads_k = key_rows.reshape(key_count, H, DH)
    heads_v = value_rows.reshape(key_count, H, DH)
    grad_heads = grad_context.reshape(query_count, H, DH)
    grad_weights = jnp.einsum(
        "qhd,khd->hqk", grad_heads, heads_v, preferred_element_type=jnp.float32
    )
    grad_values = jnp.einsum(
        "hqk,qhd->khd", low_weights, grad_heads, preferred_element_type=jnp.float32
    )
    grad_scores = weights * (grad_weights - jnp.sum(grad_weights * weights, axis=-1, keepdims=True))
    low_scores = to_low(grad_scores)
    grad_queries = jnp.einsum(
        "hqk,khd->qhd", low_scores, heads_k, preferred_element_type=jnp.float32
    )
    grad_keys = jnp.einsum("hqk,qhd->khd", low_scores, heads_q, preferred_element_type=jnp.float32)
    return (
        grad_queries.reshape(query_count, H * DH),
        grad_keys.reshape(key_count, H * DH),
        grad_values.reshape(key_count, H * DH),
        low_scores,
    )


def xor_permute(value, axis, distance):
    count = lax.axis_size(axis)
    return lax.ppermute(value, axis, [(i, i ^ distance) for i in range(count)])


def gather_wide(block):
    count = lax.axis_size("wide")
    if count != 4:
        return [block] + [xor_permute(block, "wide", v) for v in range(1, count)]
    half = block.shape[0] // 2
    first = xor_permute(block, "wide", 1)
    second = xor_permute(block, "wide", 2)
    third = jnp.concatenate(
        [xor_permute(first[:half], "wide", 2), xor_permute(second[half:], "wide", 1)], axis=0
    )
    return [block, first, second, third]


def scatter_wide(parts):
    count = lax.axis_size("wide")
    total = parts[0]
    if count != 4:
        for v in range(1, count):
            total = total + xor_permute(to_low(parts[v]), "wide", v).astype(jnp.float32)
        return total
    half = total.shape[0] // 2
    via_first = xor_permute(to_low(parts[3][:half]), "wide", 1).astype(jnp.float32)
    via_second = xor_permute(to_low(parts[3][half:]), "wide", 2).astype(jnp.float32)
    to_first = jnp.concatenate([parts[1][:half], parts[1][half:] + via_second], axis=0)
    to_second = jnp.concatenate([parts[2][:half] + via_first, parts[2][half:]], axis=0)
    total = total + xor_permute(to_low(to_first), "wide", 1).astype(jnp.float32)
    return total + xor_permute(to_low(to_second), "wide", 2).astype(jnp.float32)


def placed_rows(pieces, place):
    rows = pieces[0].shape[0]
    buffer = jnp.zeros((rows * len(pieces),) + pieces[0].shape[1:], pieces[0].dtype)
    for v, piece in enumerate(pieces):
        start = (place ^ v) * rows
        buffer = lax.dynamic_update_slice(buffer, piece, (start,) + (0,) * (piece.ndim - 1))
    return buffer


MESH = pl.DeviceIdType.MESH
HBM = pl.BlockSpec(memory_space=pl.ANY)
VM = pl.BlockSpec(memory_space=pltpu.VMEM)
TILE = 128
VMEM_LIMIT = 60 * 1024 * 1024


def peers_of(count):
    place, core = lax.axis_index("wide"), lax.axis_index("section")
    return [{"wide": place ^ v} for v in range(1, count)] + [{"section": 1 - core}]


def greet(peers):
    barrier = pltpu.get_barrier_semaphore()
    for peer in peers:
        pl.semaphore_signal(barrier, inc=1, device_id=peer, device_id_type=MESH)
    pl.semaphore_wait(barrier, len(peers))


def remote(source, target, sems, index, peer):
    return pltpu.make_async_remote_copy(
        src_ref=source,
        dst_ref=target,
        send_sem=sems[0].at[index],
        recv_sem=sems[1].at[index],
        device_id=peer,
        device_id_type=MESH,
    )


def nt(left, right):
    return lax.dot_general(left, right, (((1,), (1,)), ((), ())), preferred_element_type=jnp.float32)


def tn(left, right):
    return lax.dot_general(left, right, (((0,), (0,)), ((), ())), preferred_element_type=jnp.float32)


class GatherPlane:
    def __init__(self, blocks, sems, base, peers, rows):
        half = split_at(rows)
        rest = rows - half
        first, second = peers[0], peers[1]
        self.direct = [
            remote(blocks.at[0], blocks.at[1], sems, base, first),
            remote(blocks.at[0], blocks.at[2], sems, base + 1, second),
        ]
        self.passed = [
            remote(
                blocks.at[1, pl.ds(0, half)], blocks.at[3, pl.ds(0, half)], sems, base + 2, second
            ),
            remote(
                blocks.at[2, pl.ds(half, rest)],
                blocks.at[3, pl.ds(half, rest)],
                sems,
                base + 3,
                first,
            ),
        ]

    def start(self):
        for copy in self.direct:
            copy.start()

    def arrive(self, index):
        if index < 2:
            self.direct[index].wait_recv()
            self.passed[index].start()
        else:
            for copy in self.passed:
                copy.wait_recv()

    def finish(self):
        for copy in self.direct + self.passed:
            copy.wait_send()


class ScatterPlane:
    def __init__(self, parts, landing, sems, base, peers, rows):
        half = split_at(rows)
        first, second = peers[0], peers[1]
        low, high = pl.ds(0, half), pl.ds(half, rows - half)
        self.parts, self.landing, self.low, self.high = parts, landing, low, high
        self.far = [
            remote(parts.at[3, low], landing.at[0, low], sems, base, first),
            remote(parts.at[3, high], landing.at[0, high], sems, base + 1, second),
        ]
        self.early = [
            remote(parts.at[1, low], landing.at[1, low], sems, base + 2, first),
            remote(parts.at[2, high], landing.at[2, high], sems, base + 3, second),
        ]
        self.late = [
            remote(parts.at[1, high], landing.at[1, high], sems, base + 4, first),
            remote(parts.at[2, low], landing.at[2, low], sems, base + 5, second),
        ]

    def send_early(self, index):
        self.early[index].start()

    def send_far(self):
        for copy in self.far:
            copy.start()

    def pass_on(self):
        low, high = self.low, self.high
        self.far[0].wait_recv()
        self.parts[2, low] = (
            self.parts[2, low].astype(jnp.float32) + self.landing[0, low].astype(jnp.float32)
        ).astype(jnp.bfloat16)
        self.late[1].start()
        self.far[1].wait_recv()
        self.parts[1, high] = (
            self.parts[1, high].astype(jnp.float32) + self.landing[0, high].astype(jnp.float32)
        ).astype(jnp.bfloat16)
        self.late[0].start()

    def total(self):
        for copy in self.early + self.late:
            copy.wait_recv()
        return self.landing[1].astype(jnp.float32) + self.landing[2].astype(jnp.float32)

    def finish(self):
        for copy in self.far + self.early + self.late:
            copy.wait_send()


def rms_rows(residual):
    return lax.rsqrt(jnp.mean(residual * residual, axis=-1, keepdims=True) + EPSILON)


def norm_pull(residual, gain_row, grad_normed):
    scale = rms_rows(residual)
    unit = residual * scale
    inner = grad_normed * gain_row
    grad_residual = scale * (inner - unit * jnp.mean(inner * unit, axis=-1, keepdims=True))
    return grad_residual, jnp.sum(grad_normed * unit, axis=0, keepdims=True)


def token_groups(wide, rows):
    if rows >= 2 * TILE:
        return [[v] for v in range(wide)]
    return [list(range(wide))]


class ReduceRows:
    def __init__(self, source_in, source_out, in_buf, in_land, out_buf, out_land, sems, base, local_sem, local_base):
        row = lax.axis_index("rows")
        near, far = {"rows": row ^ 1}, {"rows": row ^ 2}
        self.bufs, self.lands, self.first, self.second = [], [], [], []
        lanes = [pl.ds(0, TILE), pl.ds(TILE, TILE)]
        views = [
            (lambda ref, i, part=part: ref.at[i, :, part], source_in, in_buf, in_land)
            for part in lanes
        ] + [(lambda ref, i: ref.at[i], source_out, out_buf, out_land)]
        for index, (view, source, buf, land) in enumerate(views):
            at = base + 3 * index
            self.first.append(
                [
                    remote(view(source, row ^ 1), view(land, 0), sems, at, near),
                    remote(view(source, row ^ 3), view(land, 1), sems, at + 1, near),
                ]
            )
            self.second.append(remote(view(buf, 1), view(land, 2), sems, at + 2, far))
            self.bufs.append([view(buf, 0), view(buf, 1)])
            self.lands.append([view(land, i) for i in range(3)])
        self.loads = [
            pltpu.make_async_copy(source.at[place], buf.at[i], local_sem.at[local_base + 2 * j + i])
            for j, (source, buf) in enumerate(((source_in, in_buf), (source_out, out_buf)))
            for i, place in enumerate((row, row ^ 2))
        ]

    def start(self):
        for pair in self.first:
            for copy in pair:
                copy.start()
        for load in self.loads:
            load.start()

    def loaded(self):
        for load in self.loads:
            load.wait()

    def add(self, index, which, land):
        ref = self.bufs[index][which]
        ref[...] = (
            ref[...].astype(jnp.float32) + self.lands[index][land][...].astype(jnp.float32)
        ).astype(jnp.bfloat16)

    def turn(self, index):
        for copy in self.first[index]:
            copy.wait_recv()
        self.add(index, 1, 1)
        self.second[index].start()
        self.add(index, 0, 0)

    def close(self, index):
        self.second[index].wait_recv()
        self.add(index, 0, 2)

    def finish(self):
        for pair, copy in zip(self.first, self.second):
            for each in pair:
                each.wait_send()
            copy.wait_send()


def reduce_rows_scratch(units):
    low = jnp.bfloat16
    return [
        pltpu.VMEM((2, D, 2 * TILE), low),
        pltpu.VMEM((3, D, 2 * TILE), low),
        pltpu.VMEM((2, units, D), low),
        pltpu.VMEM((3, units, D), low),
    ]


def ffn_forward_kernel(wide, x_ref, gain_ref, *refs):
    pieces = refs[:wide]
    y_ref, at_out, pre_out, hidden_out, weight_out = refs[wide : wide + 5]
    blocks, at, pre, hidden, weight, parts, landing, acc, send_sem, recv_sem, local_sem = refs[
        wide + 5 :
    ]
    rows = x_ref.shape[0]
    depth = pieces[0].shape[0]
    span = weight.shape[2] // 3
    core, place = lax.axis_index("section"), lax.axis_index("wide")
    peers = peers_of(wide)
    sems = (send_sem, recv_sem)
    greet(peers)
    residual = x_ref[...]
    blocks[0] = (residual * rms_rows(residual) * gain_ref[...]).astype(jnp.bfloat16)
    gather = GatherPlane(blocks, sems, 0, peers, rows)
    gather.start()
    loads, swaps = [], []
    for v in range(wide):
        place_rows = pl.ds(pl.multiple_of((place ^ v) * depth, 16), depth)
        load = pltpu.make_async_copy(pieces[v], weight.at[core, place_rows], local_sem.at[v])
        swap = remote(pieces[v], weight.at[core, place_rows], sems, 10 + v, peers[-1])
        load.start()
        swap.start()
        loads.append(load)
        swaps.append(swap)
    scatter = ScatterPlane(parts, landing, sems, 4, peers, rows)
    for group in token_groups(wide, rows):
        for v in group:
            if v > 0:
                gather.arrive(v - 1)
        if group[0] == 0:
            for load in loads:
                load.wait()
        count = len(group) * rows
        block = blocks[group[0] : group[-1] + 1].reshape(count, D)
        token_rows = pl.ds(group[0] * rows, count)
        for step in range(2):
            if group[0] == 0 and step == 1:
                for swap in swaps:
                    swap.wait_recv()
            half = core if step == 0 else 1 - core
            gate = matmul(block, weight[half, :, pl.ds(0, span)])
            up = matmul(block, weight[half, :, pl.ds(span, span)])
            pre[half, token_rows, pl.ds(0, span)] = gate.astype(jnp.bfloat16)
            pre[half, token_rows, pl.ds(span, span)] = up.astype(jnp.bfloat16)
            low = gated(gate, up).astype(jnp.bfloat16)
            hidden[half, token_rows, :] = low
            out = nt(low, weight[half, :, pl.ds(2 * span, span)])
            if step == 0:
                acc[...] = out
                continue
            for i, v in enumerate(group):
                own = slice(i * rows, (i + 1) * rows)
                if v == 0:
                    y_ref[...] = residual + acc[own] + out[own]
                else:
                    parts[v] = (acc[own] + out[own]).astype(jnp.bfloat16)
        for v in group:
            if v in (1, 2):
                scatter.send_early(v - 1)
            if v == 3:
                scatter.send_far()
    copies = [
        pltpu.make_async_copy(pre, pre_out, local_sem.at[4]),
        pltpu.make_async_copy(weight, weight_out, local_sem.at[5]),
    ]
    for copy in copies:
        copy.start()
    scatter.pass_on()
    at[...] = jnp.concatenate([blocks[v] for v in range(wide)], axis=0).T
    last = pltpu.make_async_copy(at, at_out, local_sem.at[6])
    last.start()
    copies.append(last)
    for half in range(2):
        hidden_out[half] = hidden[half].T
    y_ref[...] += scatter.total()
    for copy in copies:
        copy.wait()
    gather.finish()
    scatter.finish()
    for swap in swaps:
        swap.wait_send()


def ffn_forward_call(wide, residual, gain_row, pieces, call_id):
    rows = residual.shape[0]
    total = rows * wide
    columns = pieces[0].shape[1]
    span = columns // 3
    low = jnp.bfloat16
    return pl.pallas_call(
        lambda *refs: ffn_forward_kernel(wide, *refs),
        out_shape=[
            jax.ShapeDtypeStruct((rows, D), jnp.float32),
            jax.ShapeDtypeStruct((D, total), low),
            jax.ShapeDtypeStruct((2, total, 2 * span), low),
            jax.ShapeDtypeStruct((2, span, total), low),
            jax.ShapeDtypeStruct((2, D, columns), low),
        ],
        in_specs=[VM, VM] + [HBM] * wide,
        out_specs=[VM, HBM, HBM, VM, HBM],
        scratch_shapes=[
            pltpu.VMEM((wide, rows, D), low),
            pltpu.VMEM((D, total), low),
            pltpu.VMEM((2, total, 2 * span), low),
            pltpu.VMEM((2, total, span), low),
            pltpu.VMEM((2, D, columns), low),
            pltpu.VMEM((wide, rows, D), low),
            pltpu.VMEM((3, rows, D), low),
            pltpu.VMEM((len(token_groups(wide, rows)[0]) * rows, D), jnp.float32),
            pltpu.SemaphoreType.DMA((14,)),
            pltpu.SemaphoreType.DMA((14,)),
            pltpu.SemaphoreType.DMA((7,)),
        ],
        compiler_params=pltpu.CompilerParams(
            collective_id=call_id, has_side_effects=True, vmem_limit_bytes=VMEM_LIMIT
        ),
        name="ffn_forward_%d" % rows,
    )(residual, gain_row, *pieces)


def ffn_backward_kernel(
    wide, rows_axis, g_ref, x_ref, gain_ref, at_in, pre_in, hidden_in, weight_in, *refs
):
    carried = len(refs) > 21
    if carried:
        ready_in, ready_out = refs[:2]
        refs = refs[2:]
    gx_ref, gain_out, grad_in, grad_out = refs[:4]
    refs = refs[4:]
    if carried:
        sum_in, sum_out = refs[:2]
        refs = refs[2:]
    (
        blocks,
        at,
        pre,
        hidden,
        weight,
        parts,
        landing,
        acc,
        give_in,
        give_out,
        got_in,
        got_out,
        send_sem,
        recv_sem,
        local_sem,
    ) = refs[:15]
    rows = x_ref.shape[0]
    span = weight.shape[2] // 3
    units = FF // (wide * rows_axis * 2)
    core, row = lax.axis_index("section"), lax.axis_index("rows")
    peers = peers_of(wide)
    sems = (send_sem, recv_sem)
    greet(peers + ([{"rows": row ^ 1}, {"rows": row ^ 2}] if carried else []))
    loads = [
        pltpu.make_async_copy(weight_in, weight, local_sem.at[0]),
        pltpu.make_async_copy(pre_in, pre, local_sem.at[1]),
        pltpu.make_async_copy(hidden_in, hidden, local_sem.at[2]),
        pltpu.make_async_copy(at_in, at, local_sem.at[3]),
    ]
    blocks[0] = g_ref[...].astype(jnp.bfloat16)
    gather = GatherPlane(blocks, sems, 0, peers, rows)
    gather.start()
    for load in loads:
        load.start()
    if carried:
        line = ReduceRows(ready_in, ready_out, *refs[15:19], sems, 12, local_sem, 6)
        line.start()
    scatter = ScatterPlane(parts, landing, sems, 4, peers, rows)
    loads[0].wait()
    loads[1].wait()
    for group in token_groups(wide, rows):
        for v in group:
            if v > 0:
                if carried and v == 3:
                    line.loaded()
                    line.turn(0)
                gather.arrive(v - 1)
        count = len(group) * rows
        block = blocks[group[0] : group[-1] + 1].reshape(count, D)
        token_rows = pl.ds(group[0] * rows, count)
        for half in range(2):
            grad_hidden = matmul(block, weight[half, :, pl.ds(2 * span, span)])
            gate = pre[half, token_rows, pl.ds(0, span)].astype(jnp.float32)
            up = pre[half, token_rows, pl.ds(span, span)].astype(jnp.float32)
            square = gate * gate
            tanh = jnp.tanh(GELU_A * gate * (1.0 + GELU_B * square))
            upper = 0.5 * (1.0 + tanh)
            slope = upper + 0.5 * gate * (1.0 - tanh * tanh) * (
                GELU_A + 3.0 * GELU_A * GELU_B * square
            )
            low_gate = (grad_hidden * up * slope).astype(jnp.bfloat16)
            low_up = (grad_hidden * (gate * upper)).astype(jnp.bfloat16)
            pre[half, token_rows, pl.ds(0, span)] = low_gate
            pre[half, token_rows, pl.ds(span, span)] = low_up
            out = nt(low_gate, weight[half, :, pl.ds(0, span)]) + nt(
                low_up, weight[half, :, pl.ds(span, span)]
            )
            if half == 0:
                acc[...] = out
                continue
            for i, v in enumerate(group):
                own = slice(i * rows, (i + 1) * rows)
                if v == 0:
                    gx_ref[...] = acc[own] + out[own]
                else:
                    parts[v] = (acc[own] + out[own]).astype(jnp.bfloat16)
        for v in group:
            if v in (1, 2):
                scatter.send_early(v - 1)
            if v == 3:
                scatter.send_far()
    loads[2].wait()
    loads[3].wait()
    chunk = 2 * TILE

    def input_chunk(half, index):
        columns = pl.ds(pl.multiple_of(index * chunk, chunk), chunk)
        return matmul(at[...], pre[half, :, columns])

    def output_rows(half):
        return matmul(hidden[half], blocks[...].reshape(wide * rows, D))

    if carried:
        line.turn(1)
    out_rows = output_rows(1 - core)
    for index in range(rows_axis):
        give_out[index] = out_rows[index * TILE : index * TILE + units].astype(jnp.bfloat16)
    swap_out = remote(give_out, got_out, sems, 11, peers[-1])
    swap_out.start()
    scatter.pass_on()

    @pl.loop(0, rows_axis)
    def _(index):
        give_in[index] = input_chunk(1 - core, index).astype(jnp.bfloat16)

    swap_in = remote(give_in, got_in, sems, 10, peers[-1])
    swap_in.start()
    if carried:
        line.turn(2)
    out_rows = output_rows(core)
    swap_out.wait_recv()
    for index in range(rows_axis):
        got_out[index] = (
            out_rows[index * TILE : index * TILE + units] + got_out[index].astype(jnp.float32)
        ).astype(jnp.bfloat16)
    store_out = pltpu.make_async_copy(got_out, grad_out, local_sem.at[5])
    store_out.start()
    swap_in.wait_recv()

    @pl.loop(0, rows_axis)
    def _(index):
        got_in[index] = (
            input_chunk(core, index) + got_in[index].astype(jnp.float32)
        ).astype(jnp.bfloat16)

    store_in = pltpu.make_async_copy(got_in, grad_in, local_sem.at[4])
    store_in.start()
    total = gx_ref[...] + scatter.total()
    grad_residual, grad_gain = norm_pull(x_ref[...], gain_ref[...], total)
    gx_ref[...] = g_ref[...] + grad_residual
    gain_out[...] = grad_gain
    if carried:
        for index in range(3):
            line.close(index)
        in_buf, out_buf = refs[15], refs[17]
        stores = [
            pltpu.make_async_copy(in_buf.at[0], sum_in, local_sem.at[6]),
            pltpu.make_async_copy(out_buf.at[0], sum_out, local_sem.at[7]),
        ]
        for store in stores:
            store.start()
        for store in stores:
            store.wait()
        line.finish()
    store_in.wait()
    store_out.wait()
    swap_in.wait_send()
    swap_out.wait_send()
    gather.finish()
    scatter.finish()


GELU_A = float(np.sqrt(2.0 / np.pi))
GELU_B = 0.044715


def ffn_backward_call(wide, rows_axis, grad, residual, gain_row, kept, call_id, carried=()):
    at, pre, hidden, weight = kept
    rows = residual.shape[0]
    low = jnp.bfloat16
    units = FF // (wide * rows_axis * 2)
    share_in = (rows_axis, D, 2 * TILE)
    share_out = (rows_axis, units, D)
    sums = [jax.ShapeDtypeStruct(each.shape[1:], low) for each in carried]
    return pl.pallas_call(
        lambda *refs: ffn_backward_kernel(wide, rows_axis, *refs),
        out_shape=[
            jax.ShapeDtypeStruct((rows, D), jnp.float32),
            jax.ShapeDtypeStruct((1, D), jnp.float32),
            jax.ShapeDtypeStruct(share_in, low),
            jax.ShapeDtypeStruct(share_out, low),
        ]
        + sums,
        in_specs=[VM, VM, VM, HBM, HBM, HBM, HBM] + [HBM] * len(sums),
        out_specs=[VM, VM, HBM, HBM] + [HBM] * len(sums),
        scratch_shapes=[
            pltpu.VMEM((wide, rows, D), low),
            pltpu.VMEM(at.shape, low),
            pltpu.VMEM(pre.shape, low),
            pltpu.VMEM(hidden.shape, low),
            pltpu.VMEM(weight.shape, low),
            pltpu.VMEM((wide, rows, D), low),
            pltpu.VMEM((3, rows, D), low),
            pltpu.VMEM((len(token_groups(wide, rows)[0]) * rows, D), jnp.float32),
            pltpu.VMEM(share_in, low),
            pltpu.VMEM(share_out, low),
            pltpu.VMEM(share_in, low),
            pltpu.VMEM(share_out, low),
            pltpu.SemaphoreType.DMA((21,)),
            pltpu.SemaphoreType.DMA((21,)),
            pltpu.SemaphoreType.DMA((10,)),
        ]
        + (reduce_rows_scratch(units) if carried else []),
        compiler_params=pltpu.CompilerParams(
            collective_id=call_id, has_side_effects=True, vmem_limit_bytes=VMEM_LIMIT
        ),
        name="ffn_backward_%d" % rows,
    )(grad, residual, gain_row, at, pre, hidden, weight, *carried)


def start_weights_kernel(
    wide, rows, win_in, wout_in, cin_in, cout_in, ffn_in, ffn_out, attn_ref, dec_half, *refs
):
    enc, dec = refs[:wide], refs[wide : 2 * wide]
    held, blocks, spare, in_ref, out_ref, ffn, send_sem, recv_sem, local_sem = refs[2 * wide :]
    core, place = lax.axis_index("section"), lax.axis_index("wide")
    peers = peers_of(wide)
    sibling = peers[-1]
    sems = (send_sem, recv_sem)
    depth = blocks.shape[1]
    big = [
        pltpu.make_async_copy(ffn_in.at[0], in_ref, local_sem.at[4]),
        pltpu.make_async_copy(ffn_out.at[0], out_ref, local_sem.at[5]),
    ]
    packs = [
        pltpu.make_async_copy(each, held.at[:, pl.ds(i * HD, HD)], local_sem.at[1 + i])
        for i, each in enumerate((wout_in, cin_in.at[0], cout_in.at[0]))
    ]
    for pack in packs:
        pack.start()
    greet(peers)
    for pack in packs:
        pack.wait()

    @pl.when(core == 0)
    def _():
        keep = pltpu.make_async_copy(win_in.at[0], blocks.at[0], local_sem.at[0])
        keep.start()
        give = remote(held, blocks.at[0], sems, 0, sibling)
        give.start()
        remote(win_in.at[0], spare, sems, 1, sibling).wait_recv()
        keep.wait()

    @pl.when(core == 1)
    def _():
        keep = pltpu.make_async_copy(held, spare, local_sem.at[0])
        keep.start()
        give = remote(win_in.at[0], spare, sems, 1, sibling)
        give.start()
        remote(held, blocks.at[0], sems, 0, sibling).wait_recv()
        keep.wait()

    gather = GatherPlane(blocks, sems, 2, peers, depth)
    gather.start()
    for load in big:
        load.start()
    dec_copy = pltpu.make_async_copy(spare, dec_half, local_sem.at[0])
    dec_copy.start()
    stores, gives = [], []
    for v in range(wide):
        rows_of = pl.ds(pl.multiple_of((place ^ v) * depth, 16), depth)
        stores.append(
            pltpu.make_async_copy(blocks.at[v], attn_ref.at[core, rows_of], local_sem.at[6 + v])
        )
        gives.append(remote(blocks.at[v], attn_ref.at[core, rows_of], sems, 6 + v, sibling))
    stores[0].start()
    gives[0].start()
    for load in big:
        load.wait()
    units = FF // (wide * rows * 2)
    per_row = FF // rows
    row_ids = lax.broadcasted_iota(jnp.int32, (2 * TILE, TILE), 0)
    lane_ids = lax.broadcasted_iota(jnp.int32, (2 * TILE, TILE), 1)
    straight = (
        lax.broadcasted_iota(jnp.int32, (units, TILE), 0)
        == lax.broadcasted_iota(jnp.int32, (units, TILE), 1)
    ).astype(jnp.bfloat16)

    def prepare(index):
        target, half = index // 2, index % 2
        offset = index * units
        start, shift = offset // TILE * TILE, offset % TILE
        picks = ((row_ids == lane_ids + shift) & (lane_ids < units)).astype(jnp.bfloat16)
        window = min(2 * TILE, per_row - start)
        picks = picks[:window]
        for part in range(3):
            for row in range(rows):
                column = (part * rows + row) * TILE
                if part < 2:
                    source = in_ref[:, pl.ds(part * FF + row * per_row + start, window)]
                    tile = matmul(source, picks)
                else:
                    source = out_ref[pl.ds(row * per_row + offset, units), :]
                    tile = tn(source, straight)
                ffn[half, target ^ place, :, pl.ds(column, TILE)] = tile.astype(jnp.bfloat16)

    for index in range(2 * wide):
        prepare(index)

    def move(outs, base):
        for v in range(wide):
            pltpu.make_async_copy(ffn.at[core, v], outs[v], local_sem.at[10 + v]).start()
            remote(ffn.at[1 - core, v], outs[v], sems, base + v, sibling).start()

    def settle(outs, base):
        for v in range(wide):
            pltpu.make_async_copy(ffn.at[core, v], outs[v], local_sem.at[10 + v]).wait()
            remote(ffn.at[1 - core, v], outs[v], sems, base + v, sibling).wait_send()

    def receive(outs, base):
        for v in range(wide):
            remote(ffn.at[0, v], outs[v], sems, base + v, sibling).wait_recv()

    @pl.when(core == 0)
    def _():
        move(enc, 10)

    @pl.when(core == 1)
    def _():
        move(dec, 10 + wide)

    for v in range(1, wide):
        gather.arrive(v - 1)
        stores[v].start()
        gives[v].start()
    for v in range(wide):
        gives[v].wait_recv()
        stores[v].wait()
    dec_copy.wait()

    @pl.when(core == 0)
    def _():
        settle(enc, 10)
        receive(dec, 10 + wide)
        remote(held, blocks.at[0], sems, 0, sibling).wait_send()

    @pl.when(core == 1)
    def _():
        settle(dec, 10 + wide)
        receive(enc, 10)
        remote(win_in.at[0], spare, sems, 1, sibling).wait_send()

    gather.finish()
    for give in gives:
        give.wait_send()


def start_weights(wide, rows, attn_in, attn_out, cross_in, cross_out, ffn_in, ffn_out):
    depth = ffn_in.shape[1]
    low = jnp.bfloat16
    block = jax.ShapeDtypeStruct((depth, 3 * rows * TILE), low)
    part = (depth, 3 * HD)
    attn, dec_half, *outs = pl.pallas_call(
        lambda *refs: start_weights_kernel(wide, rows, *refs),
        out_shape=[
            jax.ShapeDtypeStruct((2, wide * depth, 3 * HD), low),
            jax.ShapeDtypeStruct(part, low),
        ]
        + [block] * (2 * wide),
        in_specs=[HBM] * 6,
        out_specs=[HBM] * (2 + 2 * wide),
        scratch_shapes=[
            pltpu.VMEM(part, low),
            pltpu.VMEM((wide,) + part, low),
            pltpu.VMEM(part, low),
            pltpu.VMEM(ffn_in.shape[1:], low),
            pltpu.VMEM(ffn_out.shape[1:], low),
            pltpu.VMEM((2, wide) + block.shape, low),
            pltpu.SemaphoreType.DMA((10 + 2 * wide,)),
            pltpu.SemaphoreType.DMA((10 + 2 * wide,)),
            pltpu.SemaphoreType.DMA((10 + wide,)),
        ],
        compiler_params=pltpu.CompilerParams(
            collective_id=1, has_side_effects=True, vmem_limit_bytes=VMEM_LIMIT
        ),
        name="start_weights",
    )(attn_in, attn_out[0].T, cross_in, cross_out, ffn_in, ffn_out)
    return attn, dec_half, outs[:wide], outs[wide:]


def place_weights_kernel(wide, *refs):
    pieces = refs[: wide + 1]
    attn_ref, send_sem, recv_sem, local_sem = refs[wide + 1 :]
    core, place = lax.axis_index("section"), lax.axis_index("wide")
    sibling = {"section": 1 - core}
    depth = pieces[0].shape[0]
    greet([sibling])
    stores, gives = [], []
    for index, piece in enumerate(pieces):
        start = (place ^ min(index, wide - 1)) * depth
        if index == wide:
            start = start + pieces[wide - 1].shape[0]
        target = attn_ref.at[core, pl.ds(pl.multiple_of(start, 16), piece.shape[0])]
        stores.append(pltpu.make_async_copy(piece, target, local_sem.at[index]))
        gives.append(remote(piece, target, (send_sem, recv_sem), index, sibling))
        stores[-1].start()
        gives[-1].start()
    for store, give in zip(stores, gives):
        store.wait()
        give.wait()


def place_weights(wide, pieces):
    depth, columns = pieces[0].shape
    return pl.pallas_call(
        lambda *refs: place_weights_kernel(wide, *refs),
        out_shape=jax.ShapeDtypeStruct((2, wide * depth, columns), jnp.bfloat16),
        in_specs=[VM] * len(pieces),
        out_specs=HBM,
        scratch_shapes=[pltpu.SemaphoreType.DMA((len(pieces),))] * 3,
        compiler_params=pltpu.CompilerParams(collective_id=6, has_side_effects=True),
        name="place_weights",
    )(*pieces)


def split_at(rows):
    return (rows // 2 + 15) // 16 * 16


def reduce_kernel(wide, rows, *refs):
    cross_ref, dec_ref, enc_ref, dec_in, dec_out, enc_in, enc_out, small_ref = refs[:8]
    out_ref, ffn_ref, small_out = refs[8:11]
    refs = refs[11:]
    batches = (cross_ref, dec_ref, enc_ref)
    count = len(batches)
    owns, lands, planes, sends, zlands = [refs[i * count : (i + 1) * count] for i in range(5)]
    refs = refs[5 * count :]
    keep, give, ready, landing, small, small_land, small_plane, small_rows = refs[:8]
    line_bufs, (send_sem, recv_sem, local_sem) = refs[8:12], refs[12:]
    core, place, row = lax.axis_index("section"), lax.axis_index("wide"), lax.axis_index("rows")
    peers = peers_of(wide)
    sibling = peers[-1]
    crossed = [{"section": 1 - core, "wide": place ^ v} for v in range(1, wide)]
    others = [{"rows": row ^ k} for k in range(1, rows)]
    sems = (send_sem, recv_sem)
    depth = cross_ref.shape[0] // wide
    size = owns[0].shape[1]
    units = dec_out.shape[0]
    low = jnp.bfloat16
    greet(peers + crossed + others)

    def rows_at(v, half):
        start = (place ^ v) * depth + half * (depth - size)
        return pl.ds(pl.multiple_of(start, 16), size)

    loads, swaps, scatters, spreads = [], [], [], []
    base, local_base = 0, 0
    for index, batch in enumerate(batches):
        loads.append(
            [
                pltpu.make_async_copy(
                    batch.at[rows_at(v, core)], owns[index].at[v], local_sem.at[local_base + v]
                )
                for v in range(wide)
            ]
        )
        local_base += wide
        swaps.append(
            [
                remote(batch.at[rows_at(v, 1 - core)], lands[index].at[v], sems, base + v, sibling)
                for v in range(wide)
            ]
        )
        base += wide
        scatters.append(ScatterPlane(owns[index], planes[index], sems, base, peers, size))
        base += 6
        chunk = batch.shape[1] // rows
        spreads.append(
            [
                remote(
                    sends[index].at[:, pl.ds(pl.multiple_of((row ^ k) * chunk, TILE), chunk)],
                    zlands[index].at[k - 1],
                    sems,
                    base + k - 1,
                    others[k - 1],
                )
                for k in range(1, rows)
            ]
        )
        base += rows - 1
    line = ReduceRows(enc_in, enc_out, *line_bufs, sems, base, local_sem, local_base)
    base += 9
    local_base += 4
    line.start()
    for v in (3, 1, 2, 0):
        for index in range(count):
            loads[index][v].start()
            swaps[index][v].start()
    first = remote(small_ref.at[1 - core], small_land, sems, base, sibling)
    first.start()
    plane = [
        remote(small, small_plane.at[v - 1], sems, base + v, peers[v - 1]) for v in range(1, wide)
    ]
    base += wide
    spread_small = [
        remote(small, small_rows.at[k - 1], sems, base + k - 1, others[k - 1])
        for k in range(1, rows)
    ]
    base += rows - 1
    straight = (
        lax.broadcasted_iota(jnp.int32, (units, TILE), 0)
        == lax.broadcasted_iota(jnp.int32, (units, TILE), 1)
    ).astype(low)

    def hand(section, source, v):
        return pltpu.make_async_remote_copy(
            src_ref=ready.at[section, v],
            dst_ref=landing.at[source, v],
            send_sem=send_sem.at[base + section * wide + v],
            recv_sem=recv_sem.at[base + source * wide + v],
            device_id={"section": section, "wide": place ^ v},
            device_id_type=MESH,
        )

    def hand_out(section, part_in, part_out):
        turned = tn(part_out, straight).astype(low)
        for owner in range(wide):
            own = slice(owner * depth, (owner + 1) * depth)
            ready[section, owner ^ place, :, pl.ds(0, 2 * TILE)] = part_in[own]
            ready[section, owner ^ place, :, pl.ds(2 * TILE, TILE)] = turned[own]
        for v in range(wide):
            target = landing.at[core, v]
            move = hand(section, core, v)
            if v > 0:
                move.start()
                continue

            @pl.when(core == section)
            def _():
                pltpu.make_async_copy(ready.at[section, 0], target, local_sem.at[local_base]).start()

            @pl.when(core != section)
            def _():
                move.start()

    def sent(section):
        for v in range(wide):
            wait = hand(section, core, v)
            if v > 0:
                wait.wait_send()
                continue

            @pl.when(core == section)
            def _():
                pltpu.make_async_copy(
                    ready.at[section, 0], landing.at[core, 0], local_sem.at[local_base]
                ).wait()

            @pl.when(core != section)
            def _():
                wait.wait_send()

    def came(source):
        for v in range(wide):
            wait = hand(0, source, v)
            if v > 0:
                wait.wait_recv()
                continue

            @pl.when(core != source)
            def _():
                wait.wait_recv()

    def join(index, v):
        loads[index][v].wait()
        swaps[index][v].wait_recv()
        owns[index][v] = (
            owns[index][v].astype(jnp.float32) + lands[index][v].astype(jnp.float32)
        ).astype(low)

    for index in range(count):
        join(index, 3)
        scatters[index].send_far()
    for index in range(count):
        join(index, 1)
        scatters[index].send_early(0)
        join(index, 2)
        scatters[index].send_early(1)
        join(index, 0)
    first.wait_recv()
    small[...] = small_ref[core] + small_land[...]
    for copy in plane:
        copy.start()
    hand_out(1, dec_in[...], dec_out[...])
    line.loaded()
    line.turn(0)
    scatters[0].pass_on()
    scatters[1].pass_on()
    line.turn(1)
    scatters[2].pass_on()
    for copy in plane:
        copy.wait()
    small[...] = small[...] + jnp.sum(small_plane[...], axis=0)
    for copy in spread_small:
        copy.start()
    line.turn(2)
    for index in range(count):
        sends[index][...] = (
            owns[index][0].astype(jnp.float32) + scatters[index].total()
        ).astype(low)
        for spread in spreads[index]:
            spread.start()
    for index in range(3):
        line.close(index)
    hand_out(0, line_bufs[0][0], line_bufs[2][0])

    def total(index, start, width):
        chunk = batches[index].shape[1] // rows
        lanes = pl.ds(pl.multiple_of(row * chunk + start, TILE), width)
        out = sends[index][:, lanes].astype(jnp.float32)
        for k in range(rows - 1):
            out = out + zlands[index][k, :, pl.ds(start, width)].astype(jnp.float32)
        return out

    for index in range(count):
        for spread in spreads[index]:
            spread.wait_recv()
    span = dec_ref.shape[1] // rows
    extra = cross_ref.shape[1] // rows // 2
    for own in range(2):

        @pl.when(core == own)
        def _():
            keep[:, pl.ds(0, span)] = total(2 if own == 0 else 1, 0, span)
            keep[:, pl.ds(span, extra)] = total(0, own * extra, extra)
            give[:, pl.ds(0, span)] = total(1 if own == 0 else 2, 0, span)
            give[:, pl.ds(span, extra)] = total(0, (1 - own) * extra, extra)

    store = pltpu.make_async_copy(keep, out_ref.at[core], local_sem.at[local_base + 1])
    last = remote(give, out_ref.at[core], sems, base + 2 * wide, sibling)
    store.start()
    last.start()
    for copy in spread_small:
        copy.wait_recv()
    small_out[...] = small[...] + jnp.sum(small_rows[...], axis=0)
    sent(0)
    sent(1)
    came(0)
    came(1)
    store_ffn = pltpu.make_async_copy(landing, ffn_ref, local_sem.at[local_base + 2])
    store_ffn.start()
    store.wait()
    last.wait()
    store_ffn.wait()
    first.wait_send()
    for copy in spread_small:
        copy.wait_send()
    for index in range(count):
        for swap in swaps[index]:
            swap.wait_send()
        for spread in spreads[index]:
            spread.wait_send()
        scatters[index].finish()
    line.finish()


def reduce_weights(wide, rows, cross, dec, enc, dec_sums, enc_shares, small):
    low = jnp.bfloat16
    depth = D // wide
    size = split_at(depth)
    units = dec_sums[1].shape[0]
    batches = (cross, dec, enc)
    widths = [each.shape[1] for each in batches]
    columns = (dec.shape[1] + cross.shape[1] // 2) // rows
    copies = len(batches) * (wide + 6 + rows - 1) + 9 + wide + rows - 1 + 2 * wide + 1
    small_one = pltpu.VMEM(small.shape[1:], jnp.float32)
    return pl.pallas_call(
        lambda *refs: reduce_kernel(wide, rows, *refs),
        out_shape=[
            jax.ShapeDtypeStruct((2, size, columns), jnp.float32),
            jax.ShapeDtypeStruct((2, wide, depth, 3 * TILE), low),
            jax.ShapeDtypeStruct(small.shape[1:], jnp.float32),
        ],
        in_specs=[HBM] * 3 + [VM] * 2 + [HBM] * 2 + [VM],
        out_specs=[HBM, HBM, VM],
        scratch_shapes=[pltpu.VMEM((wide, size, w), low) for w in widths]
        + [pltpu.VMEM((wide, size, w), low) for w in widths]
        + [pltpu.VMEM((3, size, w), low) for w in widths]
        + [pltpu.VMEM((size, w), low) for w in widths]
        + [pltpu.VMEM((rows - 1, size, w // rows), low) for w in widths]
        + [
            pltpu.VMEM((size, columns), jnp.float32),
            pltpu.VMEM((size, columns), jnp.float32),
            pltpu.VMEM((2, wide, depth, 3 * TILE), low),
            pltpu.VMEM((2, wide, depth, 3 * TILE), low),
            small_one,
            small_one,
            pltpu.VMEM((wide - 1,) + small.shape[1:], jnp.float32),
            pltpu.VMEM((rows - 1,) + small.shape[1:], jnp.float32),
        ]
        + reduce_rows_scratch(units)
        + [
            pltpu.SemaphoreType.DMA((copies,)),
            pltpu.SemaphoreType.DMA((copies,)),
            pltpu.SemaphoreType.DMA((len(batches) * wide + 7,)),
        ],
        compiler_params=pltpu.CompilerParams(
            collective_id=7, has_side_effects=True, vmem_limit_bytes=VMEM_LIMIT
        ),
        name="reduce_weights",
    )(*batches, *dec_sums, *enc_shares, small)


def assemble_kernel(units, parts_ref, in_ref, out_ref):
    low = jnp.bfloat16
    wide = parts_ref.shape[1]
    place = lax.axis_index("wide")
    pairs = 2 * wide
    row_ids = lax.broadcasted_iota(jnp.int32, (TILE, TILE), 0)
    lane_ids = lax.broadcasted_iota(jnp.int32, (TILE, TILE), 1)
    for tile in range(in_ref.shape[2] // TILE):
        total = None
        for group in range(tile * TILE // units, ((tile + 1) * TILE - 1) // units + 1):
            half, chip, block = group % 2, group % pairs // 2, group // pairs
            shift = group * units - tile * TILE
            picks = ((row_ids + shift == lane_ids) & (row_ids < units)).astype(low)
            part = matmul(parts_ref[half, chip ^ place, :, pl.ds(block * TILE, TILE)], picks)
            total = part if total is None else total + part
        in_ref[0, :, pl.ds(tile * TILE, TILE)] = total
    straight = (
        lax.broadcasted_iota(jnp.int32, (units, TILE), 0)
        == lax.broadcasted_iota(jnp.int32, (units, TILE), 1)
    ).astype(low)
    for chip in range(wide):
        for half in range(2):
            start = (chip * 2 + half) * units
            out_ref[0, pl.ds(start, units), :] = nt(
                straight, parts_ref[half, chip ^ place, :, pl.ds(2 * TILE, TILE)]
            )


def assemble(rows, parts):
    wide, depth = parts.shape[1:3]
    return pl.pallas_call(
        lambda *refs: assemble_kernel(FF // (wide * rows * 2), *refs),
        out_shape=[
            jax.ShapeDtypeStruct((1, depth, 2 * FF // rows), jnp.float32),
            jax.ShapeDtypeStruct((1, FF // rows, depth), jnp.float32),
        ],
        in_specs=[VM],
        out_specs=[VM, VM],
        compiler_params=pltpu.CompilerParams(vmem_limit_bytes=VMEM_LIMIT),
        name="assemble",
    )(parts)


def bias_rows_kernel(enc_ref, dec_ref, enc_out, dec_out):
    for source, target in ((enc_ref, enc_out), (dec_ref, dec_out)):
        length, span = target.shape[1], source.shape[1]
        for head in range(H):
            row = jnp.broadcast_to(source[pl.ds(head, 1), :], (length, span))
            target[head] = pltpu.roll(row, 0, 1, stride=1, stride_axis=0)[:, :length]


def bias_rows(enc_row, dec_row):
    return pl.pallas_call(
        bias_rows_kernel,
        out_shape=[
            jax.ShapeDtypeStruct((H, LE, LE), jnp.float32),
            jax.ShapeDtypeStruct((H, LD, LD), jnp.float32),
        ],
        in_specs=[VM, VM],
        out_specs=[VM, VM],
        name="bias_rows",
    )(enc_row, dec_row)


def bias_sums_kernel(enc_ref, dec_ref, enc_out, dec_out):
    for source, target in ((enc_ref, enc_out), (dec_ref, dec_out)):
        length, span = source.shape[1], target.shape[1]
        flip = (
            lax.broadcasted_iota(jnp.int32, (length, length), 0)
            + lax.broadcasted_iota(jnp.int32, (length, length), 1)
            == length - 1
        ).astype(jnp.bfloat16)
        target[...] = jnp.zeros_like(target)
        for head in range(H):
            flipped = matmul(flip, source[head])
            wide = jnp.concatenate(
                [flipped, jnp.zeros((length, span - length), jnp.float32)], axis=1
            )
            rolled = pltpu.roll(wide, 0, 1, stride=1, stride_axis=0)
            target[pl.ds(head, 1), :] = jnp.sum(rolled, axis=0, keepdims=True)


def bias_sums(enc_scores, dec_scores):
    return pl.pallas_call(
        bias_sums_kernel,
        out_shape=[
            jax.ShapeDtypeStruct((8, 2 * LE), jnp.float32),
            jax.ShapeDtypeStruct((8, 2 * LD), jnp.float32),
        ],
        in_specs=[VM, VM],
        out_specs=[VM, VM],
        name="bias_sums",
    )(enc_scores, dec_scores)


def distance_hot(length, both_ways, first):
    table = bucket_table(length, both_ways)
    span = 2 * length
    hot = np.zeros((NB, span), np.float32)
    for entry in range(span):
        distance = entry + first
        if first == 0 and distance >= length:
            distance -= span
        if -length < distance < length:
            query = max(0, -distance)
            hot[table[query, query + distance], entry] = 1.0
    return jnp.asarray(hot)


def head_lanes(value, side):
    lanes = lax.broadcasted_iota(jnp.int32, value.shape, 1)
    return jnp.where((lanes < DH) == (side == 0), value, jnp.zeros_like(value))


def attend_heads(query_of, key_of, value_of, bias_of, allowed, context_ref, weights_ref):
    for pair in range(H // 2):
        query, key, value = query_of(pair), key_of(pair), value_of(pair)
        total = None
        for side in range(2):
            head = 2 * pair + side
            scores = nt(head_lanes(query, side), key)
            if bias_of is not None:
                scores = scores + bias_of(head)
            scores = jnp.where(allowed, scores, NEGATIVE)
            shifted = jnp.exp(scores - jnp.max(scores, axis=-1, keepdims=True))
            weights = shifted / jnp.sum(shifted, axis=-1, keepdims=True)
            weights_ref[head] = weights
            part = matmul(weights.astype(jnp.bfloat16), head_lanes(value, side))
            total = part if total is None else total + part
        context_ref[:, pl.ds(pair * TILE, TILE)] = total.astype(jnp.bfloat16)


def attend_heads_backward(query_of, key_of, value_of, weights_ref, grad_of, put, scores_ref=None):
    for pair in range(H // 2):
        query, key, value, grad = query_of(pair), key_of(pair), value_of(pair), grad_of(pair)
        sums = [None, None, None]
        for side in range(2):
            head = 2 * pair + side
            weights = weights_ref[head]
            own_grad = head_lanes(grad, side)
            grad_weights = nt(own_grad, value)
            inner = jnp.sum(grad_weights * weights, axis=-1, keepdims=True)
            low = (weights * (grad_weights - inner)).astype(jnp.bfloat16)
            if scores_ref is not None:
                scores_ref[head] = low
            parts = [
                matmul(low, head_lanes(key, side)),
                tn(low, head_lanes(query, side)),
                tn(weights.astype(jnp.bfloat16), own_grad),
            ]
            sums = [b if a is None else a + b for a, b in zip(sums, parts)]
        put(pair, *sums)


def weight_spec(half, width, index):
    return pl.BlockSpec((None, D, width), lambda step: (half, 0, index), memory_space=pltpu.VMEM)


W_IN = weight_spec(0, 3 * HD, 0)
W_OUT, C_IN, C_OUT = [weight_spec(1, HD, i) for i in range(3)]


def tile_of(ref, base):
    return lambda pair: ref[:, pl.ds(base + pair * TILE, TILE)]


def self_forward_kernel(
    causal, x_ref, gain_ref, win_ref, wout_ref, bias_ref, col_ref, row_ref, y_ref, normed_ref, projected_ref, context_ref, weights_ref
):
    residual = x_ref[...].astype(jnp.float32)
    normed_ref[...] = (residual * rms_rows(residual) * gain_ref[...]).astype(jnp.bfloat16)
    projected_ref[...] = matmul(normed_ref[...], win_ref[...]).astype(jnp.bfloat16)
    allowed = col_ref[...] == row_ref[...]
    if causal:
        length = x_ref.shape[0]
        allowed = allowed & (
            lax.broadcasted_iota(jnp.int32, (length, length), 0)
            >= lax.broadcasted_iota(jnp.int32, (length, length), 1)
        )
    attend_heads(
        tile_of(projected_ref, 0),
        tile_of(projected_ref, HD),
        tile_of(projected_ref, 2 * HD),
        lambda head: bias_ref[head],
        allowed,
        context_ref,
        weights_ref,
    )
    y_ref[...] = residual + nt(context_ref[...], wout_ref[...])


def self_forward(causal, residual, gain_row, weight, bias, items):
    rows = residual.shape[0]
    low = jnp.bfloat16
    y, *kept = pl.pallas_call(
        lambda *refs: self_forward_kernel(causal, *refs),
        out_shape=[
            jax.ShapeDtypeStruct((rows, D), jnp.float32),
            jax.ShapeDtypeStruct((rows, D), low),
            jax.ShapeDtypeStruct((rows, 3 * HD), low),
            jax.ShapeDtypeStruct((rows, HD), low),
            jax.ShapeDtypeStruct((H, rows, rows), jnp.float32),
        ],
        in_specs=[VM, VM, W_IN, W_OUT, VM, VM, VM],
        out_specs=[VM] * 5,
        grid=(1,),
        compiler_params=pltpu.CompilerParams(vmem_limit_bytes=VMEM_LIMIT),
        name="self_forward_%d" % rows,
    )(residual, gain_row, weight, weight, bias, items[:, None], items[None, :])
    return y, kept


def self_backward_kernel(
    g_ref,
    x_ref,
    gain_ref,
    win_ref,
    wout_ref,
    normed_ref,
    projected_ref,
    context_ref,
    weights_ref,
    gx_ref,
    gain_out,
    scores_ref,
    grad_ref,
    context_grad,
    projected_grad,
):
    low = jnp.bfloat16
    grad_low = g_ref[...].astype(low)
    context_grad[...] = matmul(grad_low, wout_ref[...]).astype(low)

    def put(pair, query, key, value):
        for index, part in enumerate((query, key, value)):
            projected_grad[:, pl.ds(index * HD + pair * TILE, TILE)] = part.astype(low)

    attend_heads_backward(
        tile_of(projected_ref, 0),
        tile_of(projected_ref, HD),
        tile_of(projected_ref, 2 * HD),
        weights_ref,
        tile_of(context_grad, 0),
        put,
        scores_ref,
    )
    grad_normed = nt(projected_grad[...], win_ref[...])
    residual = x_ref[...].astype(jnp.float32)
    grad_residual, gain_out[...] = norm_pull(residual, gain_ref[...], grad_normed)
    gx_ref[...] = g_ref[...] + grad_residual
    both = jnp.concatenate([normed_ref[...], grad_low], axis=0)
    chunks = grad_ref.shape[1] // HD
    part_in, part_out = 3 * HD // chunks, HD // chunks

    def picked(source, start, window, first, width):
        base = start // TILE * TILE
        window = min(window, source.shape[1] - base)
        lanes = lax.broadcasted_iota(jnp.int32, (window, HD), 1) - first
        rows_of = lax.broadcasted_iota(jnp.int32, (window, HD), 0) + (base - start)
        pick = ((rows_of == lanes) & (lanes >= 0) & (lanes < width)).astype(low)
        return matmul(source[:, pl.ds(base, window)], pick).astype(low)

    for chunk in range(chunks):
        right = jnp.concatenate(
            [
                picked(projected_grad, chunk * part_in, HD, 0, part_in),
                picked(context_ref, chunk * part_out, 2 * TILE, part_in, part_out),
            ],
            axis=0,
        )
        grad_ref[:, pl.ds(chunk * HD, HD)] = tn(both, right).astype(low)


def self_backward(grad, residual, gain_row, weight, kept):
    rows = residual.shape[0]
    low = jnp.bfloat16
    return pl.pallas_call(
        self_backward_kernel,
        out_shape=[
            jax.ShapeDtypeStruct((rows, D), jnp.float32),
            jax.ShapeDtypeStruct((1, D), jnp.float32),
            jax.ShapeDtypeStruct((H, rows, rows), low),
            jax.ShapeDtypeStruct((D, 4 * HD), low),
        ],
        in_specs=[VM, VM, VM, W_IN, W_OUT] + [VM] * 4,
        out_specs=[VM] * 4,
        scratch_shapes=[pltpu.VMEM((rows, HD), low), pltpu.VMEM((rows, 3 * HD), low)],
        grid=(1,),
        compiler_params=pltpu.CompilerParams(vmem_limit_bytes=VMEM_LIMIT),
        name="self_backward_%d" % rows,
    )(grad, residual, gain_row, weight, weight, *kept)


def cross_forward_kernel(
    x_ref, final_ref, wkey_ref, wvalue_ref, y_ref, gain_ref, wquery_ref, wout_ref, col_ref, row_ref,
    out_ref, memory_ref, kv_ref, normed_ref, query_ref, context_ref, weights_ref,
):
    low = jnp.bfloat16
    residual = x_ref[...]
    memory_ref[...] = (residual * rms_rows(residual) * final_ref[...]).astype(low)
    kv_ref[:, pl.ds(0, HD)] = matmul(memory_ref[...], wkey_ref[...]).astype(low)
    kv_ref[:, pl.ds(HD, HD)] = matmul(memory_ref[...], wvalue_ref[...]).astype(low)
    target = y_ref[...]
    normed_ref[...] = (target * rms_rows(target) * gain_ref[...]).astype(low)
    query_ref[...] = matmul(normed_ref[...], wquery_ref[...]).astype(low)
    attend_heads(
        tile_of(query_ref, 0),
        tile_of(kv_ref, 0),
        tile_of(kv_ref, HD),
        None,
        col_ref[...] == row_ref[...],
        context_ref,
        weights_ref,
    )
    out_ref[...] = target + nt(context_ref[...], wout_ref[...])


def cross_forward(x2, final_gain, enc_weight, y1, gain_row, dec_weight, dec_items, enc_items):
    low = jnp.bfloat16
    y2, *kept = pl.pallas_call(
        cross_forward_kernel,
        out_shape=[
            jax.ShapeDtypeStruct((LD, D), jnp.float32),
            jax.ShapeDtypeStruct((LE, D), low),
            jax.ShapeDtypeStruct((LE, 2 * HD), low),
            jax.ShapeDtypeStruct((LD, D), low),
            jax.ShapeDtypeStruct((LD, HD), low),
            jax.ShapeDtypeStruct((LD, HD), low),
            jax.ShapeDtypeStruct((H, LD, LE), jnp.float32),
        ],
        in_specs=[VM, VM, C_IN, C_OUT, VM, VM, C_IN, C_OUT, VM, VM],
        out_specs=[VM] * 7,
        grid=(1,),
        compiler_params=pltpu.CompilerParams(vmem_limit_bytes=VMEM_LIMIT),
        name="cross_forward",
    )(
        x2,
        final_gain,
        enc_weight,
        enc_weight,
        y1,
        gain_row,
        dec_weight,
        dec_weight,
        dec_items[:, None],
        enc_items[None, :],
    )
    return y2, kept


def cross_backward_kernel(
    g_ref, x_ref, final_ref, wkey_ref, wvalue_ref, y_ref, gain_ref, wquery_ref, wout_ref, kv_ref, query_ref, weights_ref,
    gx_ref, gy_ref, final_out, gain_out, kv_grad, query_grad, context_grad,
):
    low = jnp.bfloat16
    grad_low = g_ref[...].astype(low)
    context_grad[...] = matmul(grad_low, wout_ref[...]).astype(low)

    def put(pair, query, key, value):
        query_grad[:, pl.ds(pair * TILE, TILE)] = query.astype(low)
        kv_grad[:, pl.ds(pair * TILE, TILE)] = key.astype(low)
        kv_grad[:, pl.ds(HD + pair * TILE, TILE)] = value.astype(low)

    attend_heads_backward(
        tile_of(query_ref, 0),
        tile_of(kv_ref, 0),
        tile_of(kv_ref, HD),
        weights_ref,
        tile_of(context_grad, 0),
        put,
    )
    grad_memory = nt(kv_grad[:, pl.ds(0, HD)], wkey_ref[...]) + nt(
        kv_grad[:, pl.ds(HD, HD)], wvalue_ref[...]
    )
    gx_ref[...], final_out[...] = norm_pull(x_ref[...], final_ref[...], grad_memory)
    grad_residual, gain_out[...] = norm_pull(
        y_ref[...], gain_ref[...], nt(query_grad[...], wquery_ref[...])
    )
    gy_ref[...] = g_ref[...] + grad_residual


def cross_backward(g2, x2, final_gain, enc_weight, y1, gain_row, dec_weight, kv, query, weights):
    low = jnp.bfloat16
    return pl.pallas_call(
        cross_backward_kernel,
        out_shape=[
            jax.ShapeDtypeStruct((LE, D), jnp.float32),
            jax.ShapeDtypeStruct((LD, D), jnp.float32),
            jax.ShapeDtypeStruct((1, D), jnp.float32),
            jax.ShapeDtypeStruct((1, D), jnp.float32),
            jax.ShapeDtypeStruct((LE, 2 * HD), low),
            jax.ShapeDtypeStruct((LD, HD), low),
        ],
        in_specs=[VM, VM, VM, C_IN, C_OUT, VM, VM, C_IN, C_OUT, VM, VM, VM],
        out_specs=[VM] * 6,
        scratch_shapes=[pltpu.VMEM((LD, HD), low)],
        grid=(1,),
        compiler_params=pltpu.CompilerParams(vmem_limit_bytes=VMEM_LIMIT),
        name="cross_backward",
    )(g2, x2, final_gain, enc_weight, enc_weight, y1, gain_row, dec_weight, dec_weight, kv, query, weights)


def column_picks(widths, rows, chunk):
    picks, base = [], 0
    for width in widths:
        part = width // rows
        pick = np.zeros((width, rows * chunk), np.float32)
        for row in range(rows):
            for lane in range(part):
                pick[row * part + lane, row * chunk + base + lane] = 1.0
        picks.append(jnp.asarray(pick, jnp.bfloat16))
        base += part
    return picks


def plain_self_forward(residual, gain_row, weight, bias_full, allowed):
    normed = to_low(rms_norm(residual, gain_row))
    projected = to_low(matmul(normed, weight[:, : 3 * HD]))
    context, weights, low_weights = attend_forward(
        projected[:, :HD], projected[:, HD : 2 * HD], projected[:, 2 * HD :], bias_full, allowed
    )
    return (
        residual + matmul(context, weight[:, 3 * HD : 4 * HD].T),
        (residual, normed, projected, context, weights, low_weights),
    )


def plain_self_backward(kept, gain_row, weight, hot, grad_out):
    residual, normed, projected, context, weights, low_weights = kept
    grad_low = to_low(grad_out)
    grad_wout = matmul(grad_low.T, context)
    grad_context = to_low(matmul(grad_low, weight[:, 3 * HD : 4 * HD]))
    grad_queries, grad_keys, grad_values, low_scores = attend_backward(
        projected[:, :HD],
        projected[:, HD : 2 * HD],
        projected[:, 2 * HD :],
        weights,
        low_weights,
        grad_context,
    )
    grad_projected = to_low(jnp.concatenate([grad_queries, grad_keys, grad_values], axis=1))
    grad_win = matmul(normed.T, grad_projected)
    grad_residual, grad_gain = plain_norm_backward(
        residual, gain_row, matmul(grad_projected, weight[:, : 3 * HD].T)
    )
    grad_bias = jnp.einsum(
        "hqk,qkb->bh", low_scores, hot.astype(jnp.bfloat16), preferred_element_type=jnp.float32
    )
    return grad_out + grad_residual, grad_gain, grad_win, grad_wout, grad_bias


def plain_reduce_attn(grad, core, wide, rows):
    depth, columns = grad.shape
    halves = plain_core_halves(grad, core, wide)
    place = lax.axis_index("wide")
    parts = [
        lax.dynamic_index_in_dim(halves, place ^ v, 0, keepdims=False) for v in range(wide)
    ]
    mine = to_low(scatter_wide(parts))
    pieces, start = [], 0
    for width in (3 * HD, HD, HD, HD):
        pieces.append(mine[:, start : start + width].reshape(mine.shape[0], rows, width // rows))
        start += width
    stacked = jnp.concatenate(pieces, axis=2).transpose(1, 0, 2)
    return lax.psum_scatter(stacked, "rows", scatter_dimension=0, tiled=True)[0]


def plain_core_halves(grad, core, wide):
    depth, columns = grad.shape
    split = to_low(grad).reshape(wide, 2, depth // wide // 2, columns)
    mine = lax.dynamic_index_in_dim(split, core, 1, keepdims=False)
    sent = lax.dynamic_index_in_dim(split, 1 - core, 1, keepdims=False)
    return mine.astype(jnp.float32) + xor_permute(sent, "section", 1).astype(jnp.float32)


def plain_both_sections(own, section):
    other = xor_permute(own, "section", 1)
    is_dec = section == 1
    return jnp.where(is_dec, other, own), jnp.where(is_dec, own, other)


def plain_norm_backward(residual, gain_row, grad_normed):
    _, norm_pull = jax.vjp(rms_norm, residual, gain_row)
    return norm_pull(grad_normed)


def plain_hidden_columns(weight):
    width = weight.shape[1] * 2 // 3
    return weight[:, :width], weight[:, width:]


def plain_ffn_hidden(blocks, weight):
    w_in, _ = plain_hidden_columns(weight)
    both = [matmul(block, w_in) for block in blocks]
    units = w_in.shape[1] // 2
    return both, [to_low(gated(part[:, :units], part[:, units:])) for part in both]


def plain_ffn_forward(residual, gain_row, weight):
    blocks = gather_wide(to_low(rms_norm(residual, gain_row)))
    both, hidden = plain_ffn_hidden(blocks, weight)
    _, w_out = plain_hidden_columns(weight)
    out = residual + scatter_wide([matmul(part, w_out.T) for part in hidden])
    return out, (residual, blocks, both, hidden)


def plain_ffn_backward(kept, gain_row, weight, grad_out, grad_blocks):
    residual, blocks, both, hidden = kept
    w_in, w_out = plain_hidden_columns(weight)
    units = w_out.shape[1]
    parts, grad_both = [], []
    for block, pre in zip(grad_blocks, both):
        _, pull = jax.vjp(gated, pre[:, :units], pre[:, units:])
        grad_gate, grad_up = pull(matmul(block, w_out))
        low = to_low(jnp.concatenate([grad_gate, grad_up], axis=1))
        grad_both.append(low)
        parts.append(matmul(low, w_in.T))
    grad_residual, grad_gain = plain_norm_backward(residual, gain_row, scatter_wide(parts))
    joined = jnp.concatenate(grad_both, axis=0)
    grad_in = matmul(jnp.concatenate(blocks, axis=0).T, joined)
    grad_wout = matmul(jnp.concatenate(grad_blocks, axis=0).T, jnp.concatenate(hidden, axis=0))
    return grad_out + grad_residual, grad_gain, (grad_in, grad_wout)


def plain_reduce_ffn(grads, core, wide, rows):
    grad_in, grad_wout = grads
    depth = grad_in.shape[0]
    both = jnp.concatenate(
        [grad_in.reshape(depth, rows, -1), grad_wout.reshape(depth, rows, -1)], axis=2
    )
    columns = both.shape[2]
    halves = plain_core_halves(both.reshape(depth, rows * columns), core, wide)
    halves = to_low(halves).reshape(wide * (depth // wide // 2), rows, columns).transpose(1, 0, 2)
    summed = lax.psum_scatter(halves, "rows", scatter_dimension=0, tiled=True)[0]
    blocks = summed.reshape(wide, depth // wide // 2, columns)
    place = lax.axis_index("wide")
    out = [lax.dynamic_index_in_dim(blocks, place, 0, keepdims=False)]
    for v in range(1, wide):
        block = lax.dynamic_index_in_dim(blocks, place ^ v, 0, keepdims=False)
        out.append(xor_permute(block, "wide", v))
    return placed_rows([piece[None] for piece in out], place)


def plain_to_section(enc_half, dec_half, core):
    is_dec = core == 1
    own = jnp.where(is_dec, dec_half, enc_half)
    got = xor_permute(jnp.where(is_dec, enc_half, dec_half), "section", 1)
    low, high = jnp.where(is_dec, got, own), jnp.where(is_dec, own, got)
    return jnp.concatenate([low, high], axis=-2).astype(jnp.float32)


def plain_shards(
    enc_embed,
    dec_embed,
    out_cot,
    enc_lengths,
    dec_lengths,
    norm_gains,
    rel_bias,
    attn_in,
    attn_out,
    ffn_in,
    ffn_out,
    cross_in,
    cross_out,
):
    core = lax.axis_index("section")
    place = lax.axis_index("wide")
    wide, rows = lax.axis_size("wide"), lax.axis_size("rows")
    depth = attn_in.shape[1]
    unit = FF // (wide * rows)

    small = jnp.concatenate([norm_gains[0].reshape(-1), rel_bias[0].reshape(-1)])
    enc_small, dec_small = plain_both_sections(small, core)
    gains = [each[: 3 * D].reshape(3, D) for each in (enc_small, dec_small)]
    biases = [each[3 * D :].reshape(NB, H) for each in (enc_small, dec_small)]

    attn_shard = jnp.concatenate([attn_in[0], attn_out[0].T, cross_in[0], cross_out[0]], axis=1)
    attn_own = placed_rows(gather_wide(attn_shard), place)
    ffn_blocks = jnp.concatenate(
        [
            ffn_in[0].reshape(depth, 2 * rows, wide, unit).transpose(2, 0, 1, 3).reshape(wide, depth, -1),
            ffn_out[0].T.reshape(depth, rows, wide, unit).transpose(2, 0, 1, 3).reshape(wide, depth, -1),
        ],
        axis=2,
    )
    ffn_got = [lax.dynamic_index_in_dim(ffn_blocks, place, 0, keepdims=False)]
    for v in range(1, wide):
        block = lax.dynamic_index_in_dim(ffn_blocks, place ^ v, 0, keepdims=False)
        ffn_got.append(xor_permute(block, "wide", v))
    ffn_own = placed_rows(ffn_got, place)
    attn_enc, attn_dec = plain_both_sections(attn_own, core)
    ffn_enc, ffn_dec = plain_both_sections(ffn_own, core)
    memory_weight = attn_enc[:, 4 * HD :]
    cross_w_in, cross_w_out = attn_dec[:, 4 * HD : 5 * HD], attn_dec[:, 5 * HD :]

    def own_row(array):
        return lax.dynamic_index_in_dim(array[:, 0], core, 0, keepdims=False)

    enc_row = own_row(enc_embed).astype(jnp.float32)
    dec_row = own_row(dec_embed).astype(jnp.float32)
    cot_row = own_row(out_cot)
    enc_items = item_ids(own_row(enc_lengths), LE)
    dec_items = item_ids(own_row(dec_lengths), LD)
    enc_hot, dec_hot = one_hot(LE, True), one_hot(LD, False)
    enc_bias = jnp.einsum("qkb,bh->hqk", enc_hot, biases[0], precision=HIGHEST)
    dec_bias = jnp.einsum("qkb,bh->hqk", dec_hot, biases[1], precision=HIGHEST)
    causal = jnp.arange(LD)[:, None] >= jnp.arange(LD)[None, :]

    cot_blocks = gather_wide(cot_row)
    x1, enc_self = plain_self_forward(
        enc_row, gains[0][0], attn_enc, enc_bias, enc_items[:, None] == enc_items[None, :]
    )
    y1, dec_self = plain_self_forward(
        dec_row,
        gains[1][0],
        attn_dec,
        dec_bias,
        (dec_items[:, None] == dec_items[None, :]) & causal,
    )
    x2, enc_ffn = plain_ffn_forward(x1, gains[0][1], ffn_enc)
    memory = to_low(rms_norm(x2, gains[0][2]))
    memory_kv = to_low(matmul(memory, memory_weight))
    cross_normed = to_low(rms_norm(y1, gains[1][1]))
    queries = to_low(matmul(cross_normed, cross_w_in))
    context, weights, low_weights = attend_forward(
        queries,
        memory_kv[:, :HD],
        memory_kv[:, HD:],
        0.0,
        dec_items[:, None] == enc_items[None, :],
    )
    y2 = y1 + matmul(context, cross_w_out.T)
    y3, dec_ffn = plain_ffn_forward(y2, gains[1][2], ffn_dec)

    g2, dec_ffn_gain, dec_ffn_grads = plain_ffn_backward(
        dec_ffn, gains[1][2], ffn_dec, cot_row.astype(jnp.float32), cot_blocks
    )
    dec_ffn_share = plain_reduce_ffn(dec_ffn_grads, core, wide, rows)
    g2_low = to_low(g2)
    grad_cross_out = matmul(g2_low.T, context)
    grad_context = to_low(matmul(g2_low, cross_w_out))
    grad_queries, grad_keys, grad_values, _ = attend_backward(
        queries, memory_kv[:, :HD], memory_kv[:, HD:], weights, low_weights, grad_context
    )
    grad_query_low = to_low(grad_queries)
    grad_kv = to_low(jnp.concatenate([grad_keys, grad_values], axis=1))
    grad_x2, enc_final_gain = plain_norm_backward(x2, gains[0][2], matmul(grad_kv, memory_weight.T))
    grad_x1, enc_ffn_gain, enc_ffn_grads = plain_ffn_backward(
        enc_ffn, gains[0][1], ffn_enc, grad_x2, gather_wide(to_low(grad_x2))
    )
    enc_ffn_share = plain_reduce_ffn(enc_ffn_grads, core, wide, rows)

    grad_cross_in = matmul(cross_normed.T, grad_query_low)
    grad_memory = matmul(memory.T, grad_kv)
    from_cross, dec_cross_gain = plain_norm_backward(
        y1, gains[1][1], matmul(grad_query_low, cross_w_in.T)
    )
    grad_y, dec_self_gain, dec_win, dec_wout, dec_bias_grad = plain_self_backward(
        dec_self, gains[1][0], attn_dec, dec_hot, g2 + from_cross
    )
    dec_attn_share = plain_reduce_attn(
        jnp.concatenate([dec_win, dec_wout, grad_cross_in, grad_cross_out], axis=1),
        core,
        wide,
        rows,
    )
    grad_x, enc_self_gain, enc_win, enc_wout, enc_bias_grad = plain_self_backward(
        enc_self, gains[0][0], attn_enc, enc_hot, grad_x1
    )
    enc_attn_share = plain_reduce_attn(
        jnp.concatenate([enc_win, enc_wout, grad_memory], axis=1), core, wide, rows
    )

    small_grads = jnp.stack(
        [
            jnp.concatenate(
                [enc_self_gain, enc_ffn_gain, enc_final_gain, enc_bias_grad.reshape(-1)]
            ),
            jnp.concatenate(
                [dec_self_gain, dec_cross_gain, dec_ffn_gain, dec_bias_grad.reshape(-1)]
            ),
        ]
    )
    small_total = lax.psum(small_grads, ("section", "wide", "rows"))
    small_own = jnp.where(core == 1, small_total[1], small_total[0])

    attn_share = plain_to_section(enc_attn_share, dec_attn_share, core)
    ffn_share = plain_to_section(enc_ffn_share, dec_ffn_share, core)
    in_width = 2 * FF // rows // wide
    ffn_in_grad = (
        ffn_share[:, :, :in_width]
        .reshape(wide, depth, 2, unit)
        .transpose(1, 2, 0, 3)
        .reshape(depth, 2 * FF // rows)
    )
    ffn_out_grad = ffn_share[:, :, in_width:].transpose(0, 2, 1).reshape(FF // rows, depth)
    widths = [3 * HD // rows, HD // rows, HD // rows]
    edges = np.cumsum([0] + widths + [HD // rows])
    win, wout, cin, cout = [attn_share[:, a:b] for a, b in zip(edges[:-1], edges[1:])]

    half = D // 2

    def by_half(own):
        halves = jnp.stack([own[:, :half], own[:, half:]])
        keep = lax.dynamic_index_in_dim(halves, core, 0, keepdims=False)
        send = lax.dynamic_index_in_dim(halves, 1 - core, 0, keepdims=False)
        got = xor_permute(send, "section", 1)
        is_dec = core == 1
        return jnp.stack([jnp.where(is_dec, got, keep), jnp.where(is_dec, keep, got)])[:, None]

    return (
        by_half(to_low(y3)),
        by_half(grad_x),
        by_half(grad_y),
        small_own[: 3 * D].reshape(1, 3, D),
        small_own[3 * D :].reshape(1, NB, H),
        win[None],
        wout.T[None],
        ffn_in_grad[None],
        ffn_out_grad[None],
        cin[None],
        cout[None],
    )


def shards(
    enc_embed,
    dec_embed,
    out_cot,
    enc_lengths,
    dec_lengths,
    norm_gains,
    rel_bias,
    attn_in,
    attn_out,
    ffn_in,
    ffn_out,
    cross_in,
    cross_out,
):
    core = lax.axis_index("section")
    wide, rows = lax.axis_size("wide"), lax.axis_size("rows")
    depth = attn_in.shape[1]
    is_dec = core == 1

    def own_row(array):
        return lax.dynamic_index_in_dim(array[:, 0], core, 0, keepdims=False)

    enc_attn, dec_half, enc_blocks, dec_blocks = start_weights(
        wide, rows, attn_in, attn_out, cross_in, cross_out, ffn_in, ffn_out
    )
    enc_pieces = [enc_blocks[0]] + [xor_permute(enc_blocks[v], "wide", v) for v in range(1, wide)]

    small = jnp.concatenate([norm_gains[0].reshape(-1), rel_bias[0].reshape(-1)])
    other = xor_permute(small, "section", 1)
    smalls = (jnp.where(is_dec, other, small), jnp.where(is_dec, small, other))
    gains = [each[: 3 * D].reshape(3, D) for each in smalls]
    biases = [each[3 * D :].reshape(NB, H) for each in smalls]
    bias_lines = [
        jnp.pad(
            lax.dot_general(
                bias, distance_hot(length, both, 0), (((0,), (0,)), ((), ())), precision=HIGHEST
            ),
            ((0, 2), (0, 0)),
        )
        for bias, length, both in ((biases[0], LE, True), (biases[1], LD, False))
    ]
    enc_bias, dec_bias = bias_rows(*bias_lines)
    enc_row, dec_row, cot_row = own_row(enc_embed), own_row(dec_embed), own_row(out_cot)
    enc_items = item_ids(own_row(enc_lengths), LE)
    dec_items = item_ids(own_row(dec_lengths), LD)

    x1, enc_self = self_forward(False, enc_row, gains[0][0:1], enc_attn, enc_bias, enc_items)
    dec_half, dec_blocks, _ = lax.optimization_barrier((dec_half, dec_blocks, enc_pieces))
    x2, *enc_ffn = ffn_forward_call(wide, x1, gains[0][1:2], enc_pieces, 2)
    cut = split_at(depth)
    first, second = xor_permute(dec_half, "wide", 1), xor_permute(dec_half, "wide", 2)
    far = [xor_permute(first[:cut], "wide", 2), xor_permute(second[cut:], "wide", 1)]
    dec_attn = place_weights(wide, [dec_half, first, second] + far)
    dec_pieces = [dec_blocks[0]] + [xor_permute(dec_blocks[v], "wide", v) for v in range(1, wide)]
    y1, dec_self = self_forward(True, dec_row, gains[1][0:1], dec_attn, dec_bias, dec_items)
    y2, (memory, kv, normed, query, context, weights) = cross_forward(
        x2, gains[0][2:3], enc_attn, y1, gains[1][1:2], dec_attn, dec_items, enc_items
    )
    y3, *dec_ffn = ffn_forward_call(wide, y2, gains[1][2:3], dec_pieces, 3)

    g2, dec_ffn_gain, *dec_ffn_grads = ffn_backward_call(
        wide, rows, cot_row.astype(jnp.float32), y2, gains[1][2:3], dec_ffn, 4
    )
    grad_x2, g1, enc_final_gain, dec_cross_gain, kv_grad, query_grad = cross_backward(
        g2, x2, gains[0][2:3], enc_attn, y1, gains[1][1:2], dec_attn, kv, query, weights
    )
    grad_x1, enc_ffn_gain, enc_in, enc_out, *dec_sums = ffn_backward_call(
        wide, rows, grad_x2, x1, gains[0][1:2], enc_ffn, 5, dec_ffn_grads
    )
    grad_y, dec_self_gain, dec_scores, dec_grads = self_backward(
        g1, dec_row, gains[1][0:1], dec_attn, dec_self
    )
    grad_x, enc_self_gain, enc_scores, enc_grads = self_backward(
        grad_x1, enc_row, gains[0][0:1], enc_attn, enc_self
    )
    pair_picks = jnp.concatenate(column_picks((HD, HD), rows, 4 * TILE), axis=0)
    shifted_picks = jnp.roll(pair_picks, 2 * TILE, axis=1)
    cross_grads = to_low(
        matmul(
            jnp.concatenate([memory, normed, to_low(g2)], axis=0).T,
            to_low(
                jnp.concatenate(
                    [
                        matmul(kv_grad, pair_picks),
                        matmul(query_grad, shifted_picks[:HD]),
                        matmul(context, shifted_picks[HD:]),
                    ],
                    axis=0,
                )
            ),
        )
    )
    enc_line, dec_line = bias_sums(enc_scores, dec_scores)
    line_sums = [
        matmul_exact(distance_hot(length, both, 1 - length), line[:H].T).reshape(1, -1)
        for line, length, both in ((enc_line, LE, True), (dec_line, LD, False))
    ]
    lanes = (D + TILE - 1) // TILE * TILE
    small_grads = jnp.stack(
        [
            jnp.concatenate(
                [jnp.pad(each, ((0, 0), (0, lanes - each.shape[1]))) for each in group]
                + [jnp.zeros((4, lanes), jnp.float32)],
                axis=0,
            )
            for group in (
                (enc_self_gain, enc_ffn_gain, enc_final_gain, line_sums[0]),
                (dec_self_gain, dec_cross_gain, dec_ffn_gain, line_sums[1]),
            )
        ]
    )
    attn_parts, ffn_parts, small_own = reduce_weights(
        wide, rows, cross_grads, dec_grads, enc_grads, dec_sums, (enc_in, enc_out), small_grads
    )
    ffn_in_grad, ffn_out_grad = assemble(rows, ffn_parts)
    attn_share = jnp.concatenate([attn_parts[0], attn_parts[1, 2 * cut - depth :]], axis=0)
    edges = np.cumsum([0, 3 * HD // rows] + [HD // rows] * 3)
    win, wout, cin, cout = [attn_share[:, a:b] for a, b in zip(edges[:-1], edges[1:])]

    half = D // 2

    def by_half(own):
        halves = jnp.stack([own[:, :half], own[:, half:]])
        keep = lax.dynamic_index_in_dim(halves, core, 0, keepdims=False)
        send = lax.dynamic_index_in_dim(halves, 1 - core, 0, keepdims=False)
        got = xor_permute(send, "section", 1)
        return jnp.stack([jnp.where(is_dec, got, keep), jnp.where(is_dec, keep, got)])[:, None]

    return (
        by_half(to_low(y3)),
        by_half(grad_x),
        by_half(grad_y),
        small_own[None, :3, :D],
        small_own[3, : NB * H].reshape(1, NB, H),
        win[None],
        wout.T[None],
        ffn_in_grad,
        ffn_out_grad,
        cin[None],
        cout[None],
    )


def solution(mesh):
    placed = (
        P(None, ("wide", "rows"), None, None),
        P(None, ("wide", "rows"), None, None),
        P(None, ("wide", "rows"), None, None),
        P(None, ("wide", "rows"), None),
        P(None, ("wide", "rows"), None),
        P("section", None, None),
        P("section", None, None),
        P("section", "wide", None),
        P("section", None, "wide"),
        P("section", "wide", None),
        P("section", None, "wide"),
        P("section", "wide", None),
        P("section", "wide", None),
    )
    wide, rows = mesh.shape["wide"], mesh.shape["rows"]
    in_tiles = D // wide % 16 == 0 and FF // (wide * rows) % 32 == 0
    return jax.shard_map(
        shards if wide == 4 and rows == 4 and in_tiles else plain_shards,
        mesh=mesh,
        in_specs=placed,
        out_specs=(
            P(None, ("wide", "rows"), None, "section"),
            P(None, ("wide", "rows"), None, "section"),
            P(None, ("wide", "rows"), None, "section"),
            P("section", None, None),
            P("section", None, None),
            P("section", "wide", "rows"),
            P("section", "rows", "wide"),
            P("section", "wide", "rows"),
            P("section", "rows", "wide"),
            P("section", "wide", "rows"),
            P("section", "wide", "rows"),
        ),
        check_vma=False,
    )
```

```python
import jax
import jax.numpy as jnp
import numpy as np
from jax import lax
from jax.experimental import pallas as pl
from jax.experimental.pallas import tpu as pltpu
from jax.sharding import PartitionSpec as P

D = 1472
H = 6
DH = 64
FF = 3584
NB = 32
MAXDIST = 128
MB = 2
LE = 256
LD = 64
HD = 384


EPSILON = 1e-06
NEGATIVE = -1000000000.0
HIGHEST = lax.Precision.HIGHEST


def bucket_table(length, both_ways):
    positions = np.arange(length)
    offsets = positions[None, :] - positions[:, None]
    buckets = NB
    result = np.zeros(offsets.shape, np.int64)
    if both_ways:
        buckets = buckets // 2
        result = result + (offsets > 0) * buckets
        distance = np.abs(offsets)
    else:
        distance = np.maximum(-offsets, 0)
    exact_count = buckets // 2
    log_ratio = np.log(np.maximum(distance, 1) / exact_count) / np.log(MAXDIST / exact_count)
    far_bucket = np.minimum(
        exact_count + np.floor(log_ratio * (buckets - exact_count)).astype(np.int64), buckets - 1
    )
    return result + np.where(distance < exact_count, distance, far_bucket)


def one_hot(length, both_ways):
    bucket_ids = jnp.asarray(bucket_table(length, both_ways), jnp.int32)
    return (bucket_ids[:, :, None] == jnp.arange(NB, dtype=jnp.int32)[None, None, :]).astype(
        jnp.float32
    )


def item_ids(lengths, length):
    item_ends = jnp.cumsum(lengths)
    positions = jnp.arange(length, dtype=jnp.int32)
    return jnp.sum((positions[:, None] >= item_ends[None, :-1]).astype(jnp.int32), axis=1)


def rms_norm(residual, gain_row):
    return (
        residual
        * lax.rsqrt(jnp.mean(residual * residual, axis=-1, keepdims=True) + EPSILON)
        * gain_row
    )


def matmul(left_side, right_side):
    return jnp.dot(left_side, right_side, preferred_element_type=jnp.float32)


def matmul_exact(left_side, right_side):
    return jnp.dot(left_side, right_side, precision=HIGHEST)


def to_low(tensor):
    return tensor.astype(jnp.bfloat16)


def gated(gate_part, up_part):
    return jax.nn.gelu(gate_part, approximate=True) * up_part


def attend_forward(queries, key_rows, value_rows, bias_full, allowed):
    query_count = queries.shape[0]
    heads_q = queries.reshape(query_count, H, DH)
    heads_k = key_rows.reshape(key_rows.shape[0], H, DH)
    heads_v = value_rows.reshape(value_rows.shape[0], H, DH)
    scores = (
        jnp.einsum("qhd,khd->hqk", heads_q, heads_k, preferred_element_type=jnp.float32) + bias_full
    )
    scores = jnp.where(allowed[None], scores, NEGATIVE)
    shifted = jnp.exp(scores - jnp.max(scores, axis=-1, keepdims=True))
    weights = shifted / jnp.sum(shifted, axis=-1, keepdims=True)
    low_weights = to_low(weights)
    context = jnp.einsum("hqk,khd->qhd", low_weights, heads_v, preferred_element_type=jnp.float32)
    return (to_low(context.reshape(query_count, H * DH)), weights, low_weights)


def attend_backward(queries, key_rows, value_rows, weights, low_weights, grad_context):
    query_count = queries.shape[0]
    key_count = key_rows.shape[0]
    heads_q = queries.reshape(query_count, H, DH)
    heads_k = key_rows.reshape(key_count, H, DH)
    heads_v = value_rows.reshape(key_count, H, DH)
    grad_heads = grad_context.reshape(query_count, H, DH)
    grad_weights = jnp.einsum(
        "qhd,khd->hqk", grad_heads, heads_v, preferred_element_type=jnp.float32
    )
    grad_values = jnp.einsum(
        "hqk,qhd->khd", low_weights, grad_heads, preferred_element_type=jnp.float32
    )
    grad_scores = weights * (grad_weights - jnp.sum(grad_weights * weights, axis=-1, keepdims=True))
    low_scores = to_low(grad_scores)
    grad_queries = jnp.einsum(
        "hqk,khd->qhd", low_scores, heads_k, preferred_element_type=jnp.float32
    )
    grad_keys = jnp.einsum("hqk,qhd->khd", low_scores, heads_q, preferred_element_type=jnp.float32)
    return (
        grad_queries.reshape(query_count, H * DH),
        grad_keys.reshape(key_count, H * DH),
        grad_values.reshape(key_count, H * DH),
        low_scores,
    )


def xor_permute(value, axis, distance):
    count = lax.axis_size(axis)
    return lax.ppermute(value, axis, [(i, i ^ distance) for i in range(count)])


def gather_wide(block):
    count = lax.axis_size("wide")
    if count != 4:
        return [block] + [xor_permute(block, "wide", v) for v in range(1, count)]
    half = block.shape[0] // 2
    first = xor_permute(block, "wide", 1)
    second = xor_permute(block, "wide", 2)
    third = jnp.concatenate(
        [xor_permute(first[:half], "wide", 2), xor_permute(second[half:], "wide", 1)], axis=0
    )
    return [block, first, second, third]


def scatter_wide(parts):
    count = lax.axis_size("wide")
    total = parts[0]
    if count != 4:
        for v in range(1, count):
            total = total + xor_permute(to_low(parts[v]), "wide", v).astype(jnp.float32)
        return total
    half = total.shape[0] // 2
    via_first = xor_permute(to_low(parts[3][:half]), "wide", 1).astype(jnp.float32)
    via_second = xor_permute(to_low(parts[3][half:]), "wide", 2).astype(jnp.float32)
    to_first = jnp.concatenate([parts[1][:half], parts[1][half:] + via_second], axis=0)
    to_second = jnp.concatenate([parts[2][:half] + via_first, parts[2][half:]], axis=0)
    total = total + xor_permute(to_low(to_first), "wide", 1).astype(jnp.float32)
    return total + xor_permute(to_low(to_second), "wide", 2).astype(jnp.float32)


def placed_rows(pieces, place):
    rows = pieces[0].shape[0]
    buffer = jnp.zeros((rows * len(pieces),) + pieces[0].shape[1:], pieces[0].dtype)
    for v, piece in enumerate(pieces):
        start = (place ^ v) * rows
        buffer = lax.dynamic_update_slice(buffer, piece, (start,) + (0,) * (piece.ndim - 1))
    return buffer


MESH = pl.DeviceIdType.MESH
HBM = pl.BlockSpec(memory_space=pl.ANY)
VM = pl.BlockSpec(memory_space=pltpu.VMEM)
TILE = 128
VMEM_LIMIT = 60 * 1024 * 1024


def peers_of(count):
    place, core = lax.axis_index("wide"), lax.axis_index("section")
    return [{"wide": place ^ v} for v in range(1, count)] + [{"section": 1 - core}]


def greet(peers):
    barrier = pltpu.get_barrier_semaphore()
    for peer in peers:
        pl.semaphore_signal(barrier, inc=1, device_id=peer, device_id_type=MESH)
    pl.semaphore_wait(barrier, len(peers))


def remote(source, target, sems, index, peer):
    return pltpu.make_async_remote_copy(
        src_ref=source,
        dst_ref=target,
        send_sem=sems[0].at[index],
        recv_sem=sems[1].at[index],
        device_id=peer,
        device_id_type=MESH,
    )


def nt(left, right):
    return lax.dot_general(left, right, (((1,), (1,)), ((), ())), preferred_element_type=jnp.float32)


def tn(left, right):
    return lax.dot_general(left, right, (((0,), (0,)), ((), ())), preferred_element_type=jnp.float32)


class GatherPlane:
    def __init__(self, blocks, sems, base, peers, rows):
        half = split_at(rows)
        rest = rows - half
        first, second = peers[0], peers[1]
        self.direct = [
            remote(blocks.at[0], blocks.at[1], sems, base, first),
            remote(blocks.at[0], blocks.at[2], sems, base + 1, second),
        ]
        self.passed = [
            remote(
                blocks.at[1, pl.ds(0, half)], blocks.at[3, pl.ds(0, half)], sems, base + 2, second
            ),
            remote(
                blocks.at[2, pl.ds(half, rest)],
                blocks.at[3, pl.ds(half, rest)],
                sems,
                base + 3,
                first,
            ),
        ]

    def start(self):
        for copy in self.direct:
            copy.start()

    def arrive(self, index):
        if index < 2:
            self.direct[index].wait_recv()
            self.passed[index].start()
        else:
            for copy in self.passed:
                copy.wait_recv()

    def finish(self):
        for copy in self.direct + self.passed:
            copy.wait_send()


class ScatterPlane:
    def __init__(self, parts, landing, sems, base, peers, rows):
        half = split_at(rows)
        first, second = peers[0], peers[1]
        low, high = pl.ds(0, half), pl.ds(half, rows - half)
        self.parts, self.landing, self.low, self.high = parts, landing, low, high
        self.far = [
            remote(parts.at[3, low], landing.at[0, low], sems, base, first),
            remote(parts.at[3, high], landing.at[0, high], sems, base + 1, second),
        ]
        self.early = [
            remote(parts.at[1, low], landing.at[1, low], sems, base + 2, first),
            remote(parts.at[2, high], landing.at[2, high], sems, base + 3, second),
        ]
        self.late = [
            remote(parts.at[1, high], landing.at[1, high], sems, base + 4, first),
            remote(parts.at[2, low], landing.at[2, low], sems, base + 5, second),
        ]

    def send_early(self, index):
        self.early[index].start()

    def send_far(self):
        for copy in self.far:
            copy.start()

    def pass_on(self):
        low, high = self.low, self.high
        self.far[0].wait_recv()
        self.parts[2, low] = (
            self.parts[2, low].astype(jnp.float32) + self.landing[0, low].astype(jnp.float32)
        ).astype(jnp.bfloat16)
        self.late[1].start()
        self.far[1].wait_recv()
        self.parts[1, high] = (
            self.parts[1, high].astype(jnp.float32) + self.landing[0, high].astype(jnp.float32)
        ).astype(jnp.bfloat16)
        self.late[0].start()

    def total(self):
        for copy in self.early + self.late:
            copy.wait_recv()
        return self.landing[1].astype(jnp.float32) + self.landing[2].astype(jnp.float32)

    def finish(self):
        for copy in self.far + self.early + self.late:
            copy.wait_send()


def rms_rows(residual):
    return lax.rsqrt(jnp.mean(residual * residual, axis=-1, keepdims=True) + EPSILON)


def norm_pull(residual, gain_row, grad_normed):
    scale = rms_rows(residual)
    unit = residual * scale
    inner = grad_normed * gain_row
    grad_residual = scale * (inner - unit * jnp.mean(inner * unit, axis=-1, keepdims=True))
    return grad_residual, jnp.sum(grad_normed * unit, axis=0, keepdims=True)


def token_rows_at_once(wide, rows):
    return rows if rows >= 2 * TILE else wide * rows


def block_at(blocks, group, count):
    if count == blocks.shape[1]:
        return blocks[group]
    return blocks[...].reshape(count, blocks.shape[2])


def before_group(gather, group, groups):
    if groups == 1:
        for index in range(3):
            gather.arrive(index)
        return
    for index in range(3):

        @pl.when(group == index + 1)
        def _():
            gather.arrive(index)


def put_parts(acc, parts, own_ref, group, groups, rows):
    if groups == 1:
        own_ref[...] = acc[pl.ds(0, rows)]
        for v in range(1, parts.shape[0]):
            parts[v] = acc[pl.ds(v * rows, rows)].astype(parts.dtype)
        return

    @pl.when(group == 0)
    def _():
        own_ref[...] = acc[...]

    @pl.when(group > 0)
    def _():
        parts[group] = acc[...].astype(parts.dtype)


def after_group(scatter, group, groups):
    if groups == 1:
        scatter.send_far()
        scatter.send_early(0)
        scatter.send_early(1)
        return

    @pl.when(group == 1)
    def _():
        scatter.send_early(0)

    @pl.when(group == 2)
    def _():
        scatter.send_early(1)

    @pl.when(group == 3)
    def _():
        scatter.send_far()


class Reshard:
    def __init__(self, blocks, pieces, direct, sems, base, peers):
        row = lax.axis_index("rows")
        shared = (blocks[0].shape[0] - direct) // 2
        mine = pl.ds(direct + row % 2 * shared, shared)
        other = {"rows": row ^ 1}
        self.shared, self.direct, self.passed = [], [], []
        for v, (block, piece) in enumerate(zip(blocks, pieces)):
            at, peer, first = base + 3 * v, peers[v], pl.ds(0, direct)
            self.shared.append(remote(block.at[mine], piece.at[mine], sems, at, peer))
            self.passed.append(remote(piece.at[mine], piece.at[mine], sems, at + 1, other))
            self.direct.append(remote(block.at[first], piece.at[first], sems, at + 2, peer))

    def start(self):
        for copy in self.shared:
            copy.start()

    def pass_on(self):
        for copy in self.shared:
            copy.wait_recv()
        for copy in self.direct + self.passed:
            copy.start()

    def finish(self):
        for copy in self.direct + self.passed:
            copy.wait()
        for copy in self.shared:
            copy.wait_send()


class ReduceRows:
    def __init__(self, source_in, source_out, in_buf, in_land, out_buf, out_land, sems, base, local_sem, local_base):
        row = lax.axis_index("rows")
        near, far = {"rows": row ^ 1}, {"rows": row ^ 2}
        self.bufs, self.lands, self.first, self.second = [], [], [], []
        views = [
            (lambda ref, i, part=part: ref.at[i, part], source_in, in_buf, in_land)
            for part in range(2)
        ] + [(lambda ref, i: ref.at[i], source_out, out_buf, out_land)]
        for index, (view, source, buf, land) in enumerate(views):
            at = base + 3 * index
            self.first.append(
                [
                    remote(view(source, row ^ 1), view(land, 0), sems, at, near),
                    remote(view(source, row ^ 3), view(land, 1), sems, at + 1, near),
                ]
            )
            self.second.append(remote(view(buf, 1), view(land, 2), sems, at + 2, far))
            self.bufs.append([view(buf, 0), view(buf, 1)])
            self.lands.append([view(land, i) for i in range(3)])
        self.loads = [
            pltpu.make_async_copy(source.at[place], buf.at[i], local_sem.at[local_base + 2 * j + i])
            for j, (source, buf) in enumerate(((source_in, in_buf), (source_out, out_buf)))
            for i, place in enumerate((row, row ^ 2))
        ]

    def start(self):
        for copy in self.first[0]:
            copy.start()
        for load in self.loads:
            load.start()

    def loaded(self):
        for load in self.loads:
            load.wait()

    def add(self, index, which, land):
        ref = self.bufs[index][which]
        ref[...] = (
            ref[...].astype(jnp.float32) + self.lands[index][land][...].astype(jnp.float32)
        ).astype(jnp.bfloat16)

    def turn(self, index):
        for copy in self.first[index]:
            copy.wait_recv()
        for copy in self.first[index + 1] if index < 2 else ():
            copy.start()
        self.add(index, 1, 1)
        self.second[index].start()
        self.add(index, 0, 0)

    def close(self, index):
        self.second[index].wait_recv()
        self.add(index, 0, 2)

    def finish(self):
        for pair, copy in zip(self.first, self.second):
            for each in pair:
                each.wait_send()
            copy.wait_send()


def reduce_rows_scratch(units):
    low = jnp.bfloat16
    return [
        pltpu.VMEM((2, 2, D, TILE), low),
        pltpu.VMEM((3, 2, D, TILE), low),
        pltpu.VMEM((2, units, D), low),
        pltpu.VMEM((3, units, D), low),
    ]


def weight_tiles(weight, half, part):
    lanes = pl.ds(part * TILE, TILE)
    return jnp.concatenate(
        [weight[half, quarter, :, lanes] for quarter in range(weight.shape[1])], axis=1
    )


def ffn_forward_kernel(wide, carried, count, x_ref, gain_ref, *refs):
    pieces, refs = refs[:count], refs[count:]
    if carried:
        dec_half, dec_blocks, refs = refs[0], refs[1:wide], refs[wide:]
    y_ref, at_out, pre_out, hidden_out, weight_out = refs[:5]
    refs = refs[5:]
    if carried:
        dec_attn, dec_pieces, refs = refs[0], refs[1:wide], refs[wide:]
    blocks, at, pre, hidden, weight, parts, landing, acc, send_sem, recv_sem, local_sem = refs[:11]
    rows = x_ref.shape[0]
    depth = pieces[0].shape[1]
    span = weight.shape[1] * TILE
    core, place = lax.axis_index("section"), lax.axis_index("wide")
    peers = peers_of(wide)
    sems = (send_sem, recv_sem)
    greet(peers + ([{"rows": lax.axis_index("rows") ^ 1}] if carried else []))
    residual = x_ref[...]
    blocks[0] = (residual * rms_rows(residual) * gain_ref[...]).astype(jnp.bfloat16)
    gather = GatherPlane(blocks, sems, 0, peers, rows)
    gather.start()
    loads, swaps = [], []
    for index, piece in enumerate(pieces):
        v = index if index < wide else index - wide + 1
        place_rows = pl.ds(pl.multiple_of((place ^ v) * depth, 16), depth)
        target = weight.at[core, :, place_rows]
        quarters = piece.shape[0]
        if quarters < weight.shape[1]:
            part = lax.axis_index("rows") % 2
            part = part if index < wide else 1 - part
            target = weight.at[core, pl.ds(part * quarters, quarters), place_rows]
        load = pltpu.make_async_copy(piece, target, local_sem.at[12 + index])
        swap = remote(piece, target, sems, 10 + index, peers[-1])
        load.start()
        swap.start()
        loads.append(load)
        swaps.append(swap)
    scatter = ScatterPlane(parts, landing, sems, 4, peers, rows)
    if carried:
        held = refs[11]
        other = {"rows": lax.axis_index("rows") ^ 1}
        passed = [
            remote(block, piece, sems, 24 + v, other)
            for v, (block, piece) in enumerate(zip(dec_blocks, dec_pieces))
        ]
        for copy in passed:
            copy.start()
        dec_gather = GatherPlane(held, sems, 27, peers, depth)
        fetch = pltpu.make_async_copy(dec_half, held.at[0], local_sem.at[7])
        fetch.start()
        stores, gives = [], []
        for v in range(wide):
            target = dec_attn.at[core, pl.ds(pl.multiple_of((place ^ v) * depth, 16), depth)]
            stores.append(pltpu.make_async_copy(held.at[v], target, local_sem.at[8 + v]))
            gives.append(remote(held.at[v], target, sems, 31 + v, peers[-1]))
    count = token_rows_at_once(wide, rows)
    groups = wide * rows // count

    @pl.loop(0, groups)
    def _(group):
        before_group(gather, group, groups)

        @pl.when(group == 0)
        def _():
            for load in loads:
                load.wait()

        token_rows = pl.ds(pl.multiple_of(group * count, count), count)

        @pl.loop(0, 2)
        def _(step):
            @pl.when((group == 0) & (step == 1))
            def _():
                for swap in swaps:
                    swap.wait_recv()

            half = lax.rem(core + step, 2)
            block = block_at(blocks, group, count)
            gate = matmul(block, weight_tiles(weight, half, 0))
            up = matmul(block, weight_tiles(weight, half, 1))
            pre[half, token_rows, pl.ds(0, span)] = gate.astype(jnp.bfloat16)
            pre[half, token_rows, pl.ds(span, span)] = up.astype(jnp.bfloat16)
            low = gated(gate, up).astype(jnp.bfloat16)
            hidden[half, token_rows, :] = low
            out = nt(low, weight_tiles(weight, half, 2))
            acc[...] = jnp.where(step == 0, 0.0, acc[...]) + out

        put_parts(acc, parts, y_ref, group, groups, rows)
        after_group(scatter, group, groups)
        if carried:

            @pl.when(group == 0)
            def _():
                fetch.wait()
                stores[0].start()
                gives[0].start()

            @pl.when(group == 1)
            def _():
                dec_gather.start()

    y_ref[...] += residual
    copies = [
        pltpu.make_async_copy(pre, pre_out, local_sem.at[4]),
        pltpu.make_async_copy(weight, weight_out, local_sem.at[5]),
    ]
    for copy in copies:
        copy.start()
    scatter.pass_on()
    if carried:
        for v in range(1, 3):
            dec_gather.arrive(v - 1)
            stores[v].start()
            gives[v].start()
    at[...] = jnp.concatenate([blocks[v] for v in range(wide)], axis=0).T
    last = pltpu.make_async_copy(at, at_out, local_sem.at[6])
    last.start()
    copies.append(last)
    for half in range(2):
        hidden_out[half] = hidden[half].T
    y_ref[...] += scatter.total()
    if carried:
        dec_gather.arrive(2)
        stores[3].start()
        gives[3].start()
        for store, give in zip(stores, gives):
            store.wait()
            give.wait()
        dec_gather.finish()
        for copy in passed:
            copy.wait()
    for copy in copies:
        copy.wait()
    gather.finish()
    scatter.finish()
    for swap in swaps:
        swap.wait_send()


def ffn_forward_call(wide, residual, gain_row, pieces, call_id, carried=()):
    rows = residual.shape[0]
    total = rows * wide
    quarters, _, columns = pieces[0].shape
    span = quarters * TILE
    low = jnp.bfloat16
    extra_out, extra_scratch = [], []
    if carried:
        depth, attn_columns = carried[0].shape
        extra_out = [jax.ShapeDtypeStruct((2, D, attn_columns), low)] + [
            jax.ShapeDtypeStruct(each.shape, low) for each in carried[1:]
        ]
        extra_scratch = [pltpu.VMEM((wide, depth, attn_columns), low)]
    return pl.pallas_call(
        lambda *refs: ffn_forward_kernel(wide, bool(carried), len(pieces), *refs),
        out_shape=[
            jax.ShapeDtypeStruct((rows, D), jnp.float32),
            jax.ShapeDtypeStruct((D, total), low),
            jax.ShapeDtypeStruct((2, total, 2 * span), low),
            jax.ShapeDtypeStruct((2, span, total), low),
            jax.ShapeDtypeStruct((2, quarters, D, columns), low),
        ]
        + extra_out,
        in_specs=[VM, VM] + [HBM] * (len(pieces) + len(carried)),
        out_specs=[VM, HBM, HBM, VM, HBM] + [HBM] * len(extra_out),
        scratch_shapes=[
            pltpu.VMEM((wide, rows, D), low),
            pltpu.VMEM((D, total), low),
            pltpu.VMEM((2, total, 2 * span), low),
            pltpu.VMEM((2, total, span), low),
            pltpu.VMEM((2, quarters, D, columns), low),
            pltpu.VMEM((wide, rows, D), low),
            pltpu.VMEM((3, rows, D), low),
            pltpu.VMEM((token_rows_at_once(wide, rows), D), jnp.float32),
            pltpu.SemaphoreType.DMA((35,)),
            pltpu.SemaphoreType.DMA((35,)),
            pltpu.SemaphoreType.DMA((19,)),
        ]
        + extra_scratch,
        compiler_params=pltpu.CompilerParams(
            collective_id=call_id, has_side_effects=True, vmem_limit_bytes=VMEM_LIMIT
        ),
        name="ffn_forward_%d" % rows,
    )(residual, gain_row, *pieces, *carried)


def ffn_backward_kernel(
    wide, rows_axis, g_ref, x_ref, gain_ref, at_in, pre_in, hidden_in, weight_in, *refs
):
    carried = len(refs) > 21
    if carried:
        ready_in, ready_out = refs[:2]
        refs = refs[2:]
    gx_ref, gain_out, grad_in, grad_out = refs[:4]
    refs = refs[4:]
    if carried:
        sum_in, sum_out = refs[:2]
        refs = refs[2:]
    (
        blocks,
        at,
        pre,
        hidden,
        weight,
        parts,
        landing,
        acc,
        give_in,
        give_out,
        got_in,
        got_out,
        send_sem,
        recv_sem,
        local_sem,
    ) = refs[:15]
    rows = x_ref.shape[0]
    span = weight.shape[1] * TILE
    units = FF // (wide * rows_axis * 2)
    core, row = lax.axis_index("section"), lax.axis_index("rows")
    peers = peers_of(wide)
    sems = (send_sem, recv_sem)
    greet(peers + ([{"rows": row ^ 1}, {"rows": row ^ 2}] if carried else []))
    loads = [
        pltpu.make_async_copy(weight_in, weight, local_sem.at[0]),
        pltpu.make_async_copy(pre_in, pre, local_sem.at[1]),
        pltpu.make_async_copy(hidden_in, hidden, local_sem.at[2]),
        pltpu.make_async_copy(at_in, at, local_sem.at[3]),
    ]
    blocks[0] = g_ref[...].astype(jnp.bfloat16)
    gather = GatherPlane(blocks, sems, 0, peers, rows)
    gather.start()
    for load in loads:
        load.start()
    if carried:
        line = ReduceRows(ready_in, ready_out, *refs[15:19], sems, 12, local_sem, 6)
        line.start()
    scatter = ScatterPlane(parts, landing, sems, 4, peers, rows)
    loads[0].wait()
    loads[1].wait()
    count = token_rows_at_once(wide, rows)
    groups = wide * rows // count

    @pl.loop(0, groups)
    def _(group):
        before_group(gather, group, groups)
        token_rows = pl.ds(pl.multiple_of(group * count, count), count)

        @pl.loop(0, 2)
        def _(half):
            block = block_at(blocks, group, count)
            grad_hidden = matmul(block, weight_tiles(weight, half, 2))
            gate = pre[half, token_rows, pl.ds(0, span)].astype(jnp.float32)
            up = pre[half, token_rows, pl.ds(span, span)].astype(jnp.float32)
            square = gate * gate
            tanh = jnp.tanh(GELU_A * gate * (1.0 + GELU_B * square))
            upper = 0.5 * (1.0 + tanh)
            slope = upper + 0.5 * gate * (1.0 - tanh * tanh) * (
                GELU_A + 3.0 * GELU_A * GELU_B * square
            )
            low_gate = (grad_hidden * up * slope).astype(jnp.bfloat16)
            low_up = (grad_hidden * (gate * upper)).astype(jnp.bfloat16)
            pre[half, token_rows, pl.ds(0, span)] = low_gate
            pre[half, token_rows, pl.ds(span, span)] = low_up
            out = nt(low_gate, weight_tiles(weight, half, 0)) + nt(
                low_up, weight_tiles(weight, half, 1)
            )
            acc[...] = jnp.where(half == 0, 0.0, acc[...]) + out

        put_parts(acc, parts, gx_ref, group, groups, rows)
        after_group(scatter, group, groups)
        if carried:

            @pl.when(group == 1)
            def _():
                line.loaded()
                line.turn(0)

    loads[2].wait()
    loads[3].wait()
    chunk = 2 * TILE
    swap_out = remote(give_out, got_out, sems, 11, peers[-1])
    swap_in = remote(give_in, got_in, sems, 10, peers[-1])
    store_in = pltpu.make_async_copy(got_in, grad_in, local_sem.at[4])
    store_out = pltpu.make_async_copy(got_out, grad_out, local_sem.at[5])
    if carried:
        line.turn(1)

    @pl.loop(0, 2)
    def _(step):
        half = lax.rem(core + 1 + step, 2)
        total = matmul(hidden[half], blocks[...].reshape(wide * rows, D))

        @pl.when(step == 0)
        def _():
            for index in range(rows_axis):
                give_out[index] = total[index * TILE : index * TILE + units].astype(jnp.bfloat16)
            swap_out.start()
            scatter.pass_on()

        @pl.when(step == 1)
        def _():
            swap_out.wait_recv()
            for index in range(rows_axis):
                got_out[index] = (
                    total[index * TILE : index * TILE + units]
                    + got_out[index].astype(jnp.float32)
                ).astype(jnp.bfloat16)
            store_out.start()

    @pl.loop(0, 2 * rows_axis)
    def _(step):
        half = jnp.where(step < rows_axis, 1 - core, core)
        index = lax.rem(step, rows_axis)
        columns = pl.ds(pl.multiple_of(index * chunk, chunk), chunk)
        total = matmul(at[...], pre[half, :, columns])

        @pl.when(step < rows_axis)
        def _():
            for part in range(2):
                give_in[index, part] = total[:, part * TILE : (part + 1) * TILE].astype(
                    jnp.bfloat16
                )

        @pl.when(step == rows_axis - 1)
        def _():
            swap_in.start()
            if carried:
                line.turn(2)

        @pl.when(step == rows_axis)
        def _():
            swap_in.wait_recv()

        @pl.when(step >= rows_axis)
        def _():
            for part in range(2):
                got_in[index, part] = (
                    total[:, part * TILE : (part + 1) * TILE]
                    + got_in[index, part].astype(jnp.float32)
                ).astype(jnp.bfloat16)

    store_in.start()
    total = gx_ref[...] + scatter.total()
    grad_residual, grad_gain = norm_pull(x_ref[...], gain_ref[...], total)
    gx_ref[...] = g_ref[...] + grad_residual
    gain_out[...] = grad_gain
    if carried:
        for index in range(3):
            line.close(index)
        in_buf, out_buf = refs[15], refs[17]
        stores = [
            pltpu.make_async_copy(in_buf.at[0], sum_in, local_sem.at[6]),
            pltpu.make_async_copy(out_buf.at[0], sum_out, local_sem.at[7]),
        ]
        for store in stores:
            store.start()
        for store in stores:
            store.wait()
        line.finish()
    store_in.wait()
    store_out.wait()
    swap_in.wait_send()
    swap_out.wait_send()
    gather.finish()
    scatter.finish()


GELU_A = float(np.sqrt(2.0 / np.pi))
GELU_B = 0.044715


def ffn_backward_call(wide, rows_axis, grad, residual, gain_row, kept, call_id, carried=()):
    at, pre, hidden, weight = kept
    rows = residual.shape[0]
    low = jnp.bfloat16
    units = FF // (wide * rows_axis * 2)
    share_in = (rows_axis, 2, D, TILE)
    share_out = (rows_axis, units, D)
    sums = [jax.ShapeDtypeStruct(each.shape[1:], low) for each in carried]
    return pl.pallas_call(
        lambda *refs: ffn_backward_kernel(wide, rows_axis, *refs),
        out_shape=[
            jax.ShapeDtypeStruct((rows, D), jnp.float32),
            jax.ShapeDtypeStruct((1, D), jnp.float32),
            jax.ShapeDtypeStruct(share_in, low),
            jax.ShapeDtypeStruct(share_out, low),
        ]
        + sums,
        in_specs=[VM, VM, VM, HBM, HBM, HBM, HBM] + [HBM] * len(sums),
        out_specs=[VM, VM, HBM, HBM] + [HBM] * len(sums),
        scratch_shapes=[
            pltpu.VMEM((wide, rows, D), low),
            pltpu.VMEM(at.shape, low),
            pltpu.VMEM(pre.shape, low),
            pltpu.VMEM(hidden.shape, low),
            pltpu.VMEM(weight.shape, low),
            pltpu.VMEM((wide, rows, D), low),
            pltpu.VMEM((3, rows, D), low),
            pltpu.VMEM((token_rows_at_once(wide, rows), D), jnp.float32),
            pltpu.VMEM(share_in, low),
            pltpu.VMEM(share_out, low),
            pltpu.VMEM(share_in, low),
            pltpu.VMEM(share_out, low),
            pltpu.SemaphoreType.DMA((21,)),
            pltpu.SemaphoreType.DMA((21,)),
            pltpu.SemaphoreType.DMA((10,)),
        ]
        + (reduce_rows_scratch(units) if carried else []),
        compiler_params=pltpu.CompilerParams(
            collective_id=call_id, has_side_effects=True, vmem_limit_bytes=VMEM_LIMIT
        ),
        name="ffn_backward_%d" % rows,
    )(grad, residual, gain_row, at, pre, hidden, weight, *carried)


def start_weights_kernel(
    wide, rows, win_in, wout_in, cin_in, cout_in, ffn_in, ffn_out, attn_ref, dec_half, *refs
):
    enc, dec = refs[:wide], refs[wide : 2 * wide]
    held, blocks, spare, in_ref, out_ref, ffn, send_sem, recv_sem, local_sem = refs[2 * wide :]
    core, place = lax.axis_index("section"), lax.axis_index("wide")
    peers = peers_of(wide)
    sibling = peers[-1]
    sems = (send_sem, recv_sem)
    depth = blocks.shape[1]
    big = [
        pltpu.make_async_copy(ffn_in.at[0], in_ref, local_sem.at[4]),
        pltpu.make_async_copy(ffn_out, out_ref, local_sem.at[5]),
    ]
    packs = [
        pltpu.make_async_copy(each, held.at[:, pl.ds(i * HD, HD)], local_sem.at[1 + i])
        for i, each in enumerate((wout_in, cin_in.at[0], cout_in.at[0]))
    ]
    for pack in packs:
        pack.start()
    greet(peers)
    for pack in packs:
        pack.wait()

    @pl.when(core == 0)
    def _():
        keep = pltpu.make_async_copy(win_in.at[0], blocks.at[0], local_sem.at[0])
        keep.start()
        give = remote(held, blocks.at[0], sems, 0, sibling)
        give.start()
        remote(win_in.at[0], spare, sems, 1, sibling).wait_recv()
        keep.wait()

    @pl.when(core == 1)
    def _():
        keep = pltpu.make_async_copy(held, spare, local_sem.at[0])
        keep.start()
        give = remote(win_in.at[0], spare, sems, 1, sibling)
        give.start()
        remote(held, blocks.at[0], sems, 0, sibling).wait_recv()
        keep.wait()

    gather = GatherPlane(blocks, sems, 2, peers, depth)
    gather.start()
    for load in big:
        load.start()
    dec_copy = pltpu.make_async_copy(spare, dec_half, local_sem.at[0])
    dec_copy.start()
    stores, gives = [], []
    for v in range(wide):
        rows_of = pl.ds(pl.multiple_of((place ^ v) * depth, 16), depth)
        stores.append(
            pltpu.make_async_copy(blocks.at[v], attn_ref.at[core, rows_of], local_sem.at[6 + v])
        )
        gives.append(remote(blocks.at[v], attn_ref.at[core, rows_of], sems, 6 + v, sibling))
    stores[0].start()
    gives[0].start()
    for load in big:
        load.wait()
    units = FF // (wide * rows * 2)
    per_row = FF // rows
    row_ids = lax.broadcasted_iota(jnp.int32, (2 * TILE, TILE), 0)
    lane_ids = lax.broadcasted_iota(jnp.int32, (2 * TILE, TILE), 1)
    def prepare(index):
        target, half = index // 2, index % 2
        offset = index * units
        start, shift = offset // TILE * TILE, offset % TILE
        picks = ((row_ids == lane_ids + shift) & (lane_ids < units)).astype(jnp.bfloat16)
        window = min(2 * TILE, per_row - start)
        picks = picks[:window]
        for part in range(3):
            for row in range(rows):
                if part < 2:
                    source = in_ref[:, pl.ds(part * FF + row * per_row + start, window)]
                else:
                    source = out_ref[:, pl.ds(row * per_row + start, window)]
                tile = matmul(source, picks)
                ffn[half, target ^ place, row, :, pl.ds(part * TILE, TILE)] = tile.astype(
                    jnp.bfloat16
                )

    for index in range(2 * wide):
        prepare(index)

    def move(outs, base):
        for v in range(wide):
            pltpu.make_async_copy(ffn.at[core, v], outs[v], local_sem.at[10 + v]).start()
            remote(ffn.at[1 - core, v], outs[v], sems, base + v, sibling).start()

    def settle(outs, base):
        for v in range(wide):
            pltpu.make_async_copy(ffn.at[core, v], outs[v], local_sem.at[10 + v]).wait()
            remote(ffn.at[1 - core, v], outs[v], sems, base + v, sibling).wait_send()

    def receive(outs, base):
        for v in range(wide):
            remote(ffn.at[0, v], outs[v], sems, base + v, sibling).wait_recv()

    @pl.when(core == 0)
    def _():
        move(enc, 10)

    @pl.when(core == 1)
    def _():
        move(dec, 10 + wide)

    for v in range(1, wide):
        gather.arrive(v - 1)
        stores[v].start()
        gives[v].start()
    for v in range(wide):
        gives[v].wait_recv()
        stores[v].wait()
    dec_copy.wait()

    @pl.when(core == 0)
    def _():
        settle(enc, 10)
        receive(dec, 10 + wide)
        remote(held, blocks.at[0], sems, 0, sibling).wait_send()

    @pl.when(core == 1)
    def _():
        settle(dec, 10 + wide)
        receive(enc, 10)
        remote(win_in.at[0], spare, sems, 1, sibling).wait_send()

    gather.finish()
    for give in gives:
        give.wait_send()


def start_weights(wide, rows, attn_in, attn_out, cross_in, cross_out, ffn_in, ffn_out):
    depth = ffn_in.shape[1]
    low = jnp.bfloat16
    block = jax.ShapeDtypeStruct((rows, depth, 3 * TILE), low)
    part = (depth, 3 * HD)
    attn, dec_half, *outs = pl.pallas_call(
        lambda *refs: start_weights_kernel(wide, rows, *refs),
        out_shape=[
            jax.ShapeDtypeStruct((2, wide * depth, 3 * HD), low),
            jax.ShapeDtypeStruct(part, low),
        ]
        + [block] * (2 * wide),
        in_specs=[HBM] * 6,
        out_specs=[HBM] * (2 + 2 * wide),
        scratch_shapes=[
            pltpu.VMEM(part, low),
            pltpu.VMEM((wide,) + part, low),
            pltpu.VMEM(part, low),
            pltpu.VMEM(ffn_in.shape[1:], low),
            pltpu.VMEM((depth, FF), low),
            pltpu.VMEM((2, wide) + block.shape, low),
            pltpu.SemaphoreType.DMA((10 + 2 * wide,)),
            pltpu.SemaphoreType.DMA((10 + 2 * wide,)),
            pltpu.SemaphoreType.DMA((10 + wide,)),
        ],
        compiler_params=pltpu.CompilerParams(
            collective_id=1, has_side_effects=True, vmem_limit_bytes=VMEM_LIMIT
        ),
        name="start_weights",
    )(attn_in, attn_out[0].T, cross_in, cross_out, ffn_in, ffn_out[0].T)
    return attn, dec_half, outs[:wide], outs[wide:]


def split_at(rows):
    return (rows // 2 + 15) // 16 * 16


class ReduceWeights:
    def __init__(self, batch, bufs, sems, base, local_sem, local_base, peers, others, held):
        self.own, self.land, self.plane, self.send, self.zland = bufs
        self.batch, self.held = batch, held
        core, place, row = lax.axis_index("section"), lax.axis_index("wide"), lax.axis_index("rows")
        wide, size = self.own.shape[:2]
        depth = batch.shape[0] // wide

        def rows_at(v, half):
            start = (place ^ v) * depth + half * (depth - size)
            return pl.ds(pl.multiple_of(start, 16), size)

        self.mine = [rows_at(v, core) for v in range(wide)]
        self.loads = [
            pltpu.make_async_copy(batch.at[self.mine[v]], self.own.at[v], local_sem.at[local_base + v])
            for v in range(0 if held else wide)
        ]
        self.swaps = [
            remote(batch.at[rows_at(v, 1 - core)], self.land.at[v], sems, base + v, peers[-1])
            for v in range(wide)
        ]
        base += wide
        self.scatter = ScatterPlane(self.own, self.plane, sems, base, peers, size)
        base += 6
        chunk = batch.shape[1] // (len(others) + 1)
        self.row, self.chunk = row, chunk
        self.spreads = [
            remote(
                self.send.at[:, pl.ds(pl.multiple_of((row ^ k) * chunk, TILE), chunk)],
                self.zland.at[k - 1],
                sems,
                base + k - 1,
                others[k - 1],
            )
            for k in range(1, len(others) + 1)
        ]

    def start(self):
        for v in (3, 1, 2, 0):
            self.swaps[v].start()
            if not self.held:
                self.loads[v].start()

    def join(self):
        def add(v):
            self.swaps[v].wait_recv()
            if self.held:
                own = self.batch[self.mine[v], :]
            else:
                self.loads[v].wait()
                own = self.own[v]
            self.own[v] = (own.astype(jnp.float32) + self.land[v].astype(jnp.float32)).astype(
                jnp.bfloat16
            )

        add(3)
        self.scatter.send_far()
        add(1)
        self.scatter.send_early(0)
        add(2)
        self.scatter.send_early(1)
        add(0)

    def given(self):
        for swap in self.swaps:
            swap.wait_send()

    def pass_on(self):
        self.scatter.pass_on()

    def spread(self):
        self.send[...] = (self.own[0].astype(jnp.float32) + self.scatter.total()).astype(
            jnp.bfloat16
        )
        for copy in self.spreads:
            copy.start()

    def total(self):
        for copy in self.spreads:
            copy.wait_recv()
        lanes = pl.ds(pl.multiple_of(self.row * self.chunk, TILE), self.chunk)
        out = self.send[:, lanes].astype(jnp.float32)
        for k in range(len(self.spreads)):
            out = out + self.zland[k].astype(jnp.float32)
        return out

    def finish(self):
        for copy in self.spreads:
            copy.wait_send()
        self.scatter.finish()


def reduce_weights_scratch(wide, rows, size, columns):
    low = jnp.bfloat16
    return [
        pltpu.VMEM((wide, size, columns), low),
        pltpu.VMEM((wide, size, columns), low),
        pltpu.VMEM((3, size, columns), low),
        pltpu.VMEM((size, columns), low),
        pltpu.VMEM((rows - 1, size, columns // rows), low),
    ]


def last_kernel(wide, rows, *refs):
    cross_ref, dec_in, dec_out, enc_in, enc_out, y_ref, dec_attn, enc_attn = refs[:8]
    dec_self, enc_self, gains = refs[8:15], refs[15:22], refs[22:26]
    out_ref, ffn_ref, small_out, y_half, x_half, t_half = refs[26:32]
    refs = refs[32:]
    batch_bufs = [refs[i * 5 : i * 5 + 5] for i in range(3)]
    line_bufs, refs = refs[15:19], refs[19:]
    held, win, wout, gx, gt, context_e, projected_e, context_d, projected_d = refs[:9]
    keep, give, ready, landing, small, small_land, small_plane, small_rows = refs[9:17]
    halves, (send_sem, recv_sem, local_sem) = refs[17:23], refs[23:]
    core, place, row = lax.axis_index("section"), lax.axis_index("wide"), lax.axis_index("rows")
    peers = peers_of(wide)
    sibling = peers[-1]
    crossed = [{"section": 1 - core, "wide": place ^ v} for v in range(1, wide)]
    others = [{"rows": row ^ k} for k in range(1, rows)]
    sems = (send_sem, recv_sem)
    depth = cross_ref.shape[0] // wide
    units = dec_out.shape[0]
    low = jnp.bfloat16
    straight = (
        lax.broadcasted_iota(jnp.int32, (units, TILE), 0)
        == lax.broadcasted_iota(jnp.int32, (units, TILE), 1)
    ).astype(low)

    def attn_loads(source):
        return [
            pltpu.make_async_copy(source.at[0], win, local_sem.at[0]),
            pltpu.make_async_copy(source.at[1, :, pl.ds(0, HD)], wout, local_sem.at[1]),
        ]

    for load in attn_loads(dec_attn):
        load.start()
    greet(peers + crossed + others)
    per_batch = wide + 6 + rows - 1
    batches = [
        ReduceWeights(
            batch, bufs, sems, i * per_batch, local_sem, 2, peers, others, i > 0
        )
        for i, (batch, bufs) in enumerate(zip((cross_ref, held, held), batch_bufs))
    ]
    base = 3 * per_batch
    line = ReduceRows(enc_in, enc_out, *line_bufs, sems, base, local_sem, 2 + wide)
    base += 9
    local_base = 6 + wide
    first = remote(small.at[1 - core], small_land, sems, base, sibling)
    plane = [
        remote(small.at[core], small_plane.at[v - 1], sems, base + v, peers[v - 1])
        for v in range(1, wide)
    ]
    base += wide
    spread_small = [
        remote(small.at[core], small_rows.at[k - 1], sems, base + k - 1, others[k - 1])
        for k in range(1, rows)
    ]
    base += rows - 1
    hand_base = base
    base += 2 * wide

    def hand(section, source, v):
        return pltpu.make_async_remote_copy(
            src_ref=ready.at[section, v],
            dst_ref=landing.at[source, v],
            send_sem=send_sem.at[hand_base + section * wide + v],
            recv_sem=recv_sem.at[hand_base + source * wide + v],
            device_id={"section": section, "wide": place ^ v},
            device_id_type=MESH,
        )

    def hand_home(section):
        return pltpu.make_async_copy(ready.at[section, 0], landing.at[core, 0], local_sem.at[local_base])

    def hand_out(section, part_in, part_out):
        turned = tn(part_out, straight).astype(low)
        for owner in range(wide):
            own = slice(owner * depth, (owner + 1) * depth)
            for part in range(2):
                ready[section, owner ^ place, :, pl.ds(part * TILE, TILE)] = part_in[part][own]
            ready[section, owner ^ place, :, pl.ds(2 * TILE, TILE)] = turned[own]
        for v in range(1, wide):
            hand(section, core, v).start()

        @pl.when(core == section)
        def _():
            hand_home(section).start()

        @pl.when(core != section)
        def _():
            hand(section, core, 0).start()

    def handed(section):
        for v in range(1, wide):
            hand(section, core, v).wait_send()

        @pl.when(core == section)
        def _():
            hand_home(section).wait()

        @pl.when(core != section)
        def _():
            hand(section, core, 0).wait_send()

    def came(source):
        for v in range(1, wide):
            hand(0, source, v).wait_recv()

        @pl.when(core != source)
        def _():
            hand(0, source, 0).wait_recv()

    half_copies = []

    def by_half(index, value, target):
        mine, its = halves[2 * index : 2 * index + 2]
        middle = D // 2
        for own in range(2):

            @pl.when(core == own)
            def _():
                parts = value[:, :middle], value[:, middle:]
                mine[...] = parts[own].astype(mine.dtype)
                its[...] = parts[1 - own].astype(its.dtype)

        copies = (
            pltpu.make_async_copy(mine, target.at[core], local_sem.at[local_base + 1 + index]),
            remote(its, target.at[core], sems, base + index, sibling),
        )
        for copy in copies:
            copy.start()
            half_copies.append(copy)

    line.start()
    batches[0].start()
    by_half(0, y_ref[...], y_half)
    small[...] = jnp.zeros_like(small)
    for i, gain in enumerate(gains):
        small[i // 2, pl.ds(1 + i % 2, 1), pl.ds(0, D)] = gain[...]
    hand_out(1, [dec_in[0], dec_in[1]], dec_out[...])
    g_ref, x_ref, gain_ref, normed_ref, projected_ref, context_ref, weights_ref = dec_self
    for load in attn_loads(dec_attn):
        load.wait()
    self_backward_rows(
        g_ref, x_ref, gain_ref, win, wout, projected_ref, weights_ref, gt, small.at[1], context_d, projected_d
    )
    for load in attn_loads(enc_attn):
        load.start()
    batches[0].join()
    self_backward_weights(g_ref, normed_ref, context_ref, projected_d, held)
    batches[1].start()
    by_half(2, gt[...], t_half)
    line.loaded()
    line.turn(0)
    g_ref, x_ref, gain_ref, normed_ref, projected_ref, context_ref, weights_ref = enc_self
    for load in attn_loads(enc_attn):
        load.wait()
    self_backward_rows(
        g_ref, x_ref, gain_ref, win, wout, projected_ref, weights_ref, gx, small.at[0], context_e, projected_e
    )
    first.start()
    batches[1].join()
    batches[0].pass_on()
    batches[1].given()
    self_backward_weights(g_ref, normed_ref, context_ref, projected_e, held)
    batches[2].start()
    by_half(1, gx[...], x_half)
    line.turn(1)
    batches[2].join()
    batches[0].spread()
    first.wait()
    small[core] = small[core] + small_land[...]
    for copy in plane:
        copy.start()
    batches[1].pass_on()
    line.turn(2)
    batches[1].spread()
    batches[2].pass_on()
    for copy in plane:
        copy.wait()
    small[core] = small[core] + jnp.sum(small_plane[...], axis=0)
    for copy in spread_small:
        copy.start()
    batches[2].spread()
    for index in range(3):
        line.close(index)
    hand_out(0, [line_bufs[0][0, 0], line_bufs[0][0, 1]], line_bufs[2][0])
    span, part = keep.shape[1] - cross_ref.shape[1] // rows // 2, cross_ref.shape[1] // rows // 2
    crosses = batches[0].total()
    selfs = [batches[2].total(), batches[1].total()]
    for own in range(2):

        @pl.when(core == own)
        def _():
            keep[:, pl.ds(0, span)] = selfs[own]
            keep[:, pl.ds(span, part)] = crosses[:, own * part : (own + 1) * part]
            give[:, pl.ds(0, span)] = selfs[1 - own]
            give[:, pl.ds(span, part)] = crosses[:, (1 - own) * part : (2 - own) * part]

    store = pltpu.make_async_copy(keep, out_ref.at[core], local_sem.at[local_base + 4])
    last = remote(give, out_ref.at[core], sems, base + 3, sibling)
    store.start()
    last.start()
    for copy in spread_small:
        copy.wait()
    small_out[...] = small[core] + jnp.sum(small_rows[...], axis=0)
    handed(0)
    handed(1)
    came(0)
    came(1)
    store_ffn = pltpu.make_async_copy(landing, ffn_ref, local_sem.at[local_base + 5])
    store_ffn.start()
    store.wait()
    last.wait()
    store_ffn.wait()
    for copy in half_copies:
        copy.wait()
    batches[0].given()
    batches[2].given()
    for batch in batches:
        batch.finish()
    line.finish()


def last_step(wide, rows, cross, dec_sums, enc_shares, y3, dec_attn, enc_attn, dec_self, enc_self, gains):
    low = jnp.bfloat16
    depth = D // wide
    size = split_at(depth)
    units = dec_sums[1].shape[0]
    columns = cross.shape[1]
    enc_rows, dec_rows = enc_self[0].shape[0], dec_self[0].shape[0]
    wanted = (columns + columns // 2) // rows
    copies = 3 * (wide + 6 + rows - 1) + 9 + wide + rows - 1 + 2 * wide + 4
    small = (16, (D + TILE - 1) // TILE * TILE)
    middle = D // 2
    half_shapes = [(dec_rows, low), (enc_rows, jnp.float32), (dec_rows, jnp.float32)]
    batch_scratch = reduce_weights_scratch(wide, rows, size, columns)
    return pl.pallas_call(
        lambda *refs: last_kernel(wide, rows, *refs),
        out_shape=[
            jax.ShapeDtypeStruct((2, size, wanted), jnp.float32),
            jax.ShapeDtypeStruct((2, wide, depth, 3 * TILE), low),
            jax.ShapeDtypeStruct(small, jnp.float32),
        ]
        + [jax.ShapeDtypeStruct((2, each, middle), kind) for each, kind in half_shapes],
        in_specs=[HBM, VM, VM, HBM, HBM, VM, HBM, HBM] + [VM] * 18,
        out_specs=[HBM, HBM, VM, HBM, HBM, HBM],
        scratch_shapes=batch_scratch * 3
        + reduce_rows_scratch(units)
        + [
            pltpu.VMEM((D, columns), low),
            pltpu.VMEM((D, 3 * HD), low),
            pltpu.VMEM((D, HD), low),
            pltpu.VMEM((enc_rows, D), jnp.float32),
            pltpu.VMEM((dec_rows, D), jnp.float32),
            pltpu.VMEM((enc_rows, HD), low),
            pltpu.VMEM((enc_rows, 3 * HD), low),
            pltpu.VMEM((dec_rows, HD), low),
            pltpu.VMEM((dec_rows, 3 * HD), low),
            pltpu.VMEM((size, wanted), jnp.float32),
            pltpu.VMEM((size, wanted), jnp.float32),
            pltpu.VMEM((2, wide, depth, 3 * TILE), low),
            pltpu.VMEM((2, wide, depth, 3 * TILE), low),
            pltpu.VMEM((2,) + small, jnp.float32),
            pltpu.VMEM(small, jnp.float32),
            pltpu.VMEM((wide - 1,) + small, jnp.float32),
            pltpu.VMEM((rows - 1,) + small, jnp.float32),
        ]
        + [pltpu.VMEM((each, middle), kind) for each, kind in half_shapes for _ in range(2)]
        + [
            pltpu.SemaphoreType.DMA((copies,)),
            pltpu.SemaphoreType.DMA((copies,)),
            pltpu.SemaphoreType.DMA((12 + wide,)),
        ],
        compiler_params=pltpu.CompilerParams(
            collective_id=7, has_side_effects=True, vmem_limit_bytes=VMEM_LIMIT
        ),
        name="last_step",
    )(cross, *dec_sums, *enc_shares, y3, dec_attn, enc_attn, *dec_self, *enc_self, *gains)


def assemble_kernel(
    units, parts_ref, attn_ref, small_ref, enc_hot, dec_hot,
    in_ref, out_ref, gain_ref, bias_ref, win_ref, wout_ref, cin_ref, cout_ref,
):
    low = jnp.bfloat16
    wide = parts_ref.shape[1]
    place, core = lax.axis_index("wide"), lax.axis_index("section")
    pairs = 2 * wide
    row_ids = lax.broadcasted_iota(jnp.int32, (TILE, TILE), 0)
    lane_ids = lax.broadcasted_iota(jnp.int32, (TILE, TILE), 1)

    def tile_at(tile, first, columns):
        total = None
        last = min((tile + 1) * TILE, columns) - 1
        for group in range(tile * TILE // units, last // units + 1):
            half, chip, block = group % 2, group % pairs // 2, group // pairs
            shift = group * units - tile * TILE
            picks = ((row_ids + shift == lane_ids) & (row_ids < units)).astype(low)
            part = matmul(
                parts_ref[half, chip ^ place, :, pl.ds((first + block) * TILE, TILE)], picks
            )
            total = part if total is None else total + part
        return total

    for tile in range(in_ref.shape[2] // TILE):
        in_ref[0, :, pl.ds(tile * TILE, TILE)] = tile_at(tile, 0, in_ref.shape[2])
    for tile in range(out_ref.shape[2] // TILE):
        out_ref[0, :, pl.ds(tile * TILE, TILE)] = tile_at(tile, 2, out_ref.shape[2])
    gain_ref[0] = small_ref[0:3, 0:D]
    for section, hot in enumerate((enc_hot, dec_hot)):

        @pl.when(core == section)
        def _():
            sums = small_ref[8:16, 0 : hot.shape[1]]
            bias = lax.dot_general(
                hot[...], sums, (((1,), (1,)), ((), ())), precision=HIGHEST, preferred_element_type=jnp.float32
            )
            bias_ref[0] = bias[:, :H]

    size, depth = attn_ref.shape[1], in_ref.shape[1]
    whole = jnp.concatenate([attn_ref[0], attn_ref[1, 2 * size - depth :]], axis=0)
    width_in, width = win_ref.shape[2], cin_ref.shape[2]
    win_ref[0] = whole[:, :width_in]
    base = width_in // TILE * TILE
    turned = whole[:, base : base + TILE].T
    wout_ref[0] = turned[width_in - base : width_in - base + width]
    cin_ref[0] = whole[:, width_in + width : width_in + 2 * width]
    cout_ref[0] = whole[:, width_in + 2 * width : width_in + 3 * width]


def assemble(rows, parts, attn_parts, small):
    wide, depth = parts.shape[1:3]
    shapes = [
        (depth, 2 * FF // rows),
        (depth, FF // rows),
        (3, D),
        (NB, H),
        (depth, 3 * HD // rows),
        (HD // rows, depth),
        (depth, HD // rows),
        (depth, HD // rows),
    ]
    return pl.pallas_call(
        lambda *refs: assemble_kernel(FF // (wide * rows * 2), *refs),
        out_shape=[jax.ShapeDtypeStruct((1, *shape), jnp.float32) for shape in shapes],
        in_specs=[VM] * 5,
        out_specs=[VM] * len(shapes),
        compiler_params=pltpu.CompilerParams(vmem_limit_bytes=VMEM_LIMIT),
        name="assemble",
    )(
        parts,
        attn_parts,
        small,
        distance_hot(LE, True, 1 - LE),
        distance_hot(LD, False, 1 - LD),
    )


def bias_rows_kernel(enc_ref, dec_ref, enc_out, dec_out):
    for source, target in ((enc_ref, enc_out), (dec_ref, dec_out)):
        length, span = target.shape[1], source.shape[1]
        for head in range(H):
            row = jnp.broadcast_to(source[pl.ds(head, 1), :], (length, span))
            target[head] = pltpu.roll(row, 0, 1, stride=1, stride_axis=0)[:, :length]


def bias_rows(enc_row, dec_row):
    return pl.pallas_call(
        bias_rows_kernel,
        out_shape=[
            jax.ShapeDtypeStruct((H, LE, LE), jnp.float32),
            jax.ShapeDtypeStruct((H, LD, LD), jnp.float32),
        ],
        in_specs=[VM, VM],
        out_specs=[VM, VM],
        name="bias_rows",
    )(enc_row, dec_row)


def distance_sums(scores, span):
    length = scores.shape[0]
    flip = (
        lax.broadcasted_iota(jnp.int32, (length, length), 0)
        + lax.broadcasted_iota(jnp.int32, (length, length), 1)
        == length - 1
    ).astype(jnp.bfloat16)
    flipped = matmul(flip, scores)
    padded = jnp.concatenate([flipped, jnp.zeros((length, span - length), jnp.float32)], axis=1)
    rolled = pltpu.roll(padded, 0, 1, stride=1, stride_axis=0)
    return jnp.sum(rolled, axis=0, keepdims=True)


def distance_hot(length, both_ways, first):
    table = bucket_table(length, both_ways)
    span = 2 * length
    hot = np.zeros((NB, span), np.float32)
    for entry in range(span):
        distance = entry + first
        if first == 0 and distance >= length:
            distance -= span
        if -length < distance < length:
            query = max(0, -distance)
            hot[table[query, query + distance], entry] = 1.0
    return jnp.asarray(hot)


def head_lanes(value, side):
    lanes = lax.broadcasted_iota(jnp.int32, value.shape, 1)
    return jnp.where((lanes < DH) == (side == 0), value, jnp.zeros_like(value))


def attend_heads(query_of, key_of, value_of, bias_of, allowed, context_ref, weights_ref):
    for pair in range(H // 2):
        query, key, value = query_of(pair), key_of(pair), value_of(pair)
        total = None
        for side in range(2):
            head = 2 * pair + side
            scores = nt(head_lanes(query, side), key)
            if bias_of is not None:
                scores = scores + bias_of(head)
            scores = jnp.where(allowed, scores, NEGATIVE)
            shifted = jnp.exp(scores - jnp.max(scores, axis=-1, keepdims=True))
            weights = shifted / jnp.sum(shifted, axis=-1, keepdims=True)
            weights_ref[head] = weights
            part = matmul(weights.astype(jnp.bfloat16), head_lanes(value, side))
            total = part if total is None else total + part
        context_ref[:, pl.ds(pair * TILE, TILE)] = total.astype(jnp.bfloat16)


def attend_heads_backward(query_of, key_of, value_of, weights_ref, grad_of, put, put_scores=None):
    for pair in range(H // 2):
        query, key, value, grad = query_of(pair), key_of(pair), value_of(pair), grad_of(pair)
        sums = [None, None, None]
        for side in range(2):
            head = 2 * pair + side
            weights = weights_ref[head]
            own_grad = head_lanes(grad, side)
            grad_weights = nt(own_grad, value)
            inner = jnp.sum(grad_weights * weights, axis=-1, keepdims=True)
            low = (weights * (grad_weights - inner)).astype(jnp.bfloat16)
            if put_scores is not None:
                put_scores(head, low)
            parts = [
                matmul(low, head_lanes(key, side)),
                tn(low, head_lanes(query, side)),
                tn(weights.astype(jnp.bfloat16), own_grad),
            ]
            sums = [b if a is None else a + b for a, b in zip(sums, parts)]
        put(pair, *sums)


def weight_spec(half, width, index):
    return pl.BlockSpec((None, D, width), lambda step: (half, 0, index), memory_space=pltpu.VMEM)


W_IN = weight_spec(0, 3 * HD, 0)
W_OUT, C_IN, C_OUT = [weight_spec(1, HD, i) for i in range(3)]


def tile_of(ref, base):
    return lambda pair: ref[:, pl.ds(base + pair * TILE, TILE)]


def self_forward_kernel(wide, causal, x_ref, gain_ref, win_ref, wout_ref, bias_ref, col_ref, row_ref, *refs):
    if wide:
        blocks, dec_blocks, refs = refs[: wide - 1], refs[wide - 1 : 2 * wide - 2], refs[2 * wide - 2 :]
    y_ref, normed_ref, projected_ref, context_ref, weights_ref = refs[:5]
    if wide:
        pieces, dec_pieces, sems = refs[5 : 4 + wide], refs[4 + wide : 3 + 2 * wide], refs[3 + 2 * wide :]
        peers = peers_of(wide)
        greet(peers + [{"rows": lax.axis_index("rows") ^ 1}])
        reshard = Reshard(blocks, pieces, blocks[0].shape[0] // 2, sems, 0, peers)
        reshard.start()
        half = dec_pieces[0].shape[0]
        mine = pl.ds(lax.axis_index("rows") % 2 * half, half)
        later = [
            remote(block.at[mine], piece, sems, 9 + v, peers[v])
            for v, (block, piece) in enumerate(zip(dec_blocks, dec_pieces))
        ]
    residual = x_ref[...].astype(jnp.float32)
    normed_ref[...] = (residual * rms_rows(residual) * gain_ref[...]).astype(jnp.bfloat16)
    projected_ref[...] = matmul(normed_ref[...], win_ref[...]).astype(jnp.bfloat16)
    allowed = col_ref[...] == row_ref[...]
    if causal:
        length = x_ref.shape[0]
        allowed = allowed & (
            lax.broadcasted_iota(jnp.int32, (length, length), 0)
            >= lax.broadcasted_iota(jnp.int32, (length, length), 1)
        )
    attend_heads(
        tile_of(projected_ref, 0),
        tile_of(projected_ref, HD),
        tile_of(projected_ref, 2 * HD),
        lambda head: bias_ref[head],
        allowed,
        context_ref,
        weights_ref,
    )
    y_ref[...] = residual + nt(context_ref[...], wout_ref[...])
    if wide:
        reshard.pass_on()
        for copy in later:
            copy.start()
        reshard.finish()
        for copy in later:
            copy.wait()


def self_forward(causal, residual, gain_row, weight, bias, items, blocks=(), dec_blocks=()):
    rows = residual.shape[0]
    low = jnp.bfloat16
    wide = len(blocks) + 1 if blocks else 0
    params = dict(vmem_limit_bytes=VMEM_LIMIT)
    if blocks:
        params.update(collective_id=6, has_side_effects=True)
    y, *kept = pl.pallas_call(
        lambda *refs: self_forward_kernel(wide, causal, *refs),
        out_shape=[
            jax.ShapeDtypeStruct((rows, D), jnp.float32),
            jax.ShapeDtypeStruct((rows, D), low),
            jax.ShapeDtypeStruct((rows, 3 * HD), low),
            jax.ShapeDtypeStruct((rows, HD), low),
            jax.ShapeDtypeStruct((H, rows, rows), jnp.float32),
        ]
        + [jax.ShapeDtypeStruct(each.shape, low) for each in blocks]
        + [jax.ShapeDtypeStruct((each.shape[0] // 2, *each.shape[1:]), low) for each in dec_blocks],
        in_specs=[VM, VM, W_IN, W_OUT, VM, VM, VM] + [HBM] * (2 * len(blocks)),
        out_specs=[VM] * 5 + [HBM] * (2 * len(blocks)),
        scratch_shapes=[pltpu.SemaphoreType.DMA((12,))] * 2 if blocks else [],
        grid=(1,),
        compiler_params=pltpu.CompilerParams(**params),
        name="self_forward_%d" % rows,
    )(residual, gain_row, weight, weight, bias, items[:, None], items[None, :], *blocks, *dec_blocks)
    return y, kept[:4], kept[4:]


def picked(source, start, window, first, width):
    base = start // TILE * TILE
    window = min(window, source.shape[1] - base)
    lanes = lax.broadcasted_iota(jnp.int32, (window, HD), 1) - first
    rows_of = lax.broadcasted_iota(jnp.int32, (window, HD), 0) + (base - start)
    pick = ((rows_of == lanes) & (lanes >= 0) & (lanes < width)).astype(jnp.bfloat16)
    return matmul(source[:, pl.ds(base, window)], pick)


def self_backward_rows(
    g_ref,
    x_ref,
    gain_ref,
    win_ref,
    wout_ref,
    projected_ref,
    weights_ref,
    gx_ref,
    small_ref,
    context_grad,
    projected_grad,
):
    low = jnp.bfloat16
    length = x_ref.shape[0]
    context_grad[...] = matmul(g_ref[...].astype(low), wout_ref[...]).astype(low)

    def put(pair, query, key, value):
        for index, part in enumerate((query, key, value)):
            projected_grad[:, pl.ds(index * HD + pair * TILE, TILE)] = part.astype(low)

    def put_scores(head, scores):
        small_ref[pl.ds(8 + head, 1), pl.ds(0, 2 * length)] = distance_sums(scores, 2 * length)

    attend_heads_backward(
        tile_of(projected_ref, 0),
        tile_of(projected_ref, HD),
        tile_of(projected_ref, 2 * HD),
        weights_ref,
        tile_of(context_grad, 0),
        put,
        put_scores,
    )
    grad_normed = nt(projected_grad[...], win_ref[...])
    residual = x_ref[...].astype(jnp.float32)
    grad_residual, grad_gain = norm_pull(residual, gain_ref[...], grad_normed)
    small_ref[pl.ds(0, 1), pl.ds(0, D)] = grad_gain
    gx_ref[...] = g_ref[...] + grad_residual


def self_backward_weights(g_ref, normed_ref, context_ref, projected_grad, grad_ref):
    low = jnp.bfloat16
    both = jnp.concatenate([normed_ref[...], g_ref[...].astype(low)], axis=0)
    chunks = grad_ref.shape[1] // HD
    part_in, part_out = 3 * HD // chunks, HD // chunks
    for chunk in range(chunks):
        right = jnp.concatenate(
            [
                picked(projected_grad, chunk * part_in, HD, 0, part_in),
                picked(context_ref, chunk * part_out, 2 * TILE, part_in, part_out),
            ],
            axis=0,
        ).astype(low)
        grad_ref[:, pl.ds(chunk * HD, HD)] = tn(both, right).astype(low)


def cross_forward_kernel(
    x_ref, final_ref, wkey_ref, wvalue_ref, y_ref, gain_ref, wquery_ref, wout_ref, col_ref, row_ref,
    out_ref, memory_ref, kv_ref, normed_ref, query_ref, context_ref, weights_ref,
):
    low = jnp.bfloat16
    residual = x_ref[...]
    memory_ref[...] = (residual * rms_rows(residual) * final_ref[...]).astype(low)
    kv_ref[:, pl.ds(0, HD)] = matmul(memory_ref[...], wkey_ref[...]).astype(low)
    kv_ref[:, pl.ds(HD, HD)] = matmul(memory_ref[...], wvalue_ref[...]).astype(low)
    target = y_ref[...]
    normed_ref[...] = (target * rms_rows(target) * gain_ref[...]).astype(low)
    query_ref[...] = matmul(normed_ref[...], wquery_ref[...]).astype(low)
    attend_heads(
        tile_of(query_ref, 0),
        tile_of(kv_ref, 0),
        tile_of(kv_ref, HD),
        None,
        col_ref[...] == row_ref[...],
        context_ref,
        weights_ref,
    )
    out_ref[...] = target + nt(context_ref[...], wout_ref[...])


def cross_forward(x2, final_gain, enc_weight, y1, gain_row, dec_weight, dec_items, enc_items):
    low = jnp.bfloat16
    y2, *kept = pl.pallas_call(
        cross_forward_kernel,
        out_shape=[
            jax.ShapeDtypeStruct((LD, D), jnp.float32),
            jax.ShapeDtypeStruct((LE, D), low),
            jax.ShapeDtypeStruct((LE, 2 * HD), low),
            jax.ShapeDtypeStruct((LD, D), low),
            jax.ShapeDtypeStruct((LD, HD), low),
            jax.ShapeDtypeStruct((LD, HD), low),
            jax.ShapeDtypeStruct((H, LD, LE), jnp.float32),
        ],
        in_specs=[VM, VM, C_IN, C_OUT, VM, VM, C_IN, C_OUT, VM, VM],
        out_specs=[VM] * 7,
        grid=(1,),
        compiler_params=pltpu.CompilerParams(vmem_limit_bytes=VMEM_LIMIT),
        name="cross_forward",
    )(
        x2,
        final_gain,
        enc_weight,
        enc_weight,
        y1,
        gain_row,
        dec_weight,
        dec_weight,
        dec_items[:, None],
        enc_items[None, :],
    )
    return y2, kept


def cross_backward_kernel(
    g_ref, x_ref, final_ref, wkey_ref, wvalue_ref, y_ref, gain_ref, wquery_ref, wout_ref, kv_ref, query_ref, weights_ref,
    memory_ref, normed_ref, context_ref, gx_ref, gy_ref, final_out, gain_out, grad_ref, kv_grad, query_grad, context_grad,
):
    low = jnp.bfloat16
    grad_low = g_ref[...].astype(low)
    context_grad[...] = matmul(grad_low, wout_ref[...]).astype(low)

    def put(pair, query, key, value):
        query_grad[:, pl.ds(pair * TILE, TILE)] = query.astype(low)
        kv_grad[:, pl.ds(pair * TILE, TILE)] = key.astype(low)
        kv_grad[:, pl.ds(HD + pair * TILE, TILE)] = value.astype(low)

    attend_heads_backward(
        tile_of(query_ref, 0),
        tile_of(kv_ref, 0),
        tile_of(kv_ref, HD),
        weights_ref,
        tile_of(context_grad, 0),
        put,
    )
    grad_memory = nt(kv_grad[:, pl.ds(0, HD)], wkey_ref[...]) + nt(
        kv_grad[:, pl.ds(HD, HD)], wvalue_ref[...]
    )
    gx_ref[...], final_out[...] = norm_pull(x_ref[...], final_ref[...], grad_memory)
    grad_residual, gain_out[...] = norm_pull(
        y_ref[...], gain_ref[...], nt(query_grad[...], wquery_ref[...])
    )
    gy_ref[...] = g_ref[...] + grad_residual
    lefts = jnp.concatenate([memory_ref[...], normed_ref[...], grad_low], axis=0)
    chunks = grad_ref.shape[1] // HD
    part = HD // chunks
    for chunk in range(chunks):
        start = chunk * part
        right = jnp.concatenate(
            [
                picked(kv_grad, start, 2 * TILE, 0, part)
                + picked(kv_grad, HD + start, 2 * TILE, part, part),
                picked(query_grad, start, 2 * TILE, 2 * part, part),
                picked(context_ref, start, 2 * TILE, 3 * part, part),
            ],
            axis=0,
        ).astype(low)
        grad_ref[:, pl.ds(chunk * HD, HD)] = tn(lefts, right).astype(low)


def cross_backward(g2, x2, final_gain, enc_weight, y1, gain_row, dec_weight, kept):
    memory, kv, normed, query, context, weights = kept
    low = jnp.bfloat16
    return pl.pallas_call(
        cross_backward_kernel,
        out_shape=[
            jax.ShapeDtypeStruct((LE, D), jnp.float32),
            jax.ShapeDtypeStruct((LD, D), jnp.float32),
            jax.ShapeDtypeStruct((1, D), jnp.float32),
            jax.ShapeDtypeStruct((1, D), jnp.float32),
            jax.ShapeDtypeStruct((D, 4 * HD), low),
        ],
        in_specs=[VM, VM, VM, C_IN, C_OUT, VM, VM, C_IN, C_OUT] + [VM] * 6,
        out_specs=[VM] * 5,
        scratch_shapes=[
            pltpu.VMEM((LE, 2 * HD), low),
            pltpu.VMEM((LD, HD), low),
            pltpu.VMEM((LD, HD), low),
        ],
        grid=(1,),
        compiler_params=pltpu.CompilerParams(vmem_limit_bytes=VMEM_LIMIT),
        name="cross_backward",
    )(
        g2,
        x2,
        final_gain,
        enc_weight,
        enc_weight,
        y1,
        gain_row,
        dec_weight,
        dec_weight,
        kv,
        query,
        weights,
        memory,
        normed,
        context,
    )


def plain_self_forward(residual, gain_row, weight, bias_full, allowed):
    normed = to_low(rms_norm(residual, gain_row))
    projected = to_low(matmul(normed, weight[:, : 3 * HD]))
    context, weights, low_weights = attend_forward(
        projected[:, :HD], projected[:, HD : 2 * HD], projected[:, 2 * HD :], bias_full, allowed
    )
    return (
        residual + matmul(context, weight[:, 3 * HD : 4 * HD].T),
        (residual, normed, projected, context, weights, low_weights),
    )


def plain_self_backward(kept, gain_row, weight, hot, grad_out):
    residual, normed, projected, context, weights, low_weights = kept
    grad_low = to_low(grad_out)
    grad_wout = matmul(grad_low.T, context)
    grad_context = to_low(matmul(grad_low, weight[:, 3 * HD : 4 * HD]))
    grad_queries, grad_keys, grad_values, low_scores = attend_backward(
        projected[:, :HD],
        projected[:, HD : 2 * HD],
        projected[:, 2 * HD :],
        weights,
        low_weights,
        grad_context,
    )
    grad_projected = to_low(jnp.concatenate([grad_queries, grad_keys, grad_values], axis=1))
    grad_win = matmul(normed.T, grad_projected)
    grad_residual, grad_gain = plain_norm_backward(
        residual, gain_row, matmul(grad_projected, weight[:, : 3 * HD].T)
    )
    grad_bias = jnp.einsum(
        "hqk,qkb->bh", low_scores, hot.astype(jnp.bfloat16), preferred_element_type=jnp.float32
    )
    return grad_out + grad_residual, grad_gain, grad_win, grad_wout, grad_bias


def plain_reduce_attn(grad, core, wide, rows):
    depth, columns = grad.shape
    halves = plain_core_halves(grad, core, wide)
    place = lax.axis_index("wide")
    parts = [
        lax.dynamic_index_in_dim(halves, place ^ v, 0, keepdims=False) for v in range(wide)
    ]
    mine = to_low(scatter_wide(parts))
    pieces, start = [], 0
    for width in (3 * HD, HD, HD, HD):
        pieces.append(mine[:, start : start + width].reshape(mine.shape[0], rows, width // rows))
        start += width
    stacked = jnp.concatenate(pieces, axis=2).transpose(1, 0, 2)
    return lax.psum_scatter(stacked, "rows", scatter_dimension=0, tiled=True)[0]


def plain_core_halves(grad, core, wide):
    depth, columns = grad.shape
    split = to_low(grad).reshape(wide, 2, depth // wide // 2, columns)
    mine = lax.dynamic_index_in_dim(split, core, 1, keepdims=False)
    sent = lax.dynamic_index_in_dim(split, 1 - core, 1, keepdims=False)
    return mine.astype(jnp.float32) + xor_permute(sent, "section", 1).astype(jnp.float32)


def plain_both_sections(own, section):
    other = xor_permute(own, "section", 1)
    is_dec = section == 1
    return jnp.where(is_dec, other, own), jnp.where(is_dec, own, other)


def plain_norm_backward(residual, gain_row, grad_normed):
    _, norm_pull = jax.vjp(rms_norm, residual, gain_row)
    return norm_pull(grad_normed)


def plain_hidden_columns(weight):
    width = weight.shape[1] * 2 // 3
    return weight[:, :width], weight[:, width:]


def plain_ffn_hidden(blocks, weight):
    w_in, _ = plain_hidden_columns(weight)
    both = [matmul(block, w_in) for block in blocks]
    units = w_in.shape[1] // 2
    return both, [to_low(gated(part[:, :units], part[:, units:])) for part in both]


def plain_ffn_forward(residual, gain_row, weight):
    blocks = gather_wide(to_low(rms_norm(residual, gain_row)))
    both, hidden = plain_ffn_hidden(blocks, weight)
    _, w_out = plain_hidden_columns(weight)
    out = residual + scatter_wide([matmul(part, w_out.T) for part in hidden])
    return out, (residual, blocks, both, hidden)


def plain_ffn_backward(kept, gain_row, weight, grad_out, grad_blocks):
    residual, blocks, both, hidden = kept
    w_in, w_out = plain_hidden_columns(weight)
    units = w_out.shape[1]
    parts, grad_both = [], []
    for block, pre in zip(grad_blocks, both):
        _, pull = jax.vjp(gated, pre[:, :units], pre[:, units:])
        grad_gate, grad_up = pull(matmul(block, w_out))
        low = to_low(jnp.concatenate([grad_gate, grad_up], axis=1))
        grad_both.append(low)
        parts.append(matmul(low, w_in.T))
    grad_residual, grad_gain = plain_norm_backward(residual, gain_row, scatter_wide(parts))
    joined = jnp.concatenate(grad_both, axis=0)
    grad_in = matmul(jnp.concatenate(blocks, axis=0).T, joined)
    grad_wout = matmul(jnp.concatenate(grad_blocks, axis=0).T, jnp.concatenate(hidden, axis=0))
    return grad_out + grad_residual, grad_gain, (grad_in, grad_wout)


def plain_reduce_ffn(grads, core, wide, rows):
    grad_in, grad_wout = grads
    depth = grad_in.shape[0]
    both = jnp.concatenate(
        [grad_in.reshape(depth, rows, -1), grad_wout.reshape(depth, rows, -1)], axis=2
    )
    columns = both.shape[2]
    halves = plain_core_halves(both.reshape(depth, rows * columns), core, wide)
    halves = to_low(halves).reshape(wide * (depth // wide // 2), rows, columns).transpose(1, 0, 2)
    summed = lax.psum_scatter(halves, "rows", scatter_dimension=0, tiled=True)[0]
    blocks = summed.reshape(wide, depth // wide // 2, columns)
    place = lax.axis_index("wide")
    out = [lax.dynamic_index_in_dim(blocks, place, 0, keepdims=False)]
    for v in range(1, wide):
        block = lax.dynamic_index_in_dim(blocks, place ^ v, 0, keepdims=False)
        out.append(xor_permute(block, "wide", v))
    return placed_rows([piece[None] for piece in out], place)


def plain_to_section(enc_half, dec_half, core):
    is_dec = core == 1
    own = jnp.where(is_dec, dec_half, enc_half)
    got = xor_permute(jnp.where(is_dec, enc_half, dec_half), "section", 1)
    low, high = jnp.where(is_dec, got, own), jnp.where(is_dec, own, got)
    return jnp.concatenate([low, high], axis=-2).astype(jnp.float32)


def plain_shards(
    enc_embed,
    dec_embed,
    out_cot,
    enc_lengths,
    dec_lengths,
    norm_gains,
    rel_bias,
    attn_in,
    attn_out,
    ffn_in,
    ffn_out,
    cross_in,
    cross_out,
):
    core = lax.axis_index("section")
    place = lax.axis_index("wide")
    wide, rows = lax.axis_size("wide"), lax.axis_size("rows")
    depth = attn_in.shape[1]
    unit = FF // (wide * rows)

    small = jnp.concatenate([norm_gains[0].reshape(-1), rel_bias[0].reshape(-1)])
    enc_small, dec_small = plain_both_sections(small, core)
    gains = [each[: 3 * D].reshape(3, D) for each in (enc_small, dec_small)]
    biases = [each[3 * D :].reshape(NB, H) for each in (enc_small, dec_small)]

    attn_shard = jnp.concatenate([attn_in[0], attn_out[0].T, cross_in[0], cross_out[0]], axis=1)
    attn_own = placed_rows(gather_wide(attn_shard), place)
    ffn_blocks = jnp.concatenate(
        [
            ffn_in[0].reshape(depth, 2 * rows, wide, unit).transpose(2, 0, 1, 3).reshape(wide, depth, -1),
            ffn_out[0].T.reshape(depth, rows, wide, unit).transpose(2, 0, 1, 3).reshape(wide, depth, -1),
        ],
        axis=2,
    )
    ffn_got = [lax.dynamic_index_in_dim(ffn_blocks, place, 0, keepdims=False)]
    for v in range(1, wide):
        block = lax.dynamic_index_in_dim(ffn_blocks, place ^ v, 0, keepdims=False)
        ffn_got.append(xor_permute(block, "wide", v))
    ffn_own = placed_rows(ffn_got, place)
    attn_enc, attn_dec = plain_both_sections(attn_own, core)
    ffn_enc, ffn_dec = plain_both_sections(ffn_own, core)
    memory_weight = attn_enc[:, 4 * HD :]
    cross_w_in, cross_w_out = attn_dec[:, 4 * HD : 5 * HD], attn_dec[:, 5 * HD :]

    def own_row(array):
        return lax.dynamic_index_in_dim(array[:, 0], core, 0, keepdims=False)

    enc_row = own_row(enc_embed).astype(jnp.float32)
    dec_row = own_row(dec_embed).astype(jnp.float32)
    cot_row = own_row(out_cot)
    enc_items = item_ids(own_row(enc_lengths), LE)
    dec_items = item_ids(own_row(dec_lengths), LD)
    enc_hot, dec_hot = one_hot(LE, True), one_hot(LD, False)
    enc_bias = jnp.einsum("qkb,bh->hqk", enc_hot, biases[0], precision=HIGHEST)
    dec_bias = jnp.einsum("qkb,bh->hqk", dec_hot, biases[1], precision=HIGHEST)
    causal = jnp.arange(LD)[:, None] >= jnp.arange(LD)[None, :]

    cot_blocks = gather_wide(cot_row)
    x1, enc_self = plain_self_forward(
        enc_row, gains[0][0], attn_enc, enc_bias, enc_items[:, None] == enc_items[None, :]
    )
    y1, dec_self = plain_self_forward(
        dec_row,
        gains[1][0],
        attn_dec,
        dec_bias,
        (dec_items[:, None] == dec_items[None, :]) & causal,
    )
    x2, enc_ffn = plain_ffn_forward(x1, gains[0][1], ffn_enc)
    memory = to_low(rms_norm(x2, gains[0][2]))
    memory_kv = to_low(matmul(memory, memory_weight))
    cross_normed = to_low(rms_norm(y1, gains[1][1]))
    queries = to_low(matmul(cross_normed, cross_w_in))
    context, weights, low_weights = attend_forward(
        queries,
        memory_kv[:, :HD],
        memory_kv[:, HD:],
        0.0,
        dec_items[:, None] == enc_items[None, :],
    )
    y2 = y1 + matmul(context, cross_w_out.T)
    y3, dec_ffn = plain_ffn_forward(y2, gains[1][2], ffn_dec)

    g2, dec_ffn_gain, dec_ffn_grads = plain_ffn_backward(
        dec_ffn, gains[1][2], ffn_dec, cot_row.astype(jnp.float32), cot_blocks
    )
    dec_ffn_share = plain_reduce_ffn(dec_ffn_grads, core, wide, rows)
    g2_low = to_low(g2)
    grad_cross_out = matmul(g2_low.T, context)
    grad_context = to_low(matmul(g2_low, cross_w_out))
    grad_queries, grad_keys, grad_values, _ = attend_backward(
        queries, memory_kv[:, :HD], memory_kv[:, HD:], weights, low_weights, grad_context
    )
    grad_query_low = to_low(grad_queries)
    grad_kv = to_low(jnp.concatenate([grad_keys, grad_values], axis=1))
    grad_x2, enc_final_gain = plain_norm_backward(x2, gains[0][2], matmul(grad_kv, memory_weight.T))
    grad_x1, enc_ffn_gain, enc_ffn_grads = plain_ffn_backward(
        enc_ffn, gains[0][1], ffn_enc, grad_x2, gather_wide(to_low(grad_x2))
    )
    enc_ffn_share = plain_reduce_ffn(enc_ffn_grads, core, wide, rows)

    grad_cross_in = matmul(cross_normed.T, grad_query_low)
    grad_memory = matmul(memory.T, grad_kv)
    from_cross, dec_cross_gain = plain_norm_backward(
        y1, gains[1][1], matmul(grad_query_low, cross_w_in.T)
    )
    grad_y, dec_self_gain, dec_win, dec_wout, dec_bias_grad = plain_self_backward(
        dec_self, gains[1][0], attn_dec, dec_hot, g2 + from_cross
    )
    dec_attn_share = plain_reduce_attn(
        jnp.concatenate([dec_win, dec_wout, grad_cross_in, grad_cross_out], axis=1),
        core,
        wide,
        rows,
    )
    grad_x, enc_self_gain, enc_win, enc_wout, enc_bias_grad = plain_self_backward(
        enc_self, gains[0][0], attn_enc, enc_hot, grad_x1
    )
    enc_attn_share = plain_reduce_attn(
        jnp.concatenate([enc_win, enc_wout, grad_memory], axis=1), core, wide, rows
    )

    small_grads = jnp.stack(
        [
            jnp.concatenate(
                [enc_self_gain, enc_ffn_gain, enc_final_gain, enc_bias_grad.reshape(-1)]
            ),
            jnp.concatenate(
                [dec_self_gain, dec_cross_gain, dec_ffn_gain, dec_bias_grad.reshape(-1)]
            ),
        ]
    )
    small_total = lax.psum(small_grads, ("section", "wide", "rows"))
    small_own = jnp.where(core == 1, small_total[1], small_total[0])

    attn_share = plain_to_section(enc_attn_share, dec_attn_share, core)
    ffn_share = plain_to_section(enc_ffn_share, dec_ffn_share, core)
    in_width = 2 * FF // rows // wide
    ffn_in_grad = (
        ffn_share[:, :, :in_width]
        .reshape(wide, depth, 2, unit)
        .transpose(1, 2, 0, 3)
        .reshape(depth, 2 * FF // rows)
    )
    ffn_out_grad = ffn_share[:, :, in_width:].transpose(0, 2, 1).reshape(FF // rows, depth)
    widths = [3 * HD // rows, HD // rows, HD // rows]
    edges = np.cumsum([0] + widths + [HD // rows])
    win, wout, cin, cout = [attn_share[:, a:b] for a, b in zip(edges[:-1], edges[1:])]

    half = D // 2

    def by_half(own):
        halves = jnp.stack([own[:, :half], own[:, half:]])
        keep = lax.dynamic_index_in_dim(halves, core, 0, keepdims=False)
        send = lax.dynamic_index_in_dim(halves, 1 - core, 0, keepdims=False)
        got = xor_permute(send, "section", 1)
        is_dec = core == 1
        return jnp.stack([jnp.where(is_dec, got, keep), jnp.where(is_dec, keep, got)])[:, None]

    return (
        by_half(to_low(y3)),
        by_half(grad_x),
        by_half(grad_y),
        small_own[: 3 * D].reshape(1, 3, D),
        small_own[3 * D :].reshape(1, NB, H),
        win[None],
        wout.T[None],
        ffn_in_grad[None],
        ffn_out_grad[None],
        cin[None],
        cout[None],
    )


def shards(
    enc_embed,
    dec_embed,
    out_cot,
    enc_lengths,
    dec_lengths,
    norm_gains,
    rel_bias,
    attn_in,
    attn_out,
    ffn_in,
    ffn_out,
    cross_in,
    cross_out,
):
    core = lax.axis_index("section")
    wide, rows = lax.axis_size("wide"), lax.axis_size("rows")
    depth = attn_in.shape[1]
    is_dec = core == 1

    def own_row(array):
        return lax.dynamic_index_in_dim(array[:, 0], core, 0, keepdims=False)

    enc_attn, dec_half, enc_blocks, dec_blocks = start_weights(
        wide, rows, attn_in, attn_out, cross_in, cross_out, ffn_in, ffn_out
    )
    small = jnp.concatenate([norm_gains[0].reshape(-1), rel_bias[0].reshape(-1)])
    other = xor_permute(small, "section", 1)
    smalls = (jnp.where(is_dec, other, small), jnp.where(is_dec, small, other))
    gains = [each[: 3 * D].reshape(3, D) for each in smalls]
    biases = [each[3 * D :].reshape(NB, H) for each in smalls]
    bias_lines = [
        jnp.pad(
            lax.dot_general(
                bias, distance_hot(length, both, 0), (((0,), (0,)), ((), ())), precision=HIGHEST
            ),
            ((0, 2), (0, 0)),
        )
        for bias, length, both in ((biases[0], LE, True), (biases[1], LD, False))
    ]
    enc_bias, dec_bias = bias_rows(*bias_lines)
    enc_row, dec_row, cot_row = own_row(enc_embed), own_row(dec_embed), own_row(out_cot)
    enc_items = item_ids(own_row(enc_lengths), LE)
    dec_items = item_ids(own_row(dec_lengths), LD)

    x1, enc_self, moved = self_forward(
        False,
        enc_row,
        gains[0][0:1],
        enc_attn,
        enc_bias,
        enc_items,
        tuple(enc_blocks[1:]),
        tuple(dec_blocks[1:]),
    )
    enc_pieces, dec_pieces = moved[: wide - 1], moved[wide - 1 :]
    x2, *enc_ffn = ffn_forward_call(
        wide, x1, gains[0][1:2], [enc_blocks[0], *enc_pieces], 2, (dec_half, *dec_pieces)
    )
    enc_ffn, dec_attn, dec_pieces = enc_ffn[:4], enc_ffn[4], [dec_blocks[0], *dec_pieces, *enc_ffn[5:]]
    y1, dec_self, _ = self_forward(True, dec_row, gains[1][0:1], dec_attn, dec_bias, dec_items)
    y2, cross_kept = cross_forward(
        x2, gains[0][2:3], enc_attn, y1, gains[1][1:2], dec_attn, dec_items, enc_items
    )
    y3, *dec_ffn = ffn_forward_call(wide, y2, gains[1][2:3], dec_pieces, 3)

    g2, dec_ffn_gain, *dec_ffn_grads = ffn_backward_call(
        wide, rows, cot_row.astype(jnp.float32), y2, gains[1][2:3], dec_ffn, 4
    )
    grad_x2, g1, enc_final_gain, dec_cross_gain, cross_grads = cross_backward(
        g2, x2, gains[0][2:3], enc_attn, y1, gains[1][1:2], dec_attn, cross_kept
    )
    grad_x1, enc_ffn_gain, enc_in, enc_out, *dec_sums = ffn_backward_call(
        wide, rows, grad_x2, x1, gains[0][1:2], enc_ffn, 5, dec_ffn_grads
    )
    attn_parts, ffn_parts, small_own, dec_out, enc_grad, dec_grad = last_step(
        wide,
        rows,
        cross_grads,
        dec_sums,
        (enc_in, enc_out),
        y3,
        dec_attn,
        enc_attn,
        (g1, dec_row, gains[1][0:1], *dec_self),
        (grad_x1, enc_row, gains[0][0:1], *enc_self),
        (enc_ffn_gain, enc_final_gain, dec_cross_gain, dec_ffn_gain),
    )
    ffn_in_grad, ffn_out_grad, gain_grad, bias_grad, *attn_grads = assemble(
        rows, ffn_parts, attn_parts, small_own
    )
    win, wout, cin, cout = attn_grads
    return (
        dec_out[:, None],
        enc_grad[:, None],
        dec_grad[:, None],
        gain_grad,
        bias_grad,
        win,
        wout,
        ffn_in_grad,
        jnp.swapaxes(ffn_out_grad, 1, 2),
        cin,
        cout,
    )


def solution(mesh):
    placed = (
        P(None, ("wide", "rows"), None, None),
        P(None, ("wide", "rows"), None, None),
        P(None, ("wide", "rows"), None, None),
        P(None, ("wide", "rows"), None),
        P(None, ("wide", "rows"), None),
        P("section", None, None),
        P("section", None, None),
        P("section", "wide", None),
        P("section", None, "wide"),
        P("section", "wide", None),
        P("section", None, "wide"),
        P("section", "wide", None),
        P("section", "wide", None),
    )
    wide, rows = mesh.shape["wide"], mesh.shape["rows"]
    in_tiles = D // wide % 16 == 0 and FF // (wide * rows) % 32 == 0
    return jax.shard_map(
        shards if wide == 4 and rows == 4 and in_tiles else plain_shards,
        mesh=mesh,
        in_specs=placed,
        out_specs=(
            P(None, ("wide", "rows"), None, "section"),
            P(None, ("wide", "rows"), None, "section"),
            P(None, ("wide", "rows"), None, "section"),
            P("section", None, None),
            P("section", None, None),
            P("section", "wide", "rows"),
            P("section", "rows", "wide"),
            P("section", "wide", "rows"),
            P("section", "rows", "wide"),
            P("section", "wide", "rows"),
            P("section", "wide", "rows"),
        ),
        check_vma=False,
    )
```

```python
import jax
import jax.numpy as jnp
import numpy as np
from jax import lax
from jax.experimental import pallas as pl
from jax.experimental.pallas import tpu as pltpu
from jax.sharding import PartitionSpec as P

D = 1472
H = 6
DH = 64
FF = 3584
NB = 32
MAXDIST = 128
MB = 2
LE = 256
LD = 64
HD = 384


EPSILON = 1e-06
NEGATIVE = -1000000000.0
HIGHEST = lax.Precision.HIGHEST


def bucket_table(length, both_ways):
    positions = np.arange(length)
    offsets = positions[None, :] - positions[:, None]
    buckets = NB
    result = np.zeros(offsets.shape, np.int64)
    if both_ways:
        buckets = buckets // 2
        result = result + (offsets > 0) * buckets
        distance = np.abs(offsets)
    else:
        distance = np.maximum(-offsets, 0)
    exact_count = buckets // 2
    log_ratio = np.log(np.maximum(distance, 1) / exact_count) / np.log(MAXDIST / exact_count)
    far_bucket = np.minimum(
        exact_count + np.floor(log_ratio * (buckets - exact_count)).astype(np.int64), buckets - 1
    )
    return result + np.where(distance < exact_count, distance, far_bucket)


def one_hot(length, both_ways):
    bucket_ids = jnp.asarray(bucket_table(length, both_ways), jnp.int32)
    return (bucket_ids[:, :, None] == jnp.arange(NB, dtype=jnp.int32)[None, None, :]).astype(
        jnp.float32
    )


def item_ids(lengths, length):
    item_ends = jnp.cumsum(lengths)
    positions = jnp.arange(length, dtype=jnp.int32)
    return jnp.sum((positions[:, None] >= item_ends[None, :-1]).astype(jnp.int32), axis=1)


def rms_norm(residual, gain_row):
    return (
        residual
        * lax.rsqrt(jnp.mean(residual * residual, axis=-1, keepdims=True) + EPSILON)
        * gain_row
    )


def matmul(left_side, right_side):
    return jnp.dot(left_side, right_side, preferred_element_type=jnp.float32)


def matmul_exact(left_side, right_side):
    return jnp.dot(left_side, right_side, precision=HIGHEST)


def to_low(tensor):
    return tensor.astype(jnp.bfloat16)


def gated(gate_part, up_part):
    return jax.nn.gelu(gate_part, approximate=True) * up_part


def attend_forward(queries, key_rows, value_rows, bias_full, allowed):
    query_count = queries.shape[0]
    heads_q = queries.reshape(query_count, H, DH)
    heads_k = key_rows.reshape(key_rows.shape[0], H, DH)
    heads_v = value_rows.reshape(value_rows.shape[0], H, DH)
    scores = (
        jnp.einsum("qhd,khd->hqk", heads_q, heads_k, preferred_element_type=jnp.float32) + bias_full
    )
    scores = jnp.where(allowed[None], scores, NEGATIVE)
    shifted = jnp.exp(scores - jnp.max(scores, axis=-1, keepdims=True))
    weights = shifted / jnp.sum(shifted, axis=-1, keepdims=True)
    low_weights = to_low(weights)
    context = jnp.einsum("hqk,khd->qhd", low_weights, heads_v, preferred_element_type=jnp.float32)
    return (to_low(context.reshape(query_count, H * DH)), weights, low_weights)


def attend_backward(queries, key_rows, value_rows, weights, low_weights, grad_context):
    query_count = queries.shape[0]
    key_count = key_rows.shape[0]
    heads_q = queries.reshape(query_count, H, DH)
    heads_k = key_rows.reshape(key_count, H, DH)
    heads_v = value_rows.reshape(key_count, H, DH)
    grad_heads = grad_context.reshape(query_count, H, DH)
    grad_weights = jnp.einsum(
        "qhd,khd->hqk", grad_heads, heads_v, preferred_element_type=jnp.float32
    )
    grad_values = jnp.einsum(
        "hqk,qhd->khd", low_weights, grad_heads, preferred_element_type=jnp.float32
    )
    grad_scores = weights * (grad_weights - jnp.sum(grad_weights * weights, axis=-1, keepdims=True))
    low_scores = to_low(grad_scores)
    grad_queries = jnp.einsum(
        "hqk,khd->qhd", low_scores, heads_k, preferred_element_type=jnp.float32
    )
    grad_keys = jnp.einsum("hqk,qhd->khd", low_scores, heads_q, preferred_element_type=jnp.float32)
    return (
        grad_queries.reshape(query_count, H * DH),
        grad_keys.reshape(key_count, H * DH),
        grad_values.reshape(key_count, H * DH),
        low_scores,
    )


def xor_permute(value, axis, distance):
    count = lax.axis_size(axis)
    return lax.ppermute(value, axis, [(i, i ^ distance) for i in range(count)])


def gather_wide(block):
    count = lax.axis_size("wide")
    if count != 4:
        return [block] + [xor_permute(block, "wide", v) for v in range(1, count)]
    half = block.shape[0] // 2
    first = xor_permute(block, "wide", 1)
    second = xor_permute(block, "wide", 2)
    third = jnp.concatenate(
        [xor_permute(first[:half], "wide", 2), xor_permute(second[half:], "wide", 1)], axis=0
    )
    return [block, first, second, third]


def scatter_wide(parts):
    count = lax.axis_size("wide")
    total = parts[0]
    if count != 4:
        for v in range(1, count):
            total = total + xor_permute(to_low(parts[v]), "wide", v).astype(jnp.float32)
        return total
    half = total.shape[0] // 2
    via_first = xor_permute(to_low(parts[3][:half]), "wide", 1).astype(jnp.float32)
    via_second = xor_permute(to_low(parts[3][half:]), "wide", 2).astype(jnp.float32)
    to_first = jnp.concatenate([parts[1][:half], parts[1][half:] + via_second], axis=0)
    to_second = jnp.concatenate([parts[2][:half] + via_first, parts[2][half:]], axis=0)
    total = total + xor_permute(to_low(to_first), "wide", 1).astype(jnp.float32)
    return total + xor_permute(to_low(to_second), "wide", 2).astype(jnp.float32)


def placed_rows(pieces, place):
    rows = pieces[0].shape[0]
    buffer = jnp.zeros((rows * len(pieces),) + pieces[0].shape[1:], pieces[0].dtype)
    for v, piece in enumerate(pieces):
        start = (place ^ v) * rows
        buffer = lax.dynamic_update_slice(buffer, piece, (start,) + (0,) * (piece.ndim - 1))
    return buffer


MESH = pl.DeviceIdType.MESH
HBM = pl.BlockSpec(memory_space=pl.ANY)
VM = pl.BlockSpec(memory_space=pltpu.VMEM)
SM = pl.BlockSpec(memory_space=pltpu.SMEM)
TILE = 128
VMEM_LIMIT = 60 * 1024 * 1024


def peers_of(count):
    place, core = lax.axis_index("wide"), lax.axis_index("section")
    return [{"wide": place ^ v} for v in range(1, count)] + [{"section": 1 - core}]


def greet(peers):
    barrier = pltpu.get_barrier_semaphore()
    for peer in peers:
        pl.semaphore_signal(barrier, inc=1, device_id=peer, device_id_type=MESH)
    pl.semaphore_wait(barrier, len(peers))


def remote(source, target, sems, index, peer):
    return pltpu.make_async_remote_copy(
        src_ref=source,
        dst_ref=target,
        send_sem=sems[0].at[index],
        recv_sem=sems[1].at[index],
        device_id=peer,
        device_id_type=MESH,
    )


def nt(left, right):
    return lax.dot_general(left, right, (((1,), (1,)), ((), ())), preferred_element_type=jnp.float32)


def tn(left, right):
    return lax.dot_general(left, right, (((0,), (0,)), ((), ())), preferred_element_type=jnp.float32)


class GatherPlane:
    def __init__(self, blocks, sems, base, peers, rows):
        half = split_at(rows)
        rest = rows - half
        first, second = peers[0], peers[1]
        self.direct = [
            remote(blocks.at[0], blocks.at[1], sems, base, first),
            remote(blocks.at[0], blocks.at[2], sems, base + 1, second),
        ]
        self.passed = [
            remote(
                blocks.at[1, pl.ds(0, half)], blocks.at[3, pl.ds(0, half)], sems, base + 2, second
            ),
            remote(
                blocks.at[2, pl.ds(half, rest)],
                blocks.at[3, pl.ds(half, rest)],
                sems,
                base + 3,
                first,
            ),
        ]

    def start(self):
        for copy in self.direct:
            copy.start()

    def arrive(self, index):
        if index < 2:
            self.direct[index].wait_recv()
            self.passed[index].start()
        else:
            for copy in self.passed:
                copy.wait_recv()

    def finish(self):
        for copy in self.direct + self.passed:
            copy.wait_send()


class ScatterPlane:
    def __init__(self, parts, landing, sems, base, peers, rows):
        half = split_at(rows)
        first, second = peers[0], peers[1]
        low, high = pl.ds(0, half), pl.ds(half, rows - half)
        self.parts, self.landing, self.low, self.high = parts, landing, low, high
        self.far = [
            remote(parts.at[3, low], landing.at[0, low], sems, base, first),
            remote(parts.at[3, high], landing.at[0, high], sems, base + 1, second),
        ]
        self.early = [
            remote(parts.at[1, low], landing.at[1, low], sems, base + 2, first),
            remote(parts.at[2, high], landing.at[2, high], sems, base + 3, second),
        ]
        self.late = [
            remote(parts.at[1, high], landing.at[1, high], sems, base + 4, first),
            remote(parts.at[2, low], landing.at[2, low], sems, base + 5, second),
        ]

    def send_early(self, index):
        self.early[index].start()

    def send_far(self):
        for copy in self.far:
            copy.start()

    def pass_on(self):
        low, high = self.low, self.high
        self.far[0].wait_recv()
        self.parts[2, low] = (
            self.parts[2, low].astype(jnp.float32) + self.landing[0, low].astype(jnp.float32)
        ).astype(jnp.bfloat16)
        self.late[1].start()
        self.far[1].wait_recv()
        self.parts[1, high] = (
            self.parts[1, high].astype(jnp.float32) + self.landing[0, high].astype(jnp.float32)
        ).astype(jnp.bfloat16)
        self.late[0].start()

    def total(self):
        for copy in self.early + self.late:
            copy.wait_recv()
        return self.landing[1].astype(jnp.float32) + self.landing[2].astype(jnp.float32)

    def finish(self):
        for copy in self.far + self.early + self.late:
            copy.wait_send()


def rms_rows(residual):
    return lax.rsqrt(jnp.mean(residual * residual, axis=-1, keepdims=True) + EPSILON)


def norm_pull(residual, gain_row, grad_normed):
    scale = rms_rows(residual)
    unit = residual * scale
    inner = grad_normed * gain_row
    grad_residual = scale * (inner - unit * jnp.mean(inner * unit, axis=-1, keepdims=True))
    return grad_residual, jnp.sum(grad_normed * unit, axis=0, keepdims=True)


def token_rows_at_once(wide, rows):
    return rows if rows >= 2 * TILE else wide * rows


def block_at(blocks, group, count):
    if count == blocks.shape[1]:
        return blocks[group]
    return blocks[...].reshape(count, blocks.shape[2])


def before_group(gather, group, groups):
    if groups == 1:
        for index in range(3):
            gather.arrive(index)
        return
    for index in range(3):

        @pl.when(group == index + 1)
        def _():
            gather.arrive(index)


def put_parts(acc, parts, own_ref, group, groups, rows):
    if groups == 1:
        own_ref[...] = acc[pl.ds(0, rows)]
        for v in range(1, parts.shape[0]):
            parts[v] = acc[pl.ds(v * rows, rows)].astype(parts.dtype)
        return

    @pl.when(group == 0)
    def _():
        own_ref[...] = acc[...]

    @pl.when(group > 0)
    def _():
        parts[group] = acc[...].astype(parts.dtype)


def after_group(scatter, group, groups):
    if groups == 1:
        scatter.send_far()
        scatter.send_early(0)
        scatter.send_early(1)
        return

    @pl.when(group == 1)
    def _():
        scatter.send_early(0)

    @pl.when(group == 2)
    def _():
        scatter.send_early(1)

    @pl.when(group == 3)
    def _():
        scatter.send_far()


class Reshard:
    def __init__(self, blocks, pieces, direct, sems, base, peers):
        row = lax.axis_index("rows")
        shared = (blocks[0].shape[0] - direct) // 2
        mine = pl.ds(direct + row % 2 * shared, shared)
        other = {"rows": row ^ 1}
        self.shared, self.direct, self.passed = [], [], []
        for v, (block, piece) in enumerate(zip(blocks, pieces)):
            at, peer, first = base + 3 * v, peers[v], pl.ds(0, direct)
            self.shared.append(remote(block.at[mine], piece.at[mine], sems, at, peer))
            self.passed.append(remote(piece.at[mine], piece.at[mine], sems, at + 1, other))
            if direct:
                self.direct.append(remote(block.at[first], piece.at[first], sems, at + 2, peer))

    def start(self):
        for copy in self.shared:
            copy.start()

    def pass_on(self):
        for copy in self.direct:
            copy.start()
        for copy, after in zip(self.shared, self.passed):
            copy.wait_recv()
            after.start()

    def finish(self):
        for copy in self.direct + self.passed:
            copy.wait()
        for copy in self.shared:
            copy.wait_send()


class ReduceRows:
    def __init__(self, source_in, source_out, in_buf, in_land, out_buf, out_land, sems, base, local_sem, local_base):
        row = lax.axis_index("rows")
        near, far = {"rows": row ^ 1}, {"rows": row ^ 2}
        self.bufs, self.lands, self.first, self.second = [], [], [], []
        views = [
            (lambda ref, i, part=part: ref.at[i, part], source_in, in_buf, in_land)
            for part in range(2)
        ] + [(lambda ref, i: ref.at[i], source_out, out_buf, out_land)]
        for index, (view, source, buf, land) in enumerate(views):
            at = base + 3 * index
            self.first.append(
                [
                    remote(view(source, row ^ 1), view(land, 0), sems, at, near),
                    remote(view(source, row ^ 3), view(land, 1), sems, at + 1, near),
                ]
            )
            self.second.append(remote(view(buf, 1), view(land, 2), sems, at + 2, far))
            self.bufs.append([view(buf, 0), view(buf, 1)])
            self.lands.append([view(land, i) for i in range(3)])
        self.loads = [
            pltpu.make_async_copy(source.at[place], buf.at[i], local_sem.at[local_base + 2 * j + i])
            for j, (source, buf) in enumerate(((source_in, in_buf), (source_out, out_buf)))
            for i, place in enumerate((row, row ^ 2))
        ]

    def start(self):
        for copy in self.first[0]:
            copy.start()
        for load in self.loads:
            load.start()

    def loaded(self):
        for load in self.loads:
            load.wait()

    def add(self, index, which, land):
        ref = self.bufs[index][which]
        ref[...] = (
            ref[...].astype(jnp.float32) + self.lands[index][land][...].astype(jnp.float32)
        ).astype(jnp.bfloat16)

    def turn(self, index):
        for copy in self.first[index]:
            copy.wait_recv()
        for copy in self.first[index + 1] if index < 2 else ():
            copy.start()
        self.add(index, 1, 1)
        self.second[index].start()
        self.add(index, 0, 0)

    def close(self, index):
        self.second[index].wait_recv()
        self.add(index, 0, 2)

    def finish(self):
        for pair, copy in zip(self.first, self.second):
            for each in pair:
                each.wait_send()
            copy.wait_send()


def reduce_rows_scratch(units):
    low = jnp.bfloat16
    return [
        pltpu.VMEM((2, 2, D, TILE), low),
        pltpu.VMEM((3, 2, D, TILE), low),
        pltpu.VMEM((2, units, D), low),
        pltpu.VMEM((3, units, D), low),
    ]


def weight_tiles(weight, half, part):
    lanes = pl.ds(part * TILE, TILE)
    return jnp.concatenate(
        [weight[half, quarter, :, lanes] for quarter in range(weight.shape[1])], axis=1
    )


def weight_copies(pieces, weight, sems, base, local_sem, local_base, sibling):
    core, place = lax.axis_index("section"), lax.axis_index("wide")
    wide, depth = lax.axis_size("wide"), pieces[0].shape[1]
    loads, swaps = [], []
    for index, piece in enumerate(pieces):
        v = index if index < wide else index - wide + 1
        place_rows = pl.ds(pl.multiple_of((place ^ v) * depth, 16), depth)
        target = weight.at[core, :, place_rows]
        quarters = piece.shape[0]
        if quarters < weight.shape[1]:
            part = lax.axis_index("rows") % 2
            part = part if index < wide else 1 - part
            target = weight.at[core, pl.ds(part * quarters, quarters), place_rows]
        loads.append(pltpu.make_async_copy(piece, target, local_sem.at[local_base + index]))
        swaps.append(remote(piece, target, sems, base + index, sibling))
    return loads, swaps


def gate_slopes(gate, up):
    square = gate * gate
    tanh = jnp.tanh(GELU_A * gate * (1.0 + GELU_B * square))
    upper = 0.5 * (1.0 + tanh)
    slope = upper + 0.5 * gate * (1.0 - tanh * tanh) * (GELU_A + 3.0 * GELU_A * GELU_B * square)
    return gate * upper, slope


def ffn_forward_kernel(wide, carried, count, gain_at, x_ref, gain_ref, *refs):
    gain_ref = gain_ref.at[pl.ds(gain_at, 1)]
    pieces, refs = refs[:count], refs[count:]
    if carried:
        dec_half, dec_blocks, refs = refs[0], refs[1:wide], refs[wide:]
    y_ref, at_out, pre_out, hidden_out, weight_out = refs[:5]
    refs = refs[5:]
    if carried:
        dec_attn, dec_pieces, refs = refs[0], refs[1:wide], refs[wide:]
    blocks, at, pre, hidden, weight, parts, landing, acc, send_sem, recv_sem, local_sem = refs[:11]
    rows = x_ref.shape[0]
    depth = pieces[0].shape[1]
    span = weight.shape[1] * TILE
    core, place = lax.axis_index("section"), lax.axis_index("wide")
    peers = peers_of(wide)
    sems = (send_sem, recv_sem)
    greet(peers + ([{"rows": lax.axis_index("rows") ^ 1}] if carried else []))
    residual = x_ref[...]
    blocks[0] = (residual * rms_rows(residual) * gain_ref[...]).astype(jnp.bfloat16)
    gather = GatherPlane(blocks, sems, 0, peers, rows)
    gather.start()
    loads, swaps = weight_copies(pieces, weight, sems, 10, local_sem, 12, peers[-1])
    for load, swap in zip(loads, swaps):
        load.start()
        swap.start()
    scatter = ScatterPlane(parts, landing, sems, 4, peers, rows)
    if carried:
        held, far_held, whole = refs[11:14]
        other = {"rows": lax.axis_index("rows") ^ 1}
        passed = [
            remote(block, piece, sems, 24 + v, other)
            for v, (block, piece) in enumerate(zip(dec_blocks, dec_pieces))
        ]
        for copy in passed:
            copy.start()
        size = held.shape[1]
        rest = depth - size
        part = lax.axis_index("rows") % 2
        dec_gather = GatherPlane(held, sems, 27, peers, size)
        mine = pl.ds(pl.multiple_of(part * rest, 16), size)
        fetch = pltpu.make_async_copy(dec_half.at[mine], held.at[0], local_sem.at[7])
        fetch.start()
        stores, gives, crossings = [], [], []

        def place_block(source, v, start, index):
            target = dec_attn.at[
                core, pl.ds(pl.multiple_of((place ^ v) * depth + start, 16), source.shape[0])
            ]
            stores.append(pltpu.make_async_copy(source, target, local_sem.at[19 + index]))
            gives.append(remote(source, target, sems, 35 + index, peers[-1]))

        place_block(whole, 0, 0, 0)
        for v in range(1, wide):
            place_block(held.at[v], v, part * rest, v)
        for v in range(1, wide):
            sent = pl.ds(pl.multiple_of(part * (size - rest), 16), rest)
            crossings.append(remote(held.at[v, sent], far_held.at[v - 1], sems, 41 + v, other))
            place_block(far_held.at[v - 1], v, (1 - part) * size, wide + v - 1)
        whole_fetch = pltpu.make_async_copy(dec_half, whole, local_sem.at[8])
        whole_fetch.start()
    count = token_rows_at_once(wide, rows)
    groups = wide * rows // count

    @pl.loop(0, groups)
    def _(group):
        before_group(gather, group, groups)

        @pl.when(group == 0)
        def _():
            for load in loads:
                load.wait()

        token_rows = pl.ds(pl.multiple_of(group * count, count), count)

        @pl.loop(0, 2)
        def _(step):
            @pl.when((group == 0) & (step == 1))
            def _():
                for swap in swaps:
                    swap.wait_recv()

            half = lax.rem(core + step, 2)
            block = block_at(blocks, group, count)
            gate = matmul(block, weight_tiles(weight, half, 0))
            up = matmul(block, weight_tiles(weight, half, 1))
            pre[half, token_rows, pl.ds(0, span)] = gate.astype(jnp.bfloat16)
            pre[half, token_rows, pl.ds(span, span)] = up.astype(jnp.bfloat16)
            low = gated(gate, up).astype(jnp.bfloat16)
            hidden[half, token_rows, :] = low
            out = nt(low, weight_tiles(weight, half, 2))
            acc[...] = jnp.where(step == 0, 0.0, acc[...]) + out

        put_parts(acc, parts, y_ref, group, groups, rows)
        after_group(scatter, group, groups)
        if carried:

            @pl.when(group == 0)
            def _():
                whole_fetch.wait()
                stores[0].start()
                gives[0].start()

            @pl.when(group == 1)
            def _():
                fetch.wait()
                dec_gather.start()

    y_ref[...] += residual
    copies = [
        pltpu.make_async_copy(pre, pre_out, local_sem.at[4]),
        pltpu.make_async_copy(weight, weight_out, local_sem.at[5]),
    ]
    for copy in copies:
        copy.start()
    scatter.pass_on()
    if carried:
        for v in range(1, 3):
            dec_gather.arrive(v - 1)
            crossings[v - 1].start()
            stores[v].start()
            gives[v].start()

    @pl.loop(0, groups)
    def _(group):
        lanes = pl.ds(pl.multiple_of(group * count, count), count)
        at[:, lanes] = block_at(blocks, group, count).T

    last = pltpu.make_async_copy(at, at_out, local_sem.at[6])
    last.start()
    copies.append(last)

    @pl.loop(0, 2 * groups)
    def _(step):
        half, group = lax.rem(step, 2), step // 2
        lanes = pl.ds(pl.multiple_of(group * count, count), count)
        hidden_out[half, :, lanes] = hidden[half, lanes, :].T

    y_ref[...] += scatter.total()
    if carried:
        dec_gather.arrive(2)
        crossings[2].start()
        stores[3].start()
        gives[3].start()
        for v in range(1, wide):
            crossings[v - 1].wait()
            stores[wide + v - 1].start()
            gives[wide + v - 1].start()
        for store, give in zip(stores, gives):
            store.wait()
            give.wait()
        dec_gather.finish()
        for copy in passed:
            copy.wait()
    for copy in copies:
        copy.wait()
    gather.finish()
    scatter.finish()
    for swap in swaps:
        swap.wait_send()


def ffn_forward_call(wide, residual, gain_row, pieces, call_id, carried=()):
    gain_row, gain_at = gain_row
    rows = residual.shape[0]
    total = rows * wide
    quarters, _, columns = pieces[0].shape
    span = quarters * TILE
    low = jnp.bfloat16
    extra_out, extra_scratch = [], []
    if carried:
        depth, attn_columns = carried[0].shape
        extra_out = [jax.ShapeDtypeStruct((2, D, attn_columns), low)] + [
            jax.ShapeDtypeStruct(each.shape, low) for each in carried[1:]
        ]
        size = split_at(depth)
        extra_scratch = [
            pltpu.VMEM((wide, size, attn_columns), low),
            pltpu.VMEM((wide - 1, depth - size, attn_columns), low),
            pltpu.VMEM((depth, attn_columns), low),
        ]
    return pl.pallas_call(
        lambda *refs: ffn_forward_kernel(wide, bool(carried), len(pieces), gain_at, *refs),
        out_shape=[
            jax.ShapeDtypeStruct((rows, D), jnp.float32),
            jax.ShapeDtypeStruct((D, total), low),
            jax.ShapeDtypeStruct((2, total, 2 * span), low),
            jax.ShapeDtypeStruct((2, span, total), low),
            jax.ShapeDtypeStruct((2, quarters, D, columns), low),
        ]
        + extra_out,
        in_specs=[VM, VM] + [HBM] * (len(pieces) + len(carried)),
        out_specs=[VM, HBM, HBM, VM, HBM] + [HBM] * len(extra_out),
        scratch_shapes=[
            pltpu.VMEM((wide, rows, D), low),
            pltpu.VMEM((D, total), low),
            pltpu.VMEM((2, total, 2 * span), low),
            pltpu.VMEM((2, total, span), low),
            pltpu.VMEM((2, quarters, D, columns), low),
            pltpu.VMEM((wide, rows, D), low),
            pltpu.VMEM((3, rows, D), low),
            pltpu.VMEM((token_rows_at_once(wide, rows), D), jnp.float32),
            pltpu.SemaphoreType.DMA((45,)),
            pltpu.SemaphoreType.DMA((45,)),
            pltpu.SemaphoreType.DMA((26,)),
        ]
        + extra_scratch,
        compiler_params=pltpu.CompilerParams(
            collective_id=call_id, has_side_effects=True, vmem_limit_bytes=VMEM_LIMIT
        ),
        name="ffn_forward_%d" % rows,
    )(residual, gain_row, *pieces, *carried)


def ffn_backward_kernel(
    wide, rows_axis, gain_at, g_ref, x_ref, gain_ref, at_in, pre_in, hidden_in, weight_in, *refs
):
    gain_ref = gain_ref.at[pl.ds(gain_at, 1)]
    carried = len(refs) > 21
    if carried:
        ready_in, ready_out = refs[:2]
        refs = refs[2:]
    gx_ref, gain_out, grad_in, grad_out = refs[:4]
    refs = refs[4:]
    if carried:
        sum_in, sum_out = refs[:2]
        refs = refs[2:]
    (
        blocks,
        at,
        pre,
        hidden,
        weight,
        parts,
        landing,
        acc,
        give_in,
        give_out,
        got_in,
        got_out,
        send_sem,
        recv_sem,
        local_sem,
    ) = refs[:15]
    rows = x_ref.shape[0]
    span = weight.shape[1] * TILE
    units = FF // (wide * rows_axis * 2)
    core, row = lax.axis_index("section"), lax.axis_index("rows")
    peers = peers_of(wide)
    sems = (send_sem, recv_sem)
    greet(peers + ([{"rows": row ^ 1}, {"rows": row ^ 2}] if carried else []))
    loads = [
        pltpu.make_async_copy(weight_in, weight, local_sem.at[0]),
        pltpu.make_async_copy(pre_in, pre, local_sem.at[1]),
        pltpu.make_async_copy(hidden_in, hidden, local_sem.at[2]),
        pltpu.make_async_copy(at_in, at, local_sem.at[3]),
    ]
    blocks[0] = g_ref[...].astype(jnp.bfloat16)
    gather = GatherPlane(blocks, sems, 0, peers, rows)
    gather.start()
    for load in loads:
        load.start()
    if carried:
        line = ReduceRows(ready_in, ready_out, *refs[15:19], sems, 12, local_sem, 6)
        line.start()
    scatter = ScatterPlane(parts, landing, sems, 4, peers, rows)
    loads[0].wait()
    loads[1].wait()
    count = token_rows_at_once(wide, rows)
    groups = wide * rows // count

    @pl.loop(0, groups)
    def _(group):
        before_group(gather, group, groups)
        token_rows = pl.ds(pl.multiple_of(group * count, count), count)

        @pl.loop(0, 2)
        def _(half):
            block = block_at(blocks, group, count)
            grad_hidden = matmul(block, weight_tiles(weight, half, 2))
            gate = pre[half, token_rows, pl.ds(0, span)].astype(jnp.float32)
            up = pre[half, token_rows, pl.ds(span, span)].astype(jnp.float32)
            value, slope = gate_slopes(gate, up)
            low_gate = (grad_hidden * up * slope).astype(jnp.bfloat16)
            low_up = (grad_hidden * value).astype(jnp.bfloat16)
            pre[half, token_rows, pl.ds(0, span)] = low_gate
            pre[half, token_rows, pl.ds(span, span)] = low_up
            out = nt(low_gate, weight_tiles(weight, half, 0)) + nt(
                low_up, weight_tiles(weight, half, 1)
            )
            acc[...] = jnp.where(half == 0, 0.0, acc[...]) + out

        put_parts(acc, parts, gx_ref, group, groups, rows)
        after_group(scatter, group, groups)
        if carried:

            @pl.when(group == 1)
            def _():
                line.loaded()
                line.turn(0)

    loads[2].wait()
    loads[3].wait()
    chunk = 2 * TILE
    swap_out = remote(give_out, got_out, sems, 11, peers[-1])
    swap_in = remote(give_in, got_in, sems, 10, peers[-1])
    store_in = pltpu.make_async_copy(got_in, grad_in, local_sem.at[4])
    store_out = pltpu.make_async_copy(got_out, grad_out, local_sem.at[5])

    @pl.loop(0, 2 * rows_axis)
    def _(step):
        half = jnp.where(step < rows_axis, 1 - core, core)
        index = lax.rem(step, rows_axis)
        columns = pl.ds(pl.multiple_of(index * chunk, chunk), chunk)
        total = matmul(at[...], pre[half, :, columns])

        @pl.when(step < rows_axis)
        def _():
            for part in range(2):
                give_in[index, part] = total[:, part * TILE : (part + 1) * TILE].astype(
                    jnp.bfloat16
                )

        @pl.when(step == rows_axis - 1)
        def _():
            swap_in.start()
            if carried:
                line.turn(1)
            scatter.pass_on()

        @pl.when(step == rows_axis)
        def _():
            swap_in.wait_recv()

        @pl.when(step >= rows_axis)
        def _():
            for part in range(2):
                got_in[index, part] = (
                    total[:, part * TILE : (part + 1) * TILE]
                    + got_in[index, part].astype(jnp.float32)
                ).astype(jnp.bfloat16)

    store_in.start()

    @pl.loop(0, 2)
    def _(step):
        half = lax.rem(core + 1 + step, 2)
        total = matmul(hidden[half], blocks[...].reshape(wide * rows, D))

        @pl.when(step == 0)
        def _():
            for index in range(rows_axis):
                give_out[index] = total[index * TILE : index * TILE + units].astype(jnp.bfloat16)
            swap_out.start()

        @pl.when(step == 1)
        def _():
            swap_out.wait_recv()
            for index in range(rows_axis):
                got_out[index] = (
                    total[index * TILE : index * TILE + units]
                    + got_out[index].astype(jnp.float32)
                ).astype(jnp.bfloat16)
            store_out.start()

    if carried:
        line.turn(2)
    total = gx_ref[...] + scatter.total()
    grad_residual, grad_gain = norm_pull(x_ref[...], gain_ref[...], total)
    gx_ref[...] = g_ref[...].astype(jnp.float32) + grad_residual
    gain_out[...] = grad_gain
    if carried:
        for index in range(3):
            line.close(index)
        in_buf, out_buf = refs[15], refs[17]
        stores = [
            pltpu.make_async_copy(in_buf.at[0], sum_in, local_sem.at[6]),
            pltpu.make_async_copy(out_buf.at[0], sum_out, local_sem.at[7]),
        ]
        for store in stores:
            store.start()
        for store in stores:
            store.wait()
        line.finish()
    store_in.wait()
    store_out.wait()
    swap_in.wait_send()
    swap_out.wait_send()
    gather.finish()
    scatter.finish()


def ffn_both_kernel(wide, rows_axis, gain_at, x_ref, cot_ref, gain_ref, *refs):
    pieces, refs = refs[: 2 * wide - 1], refs[2 * wide - 1 :]
    gain_ref = gain_ref.at[pl.ds(gain_at, 1)]
    y_ref, gx_ref, gain_out, grad_in, grad_out = refs[:5]
    (
        blocks,
        cots,
        weight,
        pre,
        hidden,
        acc,
        grad_acc,
        parts,
        grad_parts,
        landing,
        grad_landing,
        give_in,
        give_out,
        got_in,
        got_out,
        send_sem,
        recv_sem,
        local_sem,
    ) = refs[5:]
    rows = x_ref.shape[0]
    total_rows = wide * rows
    span = weight.shape[1] * TILE
    units = FF // (wide * rows_axis * 2)
    core = lax.axis_index("section")
    peers = peers_of(wide)
    sems = (send_sem, recv_sem)
    low = jnp.bfloat16
    loads, swaps = weight_copies(pieces, weight, sems, 20, local_sem, 2, peers[-1])
    greet(peers)
    residual = x_ref[...]
    blocks[0] = (residual * rms_rows(residual) * gain_ref[...]).astype(low)
    cots[0] = cot_ref[...]
    gather = GatherPlane(blocks, sems, 0, peers, rows)
    cot_gather = GatherPlane(cots, sems, 4, peers, rows)
    gather.start()
    cot_gather.start()
    for load, swap in zip(loads, swaps):
        load.start()
        swap.start()
    for index in range(3):
        gather.arrive(index)
        cot_gather.arrive(index)
    for load in loads:
        load.wait()

    @pl.loop(0, 2)
    def _(step):
        @pl.when(step == 1)
        def _():
            for swap in swaps:
                swap.wait_recv()

        half = lax.rem(core + step, 2)
        block = blocks[...].reshape(total_rows, D)
        gate = matmul(block, weight_tiles(weight, half, 0))
        up = matmul(block, weight_tiles(weight, half, 1))
        value, slope = gate_slopes(gate, up)
        low_hidden = (value * up).astype(low)
        hidden[half] = low_hidden
        grad_hidden = matmul(cots[...].reshape(total_rows, D), weight_tiles(weight, half, 2))
        low_gate = (grad_hidden * up * slope).astype(low)
        low_up = (grad_hidden * value).astype(low)
        pre[half, :, pl.ds(0, span)] = low_gate
        pre[half, :, pl.ds(span, span)] = low_up
        grad = nt(low_gate, weight_tiles(weight, half, 0)) + nt(
            low_up, weight_tiles(weight, half, 1)
        )
        grad_acc[...] = jnp.where(step == 0, 0.0, grad_acc[...]) + grad
        out = nt(low_hidden, weight_tiles(weight, half, 2))
        acc[...] = jnp.where(step == 0, 0.0, acc[...]) + out

    grad_scatter = ScatterPlane(grad_parts, grad_landing, sems, 8, peers, rows)
    scatter = ScatterPlane(parts, landing, sems, 14, peers, rows)
    put_parts(grad_acc, grad_parts, gx_ref, 0, 1, rows)
    after_group(grad_scatter, 0, 1)
    put_parts(acc, parts, y_ref, 0, 1, rows)
    after_group(scatter, 0, 1)
    swap_in = remote(give_in, got_in, sems, 27, peers[-1])
    swap_out = remote(give_out, got_out, sems, 28, peers[-1])
    store_in = pltpu.make_async_copy(got_in, grad_in, local_sem.at[0])
    store_out = pltpu.make_async_copy(got_out, grad_out, local_sem.at[1])
    chunk = 2 * TILE

    @pl.loop(0, 2 * rows_axis)
    def _(step):
        half = jnp.where(step < rows_axis, 1 - core, core)
        index = lax.rem(step, rows_axis)
        columns = pl.ds(pl.multiple_of(index * chunk, chunk), chunk)
        total = tn(blocks[...].reshape(total_rows, D), pre[half, :, columns])

        @pl.when(step < rows_axis)
        def _():
            for part in range(2):
                give_in[index, part] = total[:, part * TILE : (part + 1) * TILE].astype(low)

        @pl.when(step == rows_axis - 1)
        def _():
            swap_in.start()
            grad_scatter.pass_on()
            scatter.pass_on()

        @pl.when(step == rows_axis)
        def _():
            swap_in.wait_recv()

        @pl.when(step >= rows_axis)
        def _():
            for part in range(2):
                got_in[index, part] = (
                    total[:, part * TILE : (part + 1) * TILE]
                    + got_in[index, part].astype(jnp.float32)
                ).astype(low)

    store_in.start()

    @pl.loop(0, 2)
    def _(step):
        half = lax.rem(core + 1 + step, 2)
        total = tn(hidden[half], cots[...].reshape(total_rows, D))

        @pl.when(step == 0)
        def _():
            for index in range(rows_axis):
                give_out[index] = total[index * TILE : index * TILE + units].astype(low)
            swap_out.start()

        @pl.when(step == 1)
        def _():
            swap_out.wait_recv()
            for index in range(rows_axis):
                got_out[index] = (
                    total[index * TILE : index * TILE + units]
                    + got_out[index].astype(jnp.float32)
                ).astype(low)
            store_out.start()

    grad_residual, gain_out[...] = norm_pull(
        x_ref[...], gain_ref[...], gx_ref[...] + grad_scatter.total()
    )
    gx_ref[...] = cot_ref[...].astype(jnp.float32) + grad_residual
    y_ref[...] = y_ref[...] + residual + scatter.total()
    store_in.wait()
    store_out.wait()
    swap_in.wait_send()
    swap_out.wait_send()
    for each in (gather, cot_gather, grad_scatter, scatter):
        each.finish()
    for swap in swaps:
        swap.wait_send()


def ffn_both_call(wide, rows_axis, residual, cot, gain_row, pieces, call_id):
    gain_row, gain_at = gain_row
    rows = residual.shape[0]
    total = wide * rows
    quarters, _, columns = pieces[0].shape
    span = quarters * TILE
    low = jnp.bfloat16
    units = FF // (wide * rows_axis * 2)
    share_in = (rows_axis, 2, D, TILE)
    share_out = (rows_axis, units, D)
    return pl.pallas_call(
        lambda *refs: ffn_both_kernel(wide, rows_axis, gain_at, *refs),
        out_shape=[
            jax.ShapeDtypeStruct((rows, D), jnp.float32),
            jax.ShapeDtypeStruct((rows, D), jnp.float32),
            jax.ShapeDtypeStruct((1, D), jnp.float32),
            jax.ShapeDtypeStruct(share_in, low),
            jax.ShapeDtypeStruct(share_out, low),
        ],
        in_specs=[VM, VM, VM] + [HBM] * len(pieces),
        out_specs=[VM, VM, VM, HBM, HBM],
        scratch_shapes=[
            pltpu.VMEM((wide, rows, D), low),
            pltpu.VMEM((wide, rows, D), low),
            pltpu.VMEM((2, quarters, D, columns), low),
            pltpu.VMEM((2, total, 2 * span), low),
            pltpu.VMEM((2, total, span), low),
            pltpu.VMEM((total, D), jnp.float32),
            pltpu.VMEM((total, D), jnp.float32),
            pltpu.VMEM((wide, rows, D), low),
            pltpu.VMEM((wide, rows, D), low),
            pltpu.VMEM((3, rows, D), low),
            pltpu.VMEM((3, rows, D), low),
            pltpu.VMEM(share_in, low),
            pltpu.VMEM(share_out, low),
            pltpu.VMEM(share_in, low),
            pltpu.VMEM(share_out, low),
            pltpu.SemaphoreType.DMA((29,)),
            pltpu.SemaphoreType.DMA((29,)),
            pltpu.SemaphoreType.DMA((9,)),
        ],
        compiler_params=pltpu.CompilerParams(
            collective_id=call_id, has_side_effects=True, vmem_limit_bytes=VMEM_LIMIT
        ),
        name="ffn_both_%d" % rows,
    )(residual, cot, gain_row, *pieces)


GELU_A = float(np.sqrt(2.0 / np.pi))
GELU_B = 0.044715


def ffn_backward_call(wide, rows_axis, grad, residual, gain_row, kept, call_id, carried=()):
    gain_row, gain_at = gain_row
    at, pre, hidden, weight = kept
    rows = residual.shape[0]
    low = jnp.bfloat16
    units = FF // (wide * rows_axis * 2)
    share_in = (rows_axis, 2, D, TILE)
    share_out = (rows_axis, units, D)
    sums = [jax.ShapeDtypeStruct(each.shape[1:], low) for each in carried]
    return pl.pallas_call(
        lambda *refs: ffn_backward_kernel(wide, rows_axis, gain_at, *refs),
        out_shape=[
            jax.ShapeDtypeStruct((rows, D), jnp.float32),
            jax.ShapeDtypeStruct((1, D), jnp.float32),
            jax.ShapeDtypeStruct(share_in, low),
            jax.ShapeDtypeStruct(share_out, low),
        ]
        + sums,
        in_specs=[VM, VM, VM, HBM, HBM, HBM, HBM] + [HBM] * len(sums),
        out_specs=[VM, VM, HBM, HBM] + [HBM] * len(sums),
        scratch_shapes=[
            pltpu.VMEM((wide, rows, D), low),
            pltpu.VMEM(at.shape, low),
            pltpu.VMEM(pre.shape, low),
            pltpu.VMEM(hidden.shape, low),
            pltpu.VMEM(weight.shape, low),
            pltpu.VMEM((wide, rows, D), low),
            pltpu.VMEM((3, rows, D), low),
            pltpu.VMEM((token_rows_at_once(wide, rows), D), jnp.float32),
            pltpu.VMEM(share_in, low),
            pltpu.VMEM(share_out, low),
            pltpu.VMEM(share_in, low),
            pltpu.VMEM(share_out, low),
            pltpu.SemaphoreType.DMA((21,)),
            pltpu.SemaphoreType.DMA((21,)),
            pltpu.SemaphoreType.DMA((10,)),
        ]
        + (reduce_rows_scratch(units) if carried else []),
        compiler_params=pltpu.CompilerParams(
            collective_id=call_id, has_side_effects=True, vmem_limit_bytes=VMEM_LIMIT
        ),
        name="ffn_backward_%d" % rows,
    )(grad, residual, gain_row, at, pre, hidden, weight, *carried)


def start_weights_kernel(
    wide, rows, win_in, wout_in, cin_in, cout_in, ffn_in, ffn_out, gains, enc_line, dec_line,
    attn_ref, dec_half, enc_gains, dec_gains, enc_bias, dec_bias, *refs
):
    enc, dec = refs[:wide], refs[wide : 2 * wide]
    held, blocks, spare, in_ref, out_ref, ffn, enc_row, dec_row, send_sem, recv_sem, local_sem = refs[2 * wide :]
    core, place = lax.axis_index("section"), lax.axis_index("wide")
    peers = peers_of(wide)
    sibling = peers[-1]
    sems = (send_sem, recv_sem)
    depth = blocks.shape[1]
    big = [
        pltpu.make_async_copy(ffn_in.at[0], in_ref, local_sem.at[4]),
        pltpu.make_async_copy(ffn_out, out_ref, local_sem.at[5]),
    ]
    packs = [
        pltpu.make_async_copy(each, held.at[:, pl.ds(i * HD, HD)], local_sem.at[1 + i])
        for i, each in enumerate((wout_in, cin_in.at[0], cout_in.at[0]))
    ]
    for pack in packs:
        pack.start()
    greet(peers)
    for pack in packs:
        pack.wait()

    @pl.when(core == 0)
    def _():
        keep = pltpu.make_async_copy(win_in.at[0], blocks.at[0], local_sem.at[0])
        keep.start()
        give = remote(held, blocks.at[0], sems, 0, sibling)
        give.start()
        remote(win_in.at[0], spare, sems, 1, sibling).wait_recv()
        keep.wait()

    @pl.when(core == 1)
    def _():
        keep = pltpu.make_async_copy(held, spare, local_sem.at[0])
        keep.start()
        give = remote(win_in.at[0], spare, sems, 1, sibling)
        give.start()
        remote(held, blocks.at[0], sems, 0, sibling).wait_recv()
        keep.wait()

    gather = GatherPlane(blocks, sems, 2, peers, depth)
    gather.start()
    for load in big:
        load.start()
    dec_copy = pltpu.make_async_copy(spare, dec_half, local_sem.at[0])
    dec_copy.start()
    stores, gives = [], []
    for v in range(wide):
        rows_of = pl.ds(pl.multiple_of((place ^ v) * depth, 16), depth)
        stores.append(
            pltpu.make_async_copy(blocks.at[v], attn_ref.at[core, rows_of], local_sem.at[6 + v])
        )
        gives.append(remote(blocks.at[v], attn_ref.at[core, rows_of], sems, 6 + v, sibling))
    stores[0].start()
    gives[0].start()
    for load in big:
        load.wait()
    units = FF // (wide * rows * 2)
    per_row = FF // rows
    row_ids = lax.broadcasted_iota(jnp.int32, (2 * TILE, TILE), 0)
    lane_ids = lax.broadcasted_iota(jnp.int32, (2 * TILE, TILE), 1)
    def prepare(index):
        target, half = index // 2, index % 2
        offset = index * units
        start, shift = offset // TILE * TILE, offset % TILE
        picks = ((row_ids == lane_ids + shift) & (lane_ids < units)).astype(jnp.bfloat16)
        window = min(2 * TILE, per_row - start)
        picks = picks[:window]
        for part in range(3):
            for row in range(rows):
                if part < 2:
                    source = in_ref[:, pl.ds(part * FF + row * per_row + start, window)]
                else:
                    source = out_ref[:, pl.ds(row * per_row + start, window)]
                tile = matmul(source, picks)
                ffn[half, target ^ place, row, :, pl.ds(part * TILE, TILE)] = tile.astype(
                    jnp.bfloat16
                )

    lines = 10 + 2 * wide
    gain_moves = [remote(gains, target, sems, lines, sibling) for target in (enc_gains, dec_gains)]
    line_moves = [
        remote(enc_line, enc_row, sems, lines + 1, sibling),
        remote(dec_line, dec_row, sems, lines + 1, sibling),
    ]
    for own, (gain_ref, row_ref, line_ref) in enumerate(
        ((enc_gains, enc_row, enc_line), (dec_gains, dec_row, dec_line))
    ):

        @pl.when(core == own)
        def _():
            gain_ref[...] = gains[...]
            row_ref[...] = line_ref[...]
            gain_moves[own].start()
            line_moves[own].start()

    for index in range(2 * wide):
        prepare(index)
    for own in range(2):

        @pl.when(core == own)
        def _():
            gain_moves[1 - own].wait_recv()
            line_moves[1 - own].wait_recv()
            gain_moves[own].wait_send()
            line_moves[own].wait_send()

    bias_rows(enc_row, enc_bias)
    bias_rows(dec_row, dec_bias)

    def move(outs, base):
        for v in range(wide):
            pltpu.make_async_copy(ffn.at[core, v], outs[v], local_sem.at[10 + v]).start()
            remote(ffn.at[1 - core, v], outs[v], sems, base + v, sibling).start()

    def settle(outs, base):
        for v in range(wide):
            pltpu.make_async_copy(ffn.at[core, v], outs[v], local_sem.at[10 + v]).wait()
            remote(ffn.at[1 - core, v], outs[v], sems, base + v, sibling).wait_send()

    def receive(outs, base):
        for v in range(wide):
            remote(ffn.at[0, v], outs[v], sems, base + v, sibling).wait_recv()

    @pl.when(core == 0)
    def _():
        move(enc, 10)

    @pl.when(core == 1)
    def _():
        move(dec, 10 + wide)

    for v in range(1, wide):
        gather.arrive(v - 1)
        stores[v].start()
        gives[v].start()
    for v in range(wide):
        gives[v].wait_recv()
        stores[v].wait()
    dec_copy.wait()

    @pl.when(core == 0)
    def _():
        settle(enc, 10)
        receive(dec, 10 + wide)
        remote(held, blocks.at[0], sems, 0, sibling).wait_send()

    @pl.when(core == 1)
    def _():
        settle(dec, 10 + wide)
        receive(enc, 10)
        remote(win_in.at[0], spare, sems, 1, sibling).wait_send()

    gather.finish()
    for give in gives:
        give.wait_send()


def start_weights(wide, rows, attn_in, attn_out, cross_in, cross_out, ffn_in, ffn_out, gains, lines):
    depth = ffn_in.shape[1]
    low = jnp.bfloat16
    block = jax.ShapeDtypeStruct((rows, depth, 3 * TILE), low)
    part = (depth, 3 * HD)
    attn, dec_half, *outs = pl.pallas_call(
        lambda *refs: start_weights_kernel(wide, rows, *refs),
        out_shape=[
            jax.ShapeDtypeStruct((2, wide * depth, 3 * HD), low),
            jax.ShapeDtypeStruct(part, low),
            jax.ShapeDtypeStruct(gains.shape, jnp.float32),
            jax.ShapeDtypeStruct(gains.shape, jnp.float32),
            jax.ShapeDtypeStruct((H, LE, LE), jnp.float32),
            jax.ShapeDtypeStruct((H, LD, LD), jnp.float32),
        ]
        + [block] * (2 * wide),
        in_specs=[HBM] * 6 + [VM] * 3,
        out_specs=[HBM] * 2 + [VM] * 4 + [HBM] * (2 * wide),
        scratch_shapes=[
            pltpu.VMEM(part, low),
            pltpu.VMEM((wide,) + part, low),
            pltpu.VMEM(part, low),
            pltpu.VMEM(ffn_in.shape[1:], low),
            pltpu.VMEM((depth, FF), low),
            pltpu.VMEM((2, wide) + block.shape, low),
            pltpu.VMEM(lines[0].shape, jnp.float32),
            pltpu.VMEM(lines[1].shape, jnp.float32),
            pltpu.SemaphoreType.DMA((12 + 2 * wide,)),
            pltpu.SemaphoreType.DMA((12 + 2 * wide,)),
            pltpu.SemaphoreType.DMA((10 + wide,)),
        ],
        compiler_params=pltpu.CompilerParams(
            collective_id=1, has_side_effects=True, vmem_limit_bytes=VMEM_LIMIT
        ),
        name="start_weights",
    )(attn_in, attn_out[0].T, cross_in, cross_out, ffn_in, ffn_out[0].T, gains, *lines)
    return attn, dec_half, outs[:2], outs[2:4], outs[4 : 4 + wide], outs[4 + wide :]


def split_at(rows):
    return (rows // 2 + 15) // 16 * 16


class ReduceWeights:
    def __init__(self, batch, bufs, sems, base, local_sem, local_base, peers, others, held):
        self.own, self.land, self.plane, self.send, self.zland = bufs
        self.batch, self.held = batch, held
        core, place, row = lax.axis_index("section"), lax.axis_index("wide"), lax.axis_index("rows")
        wide, size = self.own.shape[:2]
        depth = batch.shape[0] // wide

        def rows_at(v, half):
            start = (place ^ v) * depth + half * (depth - size)
            return pl.ds(pl.multiple_of(start, 16), size)

        self.mine = [rows_at(v, core) for v in range(wide)]
        self.loads = [
            pltpu.make_async_copy(batch.at[self.mine[v]], self.own.at[v], local_sem.at[local_base + v])
            for v in range(0 if held else wide)
        ]
        self.swaps = [
            remote(batch.at[rows_at(v, 1 - core)], self.land.at[v], sems, base + v, peers[-1])
            for v in range(wide)
        ]
        base += wide
        self.scatter = ScatterPlane(self.own, self.plane, sems, base, peers, size)
        base += 6
        chunk = batch.shape[1] // (len(others) + 1)

        def lanes(k):
            return pl.ds(pl.multiple_of((row ^ k) * chunk, TILE), chunk)

        self.kept, self.relayed = lanes(0), lanes(2)
        near, far = others[0], others[1]
        self.spreads = [
            remote(self.send.at[:, lanes(1)], self.zland.at[0], sems, base, near),
            remote(self.send.at[:, lanes(3)], self.zland.at[1], sems, base + 1, near),
            remote(self.send.at[:, lanes(2)], self.zland.at[2], sems, base + 2, far),
        ]

    def start(self):
        for v in (3, 1, 2, 0):
            self.swaps[v].start()
            if not self.held:
                self.loads[v].start()

    def join(self):
        def add(v):
            self.swaps[v].wait_recv()
            if self.held:
                own = self.batch[self.mine[v], :]
            else:
                self.loads[v].wait()
                own = self.own[v]
            self.own[v] = (own.astype(jnp.float32) + self.land[v].astype(jnp.float32)).astype(
                jnp.bfloat16
            )

        add(3)
        self.scatter.send_far()
        add(1)
        self.scatter.send_early(0)
        add(2)
        self.scatter.send_early(1)
        add(0)

    def given(self):
        for swap in self.swaps:
            swap.wait_send()

    def pass_on(self):
        self.scatter.pass_on()

    def spread(self):
        self.send[...] = (self.own[0].astype(jnp.float32) + self.scatter.total()).astype(
            jnp.bfloat16
        )
        self.spreads[0].start()
        self.spreads[1].start()

    def relay(self):
        self.spreads[1].wait_recv()
        self.send[:, self.relayed] = (
            self.send[:, self.relayed].astype(jnp.float32) + self.zland[1].astype(jnp.float32)
        ).astype(jnp.bfloat16)
        self.spreads[2].start()

    def total(self):
        out = self.send[:, self.kept].astype(jnp.float32)
        for index in (0, 2):
            self.spreads[index].wait_recv()
            out = out + self.zland[index].astype(jnp.float32)
        return out

    def finish(self):
        for copy in self.spreads:
            copy.wait_send()
        self.scatter.finish()


def reduce_weights_scratch(wide, rows, size, columns):
    low = jnp.bfloat16
    return [
        pltpu.VMEM((wide, size, columns), low),
        pltpu.VMEM((wide, size, columns), low),
        pltpu.VMEM((3, size, columns), low),
        pltpu.VMEM((size, columns), low),
        pltpu.VMEM((rows - 1, size, columns // rows), low),
    ]


def last_kernel(wide, rows, *refs):
    cross_ref, dec_in, dec_out, enc_in, enc_out, y_ref, dec_attn, enc_attn = refs[:8]
    dec_self, enc_self, gains = refs[8:15], refs[15:22], refs[22:26]
    out_ref, ffn_ref, small_out, y_half, x_half, t_half = refs[26:32]
    refs = refs[32:]
    batch_bufs = [refs[i * 5 : i * 5 + 5] for i in range(3)]
    line_bufs, refs = refs[15:19], refs[19:]
    held, win, wout, gx, gt, context_e, projected_e, context_d, projected_d = refs[:9]
    keep, give, ready, landing, small, small_land, small_plane, small_rows = refs[9:17]
    halves, (sums_ref, send_sem, recv_sem, local_sem) = refs[17:23], refs[23:]
    core, place, row = lax.axis_index("section"), lax.axis_index("wide"), lax.axis_index("rows")
    peers = peers_of(wide)
    sibling = peers[-1]
    crossed = [{"section": 1 - core, "wide": place ^ v} for v in range(1, wide)]
    others = [{"rows": row ^ k} for k in range(1, rows)]
    sems = (send_sem, recv_sem)
    depth = cross_ref.shape[0] // wide
    units = dec_out.shape[0]
    low = jnp.bfloat16
    straight = (
        lax.broadcasted_iota(jnp.int32, (units, TILE), 0)
        == lax.broadcasted_iota(jnp.int32, (units, TILE), 1)
    ).astype(low)

    def attn_loads(source):
        return [
            pltpu.make_async_copy(source.at[0], win, local_sem.at[0]),
            pltpu.make_async_copy(source.at[1, :, pl.ds(0, HD)], wout, local_sem.at[1]),
        ]

    for load in attn_loads(dec_attn):
        load.start()
    greet(peers + crossed + others)
    per_batch = wide + 6 + rows - 1
    batches = [
        ReduceWeights(
            batch, bufs, sems, i * per_batch, local_sem, 2, peers, others, i > 0
        )
        for i, (batch, bufs) in enumerate(zip((cross_ref, held, held), batch_bufs))
    ]
    base = 3 * per_batch
    line = ReduceRows(enc_in, enc_out, *line_bufs, sems, base, local_sem, 2 + wide)
    base += 9
    local_base = 6 + wide
    first = remote(small.at[1 - core], small_land, sems, base, sibling)
    plane = [
        remote(small.at[core], small_plane.at[v - 1], sems, base + v, peers[v - 1])
        for v in range(1, wide)
    ]
    base += wide
    spread_small = [
        remote(small.at[core], small_rows.at[k - 1], sems, base + k - 1, others[k - 1])
        for k in range(1, rows)
    ]
    base += rows - 1
    hand_base = base
    base += 6 * wide

    def hand(section, source, v, piece):
        index = piece * wide + v
        return pltpu.make_async_remote_copy(
            src_ref=ready.at[section, v, piece],
            dst_ref=landing.at[source, v, piece],
            send_sem=send_sem.at[hand_base + section * 3 * wide + index],
            recv_sem=recv_sem.at[hand_base + source * 3 * wide + index],
            device_id={"section": section, "wide": place ^ v},
            device_id_type=MESH,
        )

    def hand_out(section, piece, value):
        for owner in range(wide):
            ready[section, owner ^ place, piece] = value[owner * depth : (owner + 1) * depth]
        for v in range(1, wide):
            hand(section, core, v, piece).start()

        @pl.when(core == section)
        def _():
            landing[core, 0, piece] = ready[section, 0, piece]

        @pl.when(core != section)
        def _():
            hand(section, core, 0, piece).start()

    def handed(section):
        for piece in range(3):
            for v in range(1, wide):
                hand(section, core, v, piece).wait_send()

            @pl.when(core != section)
            def _():
                hand(section, core, 0, piece).wait_send()

    def came(source):
        for piece in range(3):
            for v in range(1, wide):
                hand(0, source, v, piece).wait_recv()

            @pl.when(core != source)
            def _():
                hand(0, source, 0, piece).wait_recv()

    half_copies = []

    def by_half(index, value, target):
        mine, its = halves[2 * index : 2 * index + 2]
        middle = D // 2
        for own in range(2):

            @pl.when(core == own)
            def _():
                parts = (value[:, :middle], value[:, middle:]) if index != 1 else (value[:middle], value[middle:])
                mine[...] = parts[own].astype(mine.dtype)
                its[...] = parts[1 - own].astype(its.dtype)

        copies = (
            pltpu.make_async_copy(mine, target.at[core], local_sem.at[local_base + 1 + index]),
            remote(its, target.at[core], sems, base + index, sibling),
        )
        for copy in copies:
            copy.start()
            half_copies.append(copy)

    line.start()
    batches[0].start()
    by_half(0, y_ref[...], y_half)
    small[...] = jnp.zeros_like(small)
    for i, gain in enumerate(gains):
        small[i // 2, pl.ds(1 + i % 2, 1), pl.ds(0, D)] = gain[...]
    batches[0].join()
    for piece in range(2):
        hand_out(1, piece, dec_in[piece])
    hand_out(1, 2, tn(dec_out[...], straight).astype(low))
    g_ref, x_ref, gain_ref, normed_ref, projected_ref, context_ref, weights_ref = dec_self
    for load in attn_loads(dec_attn):
        load.wait()
    self_backward_rows(
        g_ref, x_ref, gain_ref, win, wout, projected_ref, weights_ref, gt, small.at[1], context_d, projected_d, sums_ref
    )
    for load in attn_loads(enc_attn):
        load.start()
    self_backward_weights(g_ref, normed_ref, context_ref, projected_d, held)
    batches[1].start()
    line.loaded()
    line.turn(0)
    batches[0].pass_on()
    by_half(2, gt[...], t_half)
    g_ref, x_ref, gain_ref, normed_ref, projected_ref, context_ref, weights_ref = enc_self
    for load in attn_loads(enc_attn):
        load.wait()
    self_backward_rows(
        g_ref, x_ref, gain_ref, win, wout, projected_ref, weights_ref, gx, small.at[0], context_e, projected_e, sums_ref
    )
    first.start()
    batches[1].join()
    batches[1].given()
    self_backward_weights(g_ref, normed_ref, context_ref, projected_e, held)
    batches[2].start()
    line.turn(1)
    batches[0].spread()
    first.wait()
    small[core] = small[core] + small_land[...]
    for copy in plane:
        copy.start()
    batches[2].join()
    batches[1].pass_on()
    by_half(1, gx[...].T, x_half)
    for copy in plane:
        copy.wait()
    small[core] = small[core] + jnp.sum(small_plane[...], axis=0)
    for copy in spread_small:
        copy.start()
    line.close(0)
    hand_out(0, 0, line_bufs[0][0, 0])
    batches[0].relay()
    line.turn(2)
    batches[1].spread()
    batches[2].pass_on()
    line.close(1)
    hand_out(0, 1, line_bufs[0][0, 1])
    batches[1].relay()
    batches[2].spread()
    line.close(2)
    hand_out(0, 2, tn(line_bufs[2][0], straight).astype(low))
    batches[2].relay()
    span, part = keep.shape[1] - cross_ref.shape[1] // rows // 2, cross_ref.shape[1] // rows // 2
    crosses = batches[0].total()
    selfs = [batches[2].total(), batches[1].total()]
    for own in range(2):

        @pl.when(core == own)
        def _():
            keep[:, pl.ds(0, span)] = selfs[own]
            keep[:, pl.ds(span, part)] = crosses[:, own * part : (own + 1) * part]
            give[:, pl.ds(0, span)] = selfs[1 - own]
            give[:, pl.ds(span, part)] = crosses[:, (1 - own) * part : (2 - own) * part]

    store = pltpu.make_async_copy(keep, out_ref.at[core], local_sem.at[local_base + 4])
    last = remote(give, out_ref.at[core], sems, base + 3, sibling)
    store.start()
    last.start()
    for copy in spread_small:
        copy.wait()
    small_out[...] = small[core] + jnp.sum(small_rows[...], axis=0)
    handed(0)
    handed(1)
    came(0)
    came(1)
    store_ffn = pltpu.make_async_copy(landing, ffn_ref, local_sem.at[local_base + 5])
    store_ffn.start()
    store.wait()
    last.wait()
    store_ffn.wait()
    for copy in half_copies:
        copy.wait()
    batches[0].given()
    batches[2].given()
    for batch in batches:
        batch.finish()
    line.finish()


def last_step(wide, rows, cross, dec_sums, enc_shares, y3, dec_attn, enc_attn, dec_self, enc_self, gains):
    low = jnp.bfloat16
    depth = D // wide
    size = split_at(depth)
    units = dec_sums[1].shape[0]
    columns = cross.shape[1]
    enc_rows, dec_rows = enc_self[0].shape[0], dec_self[0].shape[0]
    wanted = (columns + columns // 2) // rows
    copies = 3 * (wide + 6 + rows - 1) + 9 + wide + rows - 1 + 6 * wide + 4
    small = (16, (D + TILE - 1) // TILE * TILE)
    middle = D // 2
    half_shapes = [
        ((dec_rows, middle), low),
        ((middle, enc_rows), jnp.float32),
        ((dec_rows, middle), jnp.float32),
    ]
    batch_scratch = reduce_weights_scratch(wide, rows, size, columns)
    return pl.pallas_call(
        lambda *refs: last_kernel(wide, rows, *refs),
        out_shape=[
            jax.ShapeDtypeStruct((2, size, wanted), jnp.float32),
            jax.ShapeDtypeStruct((2, wide, 3, depth, TILE), low),
            jax.ShapeDtypeStruct(small, jnp.float32),
        ]
        + [jax.ShapeDtypeStruct((2, *each), kind) for each, kind in half_shapes],
        in_specs=[HBM, VM, VM, HBM, HBM, VM, HBM, HBM] + [VM] * 18,
        out_specs=[HBM, HBM, VM, HBM, HBM, HBM],
        scratch_shapes=batch_scratch * 3
        + reduce_rows_scratch(units)
        + [
            pltpu.VMEM((D, columns), low),
            pltpu.VMEM((D, 3 * HD), low),
            pltpu.VMEM((D, HD), low),
            pltpu.VMEM((enc_rows, D), jnp.float32),
            pltpu.VMEM((dec_rows, D), jnp.float32),
            pltpu.VMEM((enc_rows, HD), low),
            pltpu.VMEM((enc_rows, 3 * HD), low),
            pltpu.VMEM((dec_rows, HD), low),
            pltpu.VMEM((dec_rows, 3 * HD), low),
            pltpu.VMEM((size, wanted), jnp.float32),
            pltpu.VMEM((size, wanted), jnp.float32),
            pltpu.VMEM((2, wide, 3, depth, TILE), low),
            pltpu.VMEM((2, wide, 3, depth, TILE), low),
            pltpu.VMEM((2,) + small, jnp.float32),
            pltpu.VMEM(small, jnp.float32),
            pltpu.VMEM((wide - 1,) + small, jnp.float32),
            pltpu.VMEM((rows - 1,) + small, jnp.float32),
        ]
        + [pltpu.VMEM(each, kind) for each, kind in half_shapes for _ in range(2)]
        + [
            pltpu.VMEM((H, 1, 2 * enc_rows), jnp.float32),
            pltpu.SemaphoreType.DMA((copies,)),
            pltpu.SemaphoreType.DMA((copies,)),
            pltpu.SemaphoreType.DMA((12 + wide,)),
        ],
        compiler_params=pltpu.CompilerParams(
            collective_id=7, has_side_effects=True, vmem_limit_bytes=VMEM_LIMIT
        ),
        name="last_step",
    )(cross, *dec_sums, *enc_shares, y3, dec_attn, enc_attn, *dec_self, *enc_self, *gains)


def assemble_kernel(
    units, parts_ref, attn_ref, small_ref, enc_hot, dec_hot,
    in_ref, out_ref, gain_ref, bias_ref, win_ref, wout_ref, cin_ref, cout_ref,
):
    low = jnp.bfloat16
    wide = parts_ref.shape[1]
    place, core = lax.axis_index("wide"), lax.axis_index("section")
    pairs = 2 * wide
    row_ids = lax.broadcasted_iota(jnp.int32, (TILE, TILE), 0)
    lane_ids = lax.broadcasted_iota(jnp.int32, (TILE, TILE), 1)

    def tile_at(tile, first, columns):
        total = None
        last = min((tile + 1) * TILE, columns) - 1
        for group in range(tile * TILE // units, last // units + 1):
            half, chip, block = group % 2, group % pairs // 2, group // pairs
            shift = group * units - tile * TILE
            picks = ((row_ids + shift == lane_ids) & (row_ids < units)).astype(low)
            part = matmul(
                parts_ref[half, chip ^ place, first + block], picks
            )
            total = part if total is None else total + part
        return total

    for tile in range(in_ref.shape[2] // TILE):
        in_ref[0, :, pl.ds(tile * TILE, TILE)] = tile_at(tile, 0, in_ref.shape[2])
    for tile in range(out_ref.shape[2] // TILE):
        out_ref[0, :, pl.ds(tile * TILE, TILE)] = tile_at(tile, 2, out_ref.shape[2])
    for row in range(3):
        gain_ref[row] = small_ref[row : row + 1, 0:D]
    for section, hot in enumerate((enc_hot, dec_hot)):

        @pl.when(core == section)
        def _():
            sums = small_ref[8:16, 0 : hot.shape[1]]
            bias = lax.dot_general(
                sums, hot[...], (((1,), (1,)), ((), ())), precision=HIGHEST, preferred_element_type=jnp.float32
            )
            for head in range(H):
                bias_ref[head] = bias[head : head + 1]

    size, depth = attn_ref.shape[1], in_ref.shape[1]
    whole = jnp.concatenate([attn_ref[0], attn_ref[1, 2 * size - depth :]], axis=0)
    turned = whole.T
    start = 0
    for ref in (win_ref, wout_ref, cin_ref, cout_ref):
        ref[0] = turned[start : start + ref.shape[1]]
        start += ref.shape[1]


def assemble(rows, parts, attn_parts, small):
    wide, depth = parts.shape[1], parts.shape[3]
    shapes = [
        (1, depth, 2 * FF // rows),
        (1, depth, FF // rows),
        (3, 1, D),
        (H, 1, NB),
        (1, 3 * HD // rows, depth),
        (1, HD // rows, depth),
        (1, HD // rows, depth),
        (1, HD // rows, depth),
    ]
    return pl.pallas_call(
        lambda *refs: assemble_kernel(FF // (wide * rows * 2), *refs),
        out_shape=[jax.ShapeDtypeStruct(shape, jnp.float32) for shape in shapes],
        in_specs=[VM] * 5,
        out_specs=[VM] * len(shapes),
        compiler_params=pltpu.CompilerParams(vmem_limit_bytes=VMEM_LIMIT),
        name="assemble",
    )(
        parts,
        attn_parts,
        small,
        distance_hot(LE, True, 1 - LE),
        distance_hot(LD, False, 1 - LD),
    )


def bias_rows(source, target):
    length, span = target.shape[1], source.shape[1]
    for head in range(H):
        row = jnp.broadcast_to(source[pl.ds(head, 1), :], (length, span))
        target[head] = pltpu.roll(row, 0, 1, stride=1, stride_axis=0)[:, :length]


def distance_sums(scores, span):
    length = scores.shape[0]
    flip = (
        lax.broadcasted_iota(jnp.int32, (length, length), 0)
        + lax.broadcasted_iota(jnp.int32, (length, length), 1)
        == length - 1
    ).astype(jnp.bfloat16)
    flipped = matmul(flip, scores)
    padded = jnp.concatenate([flipped, jnp.zeros((length, span - length), jnp.float32)], axis=1)
    rolled = pltpu.roll(padded, 0, 1, stride=1, stride_axis=0)
    return jnp.sum(rolled, axis=0, keepdims=True)


def distance_hot(length, both_ways, first):
    table = bucket_table(length, both_ways)
    span = 2 * length
    hot = np.zeros((NB, span), np.float32)
    for entry in range(span):
        distance = entry + first
        if first == 0 and distance >= length:
            distance -= span
        if -length < distance < length:
            query = max(0, -distance)
            hot[table[query, query + distance], entry] = 1.0
    return jnp.asarray(hot)


def head_lanes(value, side):
    lanes = lax.broadcasted_iota(jnp.int32, value.shape, 1)
    return jnp.where((lanes < DH) == (side == 0), value, jnp.zeros_like(value))


def attend_heads(query_of, key_of, value_of, bias_of, allowed, context_ref, weights_ref):
    @pl.loop(0, H // 2)
    def _(pair):
        query, key, value = query_of(pair), key_of(pair), value_of(pair)
        total = None
        for side in range(2):
            head = 2 * pair + side
            scores = nt(head_lanes(query, side), key)
            if bias_of is not None:
                scores = scores + bias_of(head)
            scores = jnp.where(allowed, scores, NEGATIVE)
            shifted = jnp.exp(scores - jnp.max(scores, axis=-1, keepdims=True))
            weights = shifted / jnp.sum(shifted, axis=-1, keepdims=True)
            weights_ref[head] = weights
            part = matmul(weights.astype(jnp.bfloat16), head_lanes(value, side))
            total = part if total is None else total + part
        context_ref[:, pair_tile(pair, 0)] = total.astype(jnp.bfloat16)


def attend_heads_backward(query_of, key_of, value_of, weights_ref, grad_of, put, put_scores=None):
    @pl.loop(0, H // 2)
    def _(pair):
        query, key, value, grad = query_of(pair), key_of(pair), value_of(pair), grad_of(pair)
        sums = [None, None, None]
        for side in range(2):
            head = 2 * pair + side
            weights = weights_ref[head]
            own_grad = head_lanes(grad, side)
            grad_weights = nt(own_grad, value)
            inner = jnp.sum(grad_weights * weights, axis=-1, keepdims=True)
            low = (weights * (grad_weights - inner)).astype(jnp.bfloat16)
            if put_scores is not None:
                put_scores(head, low)
            parts = [
                matmul(low, head_lanes(key, side)),
                tn(low, head_lanes(query, side)),
                tn(weights.astype(jnp.bfloat16), own_grad),
            ]
            sums = [b if a is None else a + b for a, b in zip(sums, parts)]
        put(pair, *sums)


def pair_tile(pair, base):
    return pl.ds(pl.multiple_of(base + pair * TILE, TILE), TILE)


def item_numbers(lengths_ref, core, shape, axis):
    positions = lax.broadcasted_iota(jnp.int32, shape, axis)
    number, end = jnp.zeros(shape, jnp.int32), 0
    for item in range(lengths_ref.shape[1] - 1):
        end = end + lengths_ref[core, item]
        number = number + (positions >= end).astype(jnp.int32)
    return number


def weight_spec(half, width, index):
    return pl.BlockSpec((None, D, width), lambda step: (half, 0, index), memory_space=pltpu.VMEM)


W_IN = weight_spec(0, 3 * HD, 0)
W_OUT, C_IN, C_OUT = [weight_spec(1, HD, i) for i in range(3)]


def tile_of(ref, base):
    return lambda pair: ref[:, pair_tile(pair, base)]


def self_forward_kernel(
    wide, causal, x_ref, gain_ref, win_ref, wout_ref, bias_ref, lengths_ref, *refs
):
    core = lax.axis_index("section")
    if wide:
        blocks, dec_blocks, refs = refs[: wide - 1], refs[wide - 1 : 2 * wide - 2], refs[2 * wide - 2 :]
    y_ref, low_ref, normed_ref, projected_ref, context_ref, weights_ref = refs[:6]
    if wide:
        pieces, dec_pieces, sems = refs[6 : 5 + wide], refs[5 + wide : 4 + 2 * wide], refs[4 + 2 * wide :]
        peers = peers_of(wide)
        greet(peers + [{"rows": lax.axis_index("rows") ^ 1}])
        reshard = Reshard(blocks, pieces, 0, sems, 0, peers)
        reshard.start()
        half = dec_pieces[0].shape[0]
        mine = pl.ds(lax.axis_index("rows") % 2 * half, half)
        later = [
            remote(block.at[mine], piece, sems, 9 + v, peers[v])
            for v, (block, piece) in enumerate(zip(dec_blocks, dec_pieces))
        ]
    low_ref[...] = x_ref[core] if causal else x_ref[core].T
    residual = low_ref[...].astype(jnp.float32)
    normed_ref[...] = (residual * rms_rows(residual) * gain_ref[pl.ds(0, 1), :]).astype(jnp.bfloat16)
    projected_ref[...] = matmul(normed_ref[...], win_ref[...]).astype(jnp.bfloat16)
    length = low_ref.shape[0]
    allowed = item_numbers(lengths_ref, core, (length, length), 0) == item_numbers(
        lengths_ref, core, (length, length), 1
    )
    if causal:
        allowed = allowed & (
            lax.broadcasted_iota(jnp.int32, (length, length), 0)
            >= lax.broadcasted_iota(jnp.int32, (length, length), 1)
        )
    attend_heads(
        tile_of(projected_ref, 0),
        tile_of(projected_ref, HD),
        tile_of(projected_ref, 2 * HD),
        lambda head: bias_ref[head],
        allowed,
        context_ref,
        weights_ref,
    )
    y_ref[...] = residual + nt(context_ref[...], wout_ref[...])
    if wide:
        for copy in later:
            copy.start()
        reshard.pass_on()
        reshard.finish()
        for copy in later:
            copy.wait()


def self_forward(causal, embed, gains, weight, bias, lengths, blocks=(), dec_blocks=()):
    rows = embed.shape[1 if causal else 2]
    low = jnp.bfloat16
    wide = len(blocks) + 1 if blocks else 0
    params = dict(vmem_limit_bytes=VMEM_LIMIT)
    if blocks:
        params.update(collective_id=6, has_side_effects=True)
    y, *kept = pl.pallas_call(
        lambda *refs: self_forward_kernel(wide, causal, *refs),
        out_shape=[
            jax.ShapeDtypeStruct((rows, D), jnp.float32),
            jax.ShapeDtypeStruct((rows, D), low),
            jax.ShapeDtypeStruct((rows, D), low),
            jax.ShapeDtypeStruct((rows, 3 * HD), low),
            jax.ShapeDtypeStruct((rows, HD), low),
            jax.ShapeDtypeStruct((H, rows, rows), jnp.float32),
        ]
        + [jax.ShapeDtypeStruct(each.shape, low) for each in blocks]
        + [jax.ShapeDtypeStruct((each.shape[0] // 2, *each.shape[1:]), low) for each in dec_blocks],
        in_specs=[VM, VM, W_IN, W_OUT, VM, SM] + [HBM] * (2 * len(blocks)),
        out_specs=[VM] * 6 + [HBM] * (2 * len(blocks)),
        scratch_shapes=[pltpu.SemaphoreType.DMA((12,))] * 2 if blocks else [],
        grid=(1,),
        compiler_params=pltpu.CompilerParams(**params),
        name="self_forward_%d" % rows,
    )(embed, gains, weight, weight, bias, lengths, *blocks, *dec_blocks)
    return y, kept[:5], kept[5:]


def picked(source, start, window, first, width):
    base = start // TILE * TILE
    window = min(window, source.shape[1] - base)
    lanes = lax.broadcasted_iota(jnp.int32, (window, HD), 1) - first
    rows_of = lax.broadcasted_iota(jnp.int32, (window, HD), 0) + (base - start)
    pick = ((rows_of == lanes) & (lanes >= 0) & (lanes < width)).astype(jnp.bfloat16)
    return matmul(source[:, pl.ds(base, window)], pick)


def self_backward_rows(
    g_ref,
    x_ref,
    gain_ref,
    win_ref,
    wout_ref,
    projected_ref,
    weights_ref,
    gx_ref,
    small_ref,
    context_grad,
    projected_grad,
    sums_ref,
):
    low = jnp.bfloat16
    length = x_ref.shape[0]
    context_grad[...] = matmul(g_ref[...].astype(low), wout_ref[...]).astype(low)

    def put(pair, query, key, value):
        for index, part in enumerate((query, key, value)):
            projected_grad[:, pair_tile(pair, index * HD)] = part.astype(low)

    def put_scores(head, scores):
        sums_ref[head, :, pl.ds(0, 2 * length)] = distance_sums(scores, 2 * length)

    attend_heads_backward(
        tile_of(projected_ref, 0),
        tile_of(projected_ref, HD),
        tile_of(projected_ref, 2 * HD),
        weights_ref,
        tile_of(context_grad, 0),
        put,
        put_scores,
    )
    for head in range(H):
        small_ref[pl.ds(8 + head, 1), pl.ds(0, 2 * length)] = sums_ref[head, :, pl.ds(0, 2 * length)]
    grad_normed = nt(projected_grad[...], win_ref[...])
    residual = x_ref[...].astype(jnp.float32)
    grad_residual, grad_gain = norm_pull(residual, gain_ref[pl.ds(0, 1), :], grad_normed)
    small_ref[pl.ds(0, 1), pl.ds(0, D)] = grad_gain
    gx_ref[...] = g_ref[...] + grad_residual


def self_backward_weights(g_ref, normed_ref, context_ref, projected_grad, grad_ref):
    low = jnp.bfloat16
    both = jnp.concatenate([normed_ref[...], g_ref[...].astype(low)], axis=0)
    chunks = grad_ref.shape[1] // HD
    part_in, part_out = 3 * HD // chunks, HD // chunks
    for chunk in range(chunks):
        right = jnp.concatenate(
            [
                picked(projected_grad, chunk * part_in, HD, 0, part_in),
                picked(context_ref, chunk * part_out, 2 * TILE, part_in, part_out),
            ],
            axis=0,
        ).astype(low)
        grad_ref[:, pl.ds(chunk * HD, HD)] = tn(both, right).astype(low)


def cross_forward_kernel(
    x_ref, final_ref, wkey_ref, wvalue_ref, y_ref, gain_ref, wquery_ref, wout_ref, dec_lengths, enc_lengths,
    out_ref, memory_ref, kv_ref, normed_ref, query_ref, context_ref, weights_ref,
):
    low = jnp.bfloat16
    core = lax.axis_index("section")
    residual = x_ref[...]
    memory_ref[...] = (residual * rms_rows(residual) * final_ref[pl.ds(2, 1), :]).astype(low)
    kv_ref[:, pl.ds(0, HD)] = matmul(memory_ref[...], wkey_ref[...]).astype(low)
    kv_ref[:, pl.ds(HD, HD)] = matmul(memory_ref[...], wvalue_ref[...]).astype(low)
    target = y_ref[...]
    normed_ref[...] = (target * rms_rows(target) * gain_ref[pl.ds(1, 1), :]).astype(low)
    query_ref[...] = matmul(normed_ref[...], wquery_ref[...]).astype(low)
    attend_heads(
        tile_of(query_ref, 0),
        tile_of(kv_ref, 0),
        tile_of(kv_ref, HD),
        None,
        item_numbers(dec_lengths, core, (LD, LE), 0) == item_numbers(enc_lengths, core, (LD, LE), 1),
        context_ref,
        weights_ref,
    )
    out_ref[...] = target + nt(context_ref[...], wout_ref[...])


def cross_forward(x2, enc_gains, enc_weight, y1, dec_gains, dec_weight, dec_lengths, enc_lengths):
    low = jnp.bfloat16
    y2, *kept = pl.pallas_call(
        cross_forward_kernel,
        out_shape=[
            jax.ShapeDtypeStruct((LD, D), jnp.float32),
            jax.ShapeDtypeStruct((LE, D), low),
            jax.ShapeDtypeStruct((LE, 2 * HD), low),
            jax.ShapeDtypeStruct((LD, D), low),
            jax.ShapeDtypeStruct((LD, HD), low),
            jax.ShapeDtypeStruct((LD, HD), low),
            jax.ShapeDtypeStruct((H, LD, LE), jnp.float32),
        ],
        in_specs=[VM, VM, C_IN, C_OUT, VM, VM, C_IN, C_OUT, SM, SM],
        out_specs=[VM] * 7,
        grid=(1,),
        compiler_params=pltpu.CompilerParams(vmem_limit_bytes=VMEM_LIMIT),
        name="cross_forward",
    )(
        x2,
        enc_gains,
        enc_weight,
        enc_weight,
        y1,
        dec_gains,
        dec_weight,
        dec_weight,
        dec_lengths,
        enc_lengths,
    )
    return y2, kept


def cross_backward_kernel(
    g_ref, x_ref, final_ref, wkey_ref, wvalue_ref, y_ref, gain_ref, wquery_ref, wout_ref, kv_ref, query_ref, weights_ref,
    memory_ref, normed_ref, context_ref, gx_ref, gy_ref, final_out, gain_out, grad_ref, kv_grad, query_grad, context_grad,
):
    low = jnp.bfloat16
    grad_low = g_ref[...].astype(low)
    context_grad[...] = matmul(grad_low, wout_ref[...]).astype(low)

    def put(pair, query, key, value):
        query_grad[:, pair_tile(pair, 0)] = query.astype(low)
        kv_grad[:, pair_tile(pair, 0)] = key.astype(low)
        kv_grad[:, pair_tile(pair, HD)] = value.astype(low)

    attend_heads_backward(
        tile_of(query_ref, 0),
        tile_of(kv_ref, 0),
        tile_of(kv_ref, HD),
        weights_ref,
        tile_of(context_grad, 0),
        put,
    )
    grad_memory = nt(kv_grad[:, pl.ds(0, HD)], wkey_ref[...]) + nt(
        kv_grad[:, pl.ds(HD, HD)], wvalue_ref[...]
    )
    gx_ref[...], final_out[...] = norm_pull(x_ref[...], final_ref[pl.ds(2, 1), :], grad_memory)
    grad_residual, gain_out[...] = norm_pull(
        y_ref[...], gain_ref[pl.ds(1, 1), :], nt(query_grad[...], wquery_ref[...])
    )
    gy_ref[...] = g_ref[...] + grad_residual
    lefts = jnp.concatenate([memory_ref[...], normed_ref[...], grad_low], axis=0)
    chunks = grad_ref.shape[1] // HD
    part = HD // chunks
    for chunk in range(chunks):
        start = chunk * part
        right = jnp.concatenate(
            [
                picked(kv_grad, start, 2 * TILE, 0, part)
                + picked(kv_grad, HD + start, 2 * TILE, part, part),
                picked(query_grad, start, 2 * TILE, 2 * part, part),
                picked(context_ref, start, 2 * TILE, 3 * part, part),
            ],
            axis=0,
        ).astype(low)
        grad_ref[:, pl.ds(chunk * HD, HD)] = tn(lefts, right).astype(low)


def cross_backward(g2, x2, enc_gains, enc_weight, y1, dec_gains, dec_weight, kept):
    memory, kv, normed, query, context, weights = kept
    low = jnp.bfloat16
    return pl.pallas_call(
        cross_backward_kernel,
        out_shape=[
            jax.ShapeDtypeStruct((LE, D), jnp.float32),
            jax.ShapeDtypeStruct((LD, D), jnp.float32),
            jax.ShapeDtypeStruct((1, D), jnp.float32),
            jax.ShapeDtypeStruct((1, D), jnp.float32),
            jax.ShapeDtypeStruct((D, 4 * HD), low),
        ],
        in_specs=[VM, VM, VM, C_IN, C_OUT, VM, VM, C_IN, C_OUT] + [VM] * 6,
        out_specs=[VM] * 5,
        scratch_shapes=[
            pltpu.VMEM((LE, 2 * HD), low),
            pltpu.VMEM((LD, HD), low),
            pltpu.VMEM((LD, HD), low),
        ],
        grid=(1,),
        compiler_params=pltpu.CompilerParams(vmem_limit_bytes=VMEM_LIMIT),
        name="cross_backward",
    )(
        g2,
        x2,
        enc_gains,
        enc_weight,
        enc_weight,
        y1,
        dec_gains,
        dec_weight,
        dec_weight,
        kv,
        query,
        weights,
        memory,
        normed,
        context,
    )


def plain_self_forward(residual, gain_row, weight, bias_full, allowed):
    normed = to_low(rms_norm(residual, gain_row))
    projected = to_low(matmul(normed, weight[:, : 3 * HD]))
    context, weights, low_weights = attend_forward(
        projected[:, :HD], projected[:, HD : 2 * HD], projected[:, 2 * HD :], bias_full, allowed
    )
    return (
        residual + matmul(context, weight[:, 3 * HD : 4 * HD].T),
        (residual, normed, projected, context, weights, low_weights),
    )


def plain_self_backward(kept, gain_row, weight, hot, grad_out):
    residual, normed, projected, context, weights, low_weights = kept
    grad_low = to_low(grad_out)
    grad_wout = matmul(grad_low.T, context)
    grad_context = to_low(matmul(grad_low, weight[:, 3 * HD : 4 * HD]))
    grad_queries, grad_keys, grad_values, low_scores = attend_backward(
        projected[:, :HD],
        projected[:, HD : 2 * HD],
        projected[:, 2 * HD :],
        weights,
        low_weights,
        grad_context,
    )
    grad_projected = to_low(jnp.concatenate([grad_queries, grad_keys, grad_values], axis=1))
    grad_win = matmul(normed.T, grad_projected)
    grad_residual, grad_gain = plain_norm_backward(
        residual, gain_row, matmul(grad_projected, weight[:, : 3 * HD].T)
    )
    grad_bias = jnp.einsum(
        "hqk,qkb->bh", low_scores, hot.astype(jnp.bfloat16), preferred_element_type=jnp.float32
    )
    return grad_out + grad_residual, grad_gain, grad_win, grad_wout, grad_bias


def plain_reduce_attn(grad, core, wide, rows):
    depth, columns = grad.shape
    halves = plain_core_halves(grad, core, wide)
    place = lax.axis_index("wide")
    parts = [
        lax.dynamic_index_in_dim(halves, place ^ v, 0, keepdims=False) for v in range(wide)
    ]
    mine = to_low(scatter_wide(parts))
    pieces, start = [], 0
    for width in (3 * HD, HD, HD, HD):
        pieces.append(mine[:, start : start + width].reshape(mine.shape[0], rows, width // rows))
        start += width
    stacked = jnp.concatenate(pieces, axis=2).transpose(1, 0, 2)
    return lax.psum_scatter(stacked, "rows", scatter_dimension=0, tiled=True)[0]


def plain_core_halves(grad, core, wide):
    depth, columns = grad.shape
    split = to_low(grad).reshape(wide, 2, depth // wide // 2, columns)
    mine = lax.dynamic_index_in_dim(split, core, 1, keepdims=False)
    sent = lax.dynamic_index_in_dim(split, 1 - core, 1, keepdims=False)
    return mine.astype(jnp.float32) + xor_permute(sent, "section", 1).astype(jnp.float32)


def plain_both_sections(own, section):
    other = xor_permute(own, "section", 1)
    is_dec = section == 1
    return jnp.where(is_dec, other, own), jnp.where(is_dec, own, other)


def plain_norm_backward(residual, gain_row, grad_normed):
    _, norm_pull = jax.vjp(rms_norm, residual, gain_row)
    return norm_pull(grad_normed)


def plain_hidden_columns(weight):
    width = weight.shape[1] * 2 // 3
    return weight[:, :width], weight[:, width:]


def plain_ffn_hidden(blocks, weight):
    w_in, _ = plain_hidden_columns(weight)
    both = [matmul(block, w_in) for block in blocks]
    units = w_in.shape[1] // 2
    return both, [to_low(gated(part[:, :units], part[:, units:])) for part in both]


def plain_ffn_forward(residual, gain_row, weight):
    blocks = gather_wide(to_low(rms_norm(residual, gain_row)))
    both, hidden = plain_ffn_hidden(blocks, weight)
    _, w_out = plain_hidden_columns(weight)
    out = residual + scatter_wide([matmul(part, w_out.T) for part in hidden])
    return out, (residual, blocks, both, hidden)


def plain_ffn_backward(kept, gain_row, weight, grad_out, grad_blocks):
    residual, blocks, both, hidden = kept
    w_in, w_out = plain_hidden_columns(weight)
    units = w_out.shape[1]
    parts, grad_both = [], []
    for block, pre in zip(grad_blocks, both):
        _, pull = jax.vjp(gated, pre[:, :units], pre[:, units:])
        grad_gate, grad_up = pull(matmul(block, w_out))
        low = to_low(jnp.concatenate([grad_gate, grad_up], axis=1))
        grad_both.append(low)
        parts.append(matmul(low, w_in.T))
    grad_residual, grad_gain = plain_norm_backward(residual, gain_row, scatter_wide(parts))
    joined = jnp.concatenate(grad_both, axis=0)
    grad_in = matmul(jnp.concatenate(blocks, axis=0).T, joined)
    grad_wout = matmul(jnp.concatenate(grad_blocks, axis=0).T, jnp.concatenate(hidden, axis=0))
    return grad_out + grad_residual, grad_gain, (grad_in, grad_wout)


def plain_reduce_ffn(grads, core, wide, rows):
    grad_in, grad_wout = grads
    depth = grad_in.shape[0]
    both = jnp.concatenate(
        [grad_in.reshape(depth, rows, -1), grad_wout.reshape(depth, rows, -1)], axis=2
    )
    columns = both.shape[2]
    halves = plain_core_halves(both.reshape(depth, rows * columns), core, wide)
    halves = to_low(halves).reshape(wide * (depth // wide // 2), rows, columns).transpose(1, 0, 2)
    summed = lax.psum_scatter(halves, "rows", scatter_dimension=0, tiled=True)[0]
    blocks = summed.reshape(wide, depth // wide // 2, columns)
    place = lax.axis_index("wide")
    out = [lax.dynamic_index_in_dim(blocks, place, 0, keepdims=False)]
    for v in range(1, wide):
        block = lax.dynamic_index_in_dim(blocks, place ^ v, 0, keepdims=False)
        out.append(xor_permute(block, "wide", v))
    return placed_rows([piece[None] for piece in out], place)


def plain_to_section(enc_half, dec_half, core):
    is_dec = core == 1
    own = jnp.where(is_dec, dec_half, enc_half)
    got = xor_permute(jnp.where(is_dec, enc_half, dec_half), "section", 1)
    low, high = jnp.where(is_dec, got, own), jnp.where(is_dec, own, got)
    return jnp.concatenate([low, high], axis=-2).astype(jnp.float32)


def plain_shards(
    enc_embed,
    dec_embed,
    out_cot,
    enc_lengths,
    dec_lengths,
    norm_gains,
    rel_bias,
    attn_in,
    attn_out,
    ffn_in,
    ffn_out,
    cross_in,
    cross_out,
):
    core = lax.axis_index("section")
    place = lax.axis_index("wide")
    wide, rows = lax.axis_size("wide"), lax.axis_size("rows")
    depth = attn_in.shape[1]
    unit = FF // (wide * rows)

    small = jnp.concatenate([norm_gains[0].reshape(-1), rel_bias[0].reshape(-1)])
    enc_small, dec_small = plain_both_sections(small, core)
    gains = [each[: 3 * D].reshape(3, D) for each in (enc_small, dec_small)]
    biases = [each[3 * D :].reshape(NB, H) for each in (enc_small, dec_small)]

    attn_shard = jnp.concatenate([attn_in[0], attn_out[0].T, cross_in[0], cross_out[0]], axis=1)
    attn_own = placed_rows(gather_wide(attn_shard), place)
    ffn_blocks = jnp.concatenate(
        [
            ffn_in[0].reshape(depth, 2 * rows, wide, unit).transpose(2, 0, 1, 3).reshape(wide, depth, -1),
            ffn_out[0].T.reshape(depth, rows, wide, unit).transpose(2, 0, 1, 3).reshape(wide, depth, -1),
        ],
        axis=2,
    )
    ffn_got = [lax.dynamic_index_in_dim(ffn_blocks, place, 0, keepdims=False)]
    for v in range(1, wide):
        block = lax.dynamic_index_in_dim(ffn_blocks, place ^ v, 0, keepdims=False)
        ffn_got.append(xor_permute(block, "wide", v))
    ffn_own = placed_rows(ffn_got, place)
    attn_enc, attn_dec = plain_both_sections(attn_own, core)
    ffn_enc, ffn_dec = plain_both_sections(ffn_own, core)
    memory_weight = attn_enc[:, 4 * HD :]
    cross_w_in, cross_w_out = attn_dec[:, 4 * HD : 5 * HD], attn_dec[:, 5 * HD :]

    def own_row(array):
        return lax.dynamic_index_in_dim(array[:, 0], core, 0, keepdims=False)

    enc_row = own_row(enc_embed).astype(jnp.float32)
    dec_row = own_row(dec_embed).astype(jnp.float32)
    cot_row = own_row(out_cot)
    enc_items = item_ids(own_row(enc_lengths), LE)
    dec_items = item_ids(own_row(dec_lengths), LD)
    enc_hot, dec_hot = one_hot(LE, True), one_hot(LD, False)
    enc_bias = jnp.einsum("qkb,bh->hqk", enc_hot, biases[0], precision=HIGHEST)
    dec_bias = jnp.einsum("qkb,bh->hqk", dec_hot, biases[1], precision=HIGHEST)
    causal = jnp.arange(LD)[:, None] >= jnp.arange(LD)[None, :]

    cot_blocks = gather_wide(cot_row)
    x1, enc_self = plain_self_forward(
        enc_row, gains[0][0], attn_enc, enc_bias, enc_items[:, None] == enc_items[None, :]
    )
    y1, dec_self = plain_self_forward(
        dec_row,
        gains[1][0],
        attn_dec,
        dec_bias,
        (dec_items[:, None] == dec_items[None, :]) & causal,
    )
    x2, enc_ffn = plain_ffn_forward(x1, gains[0][1], ffn_enc)
    memory = to_low(rms_norm(x2, gains[0][2]))
    memory_kv = to_low(matmul(memory, memory_weight))
    cross_normed = to_low(rms_norm(y1, gains[1][1]))
    queries = to_low(matmul(cross_normed, cross_w_in))
    context, weights, low_weights = attend_forward(
        queries,
        memory_kv[:, :HD],
        memory_kv[:, HD:],
        0.0,
        dec_items[:, None] == enc_items[None, :],
    )
    y2 = y1 + matmul(context, cross_w_out.T)
    y3, dec_ffn = plain_ffn_forward(y2, gains[1][2], ffn_dec)

    g2, dec_ffn_gain, dec_ffn_grads = plain_ffn_backward(
        dec_ffn, gains[1][2], ffn_dec, cot_row.astype(jnp.float32), cot_blocks
    )
    dec_ffn_share = plain_reduce_ffn(dec_ffn_grads, core, wide, rows)
    g2_low = to_low(g2)
    grad_cross_out = matmul(g2_low.T, context)
    grad_context = to_low(matmul(g2_low, cross_w_out))
    grad_queries, grad_keys, grad_values, _ = attend_backward(
        queries, memory_kv[:, :HD], memory_kv[:, HD:], weights, low_weights, grad_context
    )
    grad_query_low = to_low(grad_queries)
    grad_kv = to_low(jnp.concatenate([grad_keys, grad_values], axis=1))
    grad_x2, enc_final_gain = plain_norm_backward(x2, gains[0][2], matmul(grad_kv, memory_weight.T))
    grad_x1, enc_ffn_gain, enc_ffn_grads = plain_ffn_backward(
        enc_ffn, gains[0][1], ffn_enc, grad_x2, gather_wide(to_low(grad_x2))
    )
    enc_ffn_share = plain_reduce_ffn(enc_ffn_grads, core, wide, rows)

    grad_cross_in = matmul(cross_normed.T, grad_query_low)
    grad_memory = matmul(memory.T, grad_kv)
    from_cross, dec_cross_gain = plain_norm_backward(
        y1, gains[1][1], matmul(grad_query_low, cross_w_in.T)
    )
    grad_y, dec_self_gain, dec_win, dec_wout, dec_bias_grad = plain_self_backward(
        dec_self, gains[1][0], attn_dec, dec_hot, g2 + from_cross
    )
    dec_attn_share = plain_reduce_attn(
        jnp.concatenate([dec_win, dec_wout, grad_cross_in, grad_cross_out], axis=1),
        core,
        wide,
        rows,
    )
    grad_x, enc_self_gain, enc_win, enc_wout, enc_bias_grad = plain_self_backward(
        enc_self, gains[0][0], attn_enc, enc_hot, grad_x1
    )
    enc_attn_share = plain_reduce_attn(
        jnp.concatenate([enc_win, enc_wout, grad_memory], axis=1), core, wide, rows
    )

    small_grads = jnp.stack(
        [
            jnp.concatenate(
                [enc_self_gain, enc_ffn_gain, enc_final_gain, enc_bias_grad.reshape(-1)]
            ),
            jnp.concatenate(
                [dec_self_gain, dec_cross_gain, dec_ffn_gain, dec_bias_grad.reshape(-1)]
            ),
        ]
    )
    small_total = lax.psum(small_grads, ("section", "wide", "rows"))
    small_own = jnp.where(core == 1, small_total[1], small_total[0])

    attn_share = plain_to_section(enc_attn_share, dec_attn_share, core)
    ffn_share = plain_to_section(enc_ffn_share, dec_ffn_share, core)
    in_width = 2 * FF // rows // wide
    ffn_in_grad = (
        ffn_share[:, :, :in_width]
        .reshape(wide, depth, 2, unit)
        .transpose(1, 2, 0, 3)
        .reshape(depth, 2 * FF // rows)
    )
    ffn_out_grad = ffn_share[:, :, in_width:].transpose(0, 2, 1).reshape(FF // rows, depth)
    widths = [3 * HD // rows, HD // rows, HD // rows]
    edges = np.cumsum([0] + widths + [HD // rows])
    win, wout, cin, cout = [attn_share[:, a:b] for a, b in zip(edges[:-1], edges[1:])]

    half = D // 2

    def by_half(own):
        halves = jnp.stack([own[:, :half], own[:, half:]])
        keep = lax.dynamic_index_in_dim(halves, core, 0, keepdims=False)
        send = lax.dynamic_index_in_dim(halves, 1 - core, 0, keepdims=False)
        got = xor_permute(send, "section", 1)
        is_dec = core == 1
        return jnp.stack([jnp.where(is_dec, got, keep), jnp.where(is_dec, keep, got)])[:, None]

    return (
        by_half(to_low(y3)),
        by_half(grad_x),
        by_half(grad_y),
        small_own[: 3 * D].reshape(1, 3, D),
        small_own[3 * D :].reshape(1, NB, H),
        win[None],
        wout.T[None],
        ffn_in_grad[None],
        ffn_out_grad[None],
        cin[None],
        cout[None],
    )


def shards(
    enc_embed,
    dec_embed,
    out_cot,
    enc_lengths,
    dec_lengths,
    norm_gains,
    rel_bias,
    attn_in,
    attn_out,
    ffn_in,
    ffn_out,
    cross_in,
    cross_out,
):
    wide, rows = lax.axis_size("wide"), lax.axis_size("rows")
    lines = [
        jnp.pad(
            lax.dot_general(
                rel_bias[0], distance_hot(length, both, 0), (((0,), (0,)), ((), ())), precision=HIGHEST
            ),
            ((0, 2), (0, 0)),
        )
        for length, both in ((LE, True), (LD, False))
    ]
    enc_attn, dec_half, gains, biases, enc_blocks, dec_blocks = start_weights(
        wide, rows, attn_in, attn_out, cross_in, cross_out, ffn_in, ffn_out, norm_gains[0], lines
    )
    enc_lengths, dec_lengths = enc_lengths[:, 0], dec_lengths[:, 0]
    x1, enc_self, moved = self_forward(
        False,
        jnp.swapaxes(enc_embed[:, 0], 1, 2),
        gains[0],
        enc_attn,
        biases[0],
        enc_lengths,
        tuple(enc_blocks[1:]),
        tuple(dec_blocks[1:]),
    )
    enc_pieces, dec_pieces = moved[: wide - 1], moved[wide - 1 :]
    x2, *enc_ffn = ffn_forward_call(
        wide, x1, (gains[0], 1), [enc_blocks[0], *enc_pieces], 2, (dec_half, *dec_pieces)
    )
    enc_ffn, dec_attn, dec_pieces = enc_ffn[:4], enc_ffn[4], [dec_blocks[0], *dec_pieces, *enc_ffn[5:]]
    y1, dec_self, _ = self_forward(
        True, dec_embed[:, 0], gains[1], dec_attn, biases[1], dec_lengths
    )
    y2, cross_kept = cross_forward(
        x2, gains[0], enc_attn, y1, gains[1], dec_attn, dec_lengths, enc_lengths
    )
    cot_row = lax.dynamic_index_in_dim(out_cot[:, 0], lax.axis_index("section"), 0, keepdims=False)
    y3, g2, dec_ffn_gain, *dec_ffn_grads = ffn_both_call(
        wide, rows, y2, cot_row, (gains[1], 2), dec_pieces, 3
    )
    grad_x2, g1, enc_final_gain, dec_cross_gain, cross_grads = cross_backward(
        g2, x2, gains[0], enc_attn, y1, gains[1], dec_attn, cross_kept
    )
    grad_x1, enc_ffn_gain, enc_in, enc_out, *dec_sums = ffn_backward_call(
        wide, rows, grad_x2, x1, (gains[0], 1), enc_ffn, 5, dec_ffn_grads
    )
    attn_parts, ffn_parts, small_own, dec_out, enc_grad, dec_grad = last_step(
        wide,
        rows,
        cross_grads,
        dec_sums,
        (enc_in, enc_out),
        y3,
        dec_attn,
        enc_attn,
        (g1, dec_self[0], gains[1], *dec_self[1:]),
        (grad_x1, enc_self[0], gains[0], *enc_self[1:]),
        (enc_ffn_gain, enc_final_gain, dec_cross_gain, dec_ffn_gain),
    )
    ffn_in_grad, ffn_out_grad, gain_grad, bias_grad, win, wout, cin, cout = assemble(
        rows, ffn_parts, attn_parts, small_own
    )
    return (
        dec_out[:, None],
        jnp.swapaxes(enc_grad, 1, 2)[:, None],
        dec_grad[:, None],
        gain_grad.transpose(1, 0, 2),
        bias_grad.transpose(1, 2, 0),
        jnp.swapaxes(win, 1, 2),
        wout,
        ffn_in_grad,
        jnp.swapaxes(ffn_out_grad, 1, 2),
        jnp.swapaxes(cin, 1, 2),
        jnp.swapaxes(cout, 1, 2),
    )


def solution(mesh):
    placed = (
        P(None, ("wide", "rows"), None, None),
        P(None, ("wide", "rows"), None, None),
        P(None, ("wide", "rows"), None, None),
        P(None, ("wide", "rows"), None),
        P(None, ("wide", "rows"), None),
        P("section", None, None),
        P("section", None, None),
        P("section", "wide", None),
        P("section", None, "wide"),
        P("section", "wide", None),
        P("section", None, "wide"),
        P("section", "wide", None),
        P("section", "wide", None),
    )
    wide, rows = mesh.shape["wide"], mesh.shape["rows"]
    in_tiles = D // wide % 16 == 0 and FF // (wide * rows) % 32 == 0
    return jax.shard_map(
        shards if wide == 4 and rows == 4 and in_tiles else plain_shards,
        mesh=mesh,
        in_specs=placed,
        out_specs=(
            P(None, ("wide", "rows"), None, "section"),
            P(None, ("wide", "rows"), None, "section"),
            P(None, ("wide", "rows"), None, "section"),
            P("section", None, None),
            P("section", None, None),
            P("section", "wide", "rows"),
            P("section", "rows", "wide"),
            P("section", "wide", "rows"),
            P("section", "rows", "wide"),
            P("section", "wide", "rows"),
            P("section", "wide", "rows"),
        ),
        check_vma=False,
    )
```

```python
import jax
import jax.numpy as jnp
import numpy as np
from jax import lax
from jax.experimental import pallas as pl
from jax.experimental.pallas import tpu as pltpu
from jax.sharding import PartitionSpec as P

D = 1472
H = 6
DH = 64
FF = 3584
NB = 32
MAXDIST = 128
MB = 2
LE = 256
LD = 64
HD = 384


EPSILON = 1e-06
NEGATIVE = -1000000000.0
HIGHEST = lax.Precision.HIGHEST


def bucket_table(length, both_ways):
    positions = np.arange(length)
    offsets = positions[None, :] - positions[:, None]
    buckets = NB
    result = np.zeros(offsets.shape, np.int64)
    if both_ways:
        buckets = buckets // 2
        result = result + (offsets > 0) * buckets
        distance = np.abs(offsets)
    else:
        distance = np.maximum(-offsets, 0)
    exact_count = buckets // 2
    log_ratio = np.log(np.maximum(distance, 1) / exact_count) / np.log(MAXDIST / exact_count)
    far_bucket = np.minimum(
        exact_count + np.floor(log_ratio * (buckets - exact_count)).astype(np.int64), buckets - 1
    )
    return result + np.where(distance < exact_count, distance, far_bucket)


def one_hot(length, both_ways):
    bucket_ids = jnp.asarray(bucket_table(length, both_ways), jnp.int32)
    return (bucket_ids[:, :, None] == jnp.arange(NB, dtype=jnp.int32)[None, None, :]).astype(
        jnp.float32
    )


def item_ids(lengths, length):
    item_ends = jnp.cumsum(lengths)
    positions = jnp.arange(length, dtype=jnp.int32)
    return jnp.sum((positions[:, None] >= item_ends[None, :-1]).astype(jnp.int32), axis=1)


def rms_norm(residual, gain_row):
    return (
        residual
        * lax.rsqrt(jnp.mean(residual * residual, axis=-1, keepdims=True) + EPSILON)
        * gain_row
    )


def matmul(left_side, right_side):
    return jnp.dot(left_side, right_side, preferred_element_type=jnp.float32)


def matmul_exact(left_side, right_side):
    return jnp.dot(left_side, right_side, precision=HIGHEST)


def to_low(tensor):
    return tensor.astype(jnp.bfloat16)


def gated(gate_part, up_part):
    return jax.nn.gelu(gate_part, approximate=True) * up_part


def attend_forward(queries, key_rows, value_rows, bias_full, allowed):
    query_count = queries.shape[0]
    heads_q = queries.reshape(query_count, H, DH)
    heads_k = key_rows.reshape(key_rows.shape[0], H, DH)
    heads_v = value_rows.reshape(value_rows.shape[0], H, DH)
    scores = (
        jnp.einsum("qhd,khd->hqk", heads_q, heads_k, preferred_element_type=jnp.float32) + bias_full
    )
    scores = jnp.where(allowed[None], scores, NEGATIVE)
    shifted = jnp.exp(scores - jnp.max(scores, axis=-1, keepdims=True))
    weights = shifted / jnp.sum(shifted, axis=-1, keepdims=True)
    low_weights = to_low(weights)
    context = jnp.einsum("hqk,khd->qhd", low_weights, heads_v, preferred_element_type=jnp.float32)
    return (to_low(context.reshape(query_count, H * DH)), weights, low_weights)


def attend_backward(queries, key_rows, value_rows, weights, low_weights, grad_context):
    query_count = queries.shape[0]
    key_count = key_rows.shape[0]
    heads_q = queries.reshape(query_count, H, DH)
    heads_k = key_rows.reshape(key_count, H, DH)
    heads_v = value_rows.reshape(key_count, H, DH)
    grad_heads = grad_context.reshape(query_count, H, DH)
    grad_weights = jnp.einsum(
        "qhd,khd->hqk", grad_heads, heads_v, preferred_element_type=jnp.float32
    )
    grad_values = jnp.einsum(
        "hqk,qhd->khd", low_weights, grad_heads, preferred_element_type=jnp.float32
    )
    grad_scores = weights * (grad_weights - jnp.sum(grad_weights * weights, axis=-1, keepdims=True))
    low_scores = to_low(grad_scores)
    grad_queries = jnp.einsum(
        "hqk,khd->qhd", low_scores, heads_k, preferred_element_type=jnp.float32
    )
    grad_keys = jnp.einsum("hqk,qhd->khd", low_scores, heads_q, preferred_element_type=jnp.float32)
    return (
        grad_queries.reshape(query_count, H * DH),
        grad_keys.reshape(key_count, H * DH),
        grad_values.reshape(key_count, H * DH),
        low_scores,
    )


def xor_permute(value, axis, distance):
    count = lax.axis_size(axis)
    return lax.ppermute(value, axis, [(i, i ^ distance) for i in range(count)])


def gather_wide(block):
    count = lax.axis_size("wide")
    if count != 4:
        return [block] + [xor_permute(block, "wide", v) for v in range(1, count)]
    half = block.shape[0] // 2
    first = xor_permute(block, "wide", 1)
    second = xor_permute(block, "wide", 2)
    third = jnp.concatenate(
        [xor_permute(first[:half], "wide", 2), xor_permute(second[half:], "wide", 1)], axis=0
    )
    return [block, first, second, third]


def scatter_wide(parts):
    count = lax.axis_size("wide")
    total = parts[0]
    if count != 4:
        for v in range(1, count):
            total = total + xor_permute(to_low(parts[v]), "wide", v).astype(jnp.float32)
        return total
    half = total.shape[0] // 2
    via_first = xor_permute(to_low(parts[3][:half]), "wide", 1).astype(jnp.float32)
    via_second = xor_permute(to_low(parts[3][half:]), "wide", 2).astype(jnp.float32)
    to_first = jnp.concatenate([parts[1][:half], parts[1][half:] + via_second], axis=0)
    to_second = jnp.concatenate([parts[2][:half] + via_first, parts[2][half:]], axis=0)
    total = total + xor_permute(to_low(to_first), "wide", 1).astype(jnp.float32)
    return total + xor_permute(to_low(to_second), "wide", 2).astype(jnp.float32)


def placed_rows(pieces, place):
    rows = pieces[0].shape[0]
    buffer = jnp.zeros((rows * len(pieces),) + pieces[0].shape[1:], pieces[0].dtype)
    for v, piece in enumerate(pieces):
        start = (place ^ v) * rows
        buffer = lax.dynamic_update_slice(buffer, piece, (start,) + (0,) * (piece.ndim - 1))
    return buffer


MESH = pl.DeviceIdType.MESH
HBM = pl.BlockSpec(memory_space=pl.ANY)
VM = pl.BlockSpec(memory_space=pltpu.VMEM)
SM = pl.BlockSpec(memory_space=pltpu.SMEM)
TILE = 128
VMEM_LIMIT = 62 * 1024 * 1024


def peers_of(count):
    place, core = lax.axis_index("wide"), lax.axis_index("section")
    return [{"wide": place ^ v} for v in range(1, count)] + [{"section": 1 - core}]


def greet(peers):
    barrier = pltpu.get_barrier_semaphore()
    for peer in peers:
        pl.semaphore_signal(barrier, inc=1, device_id=peer, device_id_type=MESH)
    pl.semaphore_wait(barrier, len(peers))


def remote(source, target, sems, index, peer):
    return pltpu.make_async_remote_copy(
        src_ref=source,
        dst_ref=target,
        send_sem=sems[0].at[index],
        recv_sem=sems[1].at[index],
        device_id=peer,
        device_id_type=MESH,
    )


def nt(left, right):
    return lax.dot_general(left, right, (((1,), (1,)), ((), ())), preferred_element_type=jnp.float32)


def tn(left, right):
    return lax.dot_general(left, right, (((0,), (0,)), ((), ())), preferred_element_type=jnp.float32)


class GatherPlane:
    def __init__(self, blocks, sems, base, peers, rows):
        half = split_at(rows)
        rest = rows - half
        first, second = peers[0], peers[1]
        self.direct = [
            remote(blocks.at[0], blocks.at[1], sems, base, first),
            remote(blocks.at[0], blocks.at[2], sems, base + 1, second),
        ]
        self.passed = [
            remote(
                blocks.at[1, pl.ds(0, half)], blocks.at[3, pl.ds(0, half)], sems, base + 2, second
            ),
            remote(
                blocks.at[2, pl.ds(half, rest)],
                blocks.at[3, pl.ds(half, rest)],
                sems,
                base + 3,
                first,
            ),
        ]

    def start(self):
        for copy in self.direct:
            copy.start()

    def arrive(self, index):
        if index < 2:
            self.direct[index].wait_recv()
            self.passed[index].start()
        else:
            for copy in self.passed:
                copy.wait_recv()

    def finish(self):
        for copy in self.direct + self.passed:
            copy.wait_send()


class ScatterPlane:
    def __init__(self, parts, landing, sems, base, peers, rows):
        half = split_at(rows)
        first, second = peers[0], peers[1]
        low, high = pl.ds(0, half), pl.ds(half, rows - half)
        self.parts, self.landing, self.low, self.high = parts, landing, low, high
        self.far = [
            remote(parts.at[3, low], landing.at[0, low], sems, base, first),
            remote(parts.at[3, high], landing.at[0, high], sems, base + 1, second),
        ]
        self.early = [
            remote(parts.at[1, low], landing.at[1, low], sems, base + 2, first),
            remote(parts.at[2, high], landing.at[2, high], sems, base + 3, second),
        ]
        self.late = [
            remote(parts.at[1, high], landing.at[1, high], sems, base + 4, first),
            remote(parts.at[2, low], landing.at[2, low], sems, base + 5, second),
        ]

    def send_early(self, index):
        self.early[index].start()

    def send_far(self):
        for copy in self.far:
            copy.start()

    def pass_on(self):
        low, high = self.low, self.high
        self.far[0].wait_recv()
        self.parts[2, low] = (
            self.parts[2, low].astype(jnp.float32) + self.landing[0, low].astype(jnp.float32)
        ).astype(jnp.bfloat16)
        self.late[1].start()
        self.far[1].wait_recv()
        self.parts[1, high] = (
            self.parts[1, high].astype(jnp.float32) + self.landing[0, high].astype(jnp.float32)
        ).astype(jnp.bfloat16)
        self.late[0].start()

    def total(self):
        for copy in self.early + self.late:
            copy.wait_recv()
        return self.landing[1].astype(jnp.float32) + self.landing[2].astype(jnp.float32)

    def finish(self):
        for copy in self.far + self.early + self.late:
            copy.wait_send()


def rms_rows(residual):
    return lax.rsqrt(jnp.mean(residual * residual, axis=-1, keepdims=True) + EPSILON)


def norm_pull(residual, gain_row, grad_normed):
    scale = rms_rows(residual)
    unit = residual * scale
    inner = grad_normed * gain_row
    grad_residual = scale * (inner - unit * jnp.mean(inner * unit, axis=-1, keepdims=True))
    return grad_residual, jnp.sum(grad_normed * unit, axis=0, keepdims=True)


def token_rows_at_once(wide, rows):
    return rows if rows >= 2 * TILE else wide * rows


def block_at(blocks, group, count):
    if count == blocks.shape[1]:
        return blocks[group]
    return blocks[...].reshape(count, blocks.shape[2])


def before_group(gather, group, groups):
    if groups == 1:
        for index in range(3):
            gather.arrive(index)
        return
    for index in range(3):

        @pl.when(group == index + 1)
        def _():
            gather.arrive(index)


def put_parts(acc, parts, own_ref, group, groups, rows):
    if groups == 1:
        own_ref[...] = acc[pl.ds(0, rows)]
        for v in range(1, parts.shape[0]):
            parts[v] = acc[pl.ds(v * rows, rows)].astype(parts.dtype)
        return

    @pl.when(group == 0)
    def _():
        own_ref[...] = acc[...]

    @pl.when(group > 0)
    def _():
        parts[group] = acc[...].astype(parts.dtype)


def after_group(scatter, group, groups):
    if groups == 1:
        scatter.send_far()
        scatter.send_early(0)
        scatter.send_early(1)
        return

    @pl.when(group == 1)
    def _():
        scatter.send_early(0)

    @pl.when(group == 2)
    def _():
        scatter.send_early(1)

    @pl.when(group == 3)
    def _():
        scatter.send_far()


class Reshard:
    def __init__(self, blocks, pieces, direct, sems, base, peers):
        row = lax.axis_index("rows")
        shared = (blocks[0].shape[0] - direct) // 2
        mine = pl.ds(direct + row % 2 * shared, shared)
        other = {"rows": row ^ 1}
        self.shared, self.direct, self.passed = [], [], []
        for v, (block, piece) in enumerate(zip(blocks, pieces)):
            at, peer, first = base + 3 * v, peers[v], pl.ds(0, direct)
            self.shared.append(remote(block.at[mine], piece.at[mine], sems, at, peer))
            self.passed.append(remote(piece.at[mine], piece.at[mine], sems, at + 1, other))
            if direct:
                self.direct.append(remote(block.at[first], piece.at[first], sems, at + 2, peer))

    def start(self):
        for copy in self.shared:
            copy.start()

    def pass_on(self):
        for copy in self.direct:
            copy.start()
        for copy, after in zip(self.shared, self.passed):
            copy.wait_recv()
            after.start()

    def finish(self):
        for copy in self.direct + self.passed:
            copy.wait()
        for copy in self.shared:
            copy.wait_send()


class ReduceRows:
    def __init__(self, source_in, source_out, in_buf, in_land, out_buf, out_land, sems, base, local_sem, local_base):
        row = lax.axis_index("rows")
        near, far = {"rows": row ^ 1}, {"rows": row ^ 2}
        self.bufs, self.lands, self.first, self.second = [], [], [], []
        views = [
            (lambda ref, i, part=part: ref.at[i, part], source_in, in_buf, in_land)
            for part in range(2)
        ] + [(lambda ref, i: ref.at[i], source_out, out_buf, out_land)]
        for index, (view, source, buf, land) in enumerate(views):
            at = base + 3 * index
            self.first.append(
                [
                    remote(view(source, row ^ 1), view(land, 0), sems, at, near),
                    remote(view(source, row ^ 3), view(land, 1), sems, at + 1, near),
                ]
            )
            self.second.append(remote(view(buf, 1), view(land, 2), sems, at + 2, far))
            self.bufs.append([view(buf, 0), view(buf, 1)])
            self.lands.append([view(land, i) for i in range(3)])
        self.loads = [
            pltpu.make_async_copy(source.at[place], buf.at[i], local_sem.at[local_base + 2 * j + i])
            for j, (source, buf) in enumerate(((source_in, in_buf), (source_out, out_buf)))
            for i, place in enumerate((row, row ^ 2))
        ]

    def start(self):
        for copy in self.first[0]:
            copy.start()
        for load in self.loads:
            load.start()

    def loaded(self):
        for load in self.loads:
            load.wait()

    def add(self, index, which, land):
        ref = self.bufs[index][which]
        ref[...] = (
            ref[...].astype(jnp.float32) + self.lands[index][land][...].astype(jnp.float32)
        ).astype(jnp.bfloat16)

    def turn(self, index):
        for copy in self.first[index]:
            copy.wait_recv()
        for copy in self.first[index + 1] if index < 2 else ():
            copy.start()
        self.add(index, 1, 1)
        self.second[index].start()
        self.add(index, 0, 0)

    def close(self, index):
        self.second[index].wait_recv()
        self.add(index, 0, 2)

    def finish(self):
        for pair, copy in zip(self.first, self.second):
            for each in pair:
                each.wait_send()
            copy.wait_send()


def reduce_rows_scratch(units):
    low = jnp.bfloat16
    return [
        pltpu.VMEM((2, 2, D, TILE), low),
        pltpu.VMEM((3, 2, D, TILE), low),
        pltpu.VMEM((2, units, D), low),
        pltpu.VMEM((3, units, D), low),
    ]


def weight_tiles(weight, half, part):
    lanes = pl.ds(part * TILE, TILE)
    return jnp.concatenate(
        [weight[half, quarter, :, lanes] for quarter in range(weight.shape[1])], axis=1
    )


def weight_copies(pieces, weight, sems, base, local_sem, local_base, sibling):
    core, place = lax.axis_index("section"), lax.axis_index("wide")
    wide, depth = lax.axis_size("wide"), pieces[0].shape[1]
    loads, swaps = [], []
    for index, piece in enumerate(pieces):
        v = index if index < wide else index - wide + 1
        place_rows = pl.ds(pl.multiple_of((place ^ v) * depth, 16), depth)
        target = weight.at[core, :, place_rows]
        quarters = piece.shape[0]
        if quarters < weight.shape[1]:
            part = lax.axis_index("rows") % 2
            part = part if index < wide else 1 - part
            target = weight.at[core, pl.ds(part * quarters, quarters), place_rows]
        loads.append(pltpu.make_async_copy(piece, target, local_sem.at[local_base + index]))
        swaps.append(remote(piece, target, sems, base + index, sibling))
    return loads, swaps


def gate_slopes(gate, up):
    square = gate * gate
    tanh = jnp.tanh(GELU_A * gate * (1.0 + GELU_B * square))
    upper = 0.5 * (1.0 + tanh)
    slope = upper + 0.5 * gate * (1.0 - tanh * tanh) * (GELU_A + 3.0 * GELU_A * GELU_B * square)
    return gate * upper, slope


def ffn_forward_kernel(wide, carried, count, gain_at, x_ref, gain_ref, *refs):
    gain_ref = gain_ref.at[pl.ds(gain_at, 1)]
    pieces, refs = refs[:count], refs[count:]
    if carried:
        dec_half, dec_blocks, refs = refs[0], refs[1:wide], refs[wide:]
    y_ref, at_out, pre_out, hidden_out, weight_out = refs[:5]
    refs = refs[5:]
    if carried:
        dec_attn, dec_pieces, refs = refs[0], refs[1:wide], refs[wide:]
    blocks, at, pre, hidden, weight, parts, landing, acc, send_sem, recv_sem, local_sem = refs[:11]
    rows = x_ref.shape[0]
    depth = pieces[0].shape[1]
    span = weight.shape[1] * TILE
    core, place = lax.axis_index("section"), lax.axis_index("wide")
    peers = peers_of(wide)
    sems = (send_sem, recv_sem)
    greet(peers + ([{"rows": lax.axis_index("rows") ^ 1}] if carried else []))
    residual = x_ref[...]
    blocks[0] = (residual * rms_rows(residual) * gain_ref[...]).astype(jnp.bfloat16)
    gather = GatherPlane(blocks, sems, 0, peers, rows)
    gather.start()
    loads, swaps = weight_copies(pieces, weight, sems, 10, local_sem, 12, peers[-1])
    for load, swap in zip(loads, swaps):
        load.start()
        swap.start()
    scatter = ScatterPlane(parts, landing, sems, 4, peers, rows)
    if carried:
        held, far_held, whole = refs[11:14]
        other = {"rows": lax.axis_index("rows") ^ 1}
        passed = [
            remote(block, piece, sems, 24 + v, other)
            for v, (block, piece) in enumerate(zip(dec_blocks, dec_pieces))
        ]
        for copy in passed:
            copy.start()
        size = held.shape[1]
        rest = depth - size
        part = lax.axis_index("rows") % 2
        dec_gather = GatherPlane(held, sems, 27, peers, size)
        mine = pl.ds(pl.multiple_of(part * rest, 16), size)
        fetch = pltpu.make_async_copy(dec_half.at[mine], held.at[0], local_sem.at[7])
        fetch.start()
        stores, gives, crossings = [], [], []

        def place_block(source, v, start, index):
            target = dec_attn.at[
                core, pl.ds(pl.multiple_of((place ^ v) * depth + start, 16), source.shape[0])
            ]
            stores.append(pltpu.make_async_copy(source, target, local_sem.at[19 + index]))
            gives.append(remote(source, target, sems, 35 + index, peers[-1]))

        place_block(whole, 0, 0, 0)
        for v in range(1, wide):
            place_block(held.at[v], v, part * rest, v)
        for v in range(1, wide):
            sent = pl.ds(pl.multiple_of(part * (size - rest), 16), rest)
            crossings.append(remote(held.at[v, sent], far_held.at[v - 1], sems, 41 + v, other))
            place_block(far_held.at[v - 1], v, (1 - part) * size, wide + v - 1)
        whole_fetch = pltpu.make_async_copy(dec_half, whole, local_sem.at[8])
        whole_fetch.start()
    count = token_rows_at_once(wide, rows)
    groups = wide * rows // count

    @pl.loop(0, groups)
    def _(group):
        before_group(gather, group, groups)

        @pl.when(group == 0)
        def _():
            for load in loads:
                load.wait()

        token_rows = pl.ds(pl.multiple_of(group * count, count), count)

        @pl.loop(0, 2)
        def _(step):
            @pl.when((group == 0) & (step == 1))
            def _():
                for swap in swaps:
                    swap.wait_recv()

            half = lax.rem(core + step, 2)
            block = block_at(blocks, group, count)
            gate = matmul(block, weight_tiles(weight, half, 0))
            up = matmul(block, weight_tiles(weight, half, 1))
            pre[half, token_rows, pl.ds(0, span)] = gate.astype(jnp.bfloat16)
            pre[half, token_rows, pl.ds(span, span)] = up.astype(jnp.bfloat16)
            low = gated(gate, up).astype(jnp.bfloat16)
            hidden[half, token_rows, :] = low
            out = nt(low, weight_tiles(weight, half, 2))
            acc[...] = jnp.where(step == 0, 0.0, acc[...]) + out

        put_parts(acc, parts, y_ref, group, groups, rows)
        after_group(scatter, group, groups)
        if carried:

            @pl.when(group == 0)
            def _():
                whole_fetch.wait()
                stores[0].start()
                gives[0].start()

            @pl.when(group == 1)
            def _():
                fetch.wait()
                dec_gather.start()

    y_ref[...] += residual
    copies = [
        pltpu.make_async_copy(pre, pre_out, local_sem.at[4]),
        pltpu.make_async_copy(weight, weight_out, local_sem.at[5]),
    ]
    for copy in copies:
        copy.start()
    if carried:
        for v in range(1, 3):
            dec_gather.arrive(v - 1)
            crossings[v - 1].start()
            stores[v].start()
            gives[v].start()
    scatter.pass_on()

    @pl.loop(0, groups)
    def _(group):
        lanes = pl.ds(pl.multiple_of(group * count, count), count)
        at[:, lanes] = block_at(blocks, group, count).T

    last = pltpu.make_async_copy(at, at_out, local_sem.at[6])
    last.start()
    copies.append(last)
    if carried:
        dec_gather.arrive(2)
        crossings[2].start()
        stores[3].start()
        gives[3].start()

    @pl.loop(0, 2 * groups)
    def _(step):
        half, group = lax.rem(step, 2), step // 2
        lanes = pl.ds(pl.multiple_of(group * count, count), count)
        hidden_out[half, :, lanes] = hidden[half, lanes, :].T

    y_ref[...] += scatter.total()
    if carried:
        for v in range(1, wide):
            crossings[v - 1].wait()
            stores[wide + v - 1].start()
            gives[wide + v - 1].start()
        for store, give in zip(stores, gives):
            store.wait()
            give.wait()
        dec_gather.finish()
        for copy in passed:
            copy.wait()
    for copy in copies:
        copy.wait()
    gather.finish()
    scatter.finish()
    for swap in swaps:
        swap.wait_send()


def ffn_forward_call(wide, residual, gain_row, pieces, call_id, carried=()):
    gain_row, gain_at = gain_row
    rows = residual.shape[0]
    total = rows * wide
    quarters, _, columns = pieces[0].shape
    span = quarters * TILE
    low = jnp.bfloat16
    extra_out, extra_scratch = [], []
    if carried:
        depth, attn_columns = carried[0].shape
        extra_out = [jax.ShapeDtypeStruct((2, D, attn_columns), low)] + [
            jax.ShapeDtypeStruct(each.shape, low) for each in carried[1:]
        ]
        size = split_at(depth)
        extra_scratch = [
            pltpu.VMEM((wide, size, attn_columns), low),
            pltpu.VMEM((wide - 1, depth - size, attn_columns), low),
            pltpu.VMEM((depth, attn_columns), low),
        ]
    return pl.pallas_call(
        lambda *refs: ffn_forward_kernel(wide, bool(carried), len(pieces), gain_at, *refs),
        out_shape=[
            jax.ShapeDtypeStruct((rows, D), jnp.float32),
            jax.ShapeDtypeStruct((D, total), low),
            jax.ShapeDtypeStruct((2, total, 2 * span), low),
            jax.ShapeDtypeStruct((2, span, total), low),
            jax.ShapeDtypeStruct((2, quarters, D, columns), low),
        ]
        + extra_out,
        in_specs=[VM, VM] + [HBM] * (len(pieces) + len(carried)),
        out_specs=[VM, HBM, HBM, VM, HBM] + [HBM] * len(extra_out),
        scratch_shapes=[
            pltpu.VMEM((wide, rows, D), low),
            pltpu.VMEM((D, total), low),
            pltpu.VMEM((2, total, 2 * span), low),
            pltpu.VMEM((2, total, span), low),
            pltpu.VMEM((2, quarters, D, columns), low),
            pltpu.VMEM((wide, rows, D), low),
            pltpu.VMEM((3, rows, D), low),
            pltpu.VMEM((token_rows_at_once(wide, rows), D), jnp.float32),
            pltpu.SemaphoreType.DMA((45,)),
            pltpu.SemaphoreType.DMA((45,)),
            pltpu.SemaphoreType.DMA((26,)),
        ]
        + extra_scratch,
        compiler_params=pltpu.CompilerParams(
            collective_id=call_id, has_side_effects=True, vmem_limit_bytes=VMEM_LIMIT
        ),
        name="ffn_forward_%d" % rows,
    )(residual, gain_row, *pieces, *carried)


def ffn_backward_kernel(
    wide, rows_axis, gain_at, g_ref, x_ref, gain_ref, at_in, pre_in, hidden_in, weight_in, *refs
):
    gain_ref = gain_ref.at[pl.ds(gain_at, 1)]
    carried = len(refs) > 21
    if carried:
        ready_in, ready_out = refs[:2]
        refs = refs[2:]
    gx_ref, gain_out, grad_in, grad_out = refs[:4]
    refs = refs[4:]
    if carried:
        sum_in, sum_out = refs[:2]
        refs = refs[2:]
    (
        blocks,
        at,
        pre,
        hidden,
        weight,
        parts,
        landing,
        acc,
        give_in,
        give_out,
        got_in,
        got_out,
        send_sem,
        recv_sem,
        local_sem,
    ) = refs[:15]
    rows = x_ref.shape[0]
    span = weight.shape[1] * TILE
    units = FF // (wide * rows_axis * 2)
    core, row = lax.axis_index("section"), lax.axis_index("rows")
    peers = peers_of(wide)
    sems = (send_sem, recv_sem)
    greet(peers + ([{"rows": row ^ 1}, {"rows": row ^ 2}] if carried else []))
    loads = [
        pltpu.make_async_copy(weight_in, weight, local_sem.at[0]),
        pltpu.make_async_copy(pre_in, pre, local_sem.at[1]),
        pltpu.make_async_copy(hidden_in, hidden, local_sem.at[2]),
        pltpu.make_async_copy(at_in, at, local_sem.at[3]),
    ]
    blocks[0] = g_ref[...].astype(jnp.bfloat16)
    gather = GatherPlane(blocks, sems, 0, peers, rows)
    gather.start()
    for load in loads:
        load.start()
    if carried:
        line = ReduceRows(ready_in, ready_out, *refs[15:19], sems, 12, local_sem, 6)
        line.start()
    scatter = ScatterPlane(parts, landing, sems, 4, peers, rows)
    loads[0].wait()
    loads[1].wait()
    count = token_rows_at_once(wide, rows)
    groups = wide * rows // count

    @pl.loop(0, groups)
    def _(group):
        before_group(gather, group, groups)
        if carried:

            @pl.when(group == 1)
            def _():
                line.loaded()
                line.turn(0)

        token_rows = pl.ds(pl.multiple_of(group * count, count), count)

        @pl.loop(0, 2)
        def _(half):
            block = block_at(blocks, group, count)
            grad_hidden = matmul(block, weight_tiles(weight, half, 2))
            gate = pre[half, token_rows, pl.ds(0, span)].astype(jnp.float32)
            up = pre[half, token_rows, pl.ds(span, span)].astype(jnp.float32)
            value, slope = gate_slopes(gate, up)
            low_gate = (grad_hidden * up * slope).astype(jnp.bfloat16)
            low_up = (grad_hidden * value).astype(jnp.bfloat16)
            pre[half, token_rows, pl.ds(0, span)] = low_gate
            pre[half, token_rows, pl.ds(span, span)] = low_up
            out = nt(low_gate, weight_tiles(weight, half, 0)) + nt(
                low_up, weight_tiles(weight, half, 1)
            )
            acc[...] = jnp.where(half == 0, 0.0, acc[...]) + out

        put_parts(acc, parts, gx_ref, group, groups, rows)
        after_group(scatter, group, groups)
    if carried:
        line.turn(1)
    loads[2].wait()
    loads[3].wait()
    chunk = 2 * TILE
    swap_out = remote(give_out, got_out, sems, 11, peers[-1])
    swap_in = remote(give_in, got_in, sems, 10, peers[-1])
    store_in = pltpu.make_async_copy(got_in, grad_in, local_sem.at[4])
    store_out = pltpu.make_async_copy(got_out, grad_out, local_sem.at[5])

    @pl.loop(0, 2 * rows_axis)
    def _(step):
        half = jnp.where(step < rows_axis, 1 - core, core)
        index = lax.rem(step, rows_axis)
        columns = pl.ds(pl.multiple_of(index * chunk, chunk), chunk)
        total = matmul(at[...], pre[half, :, columns])

        @pl.when(step < rows_axis)
        def _():
            for part in range(2):
                give_in[index, part] = total[:, part * TILE : (part + 1) * TILE].astype(
                    jnp.bfloat16
                )

        @pl.when(step == rows_axis - 1)
        def _():
            swap_in.start()
            scatter.pass_on()

        @pl.when(step == rows_axis)
        def _():
            swap_in.wait_recv()

        @pl.when(step >= rows_axis)
        def _():
            for part in range(2):
                got_in[index, part] = (
                    total[:, part * TILE : (part + 1) * TILE]
                    + got_in[index, part].astype(jnp.float32)
                ).astype(jnp.bfloat16)

    store_in.start()
    if carried:
        line.turn(2)

    @pl.loop(0, 2)
    def _(step):
        half = lax.rem(core + 1 + step, 2)
        total = matmul(hidden[half], blocks[...].reshape(wide * rows, D))

        @pl.when(step == 0)
        def _():
            for index in range(rows_axis):
                give_out[index] = total[index * TILE : index * TILE + units].astype(jnp.bfloat16)
            swap_out.start()

        @pl.when(step == 1)
        def _():
            swap_out.wait_recv()
            for index in range(rows_axis):
                got_out[index] = (
                    total[index * TILE : index * TILE + units]
                    + got_out[index].astype(jnp.float32)
                ).astype(jnp.bfloat16)
            store_out.start()

    total = gx_ref[...] + scatter.total()
    grad_residual, grad_gain = norm_pull(x_ref[...], gain_ref[...], total)
    gx_ref[...] = g_ref[...].astype(jnp.float32) + grad_residual
    gain_out[...] = grad_gain
    if carried:
        for index in range(3):
            line.close(index)
        in_buf, out_buf = refs[15], refs[17]
        stores = [
            pltpu.make_async_copy(in_buf.at[0], sum_in, local_sem.at[6]),
            pltpu.make_async_copy(out_buf.at[0], sum_out, local_sem.at[7]),
        ]
        for store in stores:
            store.start()
        for store in stores:
            store.wait()
        line.finish()
    store_in.wait()
    store_out.wait()
    swap_in.wait_send()
    swap_out.wait_send()
    gather.finish()
    scatter.finish()


def ffn_both_kernel(wide, rows_axis, gain_at, x_ref, cot_ref, gain_ref, *refs):
    pieces, refs = refs[: 2 * wide - 1], refs[2 * wide - 1 :]
    gain_ref = gain_ref.at[pl.ds(gain_at, 1)]
    y_ref, gx_ref, gain_out, grad_in, grad_out = refs[:5]
    (
        blocks,
        cots,
        weight,
        pre,
        hidden,
        acc,
        grad_acc,
        parts,
        grad_parts,
        landing,
        grad_landing,
        give_in,
        give_out,
        got_in,
        got_out,
        send_sem,
        recv_sem,
        local_sem,
    ) = refs[5:]
    rows = x_ref.shape[0]
    total_rows = wide * rows
    span = weight.shape[1] * TILE
    units = FF // (wide * rows_axis * 2)
    core = lax.axis_index("section")
    peers = peers_of(wide)
    sems = (send_sem, recv_sem)
    low = jnp.bfloat16
    loads, swaps = weight_copies(pieces, weight, sems, 20, local_sem, 2, peers[-1])
    greet(peers)
    residual = x_ref[...]
    blocks[0] = (residual * rms_rows(residual) * gain_ref[...]).astype(low)
    cots[0] = cot_ref[core]
    gather = GatherPlane(blocks, sems, 0, peers, rows)
    cot_gather = GatherPlane(cots, sems, 4, peers, rows)
    gather.start()
    cot_gather.start()
    for load, swap in zip(loads, swaps):
        load.start()
        swap.start()
    for index in range(3):
        gather.arrive(index)
        cot_gather.arrive(index)
    for load in loads:
        load.wait()

    @pl.loop(0, 2)
    def _(step):
        @pl.when(step == 1)
        def _():
            for swap in swaps:
                swap.wait_recv()

        half = lax.rem(core + step, 2)
        block = blocks[...].reshape(total_rows, D)
        gate = matmul(block, weight_tiles(weight, half, 0))
        up = matmul(block, weight_tiles(weight, half, 1))
        value, slope = gate_slopes(gate, up)
        low_hidden = (value * up).astype(low)
        hidden[half] = low_hidden
        grad_hidden = matmul(cots[...].reshape(total_rows, D), weight_tiles(weight, half, 2))
        low_gate = (grad_hidden * up * slope).astype(low)
        low_up = (grad_hidden * value).astype(low)
        pre[half, :, pl.ds(0, span)] = low_gate
        pre[half, :, pl.ds(span, span)] = low_up
        grad = nt(low_gate, weight_tiles(weight, half, 0)) + nt(
            low_up, weight_tiles(weight, half, 1)
        )
        grad_acc[...] = jnp.where(step == 0, 0.0, grad_acc[...]) + grad
        out = nt(low_hidden, weight_tiles(weight, half, 2))
        acc[...] = jnp.where(step == 0, 0.0, acc[...]) + out

    grad_scatter = ScatterPlane(grad_parts, grad_landing, sems, 8, peers, rows)
    scatter = ScatterPlane(parts, landing, sems, 14, peers, rows)
    put_parts(grad_acc, grad_parts, gx_ref, 0, 1, rows)
    after_group(grad_scatter, 0, 1)
    put_parts(acc, parts, y_ref, 0, 1, rows)
    after_group(scatter, 0, 1)
    swap_in = remote(give_in, got_in, sems, 27, peers[-1])
    swap_out = remote(give_out, got_out, sems, 28, peers[-1])
    store_in = pltpu.make_async_copy(got_in, grad_in, local_sem.at[0])
    store_out = pltpu.make_async_copy(got_out, grad_out, local_sem.at[1])
    chunk = 2 * TILE

    @pl.loop(0, 2 * rows_axis)
    def _(step):
        half = jnp.where(step < rows_axis, 1 - core, core)
        index = lax.rem(step, rows_axis)
        columns = pl.ds(pl.multiple_of(index * chunk, chunk), chunk)
        total = tn(blocks[...].reshape(total_rows, D), pre[half, :, columns])

        @pl.when(step < rows_axis)
        def _():
            for part in range(2):
                give_in[index, part] = total[:, part * TILE : (part + 1) * TILE].astype(low)

        @pl.when(step == rows_axis - 1)
        def _():
            swap_in.start()
            grad_scatter.pass_on()
            scatter.pass_on()

        @pl.when(step == rows_axis)
        def _():
            swap_in.wait_recv()

        @pl.when(step >= rows_axis)
        def _():
            for part in range(2):
                got_in[index, part] = (
                    total[:, part * TILE : (part + 1) * TILE]
                    + got_in[index, part].astype(jnp.float32)
                ).astype(low)

    store_in.start()

    @pl.loop(0, 2)
    def _(step):
        half = lax.rem(core + 1 + step, 2)
        total = tn(hidden[half], cots[...].reshape(total_rows, D))

        @pl.when(step == 0)
        def _():
            for index in range(rows_axis):
                give_out[index] = total[index * TILE : index * TILE + units].astype(low)
            swap_out.start()

        @pl.when(step == 1)
        def _():
            swap_out.wait_recv()
            for index in range(rows_axis):
                got_out[index] = (
                    total[index * TILE : index * TILE + units]
                    + got_out[index].astype(jnp.float32)
                ).astype(low)
            store_out.start()

    grad_residual, gain_out[...] = norm_pull(
        x_ref[...], gain_ref[...], gx_ref[...] + grad_scatter.total()
    )
    gx_ref[...] = cot_ref[core].astype(jnp.float32) + grad_residual
    y_ref[...] = y_ref[...] + residual + scatter.total()
    store_in.wait()
    store_out.wait()
    swap_in.wait_send()
    swap_out.wait_send()
    for each in (gather, cot_gather, grad_scatter, scatter):
        each.finish()
    for swap in swaps:
        swap.wait_send()


def ffn_both_call(wide, rows_axis, residual, cot, gain_row, pieces, call_id):
    gain_row, gain_at = gain_row
    rows = residual.shape[0]
    total = wide * rows
    quarters, _, columns = pieces[0].shape
    span = quarters * TILE
    low = jnp.bfloat16
    units = FF // (wide * rows_axis * 2)
    share_in = (rows_axis, 2, D, TILE)
    share_out = (rows_axis, units, D)
    return pl.pallas_call(
        lambda *refs: ffn_both_kernel(wide, rows_axis, gain_at, *refs),
        out_shape=[
            jax.ShapeDtypeStruct((rows, D), jnp.float32),
            jax.ShapeDtypeStruct((rows, D), jnp.float32),
            jax.ShapeDtypeStruct((1, D), jnp.float32),
            jax.ShapeDtypeStruct(share_in, low),
            jax.ShapeDtypeStruct(share_out, low),
        ],
        in_specs=[VM, VM, VM] + [HBM] * len(pieces),
        out_specs=[VM, VM, VM, HBM, HBM],
        scratch_shapes=[
            pltpu.VMEM((wide, rows, D), low),
            pltpu.VMEM((wide, rows, D), low),
            pltpu.VMEM((2, quarters, D, columns), low),
            pltpu.VMEM((2, total, 2 * span), low),
            pltpu.VMEM((2, total, span), low),
            pltpu.VMEM((total, D), jnp.float32),
            pltpu.VMEM((total, D), jnp.float32),
            pltpu.VMEM((wide, rows, D), low),
            pltpu.VMEM((wide, rows, D), low),
            pltpu.VMEM((3, rows, D), low),
            pltpu.VMEM((3, rows, D), low),
            pltpu.VMEM(share_in, low),
            pltpu.VMEM(share_out, low),
            pltpu.VMEM(share_in, low),
            pltpu.VMEM(share_out, low),
            pltpu.SemaphoreType.DMA((29,)),
            pltpu.SemaphoreType.DMA((29,)),
            pltpu.SemaphoreType.DMA((9,)),
        ],
        compiler_params=pltpu.CompilerParams(
            collective_id=call_id, has_side_effects=True, vmem_limit_bytes=VMEM_LIMIT
        ),
        name="ffn_both_%d" % rows,
    )(residual, cot, gain_row, *pieces)


GELU_A = float(np.sqrt(2.0 / np.pi))
GELU_B = 0.044715


def ffn_backward_call(wide, rows_axis, grad, residual, gain_row, kept, call_id, carried=()):
    gain_row, gain_at = gain_row
    at, pre, hidden, weight = kept
    rows = residual.shape[0]
    low = jnp.bfloat16
    units = FF // (wide * rows_axis * 2)
    share_in = (rows_axis, 2, D, TILE)
    share_out = (rows_axis, units, D)
    sums = [jax.ShapeDtypeStruct(each.shape[1:], low) for each in carried]
    return pl.pallas_call(
        lambda *refs: ffn_backward_kernel(wide, rows_axis, gain_at, *refs),
        out_shape=[
            jax.ShapeDtypeStruct((rows, D), jnp.float32),
            jax.ShapeDtypeStruct((1, D), jnp.float32),
            jax.ShapeDtypeStruct(share_in, low),
            jax.ShapeDtypeStruct(share_out, low),
        ]
        + sums,
        in_specs=[VM, VM, VM, HBM, HBM, HBM, HBM] + [HBM] * len(sums),
        out_specs=[VM, VM, HBM, HBM] + [HBM] * len(sums),
        scratch_shapes=[
            pltpu.VMEM((wide, rows, D), low),
            pltpu.VMEM(at.shape, low),
            pltpu.VMEM(pre.shape, low),
            pltpu.VMEM(hidden.shape, low),
            pltpu.VMEM(weight.shape, low),
            pltpu.VMEM((wide, rows, D), low),
            pltpu.VMEM((3, rows, D), low),
            pltpu.VMEM((token_rows_at_once(wide, rows), D), jnp.float32),
            pltpu.VMEM(share_in, low),
            pltpu.VMEM(share_out, low),
            pltpu.VMEM(share_in, low),
            pltpu.VMEM(share_out, low),
            pltpu.SemaphoreType.DMA((21,)),
            pltpu.SemaphoreType.DMA((21,)),
            pltpu.SemaphoreType.DMA((10,)),
        ]
        + (reduce_rows_scratch(units) if carried else []),
        compiler_params=pltpu.CompilerParams(
            collective_id=call_id, has_side_effects=True, vmem_limit_bytes=VMEM_LIMIT
        ),
        name="ffn_backward_%d" % rows,
    )(grad, residual, gain_row, at, pre, hidden, weight, *carried)


def start_weights_kernel(
    wide, rows, win_in, wout_in, cin_in, cout_in, ffn_in, ffn_out, gains, biases, enc_hot, dec_hot,
    attn_ref, dec_half, enc_gains, dec_gains, enc_bias, dec_bias, *refs
):
    enc, dec = refs[:wide], refs[wide : 2 * wide]
    held, blocks, spare, in_ref, out_ref, ffn, enc_row, dec_row, send_sem, recv_sem, local_sem = refs[2 * wide :]
    core, place = lax.axis_index("section"), lax.axis_index("wide")
    peers = peers_of(wide)
    sibling = peers[-1]
    sems = (send_sem, recv_sem)
    depth = blocks.shape[1]
    big = [
        pltpu.make_async_copy(ffn_in.at[0], in_ref, local_sem.at[4]),
        pltpu.make_async_copy(ffn_out, out_ref, local_sem.at[5]),
    ]
    packs = [
        pltpu.make_async_copy(each, held.at[:, pl.ds(i * HD, HD)], local_sem.at[1 + i])
        for i, each in enumerate((wout_in, cin_in.at[0], cout_in.at[0]))
    ]
    for pack in packs:
        pack.start()
    greet(peers)
    for pack in packs:
        pack.wait()

    @pl.when(core == 0)
    def _():
        keep = pltpu.make_async_copy(win_in.at[0], blocks.at[0], local_sem.at[0])
        keep.start()
        give = remote(held, blocks.at[0], sems, 0, sibling)
        give.start()
        remote(win_in.at[0], spare, sems, 1, sibling).wait_recv()
        keep.wait()

    @pl.when(core == 1)
    def _():
        keep = pltpu.make_async_copy(held, spare, local_sem.at[0])
        keep.start()
        give = remote(win_in.at[0], spare, sems, 1, sibling)
        give.start()
        remote(held, blocks.at[0], sems, 0, sibling).wait_recv()
        keep.wait()

    gather = GatherPlane(blocks, sems, 2, peers, depth)
    gather.start()
    for load in big:
        load.start()
    dec_copy = pltpu.make_async_copy(spare, dec_half, local_sem.at[0])
    dec_copy.start()
    stores, gives = [], []
    for v in range(wide):
        rows_of = pl.ds(pl.multiple_of((place ^ v) * depth, 16), depth)
        stores.append(
            pltpu.make_async_copy(blocks.at[v], attn_ref.at[core, rows_of], local_sem.at[6 + v])
        )
        gives.append(remote(blocks.at[v], attn_ref.at[core, rows_of], sems, 6 + v, sibling))
    stores[0].start()
    gives[0].start()
    for load in big:
        load.wait()
    units = FF // (wide * rows * 2)
    per_row = FF // rows
    row_ids = lax.broadcasted_iota(jnp.int32, (2 * TILE, TILE), 0)
    lane_ids = lax.broadcasted_iota(jnp.int32, (2 * TILE, TILE), 1)
    def prepare(index):
        target, half = index // 2, index % 2
        offset = index * units
        start, shift = offset // TILE * TILE, offset % TILE
        picks = ((row_ids == lane_ids + shift) & (lane_ids < units)).astype(jnp.bfloat16)
        window = min(2 * TILE, per_row - start)
        picks = picks[:window]
        for part in range(3):
            for row in range(rows):
                if part < 2:
                    source = in_ref[:, pl.ds(part * FF + row * per_row + start, window)]
                else:
                    source = out_ref[:, pl.ds(row * per_row + start, window)]
                tile = matmul(source, picks)
                ffn[half, target ^ place, row, :, pl.ds(part * TILE, TILE)] = tile.astype(
                    jnp.bfloat16
                )

    lines = 10 + 2 * wide
    gain_moves = [remote(gains, target, sems, lines, sibling) for target in (enc_gains, dec_gains)]
    line_moves = [
        remote(row_ref, row_ref, sems, lines + 1, sibling) for row_ref in (enc_row, dec_row)
    ]
    for own, (gain_ref, row_ref, hot) in enumerate(
        ((enc_gains, enc_row, enc_hot), (dec_gains, dec_row, dec_hot))
    ):

        @pl.when(core == own)
        def _():
            gain_ref[...] = gains[...]
            row_ref[pl.ds(0, H), :] = jnp.dot(
                biases[...], hot[...], precision=HIGHEST, preferred_element_type=jnp.float32
            )
            gain_moves[own].start()
            line_moves[own].start()

    for index in range(2 * wide):
        prepare(index)
    for own in range(2):

        @pl.when(core == own)
        def _():
            gain_moves[1 - own].wait_recv()
            line_moves[1 - own].wait_recv()
            gain_moves[own].wait_send()
            line_moves[own].wait_send()

    bias_rows(enc_row, enc_bias)
    bias_rows(dec_row, dec_bias)

    def move(outs, base):
        for v in range(wide):
            pltpu.make_async_copy(ffn.at[core, v], outs[v], local_sem.at[10 + v]).start()
            remote(ffn.at[1 - core, v], outs[v], sems, base + v, sibling).start()

    def settle(outs, base):
        for v in range(wide):
            pltpu.make_async_copy(ffn.at[core, v], outs[v], local_sem.at[10 + v]).wait()
            remote(ffn.at[1 - core, v], outs[v], sems, base + v, sibling).wait_send()

    def receive(outs, base):
        for v in range(wide):
            remote(ffn.at[0, v], outs[v], sems, base + v, sibling).wait_recv()

    @pl.when(core == 0)
    def _():
        move(enc, 10)

    @pl.when(core == 1)
    def _():
        move(dec, 10 + wide)

    for v in range(1, wide):
        gather.arrive(v - 1)
        stores[v].start()
        gives[v].start()
    for v in range(wide):
        gives[v].wait_recv()
        stores[v].wait()
    dec_copy.wait()

    @pl.when(core == 0)
    def _():
        settle(enc, 10)
        receive(dec, 10 + wide)
        remote(held, blocks.at[0], sems, 0, sibling).wait_send()

    @pl.when(core == 1)
    def _():
        settle(dec, 10 + wide)
        receive(enc, 10)
        remote(win_in.at[0], spare, sems, 1, sibling).wait_send()

    gather.finish()
    for give in gives:
        give.wait_send()


def start_weights(wide, rows, attn_in, attn_out, cross_in, cross_out, ffn_in, ffn_out, gains, biases):
    depth = ffn_in.shape[1]
    low = jnp.bfloat16
    block = jax.ShapeDtypeStruct((rows, depth, 3 * TILE), low)
    part = (depth, 3 * HD)
    attn, dec_half, *outs = pl.pallas_call(
        lambda *refs: start_weights_kernel(wide, rows, *refs),
        out_shape=[
            jax.ShapeDtypeStruct((2, wide * depth, 3 * HD), low),
            jax.ShapeDtypeStruct(part, low),
            jax.ShapeDtypeStruct(gains.shape, jnp.float32),
            jax.ShapeDtypeStruct(gains.shape, jnp.float32),
            jax.ShapeDtypeStruct((H, LE, LE), jnp.float32),
            jax.ShapeDtypeStruct((H, LD, LD), jnp.float32),
        ]
        + [block] * (2 * wide),
        in_specs=[HBM] * 6 + [VM] * 4,
        out_specs=[HBM] * 2 + [VM] * 4 + [HBM] * (2 * wide),
        scratch_shapes=[
            pltpu.VMEM(part, low),
            pltpu.VMEM((wide,) + part, low),
            pltpu.VMEM(part, low),
            pltpu.VMEM(ffn_in.shape[1:], low),
            pltpu.VMEM((depth, FF), low),
            pltpu.VMEM((2, wide) + block.shape, low),
            pltpu.VMEM((8, 2 * LE), jnp.float32),
            pltpu.VMEM((8, 2 * LD), jnp.float32),
            pltpu.SemaphoreType.DMA((12 + 2 * wide,)),
            pltpu.SemaphoreType.DMA((12 + 2 * wide,)),
            pltpu.SemaphoreType.DMA((10 + wide,)),
        ],
        compiler_params=pltpu.CompilerParams(
            collective_id=1, has_side_effects=True, vmem_limit_bytes=VMEM_LIMIT
        ),
        name="start_weights",
    )(attn_in, attn_out[0].T, cross_in, cross_out, ffn_in, ffn_out[0].T, gains, biases, distance_hot(LE, True, 0), distance_hot(LD, False, 0))
    return attn, dec_half, outs[:2], outs[2:4], outs[4 : 4 + wide], outs[4 + wide :]


def split_at(rows):
    return (rows // 2 + 15) // 16 * 16


class ReduceWeights:
    def __init__(self, batch, bufs, sems, base, peers, others):
        self.own, self.land, self.plane, self.send, self.zland = bufs
        self.batch = batch
        core, place, row = lax.axis_index("section"), lax.axis_index("wide"), lax.axis_index("rows")
        wide, size = self.own.shape[:2]
        depth = batch.shape[0] // wide

        def rows_at(v, half):
            start = (place ^ v) * depth + half * (depth - size)
            return pl.ds(pl.multiple_of(start, 16), size)

        self.mine = [rows_at(v, core) for v in range(wide)]
        self.swaps = [
            remote(batch.at[rows_at(v, 1 - core)], self.land.at[v], sems, base + v, peers[-1])
            for v in range(wide)
        ]
        base += wide
        self.scatter = ScatterPlane(self.own, self.plane, sems, base, peers, size)
        base += 6
        chunk = batch.shape[1] // (len(others) + 1)

        def lanes(k):
            return pl.ds(pl.multiple_of((row ^ k) * chunk, TILE), chunk)

        self.kept, self.relayed = lanes(0), lanes(2)
        near, far = others[0], others[1]
        self.spreads = [
            remote(self.send.at[:, lanes(1)], self.zland.at[0], sems, base, near),
            remote(self.send.at[:, lanes(3)], self.zland.at[1], sems, base + 1, near),
            remote(self.send.at[:, lanes(2)], self.zland.at[2], sems, base + 2, far),
        ]

    def start(self):
        for v in (3, 1, 2, 0):
            self.swaps[v].start()

    def join(self):
        def add(v):
            self.swaps[v].wait_recv()
            own = self.batch[self.mine[v], :]
            self.own[v] = (own.astype(jnp.float32) + self.land[v].astype(jnp.float32)).astype(
                jnp.bfloat16
            )

        add(3)
        self.scatter.send_far()
        add(1)
        self.scatter.send_early(0)
        add(2)
        self.scatter.send_early(1)
        add(0)

    def given(self):
        for swap in self.swaps:
            swap.wait_send()

    def pass_on(self):
        self.scatter.pass_on()

    def spread(self):
        self.send[...] = (self.own[0].astype(jnp.float32) + self.scatter.total()).astype(
            jnp.bfloat16
        )
        self.spreads[0].start()
        self.spreads[1].start()

    def relay(self):
        self.spreads[1].wait_recv()
        self.send[:, self.relayed] = (
            self.send[:, self.relayed].astype(jnp.float32) + self.zland[1].astype(jnp.float32)
        ).astype(jnp.bfloat16)
        self.spreads[2].start()

    def total(self):
        out = self.send[:, self.kept].astype(jnp.float32)
        for index in (0, 2):
            self.spreads[index].wait_recv()
            out = out + self.zland[index].astype(jnp.float32)
        return out

    def finish(self):
        for copy in self.spreads:
            copy.wait_send()
        self.scatter.finish()


def reduce_weights_scratch(wide, rows, size, columns):
    low = jnp.bfloat16
    return [
        pltpu.VMEM((wide, size, columns), low),
        pltpu.VMEM((wide, size, columns), low),
        pltpu.VMEM((3, size, columns), low),
        pltpu.VMEM((size, columns), low),
        pltpu.VMEM((rows - 1, size, columns // rows), low),
    ]


def last_kernel(wide, rows, *refs):
    cross, refs = refs[:6], refs[6:]
    dec_in, dec_out, enc_in, enc_out, y_ref, dec_attn, enc_attn = refs[:7]
    dec_self, enc_self, gains = refs[7:14], refs[14:21], refs[21:25]
    out_ref, ffn_ref, small_out, y_half, x_half, t_half = refs[25:31]
    refs = refs[31:]
    batch_bufs = [refs[i * 5 : i * 5 + 5] for i in range(3)]
    line_bufs, refs = refs[15:19], refs[19:]
    held, win, wout, gx, gt, context_e, projected_e, context_d, projected_d = refs[:9]
    keep, give, ready, landing, small, small_land, small_plane, small_rows = refs[9:17]
    halves, (sums_ref, send_sem, recv_sem, local_sem) = refs[17:23], refs[23:]
    core, place, row = lax.axis_index("section"), lax.axis_index("wide"), lax.axis_index("rows")
    peers = peers_of(wide)
    sibling = peers[-1]
    crossed = [{"section": 1 - core, "wide": place ^ v} for v in range(1, wide)]
    others = [{"rows": row ^ k} for k in range(1, rows)]
    sems = (send_sem, recv_sem)
    depth = held.shape[0] // wide
    units = dec_out.shape[0]
    low = jnp.bfloat16
    straight = (
        lax.broadcasted_iota(jnp.int32, (units, TILE), 0)
        == lax.broadcasted_iota(jnp.int32, (units, TILE), 1)
    ).astype(low)

    def attn_loads(source):
        return [
            pltpu.make_async_copy(source.at[0], win, local_sem.at[0]),
            pltpu.make_async_copy(source.at[1, :, pl.ds(0, HD)], wout, local_sem.at[1]),
        ]

    for load in attn_loads(dec_attn):
        load.start()
    greet(peers + crossed + others)
    per_batch = wide + 6 + rows - 1
    batches = [
        ReduceWeights(held, bufs, sems, i * per_batch, peers, others)
        for i, bufs in enumerate(batch_bufs)
    ]
    base = 3 * per_batch
    line = ReduceRows(enc_in, enc_out, *line_bufs, sems, base, local_sem, 2 + wide)
    base += 9
    local_base = 6 + wide
    first = remote(small.at[1 - core], small_land, sems, base, sibling)
    plane = [
        remote(small.at[core], small_plane.at[v - 1], sems, base + v, peers[v - 1])
        for v in range(1, wide)
    ]
    base += wide
    spread_small = [
        remote(small.at[core], small_rows.at[k - 1], sems, base + k - 1, others[k - 1])
        for k in range(1, rows)
    ]
    base += rows - 1
    hand_base = base
    base += 6 * wide

    def hand(section, source, v, piece):
        index = piece * wide + v
        return pltpu.make_async_remote_copy(
            src_ref=ready.at[section, v, piece],
            dst_ref=landing.at[source, v, piece],
            send_sem=send_sem.at[hand_base + section * 3 * wide + index],
            recv_sem=recv_sem.at[hand_base + source * 3 * wide + index],
            device_id={"section": section, "wide": place ^ v},
            device_id_type=MESH,
        )

    def hand_out(section, piece, value):
        for owner in range(wide):
            ready[section, owner ^ place, piece] = value[owner * depth : (owner + 1) * depth]
        for v in range(1, wide):
            hand(section, core, v, piece).start()

        @pl.when(core == section)
        def _():
            landing[core, 0, piece] = ready[section, 0, piece]

        @pl.when(core != section)
        def _():
            hand(section, core, 0, piece).start()

    def handed(section):
        for piece in range(3):
            for v in range(1, wide):
                hand(section, core, v, piece).wait_send()

            @pl.when(core != section)
            def _():
                hand(section, core, 0, piece).wait_send()

    def came(source):
        for piece in range(3):
            for v in range(1, wide):
                hand(0, source, v, piece).wait_recv()

            @pl.when(core != source)
            def _():
                hand(0, source, 0, piece).wait_recv()

    half_copies = []

    def by_half(index, value, target):
        mine, its = halves[2 * index : 2 * index + 2]
        middle = D // 2
        for own in range(2):

            @pl.when(core == own)
            def _():
                parts = (value[:, :middle], value[:, middle:]) if index != 1 else (value[:middle], value[middle:])
                mine[...] = parts[own].astype(mine.dtype)
                its[...] = parts[1 - own].astype(its.dtype)

        copies = (
            pltpu.make_async_copy(mine, target.at[core], local_sem.at[local_base + 1 + index]),
            remote(its, target.at[core], sems, base + index, sibling),
        )
        for copy in copies:
            copy.start()
            half_copies.append(copy)

    line.start()
    cross_weights(*cross, held)
    batches[0].start()
    by_half(0, y_ref[...], y_half)
    small[...] = jnp.zeros_like(small)
    for i, gain in enumerate(gains):
        small[i // 2, pl.ds(1 + i % 2, 1), pl.ds(0, D)] = gain[...]
    batches[0].join()
    g_ref, x_ref, gain_ref, normed_ref, projected_ref, context_ref, weights_ref = dec_self
    for load in attn_loads(dec_attn):
        load.wait()
    self_backward_rows(
        g_ref, x_ref, gain_ref, win, wout, projected_ref, weights_ref, gt, small.at[1], context_d, projected_d, sums_ref
    )
    for load in attn_loads(enc_attn):
        load.start()
    batches[0].given()
    self_backward_weights(g_ref, normed_ref, context_ref, projected_d, held)
    batches[1].start()
    line.loaded()
    line.turn(0)
    batches[0].pass_on()
    for piece in range(2):
        hand_out(1, piece, dec_in[piece])
    hand_out(1, 2, tn(dec_out[...], straight).astype(low))
    by_half(2, gt[...], t_half)
    g_ref, x_ref, gain_ref, normed_ref, projected_ref, context_ref, weights_ref = enc_self
    for load in attn_loads(enc_attn):
        load.wait()
    self_backward_rows(
        g_ref, x_ref, gain_ref, win, wout, projected_ref, weights_ref, gx, small.at[0], context_e, projected_e, sums_ref
    )
    first.start()
    batches[1].join()
    batches[1].given()
    self_backward_weights(g_ref, normed_ref, context_ref, projected_e, held)
    batches[2].start()
    line.turn(1)
    batches[0].spread()
    first.wait()
    small[core] = small[core] + small_land[...]
    for copy in plane:
        copy.start()
    batches[2].join()
    batches[1].pass_on()
    by_half(1, gx[...].T, x_half)
    for copy in plane:
        copy.wait()
    small[core] = small[core] + jnp.sum(small_plane[...], axis=0)
    for copy in spread_small:
        copy.start()
    line.turn(2)
    batches[0].relay()
    batches[1].spread()
    batches[2].pass_on()
    batches[1].relay()
    batches[2].spread()
    line.close(0)
    hand_out(0, 0, line_bufs[0][0, 0])
    line.close(1)
    hand_out(0, 1, line_bufs[0][0, 1])
    batches[2].relay()
    line.close(2)
    hand_out(0, 2, tn(line_bufs[2][0], straight).astype(low))
    part = held.shape[1] // rows // 2
    span = keep.shape[1] - part
    crosses = batches[0].total()
    selfs = [batches[2].total(), batches[1].total()]
    for own in range(2):

        @pl.when(core == own)
        def _():
            keep[:, pl.ds(0, span)] = selfs[own]
            keep[:, pl.ds(span, part)] = crosses[:, own * part : (own + 1) * part]
            give[:, pl.ds(0, span)] = selfs[1 - own]
            give[:, pl.ds(span, part)] = crosses[:, (1 - own) * part : (2 - own) * part]

    store = pltpu.make_async_copy(keep, out_ref.at[core], local_sem.at[local_base + 4])
    last = remote(give, out_ref.at[core], sems, base + 3, sibling)
    store.start()
    last.start()
    for copy in spread_small:
        copy.wait()
    small_out[...] = small[core] + jnp.sum(small_rows[...], axis=0)
    handed(0)
    handed(1)
    came(0)
    came(1)
    store_ffn = pltpu.make_async_copy(landing, ffn_ref, local_sem.at[local_base + 5])
    store_ffn.start()
    store.wait()
    last.wait()
    store_ffn.wait()
    for copy in half_copies:
        copy.wait()
    batches[2].given()
    for batch in batches:
        batch.finish()
    line.finish()


def last_step(wide, rows, cross, dec_sums, enc_shares, y3, dec_attn, enc_attn, dec_self, enc_self, gains):
    low = jnp.bfloat16
    depth = D // wide
    size = split_at(depth)
    units = dec_sums[1].shape[0]
    columns = 4 * HD
    enc_rows, dec_rows = enc_self[0].shape[0], dec_self[0].shape[0]
    wanted = (columns + columns // 2) // rows
    copies = 3 * (wide + 6 + rows - 1) + 9 + wide + rows - 1 + 6 * wide + 4
    small = (16, (D + TILE - 1) // TILE * TILE)
    middle = D // 2
    half_shapes = [
        ((dec_rows, middle), low),
        ((middle, enc_rows), jnp.float32),
        ((dec_rows, middle), jnp.float32),
    ]
    batch_scratch = reduce_weights_scratch(wide, rows, size, columns)
    return pl.pallas_call(
        lambda *refs: last_kernel(wide, rows, *refs),
        out_shape=[
            jax.ShapeDtypeStruct((2, size, wanted), jnp.float32),
            jax.ShapeDtypeStruct((2, wide, 3, depth, TILE), low),
            jax.ShapeDtypeStruct(small, jnp.float32),
        ]
        + [jax.ShapeDtypeStruct((2, *each), kind) for each, kind in half_shapes],
        in_specs=[VM] * 6 + [VM, VM, HBM, HBM, VM, HBM, HBM] + [VM] * 18,
        out_specs=[HBM, HBM, VM, HBM, HBM, HBM],
        scratch_shapes=batch_scratch * 3
        + reduce_rows_scratch(units)
        + [
            pltpu.VMEM((D, columns), low),
            pltpu.VMEM((D, 3 * HD), low),
            pltpu.VMEM((D, HD), low),
            pltpu.VMEM((enc_rows, D), jnp.float32),
            pltpu.VMEM((dec_rows, D), jnp.float32),
            pltpu.VMEM((enc_rows, HD), low),
            pltpu.VMEM((enc_rows, 3 * HD), low),
            pltpu.VMEM((dec_rows, HD), low),
            pltpu.VMEM((dec_rows, 3 * HD), low),
            pltpu.VMEM((size, wanted), jnp.float32),
            pltpu.VMEM((size, wanted), jnp.float32),
            pltpu.VMEM((2, wide, 3, depth, TILE), low),
            pltpu.VMEM((2, wide, 3, depth, TILE), low),
            pltpu.VMEM((2,) + small, jnp.float32),
            pltpu.VMEM(small, jnp.float32),
            pltpu.VMEM((wide - 1,) + small, jnp.float32),
            pltpu.VMEM((rows - 1,) + small, jnp.float32),
        ]
        + [pltpu.VMEM(each, kind) for each, kind in half_shapes for _ in range(2)]
        + [
            pltpu.VMEM((H, 1, 2 * enc_rows), jnp.float32),
            pltpu.SemaphoreType.DMA((copies,)),
            pltpu.SemaphoreType.DMA((copies,)),
            pltpu.SemaphoreType.DMA((12 + wide,)),
        ],
        compiler_params=pltpu.CompilerParams(
            collective_id=7, has_side_effects=True, vmem_limit_bytes=VMEM_LIMIT
        ),
        name="last_step",
    )(*cross, *dec_sums, *enc_shares, y3, dec_attn, enc_attn, *dec_self, *enc_self, *gains)


def assemble_kernel(
    units, parts_ref, attn_ref, small_ref, enc_hot, dec_hot,
    in_ref, out_ref, gain_ref, bias_ref, win_ref, wout_ref, cin_ref, cout_ref,
):
    low = jnp.bfloat16
    wide = parts_ref.shape[1]
    place, core = lax.axis_index("wide"), lax.axis_index("section")
    pairs = 2 * wide
    row_ids = lax.broadcasted_iota(jnp.int32, (TILE, TILE), 0)
    lane_ids = lax.broadcasted_iota(jnp.int32, (TILE, TILE), 1)

    def tile_at(tile, first, columns):
        total = None
        last = min((tile + 1) * TILE, columns) - 1
        for group in range(tile * TILE // units, last // units + 1):
            half, chip, block = group % 2, group % pairs // 2, group // pairs
            shift = group * units - tile * TILE
            picks = ((row_ids + shift == lane_ids) & (row_ids < units)).astype(low)
            part = matmul(
                parts_ref[half, chip ^ place, first + block], picks
            )
            total = part if total is None else total + part
        return total

    for tile in range(in_ref.shape[2] // TILE):
        in_ref[0, :, pl.ds(tile * TILE, TILE)] = tile_at(tile, 0, in_ref.shape[2])
    for tile in range(out_ref.shape[2] // TILE):
        out_ref[0, :, pl.ds(tile * TILE, TILE)] = tile_at(tile, 2, out_ref.shape[2])
    for row in range(3):
        gain_ref[row] = small_ref[row : row + 1, 0:D]
    for section, hot in enumerate((enc_hot, dec_hot)):

        @pl.when(core == section)
        def _():
            sums = small_ref[8:16, 0 : hot.shape[1]]
            bias = lax.dot_general(
                sums, hot[...], (((1,), (1,)), ((), ())), precision=HIGHEST, preferred_element_type=jnp.float32
            )
            for head in range(H):
                bias_ref[head] = bias[head : head + 1]

    size, depth = attn_ref.shape[1], in_ref.shape[1]
    whole = jnp.concatenate([attn_ref[0], attn_ref[1, 2 * size - depth :]], axis=0)
    turned = whole.T
    start = 0
    for ref in (win_ref, wout_ref, cin_ref, cout_ref):
        ref[0] = turned[start : start + ref.shape[1]]
        start += ref.shape[1]


def assemble(rows, parts, attn_parts, small):
    wide, depth = parts.shape[1], parts.shape[3]
    shapes = [
        (1, depth, 2 * FF // rows),
        (1, depth, FF // rows),
        (3, 1, D),
        (H, 1, NB),
        (1, 3 * HD // rows, depth),
        (1, HD // rows, depth),
        (1, HD // rows, depth),
        (1, HD // rows, depth),
    ]
    return pl.pallas_call(
        lambda *refs: assemble_kernel(FF // (wide * rows * 2), *refs),
        out_shape=[jax.ShapeDtypeStruct(shape, jnp.float32) for shape in shapes],
        in_specs=[VM] * 5,
        out_specs=[VM] * len(shapes),
        compiler_params=pltpu.CompilerParams(vmem_limit_bytes=VMEM_LIMIT),
        name="assemble",
    )(
        parts,
        attn_parts,
        small,
        distance_hot(LE, True, 1 - LE),
        distance_hot(LD, False, 1 - LD),
    )


def bias_rows(source, target):
    length, span = target.shape[1], source.shape[1]
    for head in range(H):
        row = jnp.broadcast_to(source[pl.ds(head, 1), :], (length, span))
        target[head] = pltpu.roll(row, 0, 1, stride=1, stride_axis=0)[:, :length]


def distance_sums(scores, span):
    length = scores.shape[0]
    flip = (
        lax.broadcasted_iota(jnp.int32, (length, length), 0)
        + lax.broadcasted_iota(jnp.int32, (length, length), 1)
        == length - 1
    ).astype(jnp.bfloat16)
    flipped = matmul(flip, scores)
    padded = jnp.concatenate([flipped, jnp.zeros((length, span - length), jnp.float32)], axis=1)
    rolled = pltpu.roll(padded, 0, 1, stride=1, stride_axis=0)
    return jnp.sum(rolled, axis=0, keepdims=True)


def distance_hot(length, both_ways, first):
    table = bucket_table(length, both_ways)
    span = 2 * length
    hot = np.zeros((NB, span), np.float32)
    for entry in range(span):
        distance = entry + first
        if first == 0 and distance >= length:
            distance -= span
        if -length < distance < length:
            query = max(0, -distance)
            hot[table[query, query + distance], entry] = 1.0
    return jnp.asarray(hot)


def head_lanes(value, side):
    lanes = lax.broadcasted_iota(jnp.int32, value.shape, 1)
    return jnp.where((lanes < DH) == (side == 0), value, jnp.zeros_like(value))


def attend_heads(query_of, key_of, value_of, bias_of, allowed, context_ref, weights_ref):
    @pl.loop(0, H // 2)
    def _(pair):
        query, key, value = query_of(pair), key_of(pair), value_of(pair)
        total = None
        for side in range(2):
            head = 2 * pair + side
            scores = nt(head_lanes(query, side), key)
            if bias_of is not None:
                scores = scores + bias_of(head)
            scores = jnp.where(allowed, scores, NEGATIVE)
            shifted = jnp.exp(scores - jnp.max(scores, axis=-1, keepdims=True))
            weights = shifted / jnp.sum(shifted, axis=-1, keepdims=True)
            weights_ref[head] = weights
            part = matmul(weights.astype(jnp.bfloat16), head_lanes(value, side))
            total = part if total is None else total + part
        context_ref[:, pair_tile(pair, 0)] = total.astype(jnp.bfloat16)


def attend_heads_backward(query_of, key_of, value_of, weights_ref, grad_of, put, put_scores=None):
    @pl.loop(0, H // 2)
    def _(pair):
        query, key, value, grad = query_of(pair), key_of(pair), value_of(pair), grad_of(pair)
        sums = [None, None, None]
        for side in range(2):
            head = 2 * pair + side
            weights = weights_ref[head]
            own_grad = head_lanes(grad, side)
            grad_weights = nt(own_grad, value)
            inner = jnp.sum(grad_weights * weights, axis=-1, keepdims=True)
            low = (weights * (grad_weights - inner)).astype(jnp.bfloat16)
            if put_scores is not None:
                put_scores(head, low)
            parts = [
                matmul(low, head_lanes(key, side)),
                tn(low, head_lanes(query, side)),
                tn(weights.astype(jnp.bfloat16), own_grad),
            ]
            sums = [b if a is None else a + b for a, b in zip(sums, parts)]
        put(pair, *sums)


def pair_tile(pair, base):
    return pl.ds(pl.multiple_of(base + pair * TILE, TILE), TILE)


def item_numbers(lengths_ref, core, shape, axis):
    positions = lax.broadcasted_iota(jnp.int32, shape, axis)
    number, end = jnp.zeros(shape, jnp.int32), 0
    for item in range(lengths_ref.shape[1] - 1):
        end = end + lengths_ref[core, item]
        number = number + (positions >= end).astype(jnp.int32)
    return number


def weight_spec(half, width, index):
    return pl.BlockSpec((None, D, width), lambda step: (half, 0, index), memory_space=pltpu.VMEM)


W_IN = weight_spec(0, 3 * HD, 0)
W_OUT, C_IN, C_OUT = [weight_spec(1, HD, i) for i in range(3)]


def tile_of(ref, base):
    return lambda pair: ref[:, pair_tile(pair, base)]


def self_forward_kernel(
    wide, causal, x_ref, gain_ref, win_ref, wout_ref, bias_ref, lengths_ref, *refs
):
    core = lax.axis_index("section")
    if wide:
        blocks, dec_blocks, refs = refs[: wide - 1], refs[wide - 1 : 2 * wide - 2], refs[2 * wide - 2 :]
    y_ref, low_ref, normed_ref, projected_ref, context_ref, weights_ref = refs[:6]
    if wide:
        pieces, dec_pieces, sems = refs[6 : 5 + wide], refs[5 + wide : 4 + 2 * wide], refs[4 + 2 * wide :]
        peers = peers_of(wide)
        greet(peers + [{"rows": lax.axis_index("rows") ^ 1}])
        reshard = Reshard(blocks, pieces, 0, sems, 0, peers)
        reshard.start()
        half = dec_pieces[0].shape[0]
        mine = pl.ds(lax.axis_index("rows") % 2 * half, half)
        later = [
            remote(block.at[mine], piece, sems, 9 + v, peers[v])
            for v, (block, piece) in enumerate(zip(dec_blocks, dec_pieces))
        ]
    low_ref[...] = x_ref[core] if causal else x_ref[core].T
    residual = low_ref[...].astype(jnp.float32)
    normed_ref[...] = (residual * rms_rows(residual) * gain_ref[pl.ds(0, 1), :]).astype(jnp.bfloat16)
    projected_ref[...] = matmul(normed_ref[...], win_ref[...]).astype(jnp.bfloat16)
    length = low_ref.shape[0]
    allowed = item_numbers(lengths_ref, core, (length, length), 0) == item_numbers(
        lengths_ref, core, (length, length), 1
    )
    if causal:
        allowed = allowed & (
            lax.broadcasted_iota(jnp.int32, (length, length), 0)
            >= lax.broadcasted_iota(jnp.int32, (length, length), 1)
        )
    attend_heads(
        tile_of(projected_ref, 0),
        tile_of(projected_ref, HD),
        tile_of(projected_ref, 2 * HD),
        lambda head: bias_ref[head],
        allowed,
        context_ref,
        weights_ref,
    )
    y_ref[...] = residual + nt(context_ref[...], wout_ref[...])
    if wide:
        for copy in later:
            copy.start()
        reshard.pass_on()
        reshard.finish()
        for copy in later:
            copy.wait()


def self_forward(causal, embed, gains, weight, bias, lengths, blocks=(), dec_blocks=()):
    rows = embed.shape[1 if causal else 2]
    low = jnp.bfloat16
    wide = len(blocks) + 1 if blocks else 0
    params = dict(vmem_limit_bytes=VMEM_LIMIT)
    if blocks:
        params.update(collective_id=6, has_side_effects=True)
    y, *kept = pl.pallas_call(
        lambda *refs: self_forward_kernel(wide, causal, *refs),
        out_shape=[
            jax.ShapeDtypeStruct((rows, D), jnp.float32),
            jax.ShapeDtypeStruct((rows, D), low),
            jax.ShapeDtypeStruct((rows, D), low),
            jax.ShapeDtypeStruct((rows, 3 * HD), low),
            jax.ShapeDtypeStruct((rows, HD), low),
            jax.ShapeDtypeStruct((H, rows, rows), jnp.float32),
        ]
        + [jax.ShapeDtypeStruct(each.shape, low) for each in blocks]
        + [jax.ShapeDtypeStruct((each.shape[0] // 2, *each.shape[1:]), low) for each in dec_blocks],
        in_specs=[VM, VM, W_IN, W_OUT, VM, SM] + [HBM] * (2 * len(blocks)),
        out_specs=[VM] * 6 + [HBM] * (2 * len(blocks)),
        scratch_shapes=[pltpu.SemaphoreType.DMA((12,))] * 2 if blocks else [],
        grid=(1,),
        compiler_params=pltpu.CompilerParams(**params),
        name="self_forward_%d" % rows,
    )(embed, gains, weight, weight, bias, lengths, *blocks, *dec_blocks)
    return y, kept[:5], kept[5:]


def picked(source, start, window, first, width):
    base = start // TILE * TILE
    window = min(window, source.shape[1] - base)
    lanes = lax.broadcasted_iota(jnp.int32, (window, HD), 1) - first
    rows_of = lax.broadcasted_iota(jnp.int32, (window, HD), 0) + (base - start)
    pick = ((rows_of == lanes) & (lanes >= 0) & (lanes < width)).astype(jnp.bfloat16)
    return matmul(source[:, pl.ds(base, window)], pick)


def self_backward_rows(
    g_ref,
    x_ref,
    gain_ref,
    win_ref,
    wout_ref,
    projected_ref,
    weights_ref,
    gx_ref,
    small_ref,
    context_grad,
    projected_grad,
    sums_ref,
):
    low = jnp.bfloat16
    length = x_ref.shape[0]
    context_grad[...] = matmul(g_ref[...].astype(low), wout_ref[...]).astype(low)

    def put(pair, query, key, value):
        for index, part in enumerate((query, key, value)):
            projected_grad[:, pair_tile(pair, index * HD)] = part.astype(low)

    def put_scores(head, scores):
        sums_ref[head, :, pl.ds(0, 2 * length)] = distance_sums(scores, 2 * length)

    attend_heads_backward(
        tile_of(projected_ref, 0),
        tile_of(projected_ref, HD),
        tile_of(projected_ref, 2 * HD),
        weights_ref,
        tile_of(context_grad, 0),
        put,
        put_scores,
    )
    for head in range(H):
        small_ref[pl.ds(8 + head, 1), pl.ds(0, 2 * length)] = sums_ref[head, :, pl.ds(0, 2 * length)]
    grad_normed = nt(projected_grad[...], win_ref[...])
    residual = x_ref[...].astype(jnp.float32)
    grad_residual, grad_gain = norm_pull(residual, gain_ref[pl.ds(0, 1), :], grad_normed)
    small_ref[pl.ds(0, 1), pl.ds(0, D)] = grad_gain
    gx_ref[...] = g_ref[...] + grad_residual


def self_backward_weights(g_ref, normed_ref, context_ref, projected_grad, grad_ref):
    low = jnp.bfloat16
    both = jnp.concatenate([normed_ref[...], g_ref[...].astype(low)], axis=0)
    chunks = grad_ref.shape[1] // HD
    part_in, part_out = 3 * HD // chunks, HD // chunks
    for chunk in range(chunks):
        right = jnp.concatenate(
            [
                picked(projected_grad, chunk * part_in, HD, 0, part_in),
                picked(context_ref, chunk * part_out, 2 * TILE, part_in, part_out),
            ],
            axis=0,
        ).astype(low)
        grad_ref[:, pl.ds(chunk * HD, HD)] = tn(both, right).astype(low)


def cross_forward_kernel(
    x_ref, final_ref, wkey_ref, wvalue_ref, y_ref, gain_ref, wquery_ref, wout_ref, dec_lengths, enc_lengths,
    out_ref, memory_ref, kv_ref, normed_ref, query_ref, context_ref, weights_ref,
):
    low = jnp.bfloat16
    core = lax.axis_index("section")
    residual = x_ref[...]
    memory_ref[...] = (residual * rms_rows(residual) * final_ref[pl.ds(2, 1), :]).astype(low)
    kv_ref[:, pl.ds(0, HD)] = matmul(memory_ref[...], wkey_ref[...]).astype(low)
    kv_ref[:, pl.ds(HD, HD)] = matmul(memory_ref[...], wvalue_ref[...]).astype(low)
    target = y_ref[...]
    normed_ref[...] = (target * rms_rows(target) * gain_ref[pl.ds(1, 1), :]).astype(low)
    query_ref[...] = matmul(normed_ref[...], wquery_ref[...]).astype(low)
    attend_heads(
        tile_of(query_ref, 0),
        tile_of(kv_ref, 0),
        tile_of(kv_ref, HD),
        None,
        item_numbers(dec_lengths, core, (LD, LE), 0) == item_numbers(enc_lengths, core, (LD, LE), 1),
        context_ref,
        weights_ref,
    )
    out_ref[...] = target + nt(context_ref[...], wout_ref[...])


def cross_forward(x2, enc_gains, enc_weight, y1, dec_gains, dec_weight, dec_lengths, enc_lengths):
    low = jnp.bfloat16
    y2, *kept = pl.pallas_call(
        cross_forward_kernel,
        out_shape=[
            jax.ShapeDtypeStruct((LD, D), jnp.float32),
            jax.ShapeDtypeStruct((LE, D), low),
            jax.ShapeDtypeStruct((LE, 2 * HD), low),
            jax.ShapeDtypeStruct((LD, D), low),
            jax.ShapeDtypeStruct((LD, HD), low),
            jax.ShapeDtypeStruct((LD, HD), low),
            jax.ShapeDtypeStruct((H, LD, LE), jnp.float32),
        ],
        in_specs=[VM, VM, C_IN, C_OUT, VM, VM, C_IN, C_OUT, SM, SM],
        out_specs=[VM] * 7,
        grid=(1,),
        compiler_params=pltpu.CompilerParams(vmem_limit_bytes=VMEM_LIMIT),
        name="cross_forward",
    )(
        x2,
        enc_gains,
        enc_weight,
        enc_weight,
        y1,
        dec_gains,
        dec_weight,
        dec_weight,
        dec_lengths,
        enc_lengths,
    )
    return y2, kept


def cross_backward_kernel(
    g_ref, x_ref, final_ref, wkey_ref, wvalue_ref, y_ref, gain_ref, wquery_ref, wout_ref, kv_ref, query_ref, weights_ref,
    gx_ref, gy_ref, final_out, gain_out, kv_grad, query_grad, context_grad,
):
    low = jnp.bfloat16
    grad_low = g_ref[...].astype(low)
    context_grad[...] = matmul(grad_low, wout_ref[...]).astype(low)

    def put(pair, query, key, value):
        query_grad[:, pair_tile(pair, 0)] = query.astype(low)
        kv_grad[:, pair_tile(pair, 0)] = key.astype(low)
        kv_grad[:, pair_tile(pair, HD)] = value.astype(low)

    attend_heads_backward(
        tile_of(query_ref, 0),
        tile_of(kv_ref, 0),
        tile_of(kv_ref, HD),
        weights_ref,
        tile_of(context_grad, 0),
        put,
    )
    grad_memory = nt(kv_grad[:, pl.ds(0, HD)], wkey_ref[...]) + nt(
        kv_grad[:, pl.ds(HD, HD)], wvalue_ref[...]
    )
    gx_ref[...], final_out[...] = norm_pull(x_ref[...], final_ref[pl.ds(2, 1), :], grad_memory)
    grad_residual, gain_out[...] = norm_pull(
        y_ref[...], gain_ref[pl.ds(1, 1), :], nt(query_grad[...], wquery_ref[...])
    )
    gy_ref[...] = g_ref[...] + grad_residual


def cross_weights(g_ref, kv_grad, query_grad, memory_ref, normed_ref, context_ref, grad_ref):
    low = jnp.bfloat16
    lefts = jnp.concatenate([memory_ref[...], normed_ref[...], g_ref[...].astype(low)], axis=0)
    chunks = grad_ref.shape[1] // HD
    part = HD // chunks
    for chunk in range(chunks):
        start = chunk * part
        right = jnp.concatenate(
            [
                picked(kv_grad, start, 2 * TILE, 0, part)
                + picked(kv_grad, HD + start, 2 * TILE, part, part),
                picked(query_grad, start, 2 * TILE, 2 * part, part),
                picked(context_ref, start, 2 * TILE, 3 * part, part),
            ],
            axis=0,
        ).astype(low)
        grad_ref[:, pl.ds(chunk * HD, HD)] = tn(lefts, right).astype(low)


def cross_backward(g2, x2, enc_gains, enc_weight, y1, dec_gains, dec_weight, kept):
    _, kv, _, query, _, weights = kept
    low = jnp.bfloat16
    return pl.pallas_call(
        cross_backward_kernel,
        out_shape=[
            jax.ShapeDtypeStruct((LE, D), jnp.float32),
            jax.ShapeDtypeStruct((LD, D), jnp.float32),
            jax.ShapeDtypeStruct((1, D), jnp.float32),
            jax.ShapeDtypeStruct((1, D), jnp.float32),
            jax.ShapeDtypeStruct((LE, 2 * HD), low),
            jax.ShapeDtypeStruct((LD, HD), low),
        ],
        in_specs=[VM, VM, VM, C_IN, C_OUT, VM, VM, C_IN, C_OUT] + [VM] * 3,
        out_specs=[VM] * 6,
        scratch_shapes=[pltpu.VMEM((LD, HD), low)],
        grid=(1,),
        compiler_params=pltpu.CompilerParams(vmem_limit_bytes=VMEM_LIMIT),
        name="cross_backward",
    )(
        g2,
        x2,
        enc_gains,
        enc_weight,
        enc_weight,
        y1,
        dec_gains,
        dec_weight,
        dec_weight,
        kv,
        query,
        weights,
    )


def plain_self_forward(residual, gain_row, weight, bias_full, allowed):
    normed = to_low(rms_norm(residual, gain_row))
    projected = to_low(matmul(normed, weight[:, : 3 * HD]))
    context, weights, low_weights = attend_forward(
        projected[:, :HD], projected[:, HD : 2 * HD], projected[:, 2 * HD :], bias_full, allowed
    )
    return (
        residual + matmul(context, weight[:, 3 * HD : 4 * HD].T),
        (residual, normed, projected, context, weights, low_weights),
    )


def plain_self_backward(kept, gain_row, weight, hot, grad_out):
    residual, normed, projected, context, weights, low_weights = kept
    grad_low = to_low(grad_out)
    grad_wout = matmul(grad_low.T, context)
    grad_context = to_low(matmul(grad_low, weight[:, 3 * HD : 4 * HD]))
    grad_queries, grad_keys, grad_values, low_scores = attend_backward(
        projected[:, :HD],
        projected[:, HD : 2 * HD],
        projected[:, 2 * HD :],
        weights,
        low_weights,
        grad_context,
    )
    grad_projected = to_low(jnp.concatenate([grad_queries, grad_keys, grad_values], axis=1))
    grad_win = matmul(normed.T, grad_projected)
    grad_residual, grad_gain = plain_norm_backward(
        residual, gain_row, matmul(grad_projected, weight[:, : 3 * HD].T)
    )
    grad_bias = jnp.einsum(
        "hqk,qkb->bh", low_scores, hot.astype(jnp.bfloat16), preferred_element_type=jnp.float32
    )
    return grad_out + grad_residual, grad_gain, grad_win, grad_wout, grad_bias


def plain_reduce_attn(grad, core, wide, rows):
    depth, columns = grad.shape
    halves = plain_core_halves(grad, core, wide)
    place = lax.axis_index("wide")
    parts = [
        lax.dynamic_index_in_dim(halves, place ^ v, 0, keepdims=False) for v in range(wide)
    ]
    mine = to_low(scatter_wide(parts))
    pieces, start = [], 0
    for width in (3 * HD, HD, HD, HD):
        pieces.append(mine[:, start : start + width].reshape(mine.shape[0], rows, width // rows))
        start += width
    stacked = jnp.concatenate(pieces, axis=2).transpose(1, 0, 2)
    return lax.psum_scatter(stacked, "rows", scatter_dimension=0, tiled=True)[0]


def plain_core_halves(grad, core, wide):
    depth, columns = grad.shape
    split = to_low(grad).reshape(wide, 2, depth // wide // 2, columns)
    mine = lax.dynamic_index_in_dim(split, core, 1, keepdims=False)
    sent = lax.dynamic_index_in_dim(split, 1 - core, 1, keepdims=False)
    return mine.astype(jnp.float32) + xor_permute(sent, "section", 1).astype(jnp.float32)


def plain_both_sections(own, section):
    other = xor_permute(own, "section", 1)
    is_dec = section == 1
    return jnp.where(is_dec, other, own), jnp.where(is_dec, own, other)


def plain_norm_backward(residual, gain_row, grad_normed):
    _, norm_pull = jax.vjp(rms_norm, residual, gain_row)
    return norm_pull(grad_normed)


def plain_hidden_columns(weight):
    width = weight.shape[1] * 2 // 3
    return weight[:, :width], weight[:, width:]


def plain_ffn_hidden(blocks, weight):
    w_in, _ = plain_hidden_columns(weight)
    both = [matmul(block, w_in) for block in blocks]
    units = w_in.shape[1] // 2
    return both, [to_low(gated(part[:, :units], part[:, units:])) for part in both]


def plain_ffn_forward(residual, gain_row, weight):
    blocks = gather_wide(to_low(rms_norm(residual, gain_row)))
    both, hidden = plain_ffn_hidden(blocks, weight)
    _, w_out = plain_hidden_columns(weight)
    out = residual + scatter_wide([matmul(part, w_out.T) for part in hidden])
    return out, (residual, blocks, both, hidden)


def plain_ffn_backward(kept, gain_row, weight, grad_out, grad_blocks):
    residual, blocks, both, hidden = kept
    w_in, w_out = plain_hidden_columns(weight)
    units = w_out.shape[1]
    parts, grad_both = [], []
    for block, pre in zip(grad_blocks, both):
        _, pull = jax.vjp(gated, pre[:, :units], pre[:, units:])
        grad_gate, grad_up = pull(matmul(block, w_out))
        low = to_low(jnp.concatenate([grad_gate, grad_up], axis=1))
        grad_both.append(low)
        parts.append(matmul(low, w_in.T))
    grad_residual, grad_gain = plain_norm_backward(residual, gain_row, scatter_wide(parts))
    joined = jnp.concatenate(grad_both, axis=0)
    grad_in = matmul(jnp.concatenate(blocks, axis=0).T, joined)
    grad_wout = matmul(jnp.concatenate(grad_blocks, axis=0).T, jnp.concatenate(hidden, axis=0))
    return grad_out + grad_residual, grad_gain, (grad_in, grad_wout)


def plain_reduce_ffn(grads, core, wide, rows):
    grad_in, grad_wout = grads
    depth = grad_in.shape[0]
    both = jnp.concatenate(
        [grad_in.reshape(depth, rows, -1), grad_wout.reshape(depth, rows, -1)], axis=2
    )
    columns = both.shape[2]
    halves = plain_core_halves(both.reshape(depth, rows * columns), core, wide)
    halves = to_low(halves).reshape(wide * (depth // wide // 2), rows, columns).transpose(1, 0, 2)
    summed = lax.psum_scatter(halves, "rows", scatter_dimension=0, tiled=True)[0]
    blocks = summed.reshape(wide, depth // wide // 2, columns)
    place = lax.axis_index("wide")
    out = [lax.dynamic_index_in_dim(blocks, place, 0, keepdims=False)]
    for v in range(1, wide):
        block = lax.dynamic_index_in_dim(blocks, place ^ v, 0, keepdims=False)
        out.append(xor_permute(block, "wide", v))
    return placed_rows([piece[None] for piece in out], place)


def plain_to_section(enc_half, dec_half, core):
    is_dec = core == 1
    own = jnp.where(is_dec, dec_half, enc_half)
    got = xor_permute(jnp.where(is_dec, enc_half, dec_half), "section", 1)
    low, high = jnp.where(is_dec, got, own), jnp.where(is_dec, own, got)
    return jnp.concatenate([low, high], axis=-2).astype(jnp.float32)


def plain_shards(
    enc_embed,
    dec_embed,
    out_cot,
    enc_lengths,
    dec_lengths,
    norm_gains,
    rel_bias,
    attn_in,
    attn_out,
    ffn_in,
    ffn_out,
    cross_in,
    cross_out,
):
    core = lax.axis_index("section")
    place = lax.axis_index("wide")
    wide, rows = lax.axis_size("wide"), lax.axis_size("rows")
    depth = attn_in.shape[1]
    unit = FF // (wide * rows)

    small = jnp.concatenate([norm_gains[0].reshape(-1), rel_bias[0].reshape(-1)])
    enc_small, dec_small = plain_both_sections(small, core)
    gains = [each[: 3 * D].reshape(3, D) for each in (enc_small, dec_small)]
    biases = [each[3 * D :].reshape(NB, H) for each in (enc_small, dec_small)]

    attn_shard = jnp.concatenate([attn_in[0], attn_out[0].T, cross_in[0], cross_out[0]], axis=1)
    attn_own = placed_rows(gather_wide(attn_shard), place)
    ffn_blocks = jnp.concatenate(
        [
            ffn_in[0].reshape(depth, 2 * rows, wide, unit).transpose(2, 0, 1, 3).reshape(wide, depth, -1),
            ffn_out[0].T.reshape(depth, rows, wide, unit).transpose(2, 0, 1, 3).reshape(wide, depth, -1),
        ],
        axis=2,
    )
    ffn_got = [lax.dynamic_index_in_dim(ffn_blocks, place, 0, keepdims=False)]
    for v in range(1, wide):
        block = lax.dynamic_index_in_dim(ffn_blocks, place ^ v, 0, keepdims=False)
        ffn_got.append(xor_permute(block, "wide", v))
    ffn_own = placed_rows(ffn_got, place)
    attn_enc, attn_dec = plain_both_sections(attn_own, core)
    ffn_enc, ffn_dec = plain_both_sections(ffn_own, core)
    memory_weight = attn_enc[:, 4 * HD :]
    cross_w_in, cross_w_out = attn_dec[:, 4 * HD : 5 * HD], attn_dec[:, 5 * HD :]

    def own_row(array):
        return lax.dynamic_index_in_dim(array[:, 0], core, 0, keepdims=False)

    enc_row = own_row(enc_embed).astype(jnp.float32)
    dec_row = own_row(dec_embed).astype(jnp.float32)
    cot_row = own_row(out_cot)
    enc_items = item_ids(own_row(enc_lengths), LE)
    dec_items = item_ids(own_row(dec_lengths), LD)
    enc_hot, dec_hot = one_hot(LE, True), one_hot(LD, False)
    enc_bias = jnp.einsum("qkb,bh->hqk", enc_hot, biases[0], precision=HIGHEST)
    dec_bias = jnp.einsum("qkb,bh->hqk", dec_hot, biases[1], precision=HIGHEST)
    causal = jnp.arange(LD)[:, None] >= jnp.arange(LD)[None, :]

    cot_blocks = gather_wide(cot_row)
    x1, enc_self = plain_self_forward(
        enc_row, gains[0][0], attn_enc, enc_bias, enc_items[:, None] == enc_items[None, :]
    )
    y1, dec_self = plain_self_forward(
        dec_row,
        gains[1][0],
        attn_dec,
        dec_bias,
        (dec_items[:, None] == dec_items[None, :]) & causal,
    )
    x2, enc_ffn = plain_ffn_forward(x1, gains[0][1], ffn_enc)
    memory = to_low(rms_norm(x2, gains[0][2]))
    memory_kv = to_low(matmul(memory, memory_weight))
    cross_normed = to_low(rms_norm(y1, gains[1][1]))
    queries = to_low(matmul(cross_normed, cross_w_in))
    context, weights, low_weights = attend_forward(
        queries,
        memory_kv[:, :HD],
        memory_kv[:, HD:],
        0.0,
        dec_items[:, None] == enc_items[None, :],
    )
    y2 = y1 + matmul(context, cross_w_out.T)
    y3, dec_ffn = plain_ffn_forward(y2, gains[1][2], ffn_dec)

    g2, dec_ffn_gain, dec_ffn_grads = plain_ffn_backward(
        dec_ffn, gains[1][2], ffn_dec, cot_row.astype(jnp.float32), cot_blocks
    )
    dec_ffn_share = plain_reduce_ffn(dec_ffn_grads, core, wide, rows)
    g2_low = to_low(g2)
    grad_cross_out = matmul(g2_low.T, context)
    grad_context = to_low(matmul(g2_low, cross_w_out))
    grad_queries, grad_keys, grad_values, _ = attend_backward(
        queries, memory_kv[:, :HD], memory_kv[:, HD:], weights, low_weights, grad_context
    )
    grad_query_low = to_low(grad_queries)
    grad_kv = to_low(jnp.concatenate([grad_keys, grad_values], axis=1))
    grad_x2, enc_final_gain = plain_norm_backward(x2, gains[0][2], matmul(grad_kv, memory_weight.T))
    grad_x1, enc_ffn_gain, enc_ffn_grads = plain_ffn_backward(
        enc_ffn, gains[0][1], ffn_enc, grad_x2, gather_wide(to_low(grad_x2))
    )
    enc_ffn_share = plain_reduce_ffn(enc_ffn_grads, core, wide, rows)

    grad_cross_in = matmul(cross_normed.T, grad_query_low)
    grad_memory = matmul(memory.T, grad_kv)
    from_cross, dec_cross_gain = plain_norm_backward(
        y1, gains[1][1], matmul(grad_query_low, cross_w_in.T)
    )
    grad_y, dec_self_gain, dec_win, dec_wout, dec_bias_grad = plain_self_backward(
        dec_self, gains[1][0], attn_dec, dec_hot, g2 + from_cross
    )
    dec_attn_share = plain_reduce_attn(
        jnp.concatenate([dec_win, dec_wout, grad_cross_in, grad_cross_out], axis=1),
        core,
        wide,
        rows,
    )
    grad_x, enc_self_gain, enc_win, enc_wout, enc_bias_grad = plain_self_backward(
        enc_self, gains[0][0], attn_enc, enc_hot, grad_x1
    )
    enc_attn_share = plain_reduce_attn(
        jnp.concatenate([enc_win, enc_wout, grad_memory], axis=1), core, wide, rows
    )

    small_grads = jnp.stack(
        [
            jnp.concatenate(
                [enc_self_gain, enc_ffn_gain, enc_final_gain, enc_bias_grad.reshape(-1)]
            ),
            jnp.concatenate(
                [dec_self_gain, dec_cross_gain, dec_ffn_gain, dec_bias_grad.reshape(-1)]
            ),
        ]
    )
    small_total = lax.psum(small_grads, ("section", "wide", "rows"))
    small_own = jnp.where(core == 1, small_total[1], small_total[0])

    attn_share = plain_to_section(enc_attn_share, dec_attn_share, core)
    ffn_share = plain_to_section(enc_ffn_share, dec_ffn_share, core)
    in_width = 2 * FF // rows // wide
    ffn_in_grad = (
        ffn_share[:, :, :in_width]
        .reshape(wide, depth, 2, unit)
        .transpose(1, 2, 0, 3)
        .reshape(depth, 2 * FF // rows)
    )
    ffn_out_grad = ffn_share[:, :, in_width:].transpose(0, 2, 1).reshape(FF // rows, depth)
    widths = [3 * HD // rows, HD // rows, HD // rows]
    edges = np.cumsum([0] + widths + [HD // rows])
    win, wout, cin, cout = [attn_share[:, a:b] for a, b in zip(edges[:-1], edges[1:])]

    half = D // 2

    def by_half(own):
        halves = jnp.stack([own[:, :half], own[:, half:]])
        keep = lax.dynamic_index_in_dim(halves, core, 0, keepdims=False)
        send = lax.dynamic_index_in_dim(halves, 1 - core, 0, keepdims=False)
        got = xor_permute(send, "section", 1)
        is_dec = core == 1
        return jnp.stack([jnp.where(is_dec, got, keep), jnp.where(is_dec, keep, got)])[:, None]

    return (
        by_half(to_low(y3)),
        by_half(grad_x),
        by_half(grad_y),
        small_own[: 3 * D].reshape(1, 3, D),
        small_own[3 * D :].reshape(1, NB, H),
        win[None],
        wout.T[None],
        ffn_in_grad[None],
        ffn_out_grad[None],
        cin[None],
        cout[None],
    )


def shards(
    enc_embed,
    dec_embed,
    out_cot,
    enc_lengths,
    dec_lengths,
    norm_gains,
    rel_bias,
    attn_in,
    attn_out,
    ffn_in,
    ffn_out,
    cross_in,
    cross_out,
):
    wide, rows = lax.axis_size("wide"), lax.axis_size("rows")
    enc_attn, dec_half, gains, biases, enc_blocks, dec_blocks = start_weights(
        wide, rows, attn_in, attn_out, cross_in, cross_out, ffn_in, ffn_out, norm_gains[0], rel_bias[0].T
    )
    enc_lengths, dec_lengths = enc_lengths[:, 0], dec_lengths[:, 0]
    x1, enc_self, moved = self_forward(
        False,
        jnp.swapaxes(enc_embed[:, 0], 1, 2),
        gains[0],
        enc_attn,
        biases[0],
        enc_lengths,
        tuple(enc_blocks[1:]),
        tuple(dec_blocks[1:]),
    )
    enc_pieces, dec_pieces = moved[: wide - 1], moved[wide - 1 :]
    x2, *enc_ffn = ffn_forward_call(
        wide, x1, (gains[0], 1), [enc_blocks[0], *enc_pieces], 2, (dec_half, *dec_pieces)
    )
    enc_ffn, dec_attn, dec_pieces = enc_ffn[:4], enc_ffn[4], [dec_blocks[0], *dec_pieces, *enc_ffn[5:]]
    y1, dec_self, _ = self_forward(
        True, dec_embed[:, 0], gains[1], dec_attn, biases[1], dec_lengths
    )
    y2, cross_kept = cross_forward(
        x2, gains[0], enc_attn, y1, gains[1], dec_attn, dec_lengths, enc_lengths
    )
    y3, g2, dec_ffn_gain, *dec_ffn_grads = ffn_both_call(
        wide, rows, y2, out_cot[:, 0], (gains[1], 2), dec_pieces, 3
    )
    grad_x2, g1, enc_final_gain, dec_cross_gain, kv_grad, query_grad = cross_backward(
        g2, x2, gains[0], enc_attn, y1, gains[1], dec_attn, cross_kept
    )
    grad_x1, enc_ffn_gain, enc_in, enc_out, *dec_sums = ffn_backward_call(
        wide, rows, grad_x2, x1, (gains[0], 1), enc_ffn, 5, dec_ffn_grads
    )
    attn_parts, ffn_parts, small_own, dec_out, enc_grad, dec_grad = last_step(
        wide,
        rows,
        (g2, kv_grad, query_grad, cross_kept[0], cross_kept[2], cross_kept[4]),
        dec_sums,
        (enc_in, enc_out),
        y3,
        dec_attn,
        enc_attn,
        (g1, dec_self[0], gains[1], *dec_self[1:]),
        (grad_x1, enc_self[0], gains[0], *enc_self[1:]),
        (enc_ffn_gain, enc_final_gain, dec_cross_gain, dec_ffn_gain),
    )
    ffn_in_grad, ffn_out_grad, gain_grad, bias_grad, win, wout, cin, cout = assemble(
        rows, ffn_parts, attn_parts, small_own
    )
    return (
        dec_out[:, None],
        jnp.swapaxes(enc_grad, 1, 2)[:, None],
        dec_grad[:, None],
        gain_grad.transpose(1, 0, 2),
        bias_grad.transpose(1, 2, 0),
        jnp.swapaxes(win, 1, 2),
        wout,
        ffn_in_grad,
        jnp.swapaxes(ffn_out_grad, 1, 2),
        jnp.swapaxes(cin, 1, 2),
        jnp.swapaxes(cout, 1, 2),
    )


def solution(mesh):
    placed = (
        P(None, ("wide", "rows"), None, None),
        P(None, ("wide", "rows"), None, None),
        P(None, ("wide", "rows"), None, None),
        P(None, ("wide", "rows"), None),
        P(None, ("wide", "rows"), None),
        P("section", None, None),
        P("section", None, None),
        P("section", "wide", None),
        P("section", None, "wide"),
        P("section", "wide", None),
        P("section", None, "wide"),
        P("section", "wide", None),
        P("section", "wide", None),
    )
    wide, rows = mesh.shape["wide"], mesh.shape["rows"]
    in_tiles = D // wide % 16 == 0 and FF // (wide * rows) % 32 == 0
    return jax.shard_map(
        shards if wide == 4 and rows == 4 and in_tiles else plain_shards,
        mesh=mesh,
        in_specs=placed,
        out_specs=(
            P(None, ("wide", "rows"), None, "section"),
            P(None, ("wide", "rows"), None, "section"),
            P(None, ("wide", "rows"), None, "section"),
            P("section", None, None),
            P("section", None, None),
            P("section", "wide", "rows"),
            P("section", "rows", "wide"),
            P("section", "wide", "rows"),
            P("section", "rows", "wide"),
            P("section", "wide", "rows"),
            P("section", "wide", "rows"),
        ),
        check_vma=False,
    )
```

```python
import jax
import jax.numpy as jnp
import numpy as np
from jax import lax
from jax.experimental import pallas as pl
from jax.experimental.pallas import tpu as pltpu
from jax.sharding import PartitionSpec as P

D = 1472
H = 6
DH = 64
FF = 3584
NB = 32
MAXDIST = 128
MB = 2
LE = 256
LD = 64
HD = 384


EPSILON = 1e-06
NEGATIVE = -1000000000.0
HIGHEST = lax.Precision.HIGHEST


def bucket_table(length, both_ways):
    positions = np.arange(length)
    offsets = positions[None, :] - positions[:, None]
    buckets = NB
    result = np.zeros(offsets.shape, np.int64)
    if both_ways:
        buckets = buckets // 2
        result = result + (offsets > 0) * buckets
        distance = np.abs(offsets)
    else:
        distance = np.maximum(-offsets, 0)
    exact_count = buckets // 2
    log_ratio = np.log(np.maximum(distance, 1) / exact_count) / np.log(MAXDIST / exact_count)
    far_bucket = np.minimum(
        exact_count + np.floor(log_ratio * (buckets - exact_count)).astype(np.int64), buckets - 1
    )
    return result + np.where(distance < exact_count, distance, far_bucket)


def one_hot(length, both_ways):
    bucket_ids = jnp.asarray(bucket_table(length, both_ways), jnp.int32)
    return (bucket_ids[:, :, None] == jnp.arange(NB, dtype=jnp.int32)[None, None, :]).astype(
        jnp.float32
    )


def item_ids(lengths, length):
    item_ends = jnp.cumsum(lengths)
    positions = jnp.arange(length, dtype=jnp.int32)
    return jnp.sum((positions[:, None] >= item_ends[None, :-1]).astype(jnp.int32), axis=1)


def rms_norm(residual, gain_row):
    return (
        residual
        * lax.rsqrt(jnp.mean(residual * residual, axis=-1, keepdims=True) + EPSILON)
        * gain_row
    )


def matmul(left_side, right_side):
    return jnp.dot(left_side, right_side, preferred_element_type=jnp.float32)


def matmul_exact(left_side, right_side):
    return jnp.dot(left_side, right_side, precision=HIGHEST)


def to_low(tensor):
    return tensor.astype(jnp.bfloat16)


def gated(gate_part, up_part):
    return jax.nn.gelu(gate_part, approximate=True) * up_part


def attend_forward(queries, key_rows, value_rows, bias_full, allowed):
    query_count = queries.shape[0]
    heads_q = queries.reshape(query_count, H, DH)
    heads_k = key_rows.reshape(key_rows.shape[0], H, DH)
    heads_v = value_rows.reshape(value_rows.shape[0], H, DH)
    scores = (
        jnp.einsum("qhd,khd->hqk", heads_q, heads_k, preferred_element_type=jnp.float32) + bias_full
    )
    scores = jnp.where(allowed[None], scores, NEGATIVE)
    shifted = jnp.exp(scores - jnp.max(scores, axis=-1, keepdims=True))
    weights = shifted / jnp.sum(shifted, axis=-1, keepdims=True)
    low_weights = to_low(weights)
    context = jnp.einsum("hqk,khd->qhd", low_weights, heads_v, preferred_element_type=jnp.float32)
    return (to_low(context.reshape(query_count, H * DH)), weights, low_weights)


def attend_backward(queries, key_rows, value_rows, weights, low_weights, grad_context):
    query_count = queries.shape[0]
    key_count = key_rows.shape[0]
    heads_q = queries.reshape(query_count, H, DH)
    heads_k = key_rows.reshape(key_count, H, DH)
    heads_v = value_rows.reshape(key_count, H, DH)
    grad_heads = grad_context.reshape(query_count, H, DH)
    grad_weights = jnp.einsum(
        "qhd,khd->hqk", grad_heads, heads_v, preferred_element_type=jnp.float32
    )
    grad_values = jnp.einsum(
        "hqk,qhd->khd", low_weights, grad_heads, preferred_element_type=jnp.float32
    )
    grad_scores = weights * (grad_weights - jnp.sum(grad_weights * weights, axis=-1, keepdims=True))
    low_scores = to_low(grad_scores)
    grad_queries = jnp.einsum(
        "hqk,khd->qhd", low_scores, heads_k, preferred_element_type=jnp.float32
    )
    grad_keys = jnp.einsum("hqk,qhd->khd", low_scores, heads_q, preferred_element_type=jnp.float32)
    return (
        grad_queries.reshape(query_count, H * DH),
        grad_keys.reshape(key_count, H * DH),
        grad_values.reshape(key_count, H * DH),
        low_scores,
    )


def xor_permute(value, axis, distance):
    count = lax.axis_size(axis)
    return lax.ppermute(value, axis, [(i, i ^ distance) for i in range(count)])


def gather_wide(block):
    count = lax.axis_size("wide")
    if count != 4:
        return [block] + [xor_permute(block, "wide", v) for v in range(1, count)]
    half = block.shape[0] // 2
    first = xor_permute(block, "wide", 1)
    second = xor_permute(block, "wide", 2)
    third = jnp.concatenate(
        [xor_permute(first[:half], "wide", 2), xor_permute(second[half:], "wide", 1)], axis=0
    )
    return [block, first, second, third]


def scatter_wide(parts):
    count = lax.axis_size("wide")
    total = parts[0]
    if count != 4:
        for v in range(1, count):
            total = total + xor_permute(to_low(parts[v]), "wide", v).astype(jnp.float32)
        return total
    half = total.shape[0] // 2
    via_first = xor_permute(to_low(parts[3][:half]), "wide", 1).astype(jnp.float32)
    via_second = xor_permute(to_low(parts[3][half:]), "wide", 2).astype(jnp.float32)
    to_first = jnp.concatenate([parts[1][:half], parts[1][half:] + via_second], axis=0)
    to_second = jnp.concatenate([parts[2][:half] + via_first, parts[2][half:]], axis=0)
    total = total + xor_permute(to_low(to_first), "wide", 1).astype(jnp.float32)
    return total + xor_permute(to_low(to_second), "wide", 2).astype(jnp.float32)


def placed_rows(pieces, place):
    rows = pieces[0].shape[0]
    buffer = jnp.zeros((rows * len(pieces),) + pieces[0].shape[1:], pieces[0].dtype)
    for v, piece in enumerate(pieces):
        start = (place ^ v) * rows
        buffer = lax.dynamic_update_slice(buffer, piece, (start,) + (0,) * (piece.ndim - 1))
    return buffer


MESH = pl.DeviceIdType.MESH
HBM = pl.BlockSpec(memory_space=pl.ANY)
VM = pl.BlockSpec(memory_space=pltpu.VMEM)
SM = pl.BlockSpec(memory_space=pltpu.SMEM)
TILE = 128
VMEM_LIMIT = 62 * 1024 * 1024


def peers_of(count):
    place, core = lax.axis_index("wide"), lax.axis_index("section")
    return [{"wide": place ^ v} for v in range(1, count)] + [{"section": 1 - core}]


def greet(peers):
    barrier = pltpu.get_barrier_semaphore()
    for peer in peers:
        pl.semaphore_signal(barrier, inc=1, device_id=peer, device_id_type=MESH)
    pl.semaphore_wait(barrier, len(peers))


def remote(source, target, sems, index, peer):
    return pltpu.make_async_remote_copy(
        src_ref=source,
        dst_ref=target,
        send_sem=sems[0].at[index],
        recv_sem=sems[1].at[index],
        device_id=peer,
        device_id_type=MESH,
    )


def nt(left, right):
    return lax.dot_general(left, right, (((1,), (1,)), ((), ())), preferred_element_type=jnp.float32)


def tn(left, right):
    return lax.dot_general(left, right, (((0,), (0,)), ((), ())), preferred_element_type=jnp.float32)


class GatherPlane:
    def __init__(self, blocks, sems, base, peers, rows):
        half = split_at(rows)
        rest = rows - half
        first, second = peers[0], peers[1]
        self.direct = [
            remote(blocks.at[0], blocks.at[1], sems, base, first),
            remote(blocks.at[0], blocks.at[2], sems, base + 1, second),
        ]
        self.passed = [
            remote(
                blocks.at[1, pl.ds(0, half)], blocks.at[3, pl.ds(0, half)], sems, base + 2, second
            ),
            remote(
                blocks.at[2, pl.ds(half, rest)],
                blocks.at[3, pl.ds(half, rest)],
                sems,
                base + 3,
                first,
            ),
        ]

    def start(self):
        for copy in self.direct:
            copy.start()

    def arrive(self, index):
        if index < 2:
            self.direct[index].wait_recv()
            self.passed[index].start()
        else:
            for copy in self.passed:
                copy.wait_recv()

    def finish(self):
        for copy in self.direct + self.passed:
            copy.wait_send()


class ScatterPlane:
    def __init__(self, parts, landing, sems, base, peers, rows):
        half = split_at(rows)
        first, second = peers[0], peers[1]
        low, high = pl.ds(0, half), pl.ds(half, rows - half)
        self.parts, self.landing, self.low, self.high = parts, landing, low, high
        self.far = [
            remote(parts.at[3, low], landing.at[0, low], sems, base, first),
            remote(parts.at[3, high], landing.at[0, high], sems, base + 1, second),
        ]
        self.early = [
            remote(parts.at[1, low], landing.at[1, low], sems, base + 2, first),
            remote(parts.at[2, high], landing.at[2, high], sems, base + 3, second),
        ]
        self.late = [
            remote(parts.at[1, high], landing.at[1, high], sems, base + 4, first),
            remote(parts.at[2, low], landing.at[2, low], sems, base + 5, second),
        ]

    def send_early(self, index):
        self.early[index].start()

    def send_far(self):
        for copy in self.far:
            copy.start()

    def pass_on(self):
        low, high = self.low, self.high
        self.far[0].wait_recv()
        self.parts[2, low] = (
            self.parts[2, low].astype(jnp.float32) + self.landing[0, low].astype(jnp.float32)
        ).astype(jnp.bfloat16)
        self.late[1].start()
        self.far[1].wait_recv()
        self.parts[1, high] = (
            self.parts[1, high].astype(jnp.float32) + self.landing[0, high].astype(jnp.float32)
        ).astype(jnp.bfloat16)
        self.late[0].start()

    def total(self):
        for copy in self.early + self.late:
            copy.wait_recv()
        return self.landing[1].astype(jnp.float32) + self.landing[2].astype(jnp.float32)

    def finish(self):
        for copy in self.far + self.early + self.late:
            copy.wait_send()


def rms_rows(residual):
    return lax.rsqrt(jnp.mean(residual * residual, axis=-1, keepdims=True) + EPSILON)


def norm_pull(residual, gain_row, grad_normed):
    scale = rms_rows(residual)
    unit = residual * scale
    inner = grad_normed * gain_row
    grad_residual = scale * (inner - unit * jnp.mean(inner * unit, axis=-1, keepdims=True))
    return grad_residual, jnp.sum(grad_normed * unit, axis=0, keepdims=True)


def token_rows_at_once(wide, rows):
    return rows if rows >= 2 * TILE else wide * rows


def block_at(blocks, group, count):
    if count == blocks.shape[1]:
        return blocks[group]
    return blocks[...].reshape(count, blocks.shape[2])


def before_group(gather, group, groups):
    if groups == 1:
        for index in range(3):
            gather.arrive(index)
        return
    for index in range(3):

        @pl.when(group == index + 1)
        def _():
            gather.arrive(index)


def put_parts(acc, parts, own_ref, group, groups, rows):
    if groups == 1:
        own_ref[...] = acc[pl.ds(0, rows)]
        for v in range(1, parts.shape[0]):
            parts[v] = acc[pl.ds(v * rows, rows)].astype(parts.dtype)
        return

    @pl.when(group == 0)
    def _():
        own_ref[...] = acc[...]

    @pl.when(group > 0)
    def _():
        parts[group] = acc[...].astype(parts.dtype)


def after_group(scatter, group, groups):
    if groups == 1:
        scatter.send_far()
        scatter.send_early(0)
        scatter.send_early(1)
        return

    @pl.when(group == 1)
    def _():
        scatter.send_early(0)

    @pl.when(group == 2)
    def _():
        scatter.send_early(1)

    @pl.when(group == 3)
    def _():
        scatter.send_far()


class Reshard:
    def __init__(self, blocks, pieces, direct, sems, base, peers):
        row = lax.axis_index("rows")
        shared = (blocks[0].shape[0] - direct) // 2
        mine = pl.ds(direct + row % 2 * shared, shared)
        other = {"rows": row ^ 1}
        self.shared, self.direct, self.passed = [], [], []
        for v, (block, piece) in enumerate(zip(blocks, pieces)):
            at, peer, first = base + 3 * v, peers[v], pl.ds(0, direct)
            self.shared.append(remote(block.at[mine], piece.at[mine], sems, at, peer))
            self.passed.append(remote(piece.at[mine], piece.at[mine], sems, at + 1, other))
            if direct:
                self.direct.append(remote(block.at[first], piece.at[first], sems, at + 2, peer))

    def start(self):
        for copy in self.shared:
            copy.start()

    def pass_on(self):
        for copy in self.direct:
            copy.start()
        for copy, after in zip(self.shared, self.passed):
            copy.wait_recv()
            after.start()

    def finish(self):
        for copy in self.direct + self.passed:
            copy.wait()
        for copy in self.shared:
            copy.wait_send()


class ReduceRows:
    def __init__(self, source_in, source_out, in_buf, in_land, out_buf, out_land, sems, base, local_sem, local_base):
        row = lax.axis_index("rows")
        near, far = {"rows": row ^ 1}, {"rows": row ^ 2}
        self.bufs, self.lands, self.first, self.second = [], [], [], []
        views = [
            (lambda ref, i, part=part: ref.at[i, part], source_in, in_buf, in_land)
            for part in range(2)
        ] + [(lambda ref, i: ref.at[i], source_out, out_buf, out_land)]
        for index, (view, source, buf, land) in enumerate(views):
            at = base + 3 * index
            self.first.append(
                [
                    remote(view(source, row ^ 1), view(land, 0), sems, at, near),
                    remote(view(source, row ^ 3), view(land, 1), sems, at + 1, near),
                ]
            )
            self.second.append(remote(view(buf, 1), view(land, 2), sems, at + 2, far))
            self.bufs.append([view(buf, 0), view(buf, 1)])
            self.lands.append([view(land, i) for i in range(3)])
        self.loads = [
            pltpu.make_async_copy(source.at[place], buf.at[i], local_sem.at[local_base + 2 * j + i])
            for j, (source, buf) in enumerate(((source_in, in_buf), (source_out, out_buf)))
            for i, place in enumerate((row, row ^ 2))
        ]

    def start(self):
        for copy in self.first[0]:
            copy.start()
        for load in self.loads:
            load.start()

    def loaded(self):
        for load in self.loads:
            load.wait()

    def add(self, index, which, land):
        ref = self.bufs[index][which]
        ref[...] = (
            ref[...].astype(jnp.float32) + self.lands[index][land][...].astype(jnp.float32)
        ).astype(jnp.bfloat16)

    def turn(self, index):
        for copy in self.first[index]:
            copy.wait_recv()
        for copy in self.first[index + 1] if index < 2 else ():
            copy.start()
        self.add(index, 1, 1)
        self.second[index].start()
        self.add(index, 0, 0)

    def close(self, index):
        self.second[index].wait_recv()
        self.add(index, 0, 2)

    def finish(self):
        for pair, copy in zip(self.first, self.second):
            for each in pair:
                each.wait_send()
            copy.wait_send()


def reduce_rows_scratch(units):
    low = jnp.bfloat16
    return [
        pltpu.VMEM((2, 2, D, TILE), low),
        pltpu.VMEM((3, 2, D, TILE), low),
        pltpu.VMEM((2, units, D), low),
        pltpu.VMEM((3, units, D), low),
    ]


def weight_tiles(weight, half, part):
    lanes = pl.ds(part * TILE, TILE)
    return jnp.concatenate(
        [weight[half, quarter, :, lanes] for quarter in range(weight.shape[1])], axis=1
    )


def weight_copies(pieces, weight, sems, base, local_sem, local_base, sibling):
    core, place = lax.axis_index("section"), lax.axis_index("wide")
    wide, depth = lax.axis_size("wide"), pieces[0].shape[1]
    loads, swaps = [], []
    for index, piece in enumerate(pieces):
        v = index if index < wide else index - wide + 1
        place_rows = pl.ds(pl.multiple_of((place ^ v) * depth, 16), depth)
        target = weight.at[core, :, place_rows]
        quarters = piece.shape[0]
        if quarters < weight.shape[1]:
            part = lax.axis_index("rows") % 2
            part = part if index < wide else 1 - part
            target = weight.at[core, pl.ds(part * quarters, quarters), place_rows]
        loads.append(pltpu.make_async_copy(piece, target, local_sem.at[local_base + index]))
        swaps.append(remote(piece, target, sems, base + index, sibling))
    return loads, swaps


def gate_slopes(gate, up):
    square = gate * gate
    tanh = jnp.tanh(GELU_A * gate * (1.0 + GELU_B * square))
    upper = 0.5 * (1.0 + tanh)
    slope = upper + 0.5 * gate * (1.0 - tanh * tanh) * (GELU_A + 3.0 * GELU_A * GELU_B * square)
    return gate * upper, slope


def ffn_forward_kernel(wide, carried, count, gain_at, x_ref, gain_ref, *refs):
    gain_ref = gain_ref.at[pl.ds(gain_at, 1)]
    pieces, refs = refs[:count], refs[count:]
    if carried:
        dec_half, dec_blocks, refs = refs[0], refs[1:wide], refs[wide:]
    y_ref, at_out, pre_out, hidden_out, weight_out = refs[:5]
    refs = refs[5:]
    if carried:
        dec_attn, dec_pieces, refs = refs[0], refs[1:wide], refs[wide:]
    blocks, at, pre, hidden, weight, parts, landing, acc, send_sem, recv_sem, local_sem = refs[:11]
    rows = x_ref.shape[0]
    depth = pieces[0].shape[1]
    span = weight.shape[1] * TILE
    core, place = lax.axis_index("section"), lax.axis_index("wide")
    peers = peers_of(wide)
    sems = (send_sem, recv_sem)
    greet(peers + ([{"rows": lax.axis_index("rows") ^ 1}] if carried else []))
    residual = x_ref[...]
    blocks[0] = (residual * rms_rows(residual) * gain_ref[...]).astype(jnp.bfloat16)
    gather = GatherPlane(blocks, sems, 0, peers, rows)
    gather.start()
    loads, swaps = weight_copies(pieces, weight, sems, 10, local_sem, 12, peers[-1])
    for load, swap in zip(loads, swaps):
        load.start()
        swap.start()
    scatter = ScatterPlane(parts, landing, sems, 4, peers, rows)
    if carried:
        held, far_held, whole = refs[11:14]
        other = {"rows": lax.axis_index("rows") ^ 1}
        passed = [
            remote(block, piece, sems, 24 + v, other)
            for v, (block, piece) in enumerate(zip(dec_blocks, dec_pieces))
        ]
        for copy in passed:
            copy.start()
        size = held.shape[1]
        rest = depth - size
        part = lax.axis_index("rows") % 2
        dec_gather = GatherPlane(held, sems, 27, peers, size)
        mine = pl.ds(pl.multiple_of(part * rest, 16), size)
        fetch = pltpu.make_async_copy(dec_half.at[mine], held.at[0], local_sem.at[7])
        fetch.start()
        stores, gives, crossings = [], [], []

        def place_block(source, v, start, index):
            target = dec_attn.at[
                core, pl.ds(pl.multiple_of((place ^ v) * depth + start, 16), source.shape[0])
            ]
            stores.append(pltpu.make_async_copy(source, target, local_sem.at[19 + index]))
            gives.append(remote(source, target, sems, 35 + index, peers[-1]))

        place_block(whole, 0, 0, 0)
        for v in range(1, wide):
            place_block(held.at[v], v, part * rest, v)
        for v in range(1, wide):
            sent = pl.ds(pl.multiple_of(part * (size - rest), 16), rest)
            crossings.append(remote(held.at[v, sent], far_held.at[v - 1], sems, 41 + v, other))
            place_block(far_held.at[v - 1], v, (1 - part) * size, wide + v - 1)
        whole_fetch = pltpu.make_async_copy(dec_half, whole, local_sem.at[8])
        whole_fetch.start()
    count = token_rows_at_once(wide, rows)
    groups = wide * rows // count

    @pl.loop(0, groups)
    def _(group):
        before_group(gather, group, groups)

        @pl.when(group == 0)
        def _():
            for load in loads:
                load.wait()

        token_rows = pl.ds(pl.multiple_of(group * count, count), count)

        @pl.loop(0, 2)
        def _(step):
            @pl.when((group == 0) & (step == 1))
            def _():
                for swap in swaps:
                    swap.wait_recv()

            half = lax.rem(core + step, 2)
            block = block_at(blocks, group, count)
            gate = matmul(block, weight_tiles(weight, half, 0))
            up = matmul(block, weight_tiles(weight, half, 1))
            pre[half, token_rows, pl.ds(0, span)] = gate.astype(jnp.bfloat16)
            pre[half, token_rows, pl.ds(span, span)] = up.astype(jnp.bfloat16)
            low = gated(gate, up).astype(jnp.bfloat16)
            hidden[half, token_rows, :] = low
            out = nt(low, weight_tiles(weight, half, 2))
            acc[...] = jnp.where(step == 0, 0.0, acc[...]) + out

        put_parts(acc, parts, y_ref, group, groups, rows)
        after_group(scatter, group, groups)
        if carried:

            @pl.when(group == 0)
            def _():
                whole_fetch.wait()
                stores[0].start()
                gives[0].start()

            @pl.when(group == 1)
            def _():
                fetch.wait()
                dec_gather.start()

    y_ref[...] += residual
    copies = [
        pltpu.make_async_copy(pre, pre_out, local_sem.at[4]),
        pltpu.make_async_copy(weight, weight_out, local_sem.at[5]),
    ]
    for copy in copies:
        copy.start()
    if carried:
        for v in range(1, 3):
            dec_gather.arrive(v - 1)
            crossings[v - 1].start()
            stores[v].start()
            gives[v].start()
    scatter.pass_on()

    @pl.loop(0, groups)
    def _(group):
        lanes = pl.ds(pl.multiple_of(group * count, count), count)
        at[:, lanes] = block_at(blocks, group, count).T

    last = pltpu.make_async_copy(at, at_out, local_sem.at[6])
    last.start()
    copies.append(last)
    if carried:
        dec_gather.arrive(2)
        crossings[2].start()
        stores[3].start()
        gives[3].start()

    @pl.loop(0, 2 * groups)
    def _(step):
        half, group = lax.rem(step, 2), step // 2
        lanes = pl.ds(pl.multiple_of(group * count, count), count)
        hidden_out[half, :, lanes] = hidden[half, lanes, :].T

    y_ref[...] += scatter.total()
    if carried:
        for v in range(1, wide):
            crossings[v - 1].wait()
            stores[wide + v - 1].start()
            gives[wide + v - 1].start()
        for store, give in zip(stores, gives):
            store.wait()
            give.wait()
        dec_gather.finish()
        for copy in passed:
            copy.wait()
    for copy in copies:
        copy.wait()
    gather.finish()
    scatter.finish()
    for swap in swaps:
        swap.wait_send()


def ffn_forward_call(wide, residual, gain_row, pieces, call_id, carried=()):
    gain_row, gain_at = gain_row
    rows = residual.shape[0]
    total = rows * wide
    quarters, _, columns = pieces[0].shape
    span = quarters * TILE
    low = jnp.bfloat16
    extra_out, extra_scratch = [], []
    if carried:
        depth, attn_columns = carried[0].shape
        extra_out = [jax.ShapeDtypeStruct((2, D, attn_columns), low)] + [
            jax.ShapeDtypeStruct(each.shape, low) for each in carried[1:]
        ]
        size = split_at(depth)
        extra_scratch = [
            pltpu.VMEM((wide, size, attn_columns), low),
            pltpu.VMEM((wide - 1, depth - size, attn_columns), low),
            pltpu.VMEM((depth, attn_columns), low),
        ]
    return pl.pallas_call(
        lambda *refs: ffn_forward_kernel(wide, bool(carried), len(pieces), gain_at, *refs),
        out_shape=[
            jax.ShapeDtypeStruct((rows, D), jnp.float32),
            jax.ShapeDtypeStruct((D, total), low),
            jax.ShapeDtypeStruct((2, total, 2 * span), low),
            jax.ShapeDtypeStruct((2, span, total), low),
            jax.ShapeDtypeStruct((2, quarters, D, columns), low),
        ]
        + extra_out,
        in_specs=[VM, VM] + [HBM] * (len(pieces) + len(carried)),
        out_specs=[VM, HBM, HBM, VM, HBM] + [HBM] * len(extra_out),
        scratch_shapes=[
            pltpu.VMEM((wide, rows, D), low),
            pltpu.VMEM((D, total), low),
            pltpu.VMEM((2, total, 2 * span), low),
            pltpu.VMEM((2, total, span), low),
            pltpu.VMEM((2, quarters, D, columns), low),
            pltpu.VMEM((wide, rows, D), low),
            pltpu.VMEM((3, rows, D), low),
            pltpu.VMEM((token_rows_at_once(wide, rows), D), jnp.float32),
            pltpu.SemaphoreType.DMA((45,)),
            pltpu.SemaphoreType.DMA((45,)),
            pltpu.SemaphoreType.DMA((26,)),
        ]
        + extra_scratch,
        compiler_params=pltpu.CompilerParams(
            collective_id=call_id, has_side_effects=True, vmem_limit_bytes=VMEM_LIMIT
        ),
        name="ffn_forward_%d" % rows,
    )(residual, gain_row, *pieces, *carried)


def ffn_backward_kernel(
    wide, rows_axis, gain_at, x_ref, gains_ref, at_in, pre_in, hidden_in, weight_in, *refs
):
    gain_ref = gains_ref.at[pl.ds(gain_at, 1)]
    (
        ready_in,
        ready_out,
        enc_attn,
        dec_attn,
        dec_gains,
        g2_ref,
        x2_ref,
        y1_ref,
        kv_ref,
        query_ref,
        weights_ref,
        gx_ref,
        gain_out,
        grad_in,
        grad_out,
        sum_in,
        sum_out,
        gy_ref,
        final_out,
        cross_gain,
        kv_grad,
        query_grad,
    ) = refs[:22]
    refs = refs[22:]
    (
        blocks,
        at,
        pre,
        hidden,
        weight,
        parts,
        landing,
        acc,
        give_in,
        give_out,
        got_in,
        got_out,
        send_sem,
        recv_sem,
        local_sem,
    ) = refs[:15]
    rows = x_ref.shape[0]
    span = weight.shape[1] * TILE
    units = FF // (wide * rows_axis * 2)
    core, row = lax.axis_index("section"), lax.axis_index("rows")
    peers = peers_of(wide)
    sems = (send_sem, recv_sem)
    greet(peers + [{"rows": row ^ 1}, {"rows": row ^ 2}])
    loads = [
        pltpu.make_async_copy(weight_in, weight, local_sem.at[0]),
        pltpu.make_async_copy(pre_in, pre, local_sem.at[1]),
        pltpu.make_async_copy(hidden_in, hidden, local_sem.at[2]),
        pltpu.make_async_copy(at_in, at, local_sem.at[3]),
    ]
    line = ReduceRows(ready_in, ready_out, *refs[15:19], sems, 12, local_sem, 6)
    line.start()
    g_ref, context_grad = refs[19:21]
    fetches = [
        pltpu.make_async_copy(
            dec_attn.at[1, :, pl.ds(HD, 2 * HD)], at.at[:, pl.ds(0, 2 * HD)], local_sem.at[10]
        )
    ]
    for tile in range(2 * HD // TILE):
        fetches.append(
            pltpu.make_async_copy(
                enc_attn.at[1, :, pl.ds(HD + tile * TILE, TILE)],
                give_in.at[tile // 2, tile % 2],
                local_sem.at[11 + tile],
            )
        )
    for fetch in fetches:
        fetch.start()
    for load in loads[:3]:
        load.start()
    for fetch in fetches:
        fetch.wait()
    cross_backward_rows(
        g2_ref,
        x2_ref,
        gains_ref,
        Tiles(give_in, 0),
        Tiles(give_in, HD // TILE),
        y1_ref,
        dec_gains,
        at.at[:, pl.ds(0, HD)],
        at.at[:, pl.ds(HD, HD)],
        kv_ref,
        query_ref,
        weights_ref,
        g_ref,
        gy_ref,
        final_out,
        cross_gain,
        kv_grad,
        query_grad,
        context_grad,
    )
    blocks[0] = g_ref[...].astype(jnp.bfloat16)
    gather = GatherPlane(blocks, sems, 0, peers, rows)
    gather.start()
    loads[3].start()
    scatter = ScatterPlane(parts, landing, sems, 4, peers, rows)
    loads[0].wait()
    loads[1].wait()
    count = token_rows_at_once(wide, rows)
    groups = wide * rows // count

    @pl.loop(0, groups)
    def _(group):
        @pl.when(group == 1)
        def _():
            line.loaded()
            line.turn(0)

        @pl.when(group == 3)
        def _():
            line.turn(1)

        before_group(gather, group, groups)
        token_rows = pl.ds(pl.multiple_of(group * count, count), count)

        @pl.loop(0, 2)
        def _(half):
            block = block_at(blocks, group, count)
            grad_hidden = matmul(block, weight_tiles(weight, half, 2))
            gate = pre[half, token_rows, pl.ds(0, span)].astype(jnp.float32)
            up = pre[half, token_rows, pl.ds(span, span)].astype(jnp.float32)
            value, slope = gate_slopes(gate, up)
            low_gate = (grad_hidden * up * slope).astype(jnp.bfloat16)
            low_up = (grad_hidden * value).astype(jnp.bfloat16)
            pre[half, token_rows, pl.ds(0, span)] = low_gate
            pre[half, token_rows, pl.ds(span, span)] = low_up
            out = nt(low_gate, weight_tiles(weight, half, 0)) + nt(
                low_up, weight_tiles(weight, half, 1)
            )
            acc[...] = jnp.where(half == 0, 0.0, acc[...]) + out

        put_parts(acc, parts, gx_ref, group, groups, rows)
        after_group(scatter, group, groups)
    loads[2].wait()
    loads[3].wait()
    chunk = 2 * TILE
    swap_out = remote(give_out, got_out, sems, 11, peers[-1])
    swap_in = remote(give_in, got_in, sems, 10, peers[-1])
    store_in = pltpu.make_async_copy(got_in, grad_in, local_sem.at[4])
    store_out = pltpu.make_async_copy(got_out, grad_out, local_sem.at[5])

    @pl.loop(0, 2 * rows_axis)
    def _(step):
        half = jnp.where(step < rows_axis, 1 - core, core)
        index = lax.rem(step, rows_axis)
        columns = pl.ds(pl.multiple_of(index * chunk, chunk), chunk)
        total = matmul(at[...], pre[half, :, columns])

        @pl.when(step < rows_axis)
        def _():
            for part in range(2):
                give_in[index, part] = total[:, part * TILE : (part + 1) * TILE].astype(
                    jnp.bfloat16
                )

        @pl.when(step == rows_axis - 1)
        def _():
            swap_in.start()
            scatter.pass_on()

        @pl.when(step == rows_axis)
        def _():
            swap_in.wait_recv()

        @pl.when(step >= rows_axis)
        def _():
            for part in range(2):
                got_in[index, part] = (
                    total[:, part * TILE : (part + 1) * TILE]
                    + got_in[index, part].astype(jnp.float32)
                ).astype(jnp.bfloat16)

    store_in.start()
    line.turn(2)

    @pl.loop(0, 2)
    def _(step):
        half = lax.rem(core + 1 + step, 2)
        total = matmul(hidden[half], blocks[...].reshape(wide * rows, D))

        @pl.when(step == 0)
        def _():
            for index in range(rows_axis):
                give_out[index] = total[index * TILE : index * TILE + units].astype(jnp.bfloat16)
            swap_out.start()

        @pl.when(step == 1)
        def _():
            swap_out.wait_recv()
            for index in range(rows_axis):
                got_out[index] = (
                    total[index * TILE : index * TILE + units]
                    + got_out[index].astype(jnp.float32)
                ).astype(jnp.bfloat16)
            store_out.start()

    total = gx_ref[...] + scatter.total()
    grad_residual, grad_gain = norm_pull(x_ref[...], gain_ref[...], total)
    gx_ref[...] = g_ref[...].astype(jnp.float32) + grad_residual
    gain_out[...] = grad_gain
    for index in range(3):
        line.close(index)
    stores = [
        pltpu.make_async_copy(refs[15].at[0], sum_in, local_sem.at[6]),
        pltpu.make_async_copy(refs[17].at[0], sum_out, local_sem.at[7]),
    ]
    for store in stores:
        store.start()
    for store in stores:
        store.wait()
    line.finish()
    store_in.wait()
    store_out.wait()
    swap_in.wait_send()
    swap_out.wait_send()
    gather.finish()
    scatter.finish()


def ffn_both_kernel(wide, rows_axis, gain_at, x_ref, cot_ref, gain_ref, *refs):
    pieces, refs = refs[: 2 * wide - 1], refs[2 * wide - 1 :]
    gain_ref = gain_ref.at[pl.ds(gain_at, 1)]
    y_ref, gx_ref, gain_out, grad_in, grad_out = refs[:5]
    (
        blocks,
        cots,
        weight,
        pre,
        hidden,
        acc,
        grad_acc,
        parts,
        grad_parts,
        landing,
        grad_landing,
        give_in,
        give_out,
        got_in,
        got_out,
        send_sem,
        recv_sem,
        local_sem,
    ) = refs[5:]
    rows = x_ref.shape[0]
    total_rows = wide * rows
    span = weight.shape[1] * TILE
    units = FF // (wide * rows_axis * 2)
    core = lax.axis_index("section")
    peers = peers_of(wide)
    sems = (send_sem, recv_sem)
    low = jnp.bfloat16
    loads, swaps = weight_copies(pieces, weight, sems, 20, local_sem, 2, peers[-1])
    greet(peers)
    residual = x_ref[...]
    blocks[0] = (residual * rms_rows(residual) * gain_ref[...]).astype(low)
    cots[0] = cot_ref[core]
    gather = GatherPlane(blocks, sems, 0, peers, rows)
    cot_gather = GatherPlane(cots, sems, 4, peers, rows)
    gather.start()
    cot_gather.start()
    for load, swap in zip(loads, swaps):
        load.start()
        swap.start()
    for index in range(3):
        gather.arrive(index)
        cot_gather.arrive(index)
    for load in loads:
        load.wait()

    @pl.loop(0, 2)
    def _(step):
        @pl.when(step == 1)
        def _():
            for swap in swaps:
                swap.wait_recv()

        half = lax.rem(core + step, 2)
        block = blocks[...].reshape(total_rows, D)
        gate = matmul(block, weight_tiles(weight, half, 0))
        up = matmul(block, weight_tiles(weight, half, 1))
        value, slope = gate_slopes(gate, up)
        low_hidden = (value * up).astype(low)
        hidden[half] = low_hidden
        grad_hidden = matmul(cots[...].reshape(total_rows, D), weight_tiles(weight, half, 2))
        low_gate = (grad_hidden * up * slope).astype(low)
        low_up = (grad_hidden * value).astype(low)
        pre[half, :, pl.ds(0, span)] = low_gate
        pre[half, :, pl.ds(span, span)] = low_up
        grad = nt(low_gate, weight_tiles(weight, half, 0)) + nt(
            low_up, weight_tiles(weight, half, 1)
        )
        grad_acc[...] = jnp.where(step == 0, 0.0, grad_acc[...]) + grad
        out = nt(low_hidden, weight_tiles(weight, half, 2))
        acc[...] = jnp.where(step == 0, 0.0, acc[...]) + out

    grad_scatter = ScatterPlane(grad_parts, grad_landing, sems, 8, peers, rows)
    scatter = ScatterPlane(parts, landing, sems, 14, peers, rows)
    put_parts(grad_acc, grad_parts, gx_ref, 0, 1, rows)
    after_group(grad_scatter, 0, 1)
    put_parts(acc, parts, y_ref, 0, 1, rows)
    after_group(scatter, 0, 1)
    swap_in = remote(give_in, got_in, sems, 27, peers[-1])
    swap_out = remote(give_out, got_out, sems, 28, peers[-1])
    store_in = pltpu.make_async_copy(got_in, grad_in, local_sem.at[0])
    store_out = pltpu.make_async_copy(got_out, grad_out, local_sem.at[1])
    chunk = 2 * TILE

    @pl.loop(0, 2 * rows_axis)
    def _(step):
        half = jnp.where(step < rows_axis, 1 - core, core)
        index = lax.rem(step, rows_axis)
        columns = pl.ds(pl.multiple_of(index * chunk, chunk), chunk)
        total = tn(blocks[...].reshape(total_rows, D), pre[half, :, columns])

        @pl.when(step < rows_axis)
        def _():
            for part in range(2):
                give_in[index, part] = total[:, part * TILE : (part + 1) * TILE].astype(low)

        @pl.when(step == rows_axis - 1)
        def _():
            swap_in.start()
            grad_scatter.pass_on()
            scatter.pass_on()

        @pl.when(step == rows_axis)
        def _():
            swap_in.wait_recv()

        @pl.when(step >= rows_axis)
        def _():
            for part in range(2):
                got_in[index, part] = (
                    total[:, part * TILE : (part + 1) * TILE]
                    + got_in[index, part].astype(jnp.float32)
                ).astype(low)

    store_in.start()

    @pl.loop(0, 2)
    def _(step):
        half = lax.rem(core + 1 + step, 2)
        total = tn(hidden[half], cots[...].reshape(total_rows, D))

        @pl.when(step == 0)
        def _():
            for index in range(rows_axis):
                give_out[index] = total[index * TILE : index * TILE + units].astype(low)
            swap_out.start()

        @pl.when(step == 1)
        def _():
            swap_out.wait_recv()
            for index in range(rows_axis):
                got_out[index] = (
                    total[index * TILE : index * TILE + units]
                    + got_out[index].astype(jnp.float32)
                ).astype(low)
            store_out.start()

    grad_residual, gain_out[...] = norm_pull(
        x_ref[...], gain_ref[...], gx_ref[...] + grad_scatter.total()
    )
    gx_ref[...] = cot_ref[core].astype(jnp.float32) + grad_residual
    y_ref[...] = y_ref[...] + residual + scatter.total()
    store_in.wait()
    store_out.wait()
    swap_in.wait_send()
    swap_out.wait_send()
    for each in (gather, cot_gather, grad_scatter, scatter):
        each.finish()
    for swap in swaps:
        swap.wait_send()


def ffn_both_call(wide, rows_axis, residual, cot, gain_row, pieces, call_id):
    gain_row, gain_at = gain_row
    rows = residual.shape[0]
    total = wide * rows
    quarters, _, columns = pieces[0].shape
    span = quarters * TILE
    low = jnp.bfloat16
    units = FF // (wide * rows_axis * 2)
    share_in = (rows_axis, 2, D, TILE)
    share_out = (rows_axis, units, D)
    return pl.pallas_call(
        lambda *refs: ffn_both_kernel(wide, rows_axis, gain_at, *refs),
        out_shape=[
            jax.ShapeDtypeStruct((rows, D), jnp.float32),
            jax.ShapeDtypeStruct((rows, D), jnp.float32),
            jax.ShapeDtypeStruct((1, D), jnp.float32),
            jax.ShapeDtypeStruct(share_in, low),
            jax.ShapeDtypeStruct(share_out, low),
        ],
        in_specs=[VM, VM, VM] + [HBM] * len(pieces),
        out_specs=[VM, VM, VM, HBM, HBM],
        scratch_shapes=[
            pltpu.VMEM((wide, rows, D), low),
            pltpu.VMEM((wide, rows, D), low),
            pltpu.VMEM((2, quarters, D, columns), low),
            pltpu.VMEM((2, total, 2 * span), low),
            pltpu.VMEM((2, total, span), low),
            pltpu.VMEM((total, D), jnp.float32),
            pltpu.VMEM((total, D), jnp.float32),
            pltpu.VMEM((wide, rows, D), low),
            pltpu.VMEM((wide, rows, D), low),
            pltpu.VMEM((3, rows, D), low),
            pltpu.VMEM((3, rows, D), low),
            pltpu.VMEM(share_in, low),
            pltpu.VMEM(share_out, low),
            pltpu.VMEM(share_in, low),
            pltpu.VMEM(share_out, low),
            pltpu.SemaphoreType.DMA((29,)),
            pltpu.SemaphoreType.DMA((29,)),
            pltpu.SemaphoreType.DMA((9,)),
        ],
        compiler_params=pltpu.CompilerParams(
            collective_id=call_id, has_side_effects=True, vmem_limit_bytes=VMEM_LIMIT
        ),
        name="ffn_both_%d" % rows,
    )(residual, cot, gain_row, *pieces)


GELU_A = float(np.sqrt(2.0 / np.pi))
GELU_B = 0.044715


class Tiles:
    def __init__(self, ref, first):
        self.ref, self.first = ref, first

    def __getitem__(self, _):
        tiles = range(self.first, self.first + HD // TILE)
        return jnp.concatenate([self.ref[tile // 2, tile % 2] for tile in tiles], axis=1)


def ffn_backward_call(wide, rows_axis, residual, gain_row, kept, call_id, carried, crossed):
    gain_row, gain_at = gain_row
    at, pre, hidden, weight = kept
    rows = residual.shape[0]
    target_rows = crossed[3].shape[0]
    low = jnp.bfloat16
    units = FF // (wide * rows_axis * 2)
    share_in = (rows_axis, 2, D, TILE)
    share_out = (rows_axis, units, D)
    line_of = jax.ShapeDtypeStruct((1, D), jnp.float32)
    return pl.pallas_call(
        lambda *refs: ffn_backward_kernel(wide, rows_axis, gain_at, *refs),
        out_shape=[
            jax.ShapeDtypeStruct((rows, D), jnp.float32),
            line_of,
            jax.ShapeDtypeStruct(share_in, low),
            jax.ShapeDtypeStruct(share_out, low),
        ]
        + [jax.ShapeDtypeStruct(each.shape[1:], low) for each in carried]
        + [
            jax.ShapeDtypeStruct((target_rows, D), jnp.float32),
            line_of,
            line_of,
            jax.ShapeDtypeStruct((rows, 2 * HD), low),
            jax.ShapeDtypeStruct((target_rows, HD), low),
        ],
        in_specs=[VM, VM] + [HBM] * 8 + [VM] * 7,
        out_specs=[VM, VM, HBM, HBM, HBM, HBM] + [VM] * 5,
        scratch_shapes=[
            pltpu.VMEM((wide, rows, D), low),
            pltpu.VMEM(at.shape, low),
            pltpu.VMEM(pre.shape, low),
            pltpu.VMEM(hidden.shape, low),
            pltpu.VMEM(weight.shape, low),
            pltpu.VMEM((wide, rows, D), low),
            pltpu.VMEM((3, rows, D), low),
            pltpu.VMEM((token_rows_at_once(wide, rows), D), jnp.float32),
            pltpu.VMEM(share_in, low),
            pltpu.VMEM(share_out, low),
            pltpu.VMEM(share_in, low),
            pltpu.VMEM(share_out, low),
            pltpu.SemaphoreType.DMA((21,)),
            pltpu.SemaphoreType.DMA((21,)),
            pltpu.SemaphoreType.DMA((17,)),
        ]
        + reduce_rows_scratch(units)
        + [pltpu.VMEM((rows, D), jnp.float32), pltpu.VMEM((target_rows, HD), low)],
        compiler_params=pltpu.CompilerParams(
            collective_id=call_id, has_side_effects=True, vmem_limit_bytes=VMEM_LIMIT
        ),
        name="ffn_backward_%d" % rows,
    )(residual, gain_row, at, pre, hidden, weight, *carried, *crossed)


def start_weights_kernel(
    wide, rows, win_in, wout_in, cin_in, cout_in, ffn_in, ffn_out, gains, biases, enc_hot, dec_hot,
    attn_ref, dec_half, enc_gains, dec_gains, enc_bias, dec_bias, *refs
):
    enc, dec = refs[:wide], refs[wide : 2 * wide]
    held, blocks, spare, in_ref, out_ref, ffn, enc_row, dec_row, send_sem, recv_sem, local_sem = refs[2 * wide :]
    core, place = lax.axis_index("section"), lax.axis_index("wide")
    peers = peers_of(wide)
    sibling = peers[-1]
    sems = (send_sem, recv_sem)
    depth = blocks.shape[1]
    big = [
        pltpu.make_async_copy(ffn_in.at[0], in_ref, local_sem.at[4]),
        pltpu.make_async_copy(ffn_out, out_ref, local_sem.at[5]),
    ]
    packs = [
        pltpu.make_async_copy(each, held.at[:, pl.ds(i * HD, HD)], local_sem.at[1 + i])
        for i, each in enumerate((wout_in, cin_in.at[0], cout_in.at[0]))
    ]
    for pack in packs:
        pack.start()
    greet(peers)
    for pack in packs:
        pack.wait()

    @pl.when(core == 0)
    def _():
        keep = pltpu.make_async_copy(win_in.at[0], blocks.at[0], local_sem.at[0])
        keep.start()
        give = remote(held, blocks.at[0], sems, 0, sibling)
        give.start()
        remote(win_in.at[0], spare, sems, 1, sibling).wait_recv()
        keep.wait()

    @pl.when(core == 1)
    def _():
        keep = pltpu.make_async_copy(held, spare, local_sem.at[0])
        keep.start()
        give = remote(win_in.at[0], spare, sems, 1, sibling)
        give.start()
        remote(held, blocks.at[0], sems, 0, sibling).wait_recv()
        keep.wait()

    gather = GatherPlane(blocks, sems, 2, peers, depth)
    gather.start()
    for load in big:
        load.start()
    dec_copy = pltpu.make_async_copy(spare, dec_half, local_sem.at[0])
    dec_copy.start()
    stores, gives = [], []
    for v in range(wide):
        rows_of = pl.ds(pl.multiple_of((place ^ v) * depth, 16), depth)
        stores.append(
            pltpu.make_async_copy(blocks.at[v], attn_ref.at[core, rows_of], local_sem.at[6 + v])
        )
        gives.append(remote(blocks.at[v], attn_ref.at[core, rows_of], sems, 6 + v, sibling))
    stores[0].start()
    gives[0].start()
    for load in big:
        load.wait()
    units = FF // (wide * rows * 2)
    per_row = FF // rows
    row_ids = lax.broadcasted_iota(jnp.int32, (2 * TILE, TILE), 0)
    lane_ids = lax.broadcasted_iota(jnp.int32, (2 * TILE, TILE), 1)
    def prepare(index):
        target, half = index // 2, index % 2
        offset = index * units
        start, shift = offset // TILE * TILE, offset % TILE
        picks = ((row_ids == lane_ids + shift) & (lane_ids < units)).astype(jnp.bfloat16)
        window = min(2 * TILE, per_row - start)
        picks = picks[:window]
        for part in range(3):
            for row in range(rows):
                if part < 2:
                    source = in_ref[:, pl.ds(part * FF + row * per_row + start, window)]
                else:
                    source = out_ref[:, pl.ds(row * per_row + start, window)]
                tile = matmul(source, picks)
                ffn[half, target ^ place, row, :, pl.ds(part * TILE, TILE)] = tile.astype(
                    jnp.bfloat16
                )

    lines = 10 + 2 * wide
    gain_moves = [remote(gains, target, sems, lines, sibling) for target in (enc_gains, dec_gains)]
    line_moves = [
        remote(row_ref, row_ref, sems, lines + 1, sibling) for row_ref in (enc_row, dec_row)
    ]
    for own, (gain_ref, row_ref, hot) in enumerate(
        ((enc_gains, enc_row, enc_hot), (dec_gains, dec_row, dec_hot))
    ):

        @pl.when(core == own)
        def _():
            gain_ref[...] = gains[...]
            row_ref[pl.ds(0, H), :] = jnp.dot(
                biases[...], hot[...], precision=HIGHEST, preferred_element_type=jnp.float32
            )
            gain_moves[own].start()
            line_moves[own].start()

    for index in range(2 * wide):
        prepare(index)
    for own in range(2):

        @pl.when(core == own)
        def _():
            gain_moves[1 - own].wait_recv()
            line_moves[1 - own].wait_recv()
            gain_moves[own].wait_send()
            line_moves[own].wait_send()

    bias_rows(enc_row, enc_bias)
    bias_rows(dec_row, dec_bias)

    def move(outs, base):
        for v in range(wide):
            pltpu.make_async_copy(ffn.at[core, v], outs[v], local_sem.at[10 + v]).start()
            remote(ffn.at[1 - core, v], outs[v], sems, base + v, sibling).start()

    def settle(outs, base):
        for v in range(wide):
            pltpu.make_async_copy(ffn.at[core, v], outs[v], local_sem.at[10 + v]).wait()
            remote(ffn.at[1 - core, v], outs[v], sems, base + v, sibling).wait_send()

    def receive(outs, base):
        for v in range(wide):
            remote(ffn.at[0, v], outs[v], sems, base + v, sibling).wait_recv()

    @pl.when(core == 0)
    def _():
        move(enc, 10)

    @pl.when(core == 1)
    def _():
        move(dec, 10 + wide)

    for v in range(1, wide):
        gather.arrive(v - 1)
        stores[v].start()
        gives[v].start()
    for v in range(wide):
        gives[v].wait_recv()
        stores[v].wait()
    dec_copy.wait()

    @pl.when(core == 0)
    def _():
        settle(enc, 10)
        receive(dec, 10 + wide)
        remote(held, blocks.at[0], sems, 0, sibling).wait_send()

    @pl.when(core == 1)
    def _():
        settle(dec, 10 + wide)
        receive(enc, 10)
        remote(win_in.at[0], spare, sems, 1, sibling).wait_send()

    gather.finish()
    for give in gives:
        give.wait_send()


def start_weights(wide, rows, attn_in, attn_out, cross_in, cross_out, ffn_in, ffn_out, gains, biases):
    depth = ffn_in.shape[1]
    low = jnp.bfloat16
    block = jax.ShapeDtypeStruct((rows, depth, 3 * TILE), low)
    part = (depth, 3 * HD)
    attn, dec_half, *outs = pl.pallas_call(
        lambda *refs: start_weights_kernel(wide, rows, *refs),
        out_shape=[
            jax.ShapeDtypeStruct((2, wide * depth, 3 * HD), low),
            jax.ShapeDtypeStruct(part, low),
            jax.ShapeDtypeStruct(gains.shape, jnp.float32),
            jax.ShapeDtypeStruct(gains.shape, jnp.float32),
            jax.ShapeDtypeStruct((H, LE, LE), jnp.float32),
            jax.ShapeDtypeStruct((H, LD, LD), jnp.float32),
        ]
        + [block] * (2 * wide),
        in_specs=[HBM] * 6 + [VM] * 4,
        out_specs=[HBM] * 2 + [VM] * 4 + [HBM] * (2 * wide),
        scratch_shapes=[
            pltpu.VMEM(part, low),
            pltpu.VMEM((wide,) + part, low),
            pltpu.VMEM(part, low),
            pltpu.VMEM(ffn_in.shape[1:], low),
            pltpu.VMEM((depth, FF), low),
            pltpu.VMEM((2, wide) + block.shape, low),
            pltpu.VMEM((8, 2 * LE), jnp.float32),
            pltpu.VMEM((8, 2 * LD), jnp.float32),
            pltpu.SemaphoreType.DMA((12 + 2 * wide,)),
            pltpu.SemaphoreType.DMA((12 + 2 * wide,)),
            pltpu.SemaphoreType.DMA((10 + wide,)),
        ],
        compiler_params=pltpu.CompilerParams(
            collective_id=1, has_side_effects=True, vmem_limit_bytes=VMEM_LIMIT
        ),
        name="start_weights",
    )(attn_in, attn_out[0].T, cross_in, cross_out, ffn_in, ffn_out[0].T, gains, biases, distance_hot(LE, True, 0), distance_hot(LD, False, 0))
    return attn, dec_half, outs[:2], outs[2:4], outs[4 : 4 + wide], outs[4 + wide :]


def split_at(rows):
    return (rows // 2 + 15) // 16 * 16


class ReduceWeights:
    def __init__(self, batch, bufs, sems, base, peers, others):
        self.own, self.land, self.plane, self.send, self.zland = bufs
        self.batch = batch
        core, place, row = lax.axis_index("section"), lax.axis_index("wide"), lax.axis_index("rows")
        wide, size = self.own.shape[:2]
        depth = batch.shape[0] // wide

        def rows_at(v, half):
            start = (place ^ v) * depth + half * (depth - size)
            return pl.ds(pl.multiple_of(start, 16), size)

        self.mine = [rows_at(v, core) for v in range(wide)]
        self.swaps = [
            remote(batch.at[rows_at(v, 1 - core)], self.land.at[v], sems, base + v, peers[-1])
            for v in range(wide)
        ]
        base += wide
        self.scatter = ScatterPlane(self.own, self.plane, sems, base, peers, size)
        base += 6
        chunk = batch.shape[1] // (len(others) + 1)

        def lanes(k):
            return pl.ds(pl.multiple_of((row ^ k) * chunk, TILE), chunk)

        self.kept, self.relayed = lanes(0), lanes(2)
        near, far = others[0], others[1]
        self.spreads = [
            remote(self.send.at[:, lanes(1)], self.zland.at[0], sems, base, near),
            remote(self.send.at[:, lanes(3)], self.zland.at[1], sems, base + 1, near),
            remote(self.send.at[:, lanes(2)], self.zland.at[2], sems, base + 2, far),
        ]

    def start(self):
        for v in (3, 1, 2, 0):
            self.swaps[v].start()

    def join(self):
        def add(v):
            self.swaps[v].wait_recv()
            own = self.batch[self.mine[v], :]
            self.own[v] = (own.astype(jnp.float32) + self.land[v].astype(jnp.float32)).astype(
                jnp.bfloat16
            )

        add(3)
        self.scatter.send_far()
        add(1)
        self.scatter.send_early(0)
        add(2)
        self.scatter.send_early(1)
        add(0)

    def given(self):
        for swap in self.swaps:
            swap.wait_send()

    def pass_on(self):
        self.scatter.pass_on()

    def spread(self):
        self.send[...] = (self.own[0].astype(jnp.float32) + self.scatter.total()).astype(
            jnp.bfloat16
        )
        self.spreads[0].start()
        self.spreads[1].start()

    def relay(self):
        self.spreads[1].wait_recv()
        self.send[:, self.relayed] = (
            self.send[:, self.relayed].astype(jnp.float32) + self.zland[1].astype(jnp.float32)
        ).astype(jnp.bfloat16)
        self.spreads[2].start()

    def total(self):
        out = self.send[:, self.kept].astype(jnp.float32)
        for index in (0, 2):
            self.spreads[index].wait_recv()
            out = out + self.zland[index].astype(jnp.float32)
        return out

    def finish(self):
        for copy in self.spreads:
            copy.wait_send()
        self.scatter.finish()


def reduce_weights_scratch(wide, rows, size, columns):
    low = jnp.bfloat16
    return [
        pltpu.VMEM((wide, size, columns), low),
        pltpu.VMEM((wide, size, columns), low),
        pltpu.VMEM((3, size, columns), low),
        pltpu.VMEM((size, columns), low),
        pltpu.VMEM((rows - 1, size, columns // rows), low),
    ]


def last_kernel(wide, rows, *refs):
    cross, refs = refs[:6], refs[6:]
    dec_in, dec_out, enc_in, enc_out, y_ref, dec_attn, enc_attn = refs[:7]
    dec_self, enc_self, gains = refs[7:14], refs[14:21], refs[21:25]
    out_ref, ffn_ref, small_out, y_half, x_half, t_half = refs[25:31]
    refs = refs[31:]
    batch_bufs = [refs[i * 5 : i * 5 + 5] for i in range(3)]
    line_bufs, refs = refs[15:19], refs[19:]
    held, win, wout, gx, gt, context_e, projected_e, context_d, projected_d = refs[:9]
    keep, give, ready, landing, small, small_land, small_plane, small_rows = refs[9:17]
    halves, (sums_ref, send_sem, recv_sem, local_sem) = refs[17:23], refs[23:]
    core, place, row = lax.axis_index("section"), lax.axis_index("wide"), lax.axis_index("rows")
    peers = peers_of(wide)
    sibling = peers[-1]
    crossed = [{"section": 1 - core, "wide": place ^ v} for v in range(1, wide)]
    others = [{"rows": row ^ k} for k in range(1, rows)]
    sems = (send_sem, recv_sem)
    depth = held.shape[0] // wide
    units = dec_out.shape[0]
    low = jnp.bfloat16
    straight = (
        lax.broadcasted_iota(jnp.int32, (units, TILE), 0)
        == lax.broadcasted_iota(jnp.int32, (units, TILE), 1)
    ).astype(low)

    def attn_loads(source):
        return [
            pltpu.make_async_copy(source.at[0], win, local_sem.at[0]),
            pltpu.make_async_copy(source.at[1, :, pl.ds(0, HD)], wout, local_sem.at[1]),
        ]

    for load in attn_loads(dec_attn):
        load.start()
    greet(peers + crossed + others)
    per_batch = wide + 6 + rows - 1
    batches = [
        ReduceWeights(held, bufs, sems, i * per_batch, peers, others)
        for i, bufs in enumerate(batch_bufs)
    ]
    base = 3 * per_batch
    line = ReduceRows(enc_in, enc_out, *line_bufs, sems, base, local_sem, 2 + wide)
    base += 9
    local_base = 6 + wide
    first = remote(small.at[1 - core], small_land, sems, base, sibling)
    plane = [
        remote(small.at[core], small_plane.at[v - 1], sems, base + v, peers[v - 1])
        for v in range(1, wide)
    ]
    base += wide
    spread_small = [
        remote(small.at[core], small_rows.at[k - 1], sems, base + k - 1, others[k - 1])
        for k in range(1, rows)
    ]
    base += rows - 1
    hand_base = base
    base += 6 * wide

    def hand(section, source, v, piece):
        index = piece * wide + v
        return pltpu.make_async_remote_copy(
            src_ref=ready.at[section, v, piece],
            dst_ref=landing.at[source, v, piece],
            send_sem=send_sem.at[hand_base + section * 3 * wide + index],
            recv_sem=recv_sem.at[hand_base + source * 3 * wide + index],
            device_id={"section": section, "wide": place ^ v},
            device_id_type=MESH,
        )

    def hand_out(section, piece, value):
        for owner in range(wide):
            ready[section, owner ^ place, piece] = value[owner * depth : (owner + 1) * depth]
        for v in range(1, wide):
            hand(section, core, v, piece).start()

        @pl.when(core == section)
        def _():
            landing[core, 0, piece] = ready[section, 0, piece]

        @pl.when(core != section)
        def _():
            hand(section, core, 0, piece).start()

    def handed(section):
        for piece in range(3):
            for v in range(1, wide):
                hand(section, core, v, piece).wait_send()

            @pl.when(core != section)
            def _():
                hand(section, core, 0, piece).wait_send()

    def came(source):
        for piece in range(3):
            for v in range(1, wide):
                hand(0, source, v, piece).wait_recv()

            @pl.when(core != source)
            def _():
                hand(0, source, 0, piece).wait_recv()

    half_copies = []

    def by_half(index, value, target):
        mine, its = halves[2 * index : 2 * index + 2]
        middle = D // 2
        for own in range(2):

            @pl.when(core == own)
            def _():
                parts = (value[:, :middle], value[:, middle:]) if index != 1 else (value[:middle], value[middle:])
                mine[...] = parts[own].astype(mine.dtype)
                its[...] = parts[1 - own].astype(its.dtype)

        copies = (
            pltpu.make_async_copy(mine, target.at[core], local_sem.at[local_base + 1 + index]),
            remote(its, target.at[core], sems, base + index, sibling),
        )
        for copy in copies:
            copy.start()
            half_copies.append(copy)

    line.start()
    cross_weights(*cross, held)
    batches[0].start()
    by_half(0, y_ref[...], y_half)
    small[...] = jnp.zeros_like(small)
    for i, gain in enumerate(gains):
        small[i // 2, pl.ds(1 + i % 2, 1), pl.ds(0, D)] = gain[...]
    batches[0].join()
    g_ref, x_ref, gain_ref, normed_ref, projected_ref, context_ref, weights_ref = dec_self
    for load in attn_loads(dec_attn):
        load.wait()
    self_backward_rows(
        g_ref, x_ref, gain_ref, win, wout, projected_ref, weights_ref, gt, small.at[1], context_d, projected_d, sums_ref
    )
    for load in attn_loads(enc_attn):
        load.start()
    batches[0].given()
    self_backward_weights(g_ref, normed_ref, context_ref, projected_d, held)
    batches[1].start()
    line.loaded()
    line.turn(0)
    batches[0].pass_on()
    for piece in range(2):
        hand_out(1, piece, dec_in[piece])
    hand_out(1, 2, tn(dec_out[...], straight).astype(low))
    by_half(2, gt[...], t_half)
    g_ref, x_ref, gain_ref, normed_ref, projected_ref, context_ref, weights_ref = enc_self
    for load in attn_loads(enc_attn):
        load.wait()
    self_backward_rows(
        g_ref, x_ref, gain_ref, win, wout, projected_ref, weights_ref, gx, small.at[0], context_e, projected_e, sums_ref
    )
    first.start()
    batches[1].join()
    batches[1].given()
    self_backward_weights(g_ref, normed_ref, context_ref, projected_e, held)
    batches[2].start()
    line.turn(1)
    batches[0].spread()
    first.wait()
    small[core] = small[core] + small_land[...]
    for copy in plane:
        copy.start()
    batches[2].join()
    batches[1].pass_on()
    by_half(1, gx[...].T, x_half)
    for copy in plane:
        copy.wait()
    small[core] = small[core] + jnp.sum(small_plane[...], axis=0)
    for copy in spread_small:
        copy.start()
    line.turn(2)
    batches[0].relay()
    batches[1].spread()
    batches[2].pass_on()
    batches[1].relay()
    batches[2].spread()
    line.close(0)
    hand_out(0, 0, line_bufs[0][0, 0])
    line.close(1)
    hand_out(0, 1, line_bufs[0][0, 1])
    batches[2].relay()
    line.close(2)
    hand_out(0, 2, tn(line_bufs[2][0], straight).astype(low))
    part = held.shape[1] // rows // 2
    span = keep.shape[1] - part
    crosses = batches[0].total()
    selfs = [batches[2].total(), batches[1].total()]
    for own in range(2):

        @pl.when(core == own)
        def _():
            keep[:, pl.ds(0, span)] = selfs[own]
            keep[:, pl.ds(span, part)] = crosses[:, own * part : (own + 1) * part]
            give[:, pl.ds(0, span)] = selfs[1 - own]
            give[:, pl.ds(span, part)] = crosses[:, (1 - own) * part : (2 - own) * part]

    store = pltpu.make_async_copy(keep, out_ref.at[core], local_sem.at[local_base + 4])
    last = remote(give, out_ref.at[core], sems, base + 3, sibling)
    store.start()
    last.start()
    for copy in spread_small:
        copy.wait()
    small_out[...] = small[core] + jnp.sum(small_rows[...], axis=0)
    handed(0)
    handed(1)
    came(0)
    came(1)
    store_ffn = pltpu.make_async_copy(landing, ffn_ref, local_sem.at[local_base + 5])
    store_ffn.start()
    store.wait()
    last.wait()
    store_ffn.wait()
    for copy in half_copies:
        copy.wait()
    batches[2].given()
    for batch in batches:
        batch.finish()
    line.finish()


def last_step(wide, rows, cross, dec_sums, enc_shares, y3, dec_attn, enc_attn, dec_self, enc_self, gains):
    low = jnp.bfloat16
    depth = D // wide
    size = split_at(depth)
    units = dec_sums[1].shape[0]
    columns = 4 * HD
    enc_rows, dec_rows = enc_self[0].shape[0], dec_self[0].shape[0]
    wanted = (columns + columns // 2) // rows
    copies = 3 * (wide + 6 + rows - 1) + 9 + wide + rows - 1 + 6 * wide + 4
    small = (16, (D + TILE - 1) // TILE * TILE)
    middle = D // 2
    half_shapes = [
        ((dec_rows, middle), low),
        ((middle, enc_rows), jnp.float32),
        ((dec_rows, middle), jnp.float32),
    ]
    batch_scratch = reduce_weights_scratch(wide, rows, size, columns)
    return pl.pallas_call(
        lambda *refs: last_kernel(wide, rows, *refs),
        out_shape=[
            jax.ShapeDtypeStruct((2, size, wanted), jnp.float32),
            jax.ShapeDtypeStruct((2, wide, 3, depth, TILE), low),
            jax.ShapeDtypeStruct(small, jnp.float32),
        ]
        + [jax.ShapeDtypeStruct((2, *each), kind) for each, kind in half_shapes],
        in_specs=[VM] * 6 + [VM, VM, HBM, HBM, VM, HBM, HBM] + [VM] * 18,
        out_specs=[HBM, HBM, VM, HBM, HBM, HBM],
        scratch_shapes=batch_scratch * 3
        + reduce_rows_scratch(units)
        + [
            pltpu.VMEM((D, columns), low),
            pltpu.VMEM((D, 3 * HD), low),
            pltpu.VMEM((D, HD), low),
            pltpu.VMEM((enc_rows, D), jnp.float32),
            pltpu.VMEM((dec_rows, D), jnp.float32),
            pltpu.VMEM((enc_rows, HD), low),
            pltpu.VMEM((enc_rows, 3 * HD), low),
            pltpu.VMEM((dec_rows, HD), low),
            pltpu.VMEM((dec_rows, 3 * HD), low),
            pltpu.VMEM((size, wanted), jnp.float32),
            pltpu.VMEM((size, wanted), jnp.float32),
            pltpu.VMEM((2, wide, 3, depth, TILE), low),
            pltpu.VMEM((2, wide, 3, depth, TILE), low),
            pltpu.VMEM((2,) + small, jnp.float32),
            pltpu.VMEM(small, jnp.float32),
            pltpu.VMEM((wide - 1,) + small, jnp.float32),
            pltpu.VMEM((rows - 1,) + small, jnp.float32),
        ]
        + [pltpu.VMEM(each, kind) for each, kind in half_shapes for _ in range(2)]
        + [
            pltpu.VMEM((H, 1, 2 * enc_rows), jnp.float32),
            pltpu.SemaphoreType.DMA((copies,)),
            pltpu.SemaphoreType.DMA((copies,)),
            pltpu.SemaphoreType.DMA((12 + wide,)),
        ],
        compiler_params=pltpu.CompilerParams(
            collective_id=7, has_side_effects=True, vmem_limit_bytes=VMEM_LIMIT
        ),
        name="last_step",
    )(*cross, *dec_sums, *enc_shares, y3, dec_attn, enc_attn, *dec_self, *enc_self, *gains)


def assemble_kernel(
    units, parts_ref, attn_ref, small_ref, enc_hot, dec_hot,
    in_ref, out_ref, gain_ref, bias_ref, win_ref, wout_ref, cin_ref, cout_ref,
):
    low = jnp.bfloat16
    wide = parts_ref.shape[1]
    place, core = lax.axis_index("wide"), lax.axis_index("section")
    pairs = 2 * wide
    row_ids = lax.broadcasted_iota(jnp.int32, (TILE, TILE), 0)
    lane_ids = lax.broadcasted_iota(jnp.int32, (TILE, TILE), 1)

    def tile_at(tile, first, columns):
        total = None
        last = min((tile + 1) * TILE, columns) - 1
        for group in range(tile * TILE // units, last // units + 1):
            half, chip, block = group % 2, group % pairs // 2, group // pairs
            shift = group * units - tile * TILE
            picks = ((row_ids + shift == lane_ids) & (row_ids < units)).astype(low)
            part = matmul(
                parts_ref[half, chip ^ place, first + block], picks
            )
            total = part if total is None else total + part
        return total

    for tile in range(in_ref.shape[2] // TILE):
        in_ref[0, :, pl.ds(tile * TILE, TILE)] = tile_at(tile, 0, in_ref.shape[2])
    for tile in range(out_ref.shape[2] // TILE):
        out_ref[0, :, pl.ds(tile * TILE, TILE)] = tile_at(tile, 2, out_ref.shape[2])
    for row in range(3):
        gain_ref[row] = small_ref[row : row + 1, 0:D]
    for section, hot in enumerate((enc_hot, dec_hot)):

        @pl.when(core == section)
        def _():
            sums = small_ref[8:16, 0 : hot.shape[1]]
            bias = lax.dot_general(
                sums, hot[...], (((1,), (1,)), ((), ())), precision=HIGHEST, preferred_element_type=jnp.float32
            )
            for head in range(H):
                bias_ref[head] = bias[head : head + 1]

    size, depth = attn_ref.shape[1], in_ref.shape[1]
    whole = jnp.concatenate([attn_ref[0], attn_ref[1, 2 * size - depth :]], axis=0)
    turned = whole.T
    start = 0
    for ref in (win_ref, wout_ref, cin_ref, cout_ref):
        ref[0] = turned[start : start + ref.shape[1]]
        start += ref.shape[1]


def assemble(rows, parts, attn_parts, small):
    wide, depth = parts.shape[1], parts.shape[3]
    shapes = [
        (1, depth, 2 * FF // rows),
        (1, depth, FF // rows),
        (3, 1, D),
        (H, 1, NB),
        (1, 3 * HD // rows, depth),
        (1, HD // rows, depth),
        (1, HD // rows, depth),
        (1, HD // rows, depth),
    ]
    return pl.pallas_call(
        lambda *refs: assemble_kernel(FF // (wide * rows * 2), *refs),
        out_shape=[jax.ShapeDtypeStruct(shape, jnp.float32) for shape in shapes],
        in_specs=[VM] * 5,
        out_specs=[VM] * len(shapes),
        compiler_params=pltpu.CompilerParams(vmem_limit_bytes=VMEM_LIMIT),
        name="assemble",
    )(
        parts,
        attn_parts,
        small,
        distance_hot(LE, True, 1 - LE),
        distance_hot(LD, False, 1 - LD),
    )


def bias_rows(source, target):
    length, span = target.shape[1], source.shape[1]
    for head in range(H):
        row = jnp.broadcast_to(source[pl.ds(head, 1), :], (length, span))
        target[head] = pltpu.roll(row, 0, 1, stride=1, stride_axis=0)[:, :length]


def distance_sums(scores, span):
    length = scores.shape[0]
    flip = (
        lax.broadcasted_iota(jnp.int32, (length, length), 0)
        + lax.broadcasted_iota(jnp.int32, (length, length), 1)
        == length - 1
    ).astype(jnp.bfloat16)
    flipped = matmul(flip, scores)
    padded = jnp.concatenate([flipped, jnp.zeros((length, span - length), jnp.float32)], axis=1)
    rolled = pltpu.roll(padded, 0, 1, stride=1, stride_axis=0)
    return jnp.sum(rolled, axis=0, keepdims=True)


def distance_hot(length, both_ways, first):
    table = bucket_table(length, both_ways)
    span = 2 * length
    hot = np.zeros((NB, span), np.float32)
    for entry in range(span):
        distance = entry + first
        if first == 0 and distance >= length:
            distance -= span
        if -length < distance < length:
            query = max(0, -distance)
            hot[table[query, query + distance], entry] = 1.0
    return jnp.asarray(hot)


def head_lanes(value, side):
    lanes = lax.broadcasted_iota(jnp.int32, value.shape, 1)
    return jnp.where((lanes < DH) == (side == 0), value, jnp.zeros_like(value))


def attend_heads(query_of, key_of, value_of, bias_of, allowed, context_ref, weights_ref):
    @pl.loop(0, H // 2)
    def _(pair):
        query, key, value = query_of(pair), key_of(pair), value_of(pair)
        total = None
        for side in range(2):
            head = 2 * pair + side
            scores = nt(head_lanes(query, side), key)
            if bias_of is not None:
                scores = scores + bias_of(head)
            scores = jnp.where(allowed, scores, NEGATIVE)
            shifted = jnp.exp(scores - jnp.max(scores, axis=-1, keepdims=True))
            weights = shifted / jnp.sum(shifted, axis=-1, keepdims=True)
            weights_ref[head] = weights
            part = matmul(weights.astype(jnp.bfloat16), head_lanes(value, side))
            total = part if total is None else total + part
        context_ref[:, pair_tile(pair, 0)] = total.astype(jnp.bfloat16)


def attend_heads_backward(query_of, key_of, value_of, weights_ref, grad_of, put, put_scores=None):
    @pl.loop(0, H // 2)
    def _(pair):
        query, key, value, grad = query_of(pair), key_of(pair), value_of(pair), grad_of(pair)
        sums = [None, None, None]
        for side in range(2):
            head = 2 * pair + side
            weights = weights_ref[head]
            own_grad = head_lanes(grad, side)
            grad_weights = nt(own_grad, value)
            inner = jnp.sum(grad_weights * weights, axis=-1, keepdims=True)
            low = (weights * (grad_weights - inner)).astype(jnp.bfloat16)
            if put_scores is not None:
                put_scores(head, low)
            parts = [
                matmul(low, head_lanes(key, side)),
                tn(low, head_lanes(query, side)),
                tn(weights.astype(jnp.bfloat16), own_grad),
            ]
            sums = [b if a is None else a + b for a, b in zip(sums, parts)]
        put(pair, *sums)


def pair_tile(pair, base):
    return pl.ds(pl.multiple_of(base + pair * TILE, TILE), TILE)


def item_numbers(lengths_ref, core, shape, axis):
    positions = lax.broadcasted_iota(jnp.int32, shape, axis)
    number, end = jnp.zeros(shape, jnp.int32), 0
    for item in range(lengths_ref.shape[1] - 1):
        end = end + lengths_ref[core, item]
        number = number + (positions >= end).astype(jnp.int32)
    return number


def weight_spec(half, width, index):
    return pl.BlockSpec((None, D, width), lambda step: (half, 0, index), memory_space=pltpu.VMEM)


W_IN = weight_spec(0, 3 * HD, 0)
W_OUT, C_IN, C_OUT = [weight_spec(1, HD, i) for i in range(3)]


def tile_of(ref, base):
    return lambda pair: ref[:, pair_tile(pair, base)]


def self_forward_kernel(
    wide, causal, x_ref, gain_ref, win_ref, wout_ref, bias_ref, lengths_ref, *refs
):
    core = lax.axis_index("section")
    if wide:
        blocks, dec_blocks, refs = refs[: wide - 1], refs[wide - 1 : 2 * wide - 2], refs[2 * wide - 2 :]
    y_ref, low_ref, normed_ref, projected_ref, context_ref, weights_ref = refs[:6]
    if wide:
        pieces, dec_pieces, sems = refs[6 : 5 + wide], refs[5 + wide : 4 + 2 * wide], refs[4 + 2 * wide :]
        peers = peers_of(wide)
        greet(peers + [{"rows": lax.axis_index("rows") ^ 1}])
        reshard = Reshard(blocks, pieces, 0, sems, 0, peers)
        reshard.start()
        half = dec_pieces[0].shape[0]
        mine = pl.ds(lax.axis_index("rows") % 2 * half, half)
        later = [
            remote(block.at[mine], piece, sems, 9 + v, peers[v])
            for v, (block, piece) in enumerate(zip(dec_blocks, dec_pieces))
        ]
    low_ref[...] = x_ref[core] if causal else x_ref[core].T
    residual = low_ref[...].astype(jnp.float32)
    normed_ref[...] = (residual * rms_rows(residual) * gain_ref[pl.ds(0, 1), :]).astype(jnp.bfloat16)
    projected_ref[...] = matmul(normed_ref[...], win_ref[...]).astype(jnp.bfloat16)
    length = low_ref.shape[0]
    allowed = item_numbers(lengths_ref, core, (length, length), 0) == item_numbers(
        lengths_ref, core, (length, length), 1
    )
    if causal:
        allowed = allowed & (
            lax.broadcasted_iota(jnp.int32, (length, length), 0)
            >= lax.broadcasted_iota(jnp.int32, (length, length), 1)
        )
    attend_heads(
        tile_of(projected_ref, 0),
        tile_of(projected_ref, HD),
        tile_of(projected_ref, 2 * HD),
        lambda head: bias_ref[head],
        allowed,
        context_ref,
        weights_ref,
    )
    y_ref[...] = residual + nt(context_ref[...], wout_ref[...])
    if wide:
        for copy in later:
            copy.start()
        reshard.pass_on()
        reshard.finish()
        for copy in later:
            copy.wait()


def self_forward(causal, embed, gains, weight, bias, lengths, blocks=(), dec_blocks=()):
    rows = embed.shape[1 if causal else 2]
    low = jnp.bfloat16
    wide = len(blocks) + 1 if blocks else 0
    params = dict(vmem_limit_bytes=VMEM_LIMIT)
    if blocks:
        params.update(collective_id=6, has_side_effects=True)
    y, *kept = pl.pallas_call(
        lambda *refs: self_forward_kernel(wide, causal, *refs),
        out_shape=[
            jax.ShapeDtypeStruct((rows, D), jnp.float32),
            jax.ShapeDtypeStruct((rows, D), low),
            jax.ShapeDtypeStruct((rows, D), low),
            jax.ShapeDtypeStruct((rows, 3 * HD), low),
            jax.ShapeDtypeStruct((rows, HD), low),
            jax.ShapeDtypeStruct((H, rows, rows), jnp.float32),
        ]
        + [jax.ShapeDtypeStruct(each.shape, low) for each in blocks]
        + [jax.ShapeDtypeStruct((each.shape[0] // 2, *each.shape[1:]), low) for each in dec_blocks],
        in_specs=[VM, VM, W_IN, W_OUT, VM, SM] + [HBM] * (2 * len(blocks)),
        out_specs=[VM] * 6 + [HBM] * (2 * len(blocks)),
        scratch_shapes=[pltpu.SemaphoreType.DMA((12,))] * 2 if blocks else [],
        grid=(1,),
        compiler_params=pltpu.CompilerParams(**params),
        name="self_forward_%d" % rows,
    )(embed, gains, weight, weight, bias, lengths, *blocks, *dec_blocks)
    return y, kept[:5], kept[5:]


def picked(source, start, window, first, width):
    base = start // TILE * TILE
    window = min(window, source.shape[1] - base)
    lanes = lax.broadcasted_iota(jnp.int32, (window, HD), 1) - first
    rows_of = lax.broadcasted_iota(jnp.int32, (window, HD), 0) + (base - start)
    pick = ((rows_of == lanes) & (lanes >= 0) & (lanes < width)).astype(jnp.bfloat16)
    return matmul(source[:, pl.ds(base, window)], pick)


def self_backward_rows(
    g_ref,
    x_ref,
    gain_ref,
    win_ref,
    wout_ref,
    projected_ref,
    weights_ref,
    gx_ref,
    small_ref,
    context_grad,
    projected_grad,
    sums_ref,
):
    low = jnp.bfloat16
    length = x_ref.shape[0]
    context_grad[...] = matmul(g_ref[...].astype(low), wout_ref[...]).astype(low)

    def put(pair, query, key, value):
        for index, part in enumerate((query, key, value)):
            projected_grad[:, pair_tile(pair, index * HD)] = part.astype(low)

    def put_scores(head, scores):
        sums_ref[head, :, pl.ds(0, 2 * length)] = distance_sums(scores, 2 * length)

    attend_heads_backward(
        tile_of(projected_ref, 0),
        tile_of(projected_ref, HD),
        tile_of(projected_ref, 2 * HD),
        weights_ref,
        tile_of(context_grad, 0),
        put,
        put_scores,
    )
    for head in range(H):
        small_ref[pl.ds(8 + head, 1), pl.ds(0, 2 * length)] = sums_ref[head, :, pl.ds(0, 2 * length)]
    grad_normed = nt(projected_grad[...], win_ref[...])
    residual = x_ref[...].astype(jnp.float32)
    grad_residual, grad_gain = norm_pull(residual, gain_ref[pl.ds(0, 1), :], grad_normed)
    small_ref[pl.ds(0, 1), pl.ds(0, D)] = grad_gain
    gx_ref[...] = g_ref[...] + grad_residual


def self_backward_weights(g_ref, normed_ref, context_ref, projected_grad, grad_ref):
    low = jnp.bfloat16
    both = jnp.concatenate([normed_ref[...], g_ref[...].astype(low)], axis=0)
    chunks = grad_ref.shape[1] // HD
    part_in, part_out = 3 * HD // chunks, HD // chunks
    for chunk in range(chunks):
        right = jnp.concatenate(
            [
                picked(projected_grad, chunk * part_in, HD, 0, part_in),
                picked(context_ref, chunk * part_out, 2 * TILE, part_in, part_out),
            ],
            axis=0,
        ).astype(low)
        grad_ref[:, pl.ds(chunk * HD, HD)] = tn(both, right).astype(low)


def cross_forward_kernel(
    x_ref, final_ref, wkey_ref, wvalue_ref, y_ref, gain_ref, wquery_ref, wout_ref, dec_lengths, enc_lengths,
    out_ref, memory_ref, kv_ref, normed_ref, query_ref, context_ref, weights_ref,
):
    low = jnp.bfloat16
    core = lax.axis_index("section")
    residual = x_ref[...]
    memory_ref[...] = (residual * rms_rows(residual) * final_ref[pl.ds(2, 1), :]).astype(low)
    kv_ref[:, pl.ds(0, HD)] = matmul(memory_ref[...], wkey_ref[...]).astype(low)
    kv_ref[:, pl.ds(HD, HD)] = matmul(memory_ref[...], wvalue_ref[...]).astype(low)
    target = y_ref[...]
    normed_ref[...] = (target * rms_rows(target) * gain_ref[pl.ds(1, 1), :]).astype(low)
    query_ref[...] = matmul(normed_ref[...], wquery_ref[...]).astype(low)
    attend_heads(
        tile_of(query_ref, 0),
        tile_of(kv_ref, 0),
        tile_of(kv_ref, HD),
        None,
        item_numbers(dec_lengths, core, (LD, LE), 0) == item_numbers(enc_lengths, core, (LD, LE), 1),
        context_ref,
        weights_ref,
    )
    out_ref[...] = target + nt(context_ref[...], wout_ref[...])


def cross_forward(x2, enc_gains, enc_weight, y1, dec_gains, dec_weight, dec_lengths, enc_lengths):
    low = jnp.bfloat16
    y2, *kept = pl.pallas_call(
        cross_forward_kernel,
        out_shape=[
            jax.ShapeDtypeStruct((LD, D), jnp.float32),
            jax.ShapeDtypeStruct((LE, D), low),
            jax.ShapeDtypeStruct((LE, 2 * HD), low),
            jax.ShapeDtypeStruct((LD, D), low),
            jax.ShapeDtypeStruct((LD, HD), low),
            jax.ShapeDtypeStruct((LD, HD), low),
            jax.ShapeDtypeStruct((H, LD, LE), jnp.float32),
        ],
        in_specs=[VM, VM, C_IN, C_OUT, VM, VM, C_IN, C_OUT, SM, SM],
        out_specs=[VM] * 7,
        grid=(1,),
        compiler_params=pltpu.CompilerParams(vmem_limit_bytes=VMEM_LIMIT),
        name="cross_forward",
    )(
        x2,
        enc_gains,
        enc_weight,
        enc_weight,
        y1,
        dec_gains,
        dec_weight,
        dec_weight,
        dec_lengths,
        enc_lengths,
    )
    return y2, kept


def cross_backward_rows(
    g_ref, x_ref, final_ref, wkey_ref, wvalue_ref, y_ref, gain_ref, wquery_ref, wout_ref, kv_ref, query_ref, weights_ref,
    gx_ref, gy_ref, final_out, gain_out, kv_grad, query_grad, context_grad,
):
    low = jnp.bfloat16
    grad_low = g_ref[...].astype(low)
    context_grad[...] = matmul(grad_low, wout_ref[...]).astype(low)

    def put(pair, query, key, value):
        query_grad[:, pair_tile(pair, 0)] = query.astype(low)
        kv_grad[:, pair_tile(pair, 0)] = key.astype(low)
        kv_grad[:, pair_tile(pair, HD)] = value.astype(low)

    attend_heads_backward(
        tile_of(query_ref, 0),
        tile_of(kv_ref, 0),
        tile_of(kv_ref, HD),
        weights_ref,
        tile_of(context_grad, 0),
        put,
    )
    grad_memory = nt(kv_grad[:, pl.ds(0, HD)], wkey_ref[...]) + nt(
        kv_grad[:, pl.ds(HD, HD)], wvalue_ref[...]
    )
    gx_ref[...], final_out[...] = norm_pull(x_ref[...], final_ref[pl.ds(2, 1), :], grad_memory)
    grad_residual, gain_out[...] = norm_pull(
        y_ref[...], gain_ref[pl.ds(1, 1), :], nt(query_grad[...], wquery_ref[...])
    )
    gy_ref[...] = g_ref[...] + grad_residual


def cross_weights(g_ref, kv_grad, query_grad, memory_ref, normed_ref, context_ref, grad_ref):
    low = jnp.bfloat16
    lefts = jnp.concatenate([memory_ref[...], normed_ref[...], g_ref[...].astype(low)], axis=0)
    chunks = grad_ref.shape[1] // HD
    part = HD // chunks
    for chunk in range(chunks):
        start = chunk * part
        right = jnp.concatenate(
            [
                picked(kv_grad, start, 2 * TILE, 0, part)
                + picked(kv_grad, HD + start, 2 * TILE, part, part),
                picked(query_grad, start, 2 * TILE, 2 * part, part),
                picked(context_ref, start, 2 * TILE, 3 * part, part),
            ],
            axis=0,
        ).astype(low)
        grad_ref[:, pl.ds(chunk * HD, HD)] = tn(lefts, right).astype(low)


def plain_self_forward(residual, gain_row, weight, bias_full, allowed):
    normed = to_low(rms_norm(residual, gain_row))
    projected = to_low(matmul(normed, weight[:, : 3 * HD]))
    context, weights, low_weights = attend_forward(
        projected[:, :HD], projected[:, HD : 2 * HD], projected[:, 2 * HD :], bias_full, allowed
    )
    return (
        residual + matmul(context, weight[:, 3 * HD : 4 * HD].T),
        (residual, normed, projected, context, weights, low_weights),
    )


def plain_self_backward(kept, gain_row, weight, hot, grad_out):
    residual, normed, projected, context, weights, low_weights = kept
    grad_low = to_low(grad_out)
    grad_wout = matmul(grad_low.T, context)
    grad_context = to_low(matmul(grad_low, weight[:, 3 * HD : 4 * HD]))
    grad_queries, grad_keys, grad_values, low_scores = attend_backward(
        projected[:, :HD],
        projected[:, HD : 2 * HD],
        projected[:, 2 * HD :],
        weights,
        low_weights,
        grad_context,
    )
    grad_projected = to_low(jnp.concatenate([grad_queries, grad_keys, grad_values], axis=1))
    grad_win = matmul(normed.T, grad_projected)
    grad_residual, grad_gain = plain_norm_backward(
        residual, gain_row, matmul(grad_projected, weight[:, : 3 * HD].T)
    )
    grad_bias = jnp.einsum(
        "hqk,qkb->bh", low_scores, hot.astype(jnp.bfloat16), preferred_element_type=jnp.float32
    )
    return grad_out + grad_residual, grad_gain, grad_win, grad_wout, grad_bias


def plain_reduce_attn(grad, core, wide, rows):
    depth, columns = grad.shape
    halves = plain_core_halves(grad, core, wide)
    place = lax.axis_index("wide")
    parts = [
        lax.dynamic_index_in_dim(halves, place ^ v, 0, keepdims=False) for v in range(wide)
    ]
    mine = to_low(scatter_wide(parts))
    pieces, start = [], 0
    for width in (3 * HD, HD, HD, HD):
        pieces.append(mine[:, start : start + width].reshape(mine.shape[0], rows, width // rows))
        start += width
    stacked = jnp.concatenate(pieces, axis=2).transpose(1, 0, 2)
    return lax.psum_scatter(stacked, "rows", scatter_dimension=0, tiled=True)[0]


def plain_core_halves(grad, core, wide):
    depth, columns = grad.shape
    split = to_low(grad).reshape(wide, 2, depth // wide // 2, columns)
    mine = lax.dynamic_index_in_dim(split, core, 1, keepdims=False)
    sent = lax.dynamic_index_in_dim(split, 1 - core, 1, keepdims=False)
    return mine.astype(jnp.float32) + xor_permute(sent, "section", 1).astype(jnp.float32)


def plain_both_sections(own, section):
    other = xor_permute(own, "section", 1)
    is_dec = section == 1
    return jnp.where(is_dec, other, own), jnp.where(is_dec, own, other)


def plain_norm_backward(residual, gain_row, grad_normed):
    _, norm_pull = jax.vjp(rms_norm, residual, gain_row)
    return norm_pull(grad_normed)


def plain_hidden_columns(weight):
    width = weight.shape[1] * 2 // 3
    return weight[:, :width], weight[:, width:]


def plain_ffn_hidden(blocks, weight):
    w_in, _ = plain_hidden_columns(weight)
    both = [matmul(block, w_in) for block in blocks]
    units = w_in.shape[1] // 2
    return both, [to_low(gated(part[:, :units], part[:, units:])) for part in both]


def plain_ffn_forward(residual, gain_row, weight):
    blocks = gather_wide(to_low(rms_norm(residual, gain_row)))
    both, hidden = plain_ffn_hidden(blocks, weight)
    _, w_out = plain_hidden_columns(weight)
    out = residual + scatter_wide([matmul(part, w_out.T) for part in hidden])
    return out, (residual, blocks, both, hidden)


def plain_ffn_backward(kept, gain_row, weight, grad_out, grad_blocks):
    residual, blocks, both, hidden = kept
    w_in, w_out = plain_hidden_columns(weight)
    units = w_out.shape[1]
    parts, grad_both = [], []
    for block, pre in zip(grad_blocks, both):
        _, pull = jax.vjp(gated, pre[:, :units], pre[:, units:])
        grad_gate, grad_up = pull(matmul(block, w_out))
        low = to_low(jnp.concatenate([grad_gate, grad_up], axis=1))
        grad_both.append(low)
        parts.append(matmul(low, w_in.T))
    grad_residual, grad_gain = plain_norm_backward(residual, gain_row, scatter_wide(parts))
    joined = jnp.concatenate(grad_both, axis=0)
    grad_in = matmul(jnp.concatenate(blocks, axis=0).T, joined)
    grad_wout = matmul(jnp.concatenate(grad_blocks, axis=0).T, jnp.concatenate(hidden, axis=0))
    return grad_out + grad_residual, grad_gain, (grad_in, grad_wout)


def plain_reduce_ffn(grads, core, wide, rows):
    grad_in, grad_wout = grads
    depth = grad_in.shape[0]
    both = jnp.concatenate(
        [grad_in.reshape(depth, rows, -1), grad_wout.reshape(depth, rows, -1)], axis=2
    )
    columns = both.shape[2]
    halves = plain_core_halves(both.reshape(depth, rows * columns), core, wide)
    halves = to_low(halves).reshape(wide * (depth // wide // 2), rows, columns).transpose(1, 0, 2)
    summed = lax.psum_scatter(halves, "rows", scatter_dimension=0, tiled=True)[0]
    blocks = summed.reshape(wide, depth // wide // 2, columns)
    place = lax.axis_index("wide")
    out = [lax.dynamic_index_in_dim(blocks, place, 0, keepdims=False)]
    for v in range(1, wide):
        block = lax.dynamic_index_in_dim(blocks, place ^ v, 0, keepdims=False)
        out.append(xor_permute(block, "wide", v))
    return placed_rows([piece[None] for piece in out], place)


def plain_to_section(enc_half, dec_half, core):
    is_dec = core == 1
    own = jnp.where(is_dec, dec_half, enc_half)
    got = xor_permute(jnp.where(is_dec, enc_half, dec_half), "section", 1)
    low, high = jnp.where(is_dec, got, own), jnp.where(is_dec, own, got)
    return jnp.concatenate([low, high], axis=-2).astype(jnp.float32)


def plain_shards(
    enc_embed,
    dec_embed,
    out_cot,
    enc_lengths,
    dec_lengths,
    norm_gains,
    rel_bias,
    attn_in,
    attn_out,
    ffn_in,
    ffn_out,
    cross_in,
    cross_out,
):
    core = lax.axis_index("section")
    place = lax.axis_index("wide")
    wide, rows = lax.axis_size("wide"), lax.axis_size("rows")
    depth = attn_in.shape[1]
    unit = FF // (wide * rows)

    small = jnp.concatenate([norm_gains[0].reshape(-1), rel_bias[0].reshape(-1)])
    enc_small, dec_small = plain_both_sections(small, core)
    gains = [each[: 3 * D].reshape(3, D) for each in (enc_small, dec_small)]
    biases = [each[3 * D :].reshape(NB, H) for each in (enc_small, dec_small)]

    attn_shard = jnp.concatenate([attn_in[0], attn_out[0].T, cross_in[0], cross_out[0]], axis=1)
    attn_own = placed_rows(gather_wide(attn_shard), place)
    ffn_blocks = jnp.concatenate(
        [
            ffn_in[0].reshape(depth, 2 * rows, wide, unit).transpose(2, 0, 1, 3).reshape(wide, depth, -1),
            ffn_out[0].T.reshape(depth, rows, wide, unit).transpose(2, 0, 1, 3).reshape(wide, depth, -1),
        ],
        axis=2,
    )
    ffn_got = [lax.dynamic_index_in_dim(ffn_blocks, place, 0, keepdims=False)]
    for v in range(1, wide):
        block = lax.dynamic_index_in_dim(ffn_blocks, place ^ v, 0, keepdims=False)
        ffn_got.append(xor_permute(block, "wide", v))
    ffn_own = placed_rows(ffn_got, place)
    attn_enc, attn_dec = plain_both_sections(attn_own, core)
    ffn_enc, ffn_dec = plain_both_sections(ffn_own, core)
    memory_weight = attn_enc[:, 4 * HD :]
    cross_w_in, cross_w_out = attn_dec[:, 4 * HD : 5 * HD], attn_dec[:, 5 * HD :]

    def own_row(array):
        return lax.dynamic_index_in_dim(array[:, 0], core, 0, keepdims=False)

    enc_row = own_row(enc_embed).astype(jnp.float32)
    dec_row = own_row(dec_embed).astype(jnp.float32)
    cot_row = own_row(out_cot)
    enc_items = item_ids(own_row(enc_lengths), LE)
    dec_items = item_ids(own_row(dec_lengths), LD)
    enc_hot, dec_hot = one_hot(LE, True), one_hot(LD, False)
    enc_bias = jnp.einsum("qkb,bh->hqk", enc_hot, biases[0], precision=HIGHEST)
    dec_bias = jnp.einsum("qkb,bh->hqk", dec_hot, biases[1], precision=HIGHEST)
    causal = jnp.arange(LD)[:, None] >= jnp.arange(LD)[None, :]

    cot_blocks = gather_wide(cot_row)
    x1, enc_self = plain_self_forward(
        enc_row, gains[0][0], attn_enc, enc_bias, enc_items[:, None] == enc_items[None, :]
    )
    y1, dec_self = plain_self_forward(
        dec_row,
        gains[1][0],
        attn_dec,
        dec_bias,
        (dec_items[:, None] == dec_items[None, :]) & causal,
    )
    x2, enc_ffn = plain_ffn_forward(x1, gains[0][1], ffn_enc)
    memory = to_low(rms_norm(x2, gains[0][2]))
    memory_kv = to_low(matmul(memory, memory_weight))
    cross_normed = to_low(rms_norm(y1, gains[1][1]))
    queries = to_low(matmul(cross_normed, cross_w_in))
    context, weights, low_weights = attend_forward(
        queries,
        memory_kv[:, :HD],
        memory_kv[:, HD:],
        0.0,
        dec_items[:, None] == enc_items[None, :],
    )
    y2 = y1 + matmul(context, cross_w_out.T)
    y3, dec_ffn = plain_ffn_forward(y2, gains[1][2], ffn_dec)

    g2, dec_ffn_gain, dec_ffn_grads = plain_ffn_backward(
        dec_ffn, gains[1][2], ffn_dec, cot_row.astype(jnp.float32), cot_blocks
    )
    dec_ffn_share = plain_reduce_ffn(dec_ffn_grads, core, wide, rows)
    g2_low = to_low(g2)
    grad_cross_out = matmul(g2_low.T, context)
    grad_context = to_low(matmul(g2_low, cross_w_out))
    grad_queries, grad_keys, grad_values, _ = attend_backward(
        queries, memory_kv[:, :HD], memory_kv[:, HD:], weights, low_weights, grad_context
    )
    grad_query_low = to_low(grad_queries)
    grad_kv = to_low(jnp.concatenate([grad_keys, grad_values], axis=1))
    grad_x2, enc_final_gain = plain_norm_backward(x2, gains[0][2], matmul(grad_kv, memory_weight.T))
    grad_x1, enc_ffn_gain, enc_ffn_grads = plain_ffn_backward(
        enc_ffn, gains[0][1], ffn_enc, grad_x2, gather_wide(to_low(grad_x2))
    )
    enc_ffn_share = plain_reduce_ffn(enc_ffn_grads, core, wide, rows)

    grad_cross_in = matmul(cross_normed.T, grad_query_low)
    grad_memory = matmul(memory.T, grad_kv)
    from_cross, dec_cross_gain = plain_norm_backward(
        y1, gains[1][1], matmul(grad_query_low, cross_w_in.T)
    )
    grad_y, dec_self_gain, dec_win, dec_wout, dec_bias_grad = plain_self_backward(
        dec_self, gains[1][0], attn_dec, dec_hot, g2 + from_cross
    )
    dec_attn_share = plain_reduce_attn(
        jnp.concatenate([dec_win, dec_wout, grad_cross_in, grad_cross_out], axis=1),
        core,
        wide,
        rows,
    )
    grad_x, enc_self_gain, enc_win, enc_wout, enc_bias_grad = plain_self_backward(
        enc_self, gains[0][0], attn_enc, enc_hot, grad_x1
    )
    enc_attn_share = plain_reduce_attn(
        jnp.concatenate([enc_win, enc_wout, grad_memory], axis=1), core, wide, rows
    )

    small_grads = jnp.stack(
        [
            jnp.concatenate(
                [enc_self_gain, enc_ffn_gain, enc_final_gain, enc_bias_grad.reshape(-1)]
            ),
            jnp.concatenate(
                [dec_self_gain, dec_cross_gain, dec_ffn_gain, dec_bias_grad.reshape(-1)]
            ),
        ]
    )
    small_total = lax.psum(small_grads, ("section", "wide", "rows"))
    small_own = jnp.where(core == 1, small_total[1], small_total[0])

    attn_share = plain_to_section(enc_attn_share, dec_attn_share, core)
    ffn_share = plain_to_section(enc_ffn_share, dec_ffn_share, core)
    in_width = 2 * FF // rows // wide
    ffn_in_grad = (
        ffn_share[:, :, :in_width]
        .reshape(wide, depth, 2, unit)
        .transpose(1, 2, 0, 3)
        .reshape(depth, 2 * FF // rows)
    )
    ffn_out_grad = ffn_share[:, :, in_width:].transpose(0, 2, 1).reshape(FF // rows, depth)
    widths = [3 * HD // rows, HD // rows, HD // rows]
    edges = np.cumsum([0] + widths + [HD // rows])
    win, wout, cin, cout = [attn_share[:, a:b] for a, b in zip(edges[:-1], edges[1:])]

    half = D // 2

    def by_half(own):
        halves = jnp.stack([own[:, :half], own[:, half:]])
        keep = lax.dynamic_index_in_dim(halves, core, 0, keepdims=False)
        send = lax.dynamic_index_in_dim(halves, 1 - core, 0, keepdims=False)
        got = xor_permute(send, "section", 1)
        is_dec = core == 1
        return jnp.stack([jnp.where(is_dec, got, keep), jnp.where(is_dec, keep, got)])[:, None]

    return (
        by_half(to_low(y3)),
        by_half(grad_x),
        by_half(grad_y),
        small_own[: 3 * D].reshape(1, 3, D),
        small_own[3 * D :].reshape(1, NB, H),
        win[None],
        wout.T[None],
        ffn_in_grad[None],
        ffn_out_grad[None],
        cin[None],
        cout[None],
    )


def shards(
    enc_embed,
    dec_embed,
    out_cot,
    enc_lengths,
    dec_lengths,
    norm_gains,
    rel_bias,
    attn_in,
    attn_out,
    ffn_in,
    ffn_out,
    cross_in,
    cross_out,
):
    wide, rows = lax.axis_size("wide"), lax.axis_size("rows")
    enc_attn, dec_half, gains, biases, enc_blocks, dec_blocks = start_weights(
        wide, rows, attn_in, attn_out, cross_in, cross_out, ffn_in, ffn_out, norm_gains[0], rel_bias[0].T
    )
    enc_lengths, dec_lengths = enc_lengths[:, 0], dec_lengths[:, 0]
    x1, enc_self, moved = self_forward(
        False,
        jnp.swapaxes(enc_embed[:, 0], 1, 2),
        gains[0],
        enc_attn,
        biases[0],
        enc_lengths,
        tuple(enc_blocks[1:]),
        tuple(dec_blocks[1:]),
    )
    enc_pieces, dec_pieces = moved[: wide - 1], moved[wide - 1 :]
    x2, *enc_ffn = ffn_forward_call(
        wide, x1, (gains[0], 1), [enc_blocks[0], *enc_pieces], 2, (dec_half, *dec_pieces)
    )
    enc_ffn, dec_attn, dec_pieces = enc_ffn[:4], enc_ffn[4], [dec_blocks[0], *dec_pieces, *enc_ffn[5:]]
    y1, dec_self, _ = self_forward(
        True, dec_embed[:, 0], gains[1], dec_attn, biases[1], dec_lengths
    )
    y2, cross_kept = cross_forward(
        x2, gains[0], enc_attn, y1, gains[1], dec_attn, dec_lengths, enc_lengths
    )
    y3, g2, dec_ffn_gain, *dec_ffn_grads = ffn_both_call(
        wide, rows, y2, out_cot[:, 0], (gains[1], 2), dec_pieces, 3
    )
    (
        grad_x1,
        enc_ffn_gain,
        enc_in,
        enc_out,
        *dec_sums,
        g1,
        enc_final_gain,
        dec_cross_gain,
        kv_grad,
        query_grad,
    ) = ffn_backward_call(
        wide,
        rows,
        x1,
        (gains[0], 1),
        enc_ffn,
        5,
        dec_ffn_grads,
        (enc_attn, dec_attn, gains[1], g2, x2, y1, cross_kept[1], cross_kept[3], cross_kept[5]),
    )
    attn_parts, ffn_parts, small_own, dec_out, enc_grad, dec_grad = last_step(
        wide,
        rows,
        (g2, kv_grad, query_grad, cross_kept[0], cross_kept[2], cross_kept[4]),
        dec_sums,
        (enc_in, enc_out),
        y3,
        dec_attn,
        enc_attn,
        (g1, dec_self[0], gains[1], *dec_self[1:]),
        (grad_x1, enc_self[0], gains[0], *enc_self[1:]),
        (enc_ffn_gain, enc_final_gain, dec_cross_gain, dec_ffn_gain),
    )
    ffn_in_grad, ffn_out_grad, gain_grad, bias_grad, win, wout, cin, cout = assemble(
        rows, ffn_parts, attn_parts, small_own
    )
    return (
        dec_out[:, None],
        jnp.swapaxes(enc_grad, 1, 2)[:, None],
        dec_grad[:, None],
        gain_grad.transpose(1, 0, 2),
        bias_grad.transpose(1, 2, 0),
        jnp.swapaxes(win, 1, 2),
        wout,
        ffn_in_grad,
        jnp.swapaxes(ffn_out_grad, 1, 2),
        jnp.swapaxes(cin, 1, 2),
        jnp.swapaxes(cout, 1, 2),
    )


def solution(mesh):
    placed = (
        P(None, ("wide", "rows"), None, None),
        P(None, ("wide", "rows"), None, None),
        P(None, ("wide", "rows"), None, None),
        P(None, ("wide", "rows"), None),
        P(None, ("wide", "rows"), None),
        P("section", None, None),
        P("section", None, None),
        P("section", "wide", None),
        P("section", None, "wide"),
        P("section", "wide", None),
        P("section", None, "wide"),
        P("section", "wide", None),
        P("section", "wide", None),
    )
    wide, rows = mesh.shape["wide"], mesh.shape["rows"]
    in_tiles = D // wide % 16 == 0 and FF // (wide * rows) % 32 == 0
    return jax.shard_map(
        shards if wide == 4 and rows == 4 and in_tiles else plain_shards,
        mesh=mesh,
        in_specs=placed,
        out_specs=(
            P(None, ("wide", "rows"), None, "section"),
            P(None, ("wide", "rows"), None, "section"),
            P(None, ("wide", "rows"), None, "section"),
            P("section", None, None),
            P("section", None, None),
            P("section", "wide", "rows"),
            P("section", "rows", "wide"),
            P("section", "wide", "rows"),
            P("section", "rows", "wide"),
            P("section", "wide", "rows"),
            P("section", "wide", "rows"),
        ),
        check_vma=False,
    )
```

```python
import jax
import jax.numpy as jnp
import numpy as np
from jax import lax
from jax.experimental import pallas as pl
from jax.experimental.pallas import tpu as pltpu
from jax.sharding import PartitionSpec as P

D = 1472
H = 6
DH = 64
FF = 3584
NB = 32
MAXDIST = 128
MB = 2
LE = 256
LD = 64
HD = 384


EPSILON = 1e-06
NEGATIVE = -1000000000.0
HIGHEST = lax.Precision.HIGHEST


def bucket_table(length, both_ways):
    positions = np.arange(length)
    offsets = positions[None, :] - positions[:, None]
    buckets = NB
    result = np.zeros(offsets.shape, np.int64)
    if both_ways:
        buckets = buckets // 2
        result = result + (offsets > 0) * buckets
        distance = np.abs(offsets)
    else:
        distance = np.maximum(-offsets, 0)
    exact_count = buckets // 2
    log_ratio = np.log(np.maximum(distance, 1) / exact_count) / np.log(MAXDIST / exact_count)
    far_bucket = np.minimum(
        exact_count + np.floor(log_ratio * (buckets - exact_count)).astype(np.int64), buckets - 1
    )
    return result + np.where(distance < exact_count, distance, far_bucket)


def one_hot(length, both_ways):
    bucket_ids = jnp.asarray(bucket_table(length, both_ways), jnp.int32)
    return (bucket_ids[:, :, None] == jnp.arange(NB, dtype=jnp.int32)[None, None, :]).astype(
        jnp.float32
    )


def item_ids(lengths, length):
    item_ends = jnp.cumsum(lengths)
    positions = jnp.arange(length, dtype=jnp.int32)
    return jnp.sum((positions[:, None] >= item_ends[None, :-1]).astype(jnp.int32), axis=1)


def rms_norm(residual, gain_row):
    return (
        residual
        * lax.rsqrt(jnp.mean(residual * residual, axis=-1, keepdims=True) + EPSILON)
        * gain_row
    )


def matmul(left_side, right_side):
    return jnp.dot(left_side, right_side, preferred_element_type=jnp.float32)


def matmul_exact(left_side, right_side):
    return jnp.dot(left_side, right_side, precision=HIGHEST)


def to_low(tensor):
    return tensor.astype(jnp.bfloat16)


def gated(gate_part, up_part):
    return jax.nn.gelu(gate_part, approximate=True) * up_part


def attend_forward(queries, key_rows, value_rows, bias_full, allowed):
    query_count = queries.shape[0]
    heads_q = queries.reshape(query_count, H, DH)
    heads_k = key_rows.reshape(key_rows.shape[0], H, DH)
    heads_v = value_rows.reshape(value_rows.shape[0], H, DH)
    scores = (
        jnp.einsum("qhd,khd->hqk", heads_q, heads_k, preferred_element_type=jnp.float32) + bias_full
    )
    scores = jnp.where(allowed[None], scores, NEGATIVE)
    shifted = jnp.exp(scores - jnp.max(scores, axis=-1, keepdims=True))
    weights = shifted / jnp.sum(shifted, axis=-1, keepdims=True)
    low_weights = to_low(weights)
    context = jnp.einsum("hqk,khd->qhd", low_weights, heads_v, preferred_element_type=jnp.float32)
    return (to_low(context.reshape(query_count, H * DH)), weights, low_weights)


def attend_backward(queries, key_rows, value_rows, weights, low_weights, grad_context):
    query_count = queries.shape[0]
    key_count = key_rows.shape[0]
    heads_q = queries.reshape(query_count, H, DH)
    heads_k = key_rows.reshape(key_count, H, DH)
    heads_v = value_rows.reshape(key_count, H, DH)
    grad_heads = grad_context.reshape(query_count, H, DH)
    grad_weights = jnp.einsum(
        "qhd,khd->hqk", grad_heads, heads_v, preferred_element_type=jnp.float32
    )
    grad_values = jnp.einsum(
        "hqk,qhd->khd", low_weights, grad_heads, preferred_element_type=jnp.float32
    )
    grad_scores = weights * (grad_weights - jnp.sum(grad_weights * weights, axis=-1, keepdims=True))
    low_scores = to_low(grad_scores)
    grad_queries = jnp.einsum(
        "hqk,khd->qhd", low_scores, heads_k, preferred_element_type=jnp.float32
    )
    grad_keys = jnp.einsum("hqk,qhd->khd", low_scores, heads_q, preferred_element_type=jnp.float32)
    return (
        grad_queries.reshape(query_count, H * DH),
        grad_keys.reshape(key_count, H * DH),
        grad_values.reshape(key_count, H * DH),
        low_scores,
    )


def xor_permute(value, axis, distance):
    count = lax.axis_size(axis)
    return lax.ppermute(value, axis, [(i, i ^ distance) for i in range(count)])


def gather_wide(block):
    count = lax.axis_size("wide")
    if count != 4:
        return [block] + [xor_permute(block, "wide", v) for v in range(1, count)]
    half = block.shape[0] // 2
    first = xor_permute(block, "wide", 1)
    second = xor_permute(block, "wide", 2)
    third = jnp.concatenate(
        [xor_permute(first[:half], "wide", 2), xor_permute(second[half:], "wide", 1)], axis=0
    )
    return [block, first, second, third]


def scatter_wide(parts):
    count = lax.axis_size("wide")
    total = parts[0]
    if count != 4:
        for v in range(1, count):
            total = total + xor_permute(to_low(parts[v]), "wide", v).astype(jnp.float32)
        return total
    half = total.shape[0] // 2
    via_first = xor_permute(to_low(parts[3][:half]), "wide", 1).astype(jnp.float32)
    via_second = xor_permute(to_low(parts[3][half:]), "wide", 2).astype(jnp.float32)
    to_first = jnp.concatenate([parts[1][:half], parts[1][half:] + via_second], axis=0)
    to_second = jnp.concatenate([parts[2][:half] + via_first, parts[2][half:]], axis=0)
    total = total + xor_permute(to_low(to_first), "wide", 1).astype(jnp.float32)
    return total + xor_permute(to_low(to_second), "wide", 2).astype(jnp.float32)


def placed_rows(pieces, place):
    rows = pieces[0].shape[0]
    buffer = jnp.zeros((rows * len(pieces),) + pieces[0].shape[1:], pieces[0].dtype)
    for v, piece in enumerate(pieces):
        start = (place ^ v) * rows
        buffer = lax.dynamic_update_slice(buffer, piece, (start,) + (0,) * (piece.ndim - 1))
    return buffer


MESH = pl.DeviceIdType.MESH
HBM = pl.BlockSpec(memory_space=pl.ANY)
VM = pl.BlockSpec(memory_space=pltpu.VMEM)
SM = pl.BlockSpec(memory_space=pltpu.SMEM)
TILE = 128
VMEM_LIMIT = 62 * 1024 * 1024


def peers_of(count):
    place, core = lax.axis_index("wide"), lax.axis_index("section")
    return [{"wide": place ^ v} for v in range(1, count)] + [{"section": 1 - core}]


def greet(peers):
    barrier = pltpu.get_barrier_semaphore()
    for peer in peers:
        pl.semaphore_signal(barrier, inc=1, device_id=peer, device_id_type=MESH)
    pl.semaphore_wait(barrier, len(peers))


def remote(source, target, sems, index, peer):
    return pltpu.make_async_remote_copy(
        src_ref=source,
        dst_ref=target,
        send_sem=sems[0].at[index],
        recv_sem=sems[1].at[index],
        device_id=peer,
        device_id_type=MESH,
    )


def nt(left, right):
    return lax.dot_general(left, right, (((1,), (1,)), ((), ())), preferred_element_type=jnp.float32)


def tn(left, right):
    return lax.dot_general(left, right, (((0,), (0,)), ((), ())), preferred_element_type=jnp.float32)


class GatherPlane:
    def __init__(self, blocks, sems, base, peers, rows):
        half = split_at(rows)
        rest = rows - half
        first, second = peers[0], peers[1]
        self.direct = [
            remote(blocks.at[0], blocks.at[1], sems, base, first),
            remote(blocks.at[0], blocks.at[2], sems, base + 1, second),
        ]
        self.passed = [
            remote(
                blocks.at[1, pl.ds(0, half)], blocks.at[3, pl.ds(0, half)], sems, base + 2, second
            ),
            remote(
                blocks.at[2, pl.ds(half, rest)],
                blocks.at[3, pl.ds(half, rest)],
                sems,
                base + 3,
                first,
            ),
        ]

    def start(self):
        for copy in self.direct:
            copy.start()

    def arrive(self, index):
        if index < 2:
            self.direct[index].wait_recv()
            self.passed[index].start()
        else:
            for copy in self.passed:
                copy.wait_recv()

    def finish(self):
        for copy in self.direct + self.passed:
            copy.wait_send()


class ScatterPlane:
    def __init__(self, parts, landing, sems, base, peers, rows):
        half = split_at(rows)
        first, second = peers[0], peers[1]
        low, high = pl.ds(0, half), pl.ds(half, rows - half)
        self.parts, self.landing, self.low, self.high = parts, landing, low, high
        self.far = [
            remote(parts.at[3, low], landing.at[0, low], sems, base, first),
            remote(parts.at[3, high], landing.at[0, high], sems, base + 1, second),
        ]
        self.early = [
            remote(parts.at[1, low], landing.at[1, low], sems, base + 2, first),
            remote(parts.at[2, high], landing.at[2, high], sems, base + 3, second),
        ]
        self.late = [
            remote(parts.at[1, high], landing.at[1, high], sems, base + 4, first),
            remote(parts.at[2, low], landing.at[2, low], sems, base + 5, second),
        ]

    def send_early(self, index):
        self.early[index].start()

    def send_far(self):
        for copy in self.far:
            copy.start()

    def pass_on(self):
        low, high = self.low, self.high
        self.far[0].wait_recv()
        self.parts[2, low] = (
            self.parts[2, low].astype(jnp.float32) + self.landing[0, low].astype(jnp.float32)
        ).astype(jnp.bfloat16)
        self.late[1].start()
        self.far[1].wait_recv()
        self.parts[1, high] = (
            self.parts[1, high].astype(jnp.float32) + self.landing[0, high].astype(jnp.float32)
        ).astype(jnp.bfloat16)
        self.late[0].start()

    def total(self):
        for copy in self.early + self.late:
            copy.wait_recv()
        return self.landing[1].astype(jnp.float32) + self.landing[2].astype(jnp.float32)

    def finish(self):
        for copy in self.far + self.early + self.late:
            copy.wait_send()


def rms_rows(residual):
    return lax.rsqrt(jnp.mean(residual * residual, axis=-1, keepdims=True) + EPSILON)


def norm_pull(residual, gain_row, grad_normed):
    scale = rms_rows(residual)
    unit = residual * scale
    inner = grad_normed * gain_row
    grad_residual = scale * (inner - unit * jnp.mean(inner * unit, axis=-1, keepdims=True))
    return grad_residual, jnp.sum(grad_normed * unit, axis=0, keepdims=True)


def token_rows_at_once(wide, rows):
    return rows if rows >= 2 * TILE else wide * rows


def block_at(blocks, group, count):
    if count == blocks.shape[1]:
        return blocks[group]
    return blocks[...].reshape(count, blocks.shape[2])


def before_group(gather, group, groups):
    if groups == 1:
        for index in range(3):
            gather.arrive(index)
        return
    for index in range(3):

        @pl.when(group == index + 1)
        def _():
            gather.arrive(index)


def put_parts(acc, parts, own_ref, group, groups, rows):
    if groups == 1:
        own_ref[...] = acc[pl.ds(0, rows)]
        for v in range(1, parts.shape[0]):
            parts[v] = acc[pl.ds(v * rows, rows)].astype(parts.dtype)
        return

    @pl.when(group == 0)
    def _():
        own_ref[...] = acc[...]

    @pl.when(group > 0)
    def _():
        parts[group] = acc[...].astype(parts.dtype)


def after_group(scatter, group, groups):
    if groups == 1:
        scatter.send_far()
        scatter.send_early(0)
        scatter.send_early(1)
        return

    @pl.when(group == 1)
    def _():
        scatter.send_early(0)

    @pl.when(group == 2)
    def _():
        scatter.send_early(1)

    @pl.when(group == 3)
    def _():
        scatter.send_far()


class Reshard:
    def __init__(self, blocks, pieces, direct, sems, base, peers):
        row = lax.axis_index("rows")
        shared = (blocks[0].shape[0] - direct) // 2
        mine = pl.ds(direct + row % 2 * shared, shared)
        other = {"rows": row ^ 1}
        self.shared, self.direct, self.passed = [], [], []
        for v, (block, piece) in enumerate(zip(blocks, pieces)):
            at, peer, first = base + 3 * v, peers[v], pl.ds(0, direct)
            self.shared.append(remote(block.at[mine], piece.at[mine], sems, at, peer))
            self.passed.append(remote(piece.at[mine], piece.at[mine], sems, at + 1, other))
            if direct:
                self.direct.append(remote(block.at[first], piece.at[first], sems, at + 2, peer))

    def start(self):
        for copy in self.shared:
            copy.start()

    def pass_on(self):
        for copy in self.direct:
            copy.start()
        for copy, after in zip(self.shared, self.passed):
            copy.wait_recv()
            after.start()

    def finish(self):
        for copy in self.direct + self.passed:
            copy.wait()
        for copy in self.shared:
            copy.wait_send()


class ReduceRows:
    def __init__(self, source_in, source_out, in_buf, in_land, out_buf, out_land, sems, base, local_sem, local_base):
        row = lax.axis_index("rows")
        near, far = {"rows": row ^ 1}, {"rows": row ^ 2}
        self.bufs, self.lands, self.first, self.second = [], [], [], []
        views = [
            (lambda ref, i, part=part: ref.at[i, part], source_in, in_buf, in_land)
            for part in range(2)
        ] + [(lambda ref, i: ref.at[i], source_out, out_buf, out_land)]
        for index, (view, source, buf, land) in enumerate(views):
            at = base + 3 * index
            self.first.append(
                [
                    remote(view(source, row ^ 1), view(land, 0), sems, at, near),
                    remote(view(source, row ^ 3), view(land, 1), sems, at + 1, near),
                ]
            )
            self.second.append(remote(view(buf, 1), view(land, 2), sems, at + 2, far))
            self.bufs.append([view(buf, 0), view(buf, 1)])
            self.lands.append([view(land, i) for i in range(3)])
        self.loads = [
            pltpu.make_async_copy(source.at[place], buf.at[i], local_sem.at[local_base + 2 * j + i])
            for j, (source, buf) in enumerate(((source_in, in_buf), (source_out, out_buf)))
            for i, place in enumerate((row, row ^ 2))
        ]

    def start(self):
        for copy in self.first[0]:
            copy.start()
        for load in self.loads:
            load.start()

    def loaded(self):
        for load in self.loads:
            load.wait()

    def add(self, index, which, land):
        ref = self.bufs[index][which]
        ref[...] = (
            ref[...].astype(jnp.float32) + self.lands[index][land][...].astype(jnp.float32)
        ).astype(jnp.bfloat16)

    def turn(self, index):
        for copy in self.first[index]:
            copy.wait_recv()
        for copy in self.first[index + 1] if index < 2 else ():
            copy.start()
        self.add(index, 1, 1)
        self.second[index].start()
        self.add(index, 0, 0)

    def close(self, index):
        self.second[index].wait_recv()
        self.add(index, 0, 2)

    def finish(self):
        for pair, copy in zip(self.first, self.second):
            for each in pair:
                each.wait_send()
            copy.wait_send()


def reduce_rows_scratch(units):
    low = jnp.bfloat16
    return [
        pltpu.VMEM((2, 2, D, TILE), low),
        pltpu.VMEM((3, 2, D, TILE), low),
        pltpu.VMEM((2, units, D), low),
        pltpu.VMEM((3, units, D), low),
    ]


def weight_tiles(weight, half, part):
    lanes = pl.ds(part * TILE, TILE)
    return jnp.concatenate(
        [weight[half, quarter, :, lanes] for quarter in range(weight.shape[1])], axis=1
    )


def weight_copies(pieces, weight, sems, base, local_sem, local_base, sibling):
    core, place = lax.axis_index("section"), lax.axis_index("wide")
    wide, depth = lax.axis_size("wide"), pieces[0].shape[1]
    loads, swaps = [], []
    for index, piece in enumerate(pieces):
        v = index if index < wide else index - wide + 1
        place_rows = pl.ds(pl.multiple_of((place ^ v) * depth, 16), depth)
        target = weight.at[core, :, place_rows]
        quarters = piece.shape[0]
        if quarters < weight.shape[1]:
            part = lax.axis_index("rows") % 2
            part = part if index < wide else 1 - part
            target = weight.at[core, pl.ds(part * quarters, quarters), place_rows]
        loads.append(pltpu.make_async_copy(piece, target, local_sem.at[local_base + index]))
        swaps.append(remote(piece, target, sems, base + index, sibling))
    return loads, swaps


def gate_slopes(gate, up):
    square = gate * gate
    tanh = jnp.tanh(GELU_A * gate * (1.0 + GELU_B * square))
    upper = 0.5 * (1.0 + tanh)
    slope = upper + 0.5 * gate * (1.0 - tanh * tanh) * (GELU_A + 3.0 * GELU_A * GELU_B * square)
    return gate * upper, slope


def ffn_forward_kernel(wide, carried, count, gain_at, x_ref, gain_ref, *refs):
    gain_ref = gain_ref.at[pl.ds(gain_at, 1)]
    pieces, refs = refs[:count], refs[count:]
    if carried:
        dec_half, dec_blocks, refs = refs[0], refs[1:wide], refs[wide:]
    y_ref, at_out, pre_out, hidden_out, weight_out = refs[:5]
    refs = refs[5:]
    if carried:
        dec_attn, dec_pieces, refs = refs[0], refs[1:wide], refs[wide:]
    blocks, at, pre, hidden, weight, parts, landing, acc, send_sem, recv_sem, local_sem = refs[:11]
    rows = x_ref.shape[0]
    depth = pieces[0].shape[1]
    span = weight.shape[1] * TILE
    core, place = lax.axis_index("section"), lax.axis_index("wide")
    peers = peers_of(wide)
    sems = (send_sem, recv_sem)
    greet(peers + ([{"rows": lax.axis_index("rows") ^ 1}] if carried else []))
    residual = x_ref[...]
    blocks[0] = (residual * rms_rows(residual) * gain_ref[...]).astype(jnp.bfloat16)
    gather = GatherPlane(blocks, sems, 0, peers, rows)
    gather.start()
    loads, swaps = weight_copies(pieces, weight, sems, 10, local_sem, 12, peers[-1])
    for load, swap in zip(loads, swaps):
        load.start()
        swap.start()
    scatter = ScatterPlane(parts, landing, sems, 4, peers, rows)
    if carried:
        held, far_held, whole = refs[11:14]
        other = {"rows": lax.axis_index("rows") ^ 1}
        passed = [
            remote(block, piece, sems, 24 + v, other)
            for v, (block, piece) in enumerate(zip(dec_blocks, dec_pieces))
        ]
        for copy in passed:
            copy.start()
        size = held.shape[1]
        rest = depth - size
        part = lax.axis_index("rows") % 2
        dec_gather = GatherPlane(held, sems, 27, peers, size)
        mine = pl.ds(pl.multiple_of(part * rest, 16), size)
        fetch = pltpu.make_async_copy(dec_half.at[mine], held.at[0], local_sem.at[7])
        fetch.start()
        stores, gives, crossings = [], [], []

        def place_block(source, v, start, index):
            target = dec_attn.at[
                core, pl.ds(pl.multiple_of((place ^ v) * depth + start, 16), source.shape[0])
            ]
            stores.append(pltpu.make_async_copy(source, target, local_sem.at[19 + index]))
            gives.append(remote(source, target, sems, 35 + index, peers[-1]))

        place_block(whole, 0, 0, 0)
        for v in range(1, wide):
            place_block(held.at[v], v, part * rest, v)
        for v in range(1, wide):
            sent = pl.ds(pl.multiple_of(part * (size - rest), 16), rest)
            crossings.append(remote(held.at[v, sent], far_held.at[v - 1], sems, 41 + v, other))
            place_block(far_held.at[v - 1], v, (1 - part) * size, wide + v - 1)
        whole_fetch = pltpu.make_async_copy(dec_half, whole, local_sem.at[8])
        whole_fetch.start()
    count = token_rows_at_once(wide, rows)
    groups = wide * rows // count

    @pl.loop(0, groups)
    def _(group):
        before_group(gather, group, groups)

        @pl.when(group == 0)
        def _():
            for load in loads:
                load.wait()

        token_rows = pl.ds(pl.multiple_of(group * count, count), count)

        @pl.loop(0, 2)
        def _(step):
            @pl.when((group == 0) & (step == 1))
            def _():
                for swap in swaps:
                    swap.wait_recv()

            half = lax.rem(core + step, 2)
            block = block_at(blocks, group, count)
            gate = matmul(block, weight_tiles(weight, half, 0))
            up = matmul(block, weight_tiles(weight, half, 1))
            pre[half, token_rows, pl.ds(0, span)] = gate.astype(jnp.bfloat16)
            pre[half, token_rows, pl.ds(span, span)] = up.astype(jnp.bfloat16)
            low = gated(gate, up).astype(jnp.bfloat16)
            hidden[half, token_rows, :] = low
            out = nt(low, weight_tiles(weight, half, 2))
            acc[...] = jnp.where(step == 0, 0.0, acc[...]) + out

        put_parts(acc, parts, y_ref, group, groups, rows)
        after_group(scatter, group, groups)
        if carried:

            @pl.when(group == 0)
            def _():
                whole_fetch.wait()
                stores[0].start()
                gives[0].start()

            @pl.when(group == 1)
            def _():
                fetch.wait()
                dec_gather.start()

    y_ref[...] += residual
    copies = [
        pltpu.make_async_copy(pre, pre_out, local_sem.at[4]),
        pltpu.make_async_copy(weight, weight_out, local_sem.at[5]),
    ]
    for copy in copies:
        copy.start()
    if carried:
        for v in range(1, 3):
            dec_gather.arrive(v - 1)
            crossings[v - 1].start()
            stores[v].start()
            gives[v].start()
    scatter.pass_on()

    @pl.loop(0, groups)
    def _(group):
        lanes = pl.ds(pl.multiple_of(group * count, count), count)
        at[:, lanes] = block_at(blocks, group, count).T

    last = pltpu.make_async_copy(at, at_out, local_sem.at[6])
    last.start()
    copies.append(last)
    if carried:
        dec_gather.arrive(2)
        crossings[2].start()
        stores[3].start()
        gives[3].start()

    @pl.loop(0, 2 * groups)
    def _(step):
        half, group = lax.rem(step, 2), step // 2
        lanes = pl.ds(pl.multiple_of(group * count, count), count)
        hidden_out[half, :, lanes] = hidden[half, lanes, :].T

    y_ref[...] += scatter.total()
    if carried:
        for v in range(1, wide):
            crossings[v - 1].wait()
            stores[wide + v - 1].start()
            gives[wide + v - 1].start()
        for store, give in zip(stores, gives):
            store.wait()
            give.wait()
        dec_gather.finish()
        for copy in passed:
            copy.wait()
    for copy in copies:
        copy.wait()
    gather.finish()
    scatter.finish()
    for swap in swaps:
        swap.wait_send()


def ffn_forward_call(wide, residual, gain_row, pieces, call_id, carried=()):
    gain_row, gain_at = gain_row
    rows = residual.shape[0]
    total = rows * wide
    quarters, _, columns = pieces[0].shape
    span = quarters * TILE
    low = jnp.bfloat16
    extra_out, extra_scratch = [], []
    if carried:
        depth, attn_columns = carried[0].shape
        extra_out = [jax.ShapeDtypeStruct((2, D, attn_columns), low)] + [
            jax.ShapeDtypeStruct(each.shape, low) for each in carried[1:]
        ]
        size = split_at(depth)
        extra_scratch = [
            pltpu.VMEM((wide, size, attn_columns), low),
            pltpu.VMEM((wide - 1, depth - size, attn_columns), low),
            pltpu.VMEM((depth, attn_columns), low),
        ]
    return pl.pallas_call(
        lambda *refs: ffn_forward_kernel(wide, bool(carried), len(pieces), gain_at, *refs),
        out_shape=[
            jax.ShapeDtypeStruct((rows, D), jnp.float32),
            jax.ShapeDtypeStruct((D, total), low),
            jax.ShapeDtypeStruct((2, total, 2 * span), low),
            jax.ShapeDtypeStruct((2, span, total), low),
            jax.ShapeDtypeStruct((2, quarters, D, columns), low),
        ]
        + extra_out,
        in_specs=[VM, VM] + [HBM] * (len(pieces) + len(carried)),
        out_specs=[VM, HBM, HBM, VM, HBM] + [HBM] * len(extra_out),
        scratch_shapes=[
            pltpu.VMEM((wide, rows, D), low),
            pltpu.VMEM((D, total), low),
            pltpu.VMEM((2, total, 2 * span), low),
            pltpu.VMEM((2, total, span), low),
            pltpu.VMEM((2, quarters, D, columns), low),
            pltpu.VMEM((wide, rows, D), low),
            pltpu.VMEM((3, rows, D), low),
            pltpu.VMEM((token_rows_at_once(wide, rows), D), jnp.float32),
            pltpu.SemaphoreType.DMA((45,)),
            pltpu.SemaphoreType.DMA((45,)),
            pltpu.SemaphoreType.DMA((26,)),
        ]
        + extra_scratch,
        compiler_params=pltpu.CompilerParams(
            collective_id=call_id, has_side_effects=True, vmem_limit_bytes=VMEM_LIMIT
        ),
        name="ffn_forward_%d" % rows,
    )(residual, gain_row, *pieces, *carried)


def ffn_backward_kernel(
    wide, rows_axis, gain_at, x_ref, gains_ref, at_in, pre_in, hidden_in, weight_in, *refs
):
    gain_ref = gains_ref.at[pl.ds(gain_at, 1)]
    (
        ready_in,
        ready_out,
        enc_attn,
        dec_attn,
        dec_gains,
        g2_ref,
        x2_ref,
        y1_ref,
        kv_ref,
        query_ref,
        weights_ref,
        gx_ref,
        gain_out,
        grad_in,
        grad_out,
        sum_in,
        sum_out,
        gy_ref,
        final_out,
        cross_gain,
        kv_grad,
        query_grad,
    ) = refs[:22]
    refs = refs[22:]
    (
        blocks,
        at,
        pre,
        hidden,
        weight,
        parts,
        landing,
        acc,
        give_in,
        give_out,
        got_in,
        got_out,
        send_sem,
        recv_sem,
        local_sem,
    ) = refs[:15]
    rows = x_ref.shape[0]
    span = weight.shape[1] * TILE
    units = FF // (wide * rows_axis * 2)
    core, row = lax.axis_index("section"), lax.axis_index("rows")
    peers = peers_of(wide)
    sems = (send_sem, recv_sem)
    greet(peers + [{"rows": row ^ 1}, {"rows": row ^ 2}])
    loads = [
        pltpu.make_async_copy(weight_in, weight, local_sem.at[0]),
        pltpu.make_async_copy(pre_in, pre, local_sem.at[1]),
        pltpu.make_async_copy(hidden_in, hidden, local_sem.at[2]),
        pltpu.make_async_copy(at_in, at, local_sem.at[3]),
    ]
    line = ReduceRows(ready_in, ready_out, *refs[15:19], sems, 12, local_sem, 6)
    line.start()
    g_ref, context_grad = refs[19:21]
    fetches = [
        pltpu.make_async_copy(
            dec_attn.at[1, :, pl.ds(HD, 2 * HD)], at.at[:, pl.ds(0, 2 * HD)], local_sem.at[10]
        )
    ]
    for tile in range(2 * HD // TILE):
        fetches.append(
            pltpu.make_async_copy(
                enc_attn.at[1, :, pl.ds(HD + tile * TILE, TILE)],
                give_in.at[tile // 2, tile % 2],
                local_sem.at[11 + tile],
            )
        )
    for fetch in fetches:
        fetch.start()
    for load in loads[:3]:
        load.start()
    for fetch in fetches:
        fetch.wait()
    cross_backward_rows(
        g2_ref,
        x2_ref,
        gains_ref,
        Tiles(give_in, 0),
        Tiles(give_in, HD // TILE),
        y1_ref,
        dec_gains,
        at.at[:, pl.ds(0, HD)],
        at.at[:, pl.ds(HD, HD)],
        kv_ref,
        query_ref,
        weights_ref,
        g_ref,
        gy_ref,
        final_out,
        cross_gain,
        kv_grad,
        query_grad,
        context_grad,
    )
    blocks[0] = g_ref[...].astype(jnp.bfloat16)
    gather = GatherPlane(blocks, sems, 0, peers, rows)
    gather.start()
    loads[3].start()
    scatter = ScatterPlane(parts, landing, sems, 4, peers, rows)
    loads[0].wait()
    loads[1].wait()
    count = token_rows_at_once(wide, rows)
    groups = wide * rows // count

    @pl.loop(0, groups)
    def _(group):
        @pl.when(group == 1)
        def _():
            line.loaded()
            line.turn(0)

        @pl.when(group == 3)
        def _():
            line.turn(1)

        before_group(gather, group, groups)
        token_rows = pl.ds(pl.multiple_of(group * count, count), count)

        @pl.loop(0, 2)
        def _(half):
            block = block_at(blocks, group, count)
            grad_hidden = matmul(block, weight_tiles(weight, half, 2))
            gate = pre[half, token_rows, pl.ds(0, span)].astype(jnp.float32)
            up = pre[half, token_rows, pl.ds(span, span)].astype(jnp.float32)
            value, slope = gate_slopes(gate, up)
            low_gate = (grad_hidden * up * slope).astype(jnp.bfloat16)
            low_up = (grad_hidden * value).astype(jnp.bfloat16)
            pre[half, token_rows, pl.ds(0, span)] = low_gate
            pre[half, token_rows, pl.ds(span, span)] = low_up
            out = nt(low_gate, weight_tiles(weight, half, 0)) + nt(
                low_up, weight_tiles(weight, half, 1)
            )
            acc[...] = jnp.where(half == 0, 0.0, acc[...]) + out

        put_parts(acc, parts, gx_ref, group, groups, rows)
        after_group(scatter, group, groups)
    loads[2].wait()
    loads[3].wait()
    chunk = 2 * TILE
    swap_out = remote(give_out, got_out, sems, 11, peers[-1])
    swap_in = remote(give_in, got_in, sems, 10, peers[-1])
    store_in = pltpu.make_async_copy(got_in, grad_in, local_sem.at[4])
    store_out = pltpu.make_async_copy(got_out, grad_out, local_sem.at[5])

    @pl.loop(0, 2 * rows_axis)
    def _(step):
        half = jnp.where(step < rows_axis, 1 - core, core)
        index = lax.rem(step, rows_axis)
        columns = pl.ds(pl.multiple_of(index * chunk, chunk), chunk)
        total = matmul(at[...], pre[half, :, columns])

        @pl.when(step < rows_axis)
        def _():
            for part in range(2):
                give_in[index, part] = total[:, part * TILE : (part + 1) * TILE].astype(
                    jnp.bfloat16
                )

        @pl.when(step == rows_axis - 1)
        def _():
            swap_in.start()
            scatter.pass_on()

        @pl.when(step == rows_axis)
        def _():
            swap_in.wait_recv()

        @pl.when(step >= rows_axis)
        def _():
            for part in range(2):
                got_in[index, part] = (
                    total[:, part * TILE : (part + 1) * TILE]
                    + got_in[index, part].astype(jnp.float32)
                ).astype(jnp.bfloat16)

    store_in.start()
    line.turn(2)

    @pl.loop(0, 2)
    def _(step):
        half = lax.rem(core + 1 + step, 2)
        total = matmul(hidden[half], blocks[...].reshape(wide * rows, D))

        @pl.when(step == 0)
        def _():
            for index in range(rows_axis):
                give_out[index] = total[index * TILE : index * TILE + units].astype(jnp.bfloat16)
            swap_out.start()

        @pl.when(step == 1)
        def _():
            swap_out.wait_recv()
            for index in range(rows_axis):
                got_out[index] = (
                    total[index * TILE : index * TILE + units]
                    + got_out[index].astype(jnp.float32)
                ).astype(jnp.bfloat16)
            store_out.start()

    total = gx_ref[...] + scatter.total()
    grad_residual, grad_gain = norm_pull(x_ref[...], gain_ref[...], total)
    gx_ref[...] = g_ref[...].astype(jnp.float32) + grad_residual
    gain_out[...] = grad_gain
    for index in range(3):
        line.close(index)
    stores = [
        pltpu.make_async_copy(refs[15].at[0], sum_in, local_sem.at[6]),
        pltpu.make_async_copy(refs[17].at[0], sum_out, local_sem.at[7]),
    ]
    for store in stores:
        store.start()
    for store in stores:
        store.wait()
    line.finish()
    store_in.wait()
    store_out.wait()
    swap_in.wait_send()
    swap_out.wait_send()
    gather.finish()
    scatter.finish()


def decoder_kernel(wide, rows_axis, gain_at, cot_ref, gains_ref, *refs):
    pieces, refs = refs[: 2 * wide - 1], refs[2 * wide - 1 :]
    gain_ref = gains_ref.at[pl.ds(gain_at, 1)]
    x2_ref, enc_gains, embed_ref, bias_ref, dec_lengths, enc_lengths, enc_attn, dec_attn = refs[:8]
    y_ref, gx_ref, gain_out, grad_in, grad_out, y1_ref = refs[8:14]
    self_kept, cross_kept, refs = refs[14:19], refs[19:25], refs[25:]
    dec_in, dec_rest, enc_rest, x_ref = refs[:4]
    refs = refs[4:]
    (
        blocks,
        cots,
        weight,
        pre,
        hidden,
        acc,
        grad_acc,
        parts,
        grad_parts,
        landing,
        grad_landing,
        give_in,
        give_out,
        got_in,
        got_out,
        send_sem,
        recv_sem,
        local_sem,
    ) = refs
    rows = x_ref.shape[0]
    total_rows = wide * rows
    span = weight.shape[1] * TILE
    units = FF // (wide * rows_axis * 2)
    core = lax.axis_index("section")
    peers = peers_of(wide)
    sems = (send_sem, recv_sem)
    low = jnp.bfloat16
    loads, swaps = weight_copies(pieces, weight, sems, 20, local_sem, 2, peers[-1])
    fetches = [
        pltpu.make_async_copy(dec_attn.at[0], dec_in, local_sem.at[9]),
        pltpu.make_async_copy(dec_attn.at[1], dec_rest, local_sem.at[10]),
        pltpu.make_async_copy(
            enc_attn.at[1, :, pl.ds(HD, 2 * HD)], enc_rest, local_sem.at[11]
        ),
    ]
    for fetch in fetches:
        fetch.start()
    greet(peers)
    cots[0] = cot_ref[core]
    gather = GatherPlane(blocks, sems, 0, peers, rows)
    cot_gather = GatherPlane(cots, sems, 4, peers, rows)
    cot_gather.start()
    for fetch in fetches:
        fetch.wait()
    for load, swap in zip(loads, swaps):
        load.start()
        swap.start()
    thirds = [pl.ds(i * HD, HD) for i in range(3)]
    self_forward_rows(
        True, embed_ref, gains_ref, dec_in, dec_rest.at[:, thirds[0]], bias_ref, dec_lengths, y1_ref, *self_kept
    )
    cross_forward_rows(
        x2_ref,
        enc_gains,
        enc_rest.at[:, thirds[0]],
        enc_rest.at[:, thirds[1]],
        y1_ref,
        gains_ref,
        dec_rest.at[:, thirds[1]],
        dec_rest.at[:, thirds[2]],
        dec_lengths,
        enc_lengths,
        x_ref,
        *cross_kept,
    )
    residual = x_ref[...]
    blocks[0] = (residual * rms_rows(residual) * gain_ref[...]).astype(low)
    gather.start()
    for index in range(3):
        cot_gather.arrive(index)
        gather.arrive(index)
    for load in loads:
        load.wait()

    @pl.loop(0, 2)
    def _(step):
        @pl.when(step == 1)
        def _():
            for swap in swaps:
                swap.wait_recv()

        half = lax.rem(core + step, 2)
        block = blocks[...].reshape(total_rows, D)
        gate = matmul(block, weight_tiles(weight, half, 0))
        up = matmul(block, weight_tiles(weight, half, 1))
        value, slope = gate_slopes(gate, up)
        low_hidden = (value * up).astype(low)
        hidden[half] = low_hidden
        grad_hidden = matmul(cots[...].reshape(total_rows, D), weight_tiles(weight, half, 2))
        low_gate = (grad_hidden * up * slope).astype(low)
        low_up = (grad_hidden * value).astype(low)
        pre[half, :, pl.ds(0, span)] = low_gate
        pre[half, :, pl.ds(span, span)] = low_up
        grad = nt(low_gate, weight_tiles(weight, half, 0)) + nt(
            low_up, weight_tiles(weight, half, 1)
        )
        grad_acc[...] = jnp.where(step == 0, 0.0, grad_acc[...]) + grad
        out = nt(low_hidden, weight_tiles(weight, half, 2))
        acc[...] = jnp.where(step == 0, 0.0, acc[...]) + out

    grad_scatter = ScatterPlane(grad_parts, grad_landing, sems, 8, peers, rows)
    scatter = ScatterPlane(parts, landing, sems, 14, peers, rows)
    put_parts(grad_acc, grad_parts, gx_ref, 0, 1, rows)
    after_group(grad_scatter, 0, 1)
    put_parts(acc, parts, y_ref, 0, 1, rows)
    after_group(scatter, 0, 1)
    swap_in = remote(give_in, got_in, sems, 27, peers[-1])
    swap_out = remote(give_out, got_out, sems, 28, peers[-1])
    store_in = pltpu.make_async_copy(got_in, grad_in, local_sem.at[0])
    store_out = pltpu.make_async_copy(got_out, grad_out, local_sem.at[1])
    chunk = 2 * TILE

    @pl.loop(0, 2 * rows_axis)
    def _(step):
        half = jnp.where(step < rows_axis, 1 - core, core)
        index = lax.rem(step, rows_axis)
        columns = pl.ds(pl.multiple_of(index * chunk, chunk), chunk)
        total = tn(blocks[...].reshape(total_rows, D), pre[half, :, columns])

        @pl.when(step < rows_axis)
        def _():
            for part in range(2):
                give_in[index, part] = total[:, part * TILE : (part + 1) * TILE].astype(low)

        @pl.when(step == rows_axis - 1)
        def _():
            swap_in.start()
            grad_scatter.pass_on()
            scatter.pass_on()

        @pl.when(step == rows_axis)
        def _():
            swap_in.wait_recv()

        @pl.when(step >= rows_axis)
        def _():
            for part in range(2):
                got_in[index, part] = (
                    total[:, part * TILE : (part + 1) * TILE]
                    + got_in[index, part].astype(jnp.float32)
                ).astype(low)

    store_in.start()

    @pl.loop(0, 2)
    def _(step):
        half = lax.rem(core + 1 + step, 2)
        total = tn(hidden[half], cots[...].reshape(total_rows, D))

        @pl.when(step == 0)
        def _():
            for index in range(rows_axis):
                give_out[index] = total[index * TILE : index * TILE + units].astype(low)
            swap_out.start()

        @pl.when(step == 1)
        def _():
            swap_out.wait_recv()
            for index in range(rows_axis):
                got_out[index] = (
                    total[index * TILE : index * TILE + units]
                    + got_out[index].astype(jnp.float32)
                ).astype(low)
            store_out.start()

    grad_residual, gain_out[...] = norm_pull(
        x_ref[...], gain_ref[...], gx_ref[...] + grad_scatter.total()
    )
    gx_ref[...] = cot_ref[core].astype(jnp.float32) + grad_residual
    y_ref[...] = y_ref[...] + residual + scatter.total()
    store_in.wait()
    store_out.wait()
    swap_in.wait_send()
    swap_out.wait_send()
    for each in (gather, cot_gather, grad_scatter, scatter):
        each.finish()
    for swap in swaps:
        swap.wait_send()


def decoder_call(
    wide, rows_axis, cot, gain_row, pieces, x2, enc_gains, embed, bias, dec_lengths, enc_lengths, enc_attn, dec_attn, call_id
):
    gain_row, gain_at = gain_row
    rows, enc_rows = embed.shape[1], x2.shape[0]
    total = wide * rows
    quarters, _, columns = pieces[0].shape
    span = quarters * TILE
    low = jnp.bfloat16
    units = FF // (wide * rows_axis * 2)
    share_in = (rows_axis, 2, D, TILE)
    share_out = (rows_axis, units, D)
    outs = [
        ((rows, D), jnp.float32),
        ((rows, D), jnp.float32),
        ((1, D), jnp.float32),
        (share_in, low),
        (share_out, low),
        ((rows, D), jnp.float32),
        ((rows, D), low),
        ((rows, D), low),
        ((rows, 3 * HD), low),
        ((rows, HD), low),
        ((H, rows, rows), jnp.float32),
        ((enc_rows, D), low),
        ((enc_rows, 2 * HD), low),
        ((rows, D), low),
        ((rows, HD), low),
        ((rows, HD), low),
        ((H, rows, enc_rows), jnp.float32),
    ]
    y3, g2, gain, grad_in, grad_out, y1, *kept = pl.pallas_call(
        lambda *refs: decoder_kernel(wide, rows_axis, gain_at, *refs),
        out_shape=[jax.ShapeDtypeStruct(shape, kind) for shape, kind in outs],
        in_specs=[VM, VM] + [HBM] * len(pieces) + [VM] * 4 + [SM, SM, HBM, HBM],
        out_specs=[VM, VM, VM, HBM, HBM] + [VM] * 12,
        scratch_shapes=[
            pltpu.VMEM((D, 3 * HD), low),
            pltpu.VMEM((D, 3 * HD), low),
            pltpu.VMEM((D, 2 * HD), low),
            pltpu.VMEM((rows, D), jnp.float32),
            pltpu.VMEM((wide, rows, D), low),
            pltpu.VMEM((wide, rows, D), low),
            pltpu.VMEM((2, quarters, D, columns), low),
            pltpu.VMEM((2, total, 2 * span), low),
            pltpu.VMEM((2, total, span), low),
            pltpu.VMEM((total, D), jnp.float32),
            pltpu.VMEM((total, D), jnp.float32),
            pltpu.VMEM((wide, rows, D), low),
            pltpu.VMEM((wide, rows, D), low),
            pltpu.VMEM((3, rows, D), low),
            pltpu.VMEM((3, rows, D), low),
            pltpu.VMEM(share_in, low),
            pltpu.VMEM(share_out, low),
            pltpu.VMEM(share_in, low),
            pltpu.VMEM(share_out, low),
            pltpu.SemaphoreType.DMA((29,)),
            pltpu.SemaphoreType.DMA((29,)),
            pltpu.SemaphoreType.DMA((12,)),
        ],
        compiler_params=pltpu.CompilerParams(
            collective_id=call_id, has_side_effects=True, vmem_limit_bytes=VMEM_LIMIT
        ),
        name="decoder",
    )(cot, gain_row, *pieces, x2, enc_gains, embed, bias, dec_lengths, enc_lengths, enc_attn, dec_attn)
    return y3, g2, gain, (grad_in, grad_out), y1, kept[:5], kept[5:]


GELU_A = float(np.sqrt(2.0 / np.pi))
GELU_B = 0.044715


class Tiles:
    def __init__(self, ref, first):
        self.ref, self.first = ref, first

    def __getitem__(self, _):
        tiles = range(self.first, self.first + HD // TILE)
        return jnp.concatenate([self.ref[tile // 2, tile % 2] for tile in tiles], axis=1)


def ffn_backward_call(wide, rows_axis, residual, gain_row, kept, call_id, carried, crossed):
    gain_row, gain_at = gain_row
    at, pre, hidden, weight = kept
    rows = residual.shape[0]
    target_rows = crossed[3].shape[0]
    low = jnp.bfloat16
    units = FF // (wide * rows_axis * 2)
    share_in = (rows_axis, 2, D, TILE)
    share_out = (rows_axis, units, D)
    line_of = jax.ShapeDtypeStruct((1, D), jnp.float32)
    return pl.pallas_call(
        lambda *refs: ffn_backward_kernel(wide, rows_axis, gain_at, *refs),
        out_shape=[
            jax.ShapeDtypeStruct((rows, D), jnp.float32),
            line_of,
            jax.ShapeDtypeStruct(share_in, low),
            jax.ShapeDtypeStruct(share_out, low),
        ]
        + [jax.ShapeDtypeStruct(each.shape[1:], low) for each in carried]
        + [
            jax.ShapeDtypeStruct((target_rows, D), jnp.float32),
            line_of,
            line_of,
            jax.ShapeDtypeStruct((rows, 2 * HD), low),
            jax.ShapeDtypeStruct((target_rows, HD), low),
        ],
        in_specs=[VM, VM] + [HBM] * 8 + [VM] * 7,
        out_specs=[VM, VM, HBM, HBM, HBM, HBM] + [VM] * 5,
        scratch_shapes=[
            pltpu.VMEM((wide, rows, D), low),
            pltpu.VMEM(at.shape, low),
            pltpu.VMEM(pre.shape, low),
            pltpu.VMEM(hidden.shape, low),
            pltpu.VMEM(weight.shape, low),
            pltpu.VMEM((wide, rows, D), low),
            pltpu.VMEM((3, rows, D), low),
            pltpu.VMEM((token_rows_at_once(wide, rows), D), jnp.float32),
            pltpu.VMEM(share_in, low),
            pltpu.VMEM(share_out, low),
            pltpu.VMEM(share_in, low),
            pltpu.VMEM(share_out, low),
            pltpu.SemaphoreType.DMA((21,)),
            pltpu.SemaphoreType.DMA((21,)),
            pltpu.SemaphoreType.DMA((17,)),
        ]
        + reduce_rows_scratch(units)
        + [pltpu.VMEM((rows, D), jnp.float32), pltpu.VMEM((target_rows, HD), low)],
        compiler_params=pltpu.CompilerParams(
            collective_id=call_id, has_side_effects=True, vmem_limit_bytes=VMEM_LIMIT
        ),
        name="ffn_backward_%d" % rows,
    )(residual, gain_row, at, pre, hidden, weight, *carried, *crossed)


def start_weights_kernel(
    wide, rows, win_in, wout_in, cin_in, cout_in, ffn_in, ffn_out, gains, biases, enc_hot, dec_hot,
    attn_ref, dec_half, enc_gains, dec_gains, enc_bias, dec_bias, *refs
):
    enc, dec = refs[:wide], refs[wide : 2 * wide]
    held, blocks, spare, in_ref, out_ref, ffn, enc_row, dec_row, send_sem, recv_sem, local_sem = refs[2 * wide :]
    core, place = lax.axis_index("section"), lax.axis_index("wide")
    peers = peers_of(wide)
    sibling = peers[-1]
    sems = (send_sem, recv_sem)
    depth = blocks.shape[1]
    big = [
        pltpu.make_async_copy(ffn_in.at[0], in_ref, local_sem.at[4]),
        pltpu.make_async_copy(ffn_out, out_ref, local_sem.at[5]),
    ]
    packs = [
        pltpu.make_async_copy(each, held.at[:, pl.ds(i * HD, HD)], local_sem.at[1 + i])
        for i, each in enumerate((wout_in, cin_in.at[0], cout_in.at[0]))
    ]
    for pack in packs:
        pack.start()
    greet(peers)
    for pack in packs:
        pack.wait()

    @pl.when(core == 0)
    def _():
        keep = pltpu.make_async_copy(win_in.at[0], blocks.at[0], local_sem.at[0])
        keep.start()
        give = remote(held, blocks.at[0], sems, 0, sibling)
        give.start()
        remote(win_in.at[0], spare, sems, 1, sibling).wait_recv()
        keep.wait()

    @pl.when(core == 1)
    def _():
        keep = pltpu.make_async_copy(held, spare, local_sem.at[0])
        keep.start()
        give = remote(win_in.at[0], spare, sems, 1, sibling)
        give.start()
        remote(held, blocks.at[0], sems, 0, sibling).wait_recv()
        keep.wait()

    gather = GatherPlane(blocks, sems, 2, peers, depth)
    gather.start()
    for load in big:
        load.start()
    dec_copy = pltpu.make_async_copy(spare, dec_half, local_sem.at[0])
    dec_copy.start()
    stores, gives = [], []
    for v in range(wide):
        rows_of = pl.ds(pl.multiple_of((place ^ v) * depth, 16), depth)
        stores.append(
            pltpu.make_async_copy(blocks.at[v], attn_ref.at[core, rows_of], local_sem.at[6 + v])
        )
        gives.append(remote(blocks.at[v], attn_ref.at[core, rows_of], sems, 6 + v, sibling))
    stores[0].start()
    gives[0].start()
    for load in big:
        load.wait()
    units = FF // (wide * rows * 2)
    per_row = FF // rows
    row_ids = lax.broadcasted_iota(jnp.int32, (2 * TILE, TILE), 0)
    lane_ids = lax.broadcasted_iota(jnp.int32, (2 * TILE, TILE), 1)
    def prepare(index):
        target, half = index // 2, index % 2
        offset = index * units
        start, shift = offset // TILE * TILE, offset % TILE
        picks = ((row_ids == lane_ids + shift) & (lane_ids < units)).astype(jnp.bfloat16)
        window = min(2 * TILE, per_row - start)
        picks = picks[:window]
        for part in range(3):
            for row in range(rows):
                if part < 2:
                    source = in_ref[:, pl.ds(part * FF + row * per_row + start, window)]
                else:
                    source = out_ref[:, pl.ds(row * per_row + start, window)]
                tile = matmul(source, picks)
                ffn[half, target ^ place, row, :, pl.ds(part * TILE, TILE)] = tile.astype(
                    jnp.bfloat16
                )

    lines = 10 + 2 * wide
    gain_moves = [remote(target, target, sems, lines, sibling) for target in (enc_gains, dec_gains)]
    line_moves = [
        remote(row_ref, row_ref, sems, lines + 1, sibling) for row_ref in (enc_row, dec_row)
    ]
    for own, (gain_ref, row_ref, hot) in enumerate(
        ((enc_gains, enc_row, enc_hot), (dec_gains, dec_row, dec_hot))
    ):

        @pl.when(core == own)
        def _():
            for index in range(gains.shape[0]):
                gain_ref[pl.ds(index, 1), :] = gains[index]
            row_ref[pl.ds(0, H), :] = jnp.dot(
                biases[:, 0, :], hot[...], precision=HIGHEST, preferred_element_type=jnp.float32
            )
            gain_moves[own].start()
            line_moves[own].start()

    for index in range(2 * wide):
        prepare(index)
    for own in range(2):

        @pl.when(core == own)
        def _():
            gain_moves[1 - own].wait_recv()
            line_moves[1 - own].wait_recv()
            gain_moves[own].wait_send()
            line_moves[own].wait_send()

    bias_rows(enc_row, enc_bias)
    bias_rows(dec_row, dec_bias)

    def move(outs, base):
        for v in range(wide):
            pltpu.make_async_copy(ffn.at[core, v], outs[v], local_sem.at[10 + v]).start()
            remote(ffn.at[1 - core, v], outs[v], sems, base + v, sibling).start()

    def settle(outs, base):
        for v in range(wide):
            pltpu.make_async_copy(ffn.at[core, v], outs[v], local_sem.at[10 + v]).wait()
            remote(ffn.at[1 - core, v], outs[v], sems, base + v, sibling).wait_send()

    def receive(outs, base):
        for v in range(wide):
            remote(ffn.at[0, v], outs[v], sems, base + v, sibling).wait_recv()

    @pl.when(core == 0)
    def _():
        move(enc, 10)

    @pl.when(core == 1)
    def _():
        move(dec, 10 + wide)

    for v in range(1, wide):
        gather.arrive(v - 1)
        stores[v].start()
        gives[v].start()
    for v in range(wide):
        gives[v].wait_recv()
        stores[v].wait()
    dec_copy.wait()

    @pl.when(core == 0)
    def _():
        settle(enc, 10)
        receive(dec, 10 + wide)
        remote(held, blocks.at[0], sems, 0, sibling).wait_send()

    @pl.when(core == 1)
    def _():
        settle(dec, 10 + wide)
        receive(enc, 10)
        remote(win_in.at[0], spare, sems, 1, sibling).wait_send()

    gather.finish()
    for give in gives:
        give.wait_send()


def start_weights(wide, rows, attn_in, attn_out, cross_in, cross_out, ffn_in, ffn_out, gains, biases):
    depth = ffn_in.shape[1]
    low = jnp.bfloat16
    block = jax.ShapeDtypeStruct((rows, depth, 3 * TILE), low)
    part = (depth, 3 * HD)
    attn, dec_half, *outs = pl.pallas_call(
        lambda *refs: start_weights_kernel(wide, rows, *refs),
        out_shape=[
            jax.ShapeDtypeStruct((2, wide * depth, 3 * HD), low),
            jax.ShapeDtypeStruct(part, low),
            jax.ShapeDtypeStruct((gains.shape[0], D), jnp.float32),
            jax.ShapeDtypeStruct((gains.shape[0], D), jnp.float32),
            jax.ShapeDtypeStruct((H, LE, LE), jnp.float32),
            jax.ShapeDtypeStruct((H, LD, LD), jnp.float32),
        ]
        + [block] * (2 * wide),
        in_specs=[HBM] * 6 + [VM] * 4,
        out_specs=[HBM] * 2 + [VM] * 4 + [HBM] * (2 * wide),
        scratch_shapes=[
            pltpu.VMEM(part, low),
            pltpu.VMEM((wide,) + part, low),
            pltpu.VMEM(part, low),
            pltpu.VMEM(ffn_in.shape[1:], low),
            pltpu.VMEM((depth, FF), low),
            pltpu.VMEM((2, wide) + block.shape, low),
            pltpu.VMEM((8, 2 * LE), jnp.float32),
            pltpu.VMEM((8, 2 * LD), jnp.float32),
            pltpu.SemaphoreType.DMA((12 + 2 * wide,)),
            pltpu.SemaphoreType.DMA((12 + 2 * wide,)),
            pltpu.SemaphoreType.DMA((10 + wide,)),
        ],
        compiler_params=pltpu.CompilerParams(
            collective_id=1, has_side_effects=True, vmem_limit_bytes=VMEM_LIMIT
        ),
        name="start_weights",
    )(attn_in, attn_out[0].T, cross_in, cross_out, ffn_in, ffn_out[0].T, gains, biases, distance_hot(LE, True, 0), distance_hot(LD, False, 0))
    return attn, dec_half, outs[:2], outs[2:4], outs[4 : 4 + wide], outs[4 + wide :]


def split_at(rows):
    return (rows // 2 + 15) // 16 * 16


class ReduceWeights:
    def __init__(self, batch, bufs, sems, base, peers, others):
        self.own, self.land, self.plane, self.send, self.zland = bufs
        self.batch = batch
        core, place, row = lax.axis_index("section"), lax.axis_index("wide"), lax.axis_index("rows")
        wide, size = self.own.shape[:2]
        depth = batch.shape[0] // wide

        def rows_at(v, half):
            start = (place ^ v) * depth + half * (depth - size)
            return pl.ds(pl.multiple_of(start, 16), size)

        self.mine = [rows_at(v, core) for v in range(wide)]
        self.swaps = [
            remote(batch.at[rows_at(v, 1 - core)], self.land.at[v], sems, base + v, peers[-1])
            for v in range(wide)
        ]
        base += wide
        self.scatter = ScatterPlane(self.own, self.plane, sems, base, peers, size)
        base += 6
        chunk = batch.shape[1] // (len(others) + 1)

        def lanes(k):
            return pl.ds(pl.multiple_of((row ^ k) * chunk, TILE), chunk)

        self.kept, self.relayed = lanes(0), lanes(2)
        near, far = others[0], others[1]
        self.spreads = [
            remote(self.send.at[:, lanes(1)], self.zland.at[0], sems, base, near),
            remote(self.send.at[:, lanes(3)], self.zland.at[1], sems, base + 1, near),
            remote(self.send.at[:, lanes(2)], self.zland.at[2], sems, base + 2, far),
        ]

    def start(self):
        for v in (3, 1, 2, 0):
            self.swaps[v].start()

    def join(self):
        def add(v):
            self.swaps[v].wait_recv()
            own = self.batch[self.mine[v], :]
            self.own[v] = (own.astype(jnp.float32) + self.land[v].astype(jnp.float32)).astype(
                jnp.bfloat16
            )

        add(3)
        self.scatter.send_far()
        add(1)
        self.scatter.send_early(0)
        add(2)
        self.scatter.send_early(1)
        add(0)

    def given(self):
        for swap in self.swaps:
            swap.wait_send()

    def pass_on(self):
        self.scatter.pass_on()

    def spread(self):
        self.send[...] = (self.own[0].astype(jnp.float32) + self.scatter.total()).astype(
            jnp.bfloat16
        )
        self.spreads[0].start()
        self.spreads[1].start()

    def relay(self):
        self.spreads[1].wait_recv()
        self.send[:, self.relayed] = (
            self.send[:, self.relayed].astype(jnp.float32) + self.zland[1].astype(jnp.float32)
        ).astype(jnp.bfloat16)
        self.spreads[2].start()

    def total(self):
        out = self.send[:, self.kept].astype(jnp.float32)
        for index in (0, 2):
            self.spreads[index].wait_recv()
            out = out + self.zland[index].astype(jnp.float32)
        return out

    def finish(self):
        for copy in self.spreads:
            copy.wait_send()
        self.scatter.finish()


def reduce_weights_scratch(wide, rows, size, columns):
    low = jnp.bfloat16
    return [
        pltpu.VMEM((wide, size, columns), low),
        pltpu.VMEM((wide, size, columns), low),
        pltpu.VMEM((3, size, columns), low),
        pltpu.VMEM((size, columns), low),
        pltpu.VMEM((rows - 1, size, columns // rows), low),
    ]


def last_kernel(wide, rows, *refs):
    cross, refs = refs[:6], refs[6:]
    dec_in, dec_out, enc_in, enc_out, y_ref, dec_attn, enc_attn = refs[:7]
    dec_self, enc_self, gains = refs[7:14], refs[14:21], refs[21:25]
    out_ref, ffn_ref, small_out, y_half, x_half, t_half = refs[25:31]
    refs = refs[31:]
    batch_bufs = [refs[i * 5 : i * 5 + 5] for i in range(3)]
    line_bufs, refs = refs[15:19], refs[19:]
    held, win, wout, gx, gt, context_e, projected_e, context_d, projected_d = refs[:9]
    keep, give, ready, landing, small, small_land, small_plane, small_rows = refs[9:17]
    halves, (sums_ref, send_sem, recv_sem, local_sem) = refs[17:23], refs[23:]
    core, place, row = lax.axis_index("section"), lax.axis_index("wide"), lax.axis_index("rows")
    peers = peers_of(wide)
    sibling = peers[-1]
    crossed = [{"section": 1 - core, "wide": place ^ v} for v in range(1, wide)]
    others = [{"rows": row ^ k} for k in range(1, rows)]
    sems = (send_sem, recv_sem)
    depth = held.shape[0] // wide
    units = dec_out.shape[0]
    low = jnp.bfloat16
    straight = (
        lax.broadcasted_iota(jnp.int32, (units, TILE), 0)
        == lax.broadcasted_iota(jnp.int32, (units, TILE), 1)
    ).astype(low)

    def attn_loads(source):
        return [
            pltpu.make_async_copy(source.at[0], win, local_sem.at[0]),
            pltpu.make_async_copy(source.at[1, :, pl.ds(0, HD)], wout, local_sem.at[1]),
        ]

    for load in attn_loads(dec_attn):
        load.start()
    greet(peers + crossed + others)
    per_batch = wide + 6 + rows - 1
    batches = [
        ReduceWeights(held, bufs, sems, i * per_batch, peers, others)
        for i, bufs in enumerate(batch_bufs)
    ]
    base = 3 * per_batch
    line = ReduceRows(enc_in, enc_out, *line_bufs, sems, base, local_sem, 2 + wide)
    base += 9
    local_base = 6 + wide
    first = remote(small.at[1 - core], small_land, sems, base, sibling)
    plane = [
        remote(small.at[core], small_plane.at[v - 1], sems, base + v, peers[v - 1])
        for v in range(1, wide)
    ]
    base += wide
    spread_small = [
        remote(small.at[core], small_rows.at[k - 1], sems, base + k - 1, others[k - 1])
        for k in range(1, rows)
    ]
    base += rows - 1
    hand_base = base
    base += 6 * wide

    def hand(section, source, v, piece):
        index = piece * wide + v
        return pltpu.make_async_remote_copy(
            src_ref=ready.at[section, v, piece],
            dst_ref=landing.at[source, v, piece],
            send_sem=send_sem.at[hand_base + section * 3 * wide + index],
            recv_sem=recv_sem.at[hand_base + source * 3 * wide + index],
            device_id={"section": section, "wide": place ^ v},
            device_id_type=MESH,
        )

    def hand_out(section, piece, value):
        for owner in range(wide):
            ready[section, owner ^ place, piece] = value[owner * depth : (owner + 1) * depth]
        for v in range(1, wide):
            hand(section, core, v, piece).start()

        @pl.when(core == section)
        def _():
            landing[core, 0, piece] = ready[section, 0, piece]

        @pl.when(core != section)
        def _():
            hand(section, core, 0, piece).start()

    def handed(section):
        for piece in range(3):
            for v in range(1, wide):
                hand(section, core, v, piece).wait_send()

            @pl.when(core != section)
            def _():
                hand(section, core, 0, piece).wait_send()

    def came(source):
        for piece in range(3):
            for v in range(1, wide):
                hand(0, source, v, piece).wait_recv()

            @pl.when(core != source)
            def _():
                hand(0, source, 0, piece).wait_recv()

    half_copies = []

    def by_half(index, value, target):
        mine, its = halves[2 * index : 2 * index + 2]
        middle = D // 2
        for own in range(2):

            @pl.when(core == own)
            def _():
                parts = (value[:, :middle], value[:, middle:]) if index != 1 else (value[:middle], value[middle:])
                mine[...] = parts[own].astype(mine.dtype)
                its[...] = parts[1 - own].astype(its.dtype)

        copies = (
            pltpu.make_async_copy(mine, target.at[core], local_sem.at[local_base + 1 + index]),
            remote(its, target.at[core], sems, base + index, sibling),
        )
        for copy in copies:
            copy.start()
            half_copies.append(copy)

    line.start()
    cross_weights(*cross, held)
    batches[0].start()
    by_half(0, y_ref[...], y_half)
    small[...] = jnp.zeros_like(small)
    for i, gain in enumerate(gains):
        small[i // 2, pl.ds(1 + i % 2, 1), pl.ds(0, D)] = gain[...]
    batches[0].join()
    g_ref, x_ref, gain_ref, normed_ref, projected_ref, context_ref, weights_ref = dec_self
    for load in attn_loads(dec_attn):
        load.wait()
    self_backward_rows(
        g_ref, x_ref, gain_ref, win, wout, projected_ref, weights_ref, gt, small.at[1], context_d, projected_d, sums_ref
    )
    for load in attn_loads(enc_attn):
        load.start()
    batches[0].given()
    self_backward_weights(g_ref, normed_ref, context_ref, projected_d, held)
    batches[1].start()
    line.loaded()
    line.turn(0)
    batches[0].pass_on()
    for piece in range(2):
        hand_out(1, piece, dec_in[piece])
    hand_out(1, 2, tn(dec_out[...], straight).astype(low))
    by_half(2, gt[...], t_half)
    g_ref, x_ref, gain_ref, normed_ref, projected_ref, context_ref, weights_ref = enc_self
    for load in attn_loads(enc_attn):
        load.wait()
    self_backward_rows(
        g_ref, x_ref, gain_ref, win, wout, projected_ref, weights_ref, gx, small.at[0], context_e, projected_e, sums_ref
    )
    first.start()
    batches[1].join()
    batches[1].given()
    self_backward_weights(g_ref, normed_ref, context_ref, projected_e, held)
    batches[2].start()
    line.turn(1)
    batches[0].spread()
    first.wait()
    small[core] = small[core] + small_land[...]
    for copy in plane:
        copy.start()
    batches[2].join()
    batches[1].pass_on()
    by_half(1, gx[...].T, x_half)
    for copy in plane:
        copy.wait()
    small[core] = small[core] + jnp.sum(small_plane[...], axis=0)
    for copy in spread_small:
        copy.start()
    line.turn(2)
    batches[0].relay()
    batches[1].spread()
    batches[2].pass_on()
    batches[1].relay()
    batches[2].spread()
    line.close(0)
    hand_out(0, 0, line_bufs[0][0, 0])
    line.close(1)
    hand_out(0, 1, line_bufs[0][0, 1])
    batches[2].relay()
    line.close(2)
    hand_out(0, 2, tn(line_bufs[2][0], straight).astype(low))
    part = held.shape[1] // rows // 2
    span = keep.shape[1] - part
    crosses = batches[0].total()
    selfs = [batches[2].total(), batches[1].total()]
    for own in range(2):

        @pl.when(core == own)
        def _():
            keep[:, pl.ds(0, span)] = selfs[own]
            keep[:, pl.ds(span, part)] = crosses[:, own * part : (own + 1) * part]
            give[:, pl.ds(0, span)] = selfs[1 - own]
            give[:, pl.ds(span, part)] = crosses[:, (1 - own) * part : (2 - own) * part]

    store = pltpu.make_async_copy(keep, out_ref.at[core], local_sem.at[local_base + 4])
    last = remote(give, out_ref.at[core], sems, base + 3, sibling)
    store.start()
    last.start()
    for copy in spread_small:
        copy.wait()
    small_out[...] = small[core] + jnp.sum(small_rows[...], axis=0)
    handed(0)
    handed(1)
    came(0)
    came(1)
    store_ffn = pltpu.make_async_copy(landing, ffn_ref, local_sem.at[local_base + 5])
    store_ffn.start()
    store.wait()
    last.wait()
    store_ffn.wait()
    for copy in half_copies:
        copy.wait()
    batches[2].given()
    for batch in batches:
        batch.finish()
    line.finish()


def last_step(wide, rows, cross, dec_sums, enc_shares, y3, dec_attn, enc_attn, dec_self, enc_self, gains):
    low = jnp.bfloat16
    depth = D // wide
    size = split_at(depth)
    units = dec_sums[1].shape[0]
    columns = 4 * HD
    enc_rows, dec_rows = enc_self[0].shape[0], dec_self[0].shape[0]
    wanted = (columns + columns // 2) // rows
    copies = 3 * (wide + 6 + rows - 1) + 9 + wide + rows - 1 + 6 * wide + 4
    small = (16, (D + TILE - 1) // TILE * TILE)
    middle = D // 2
    half_shapes = [
        ((dec_rows, middle), low),
        ((middle, enc_rows), jnp.float32),
        ((dec_rows, middle), jnp.float32),
    ]
    batch_scratch = reduce_weights_scratch(wide, rows, size, columns)
    return pl.pallas_call(
        lambda *refs: last_kernel(wide, rows, *refs),
        out_shape=[
            jax.ShapeDtypeStruct((2, size, wanted), jnp.float32),
            jax.ShapeDtypeStruct((2, wide, 3, depth, TILE), low),
            jax.ShapeDtypeStruct(small, jnp.float32),
        ]
        + [jax.ShapeDtypeStruct((2, *each), kind) for each, kind in half_shapes],
        in_specs=[VM] * 6 + [VM, VM, HBM, HBM, VM, HBM, HBM] + [VM] * 18,
        out_specs=[HBM, HBM, VM, HBM, HBM, HBM],
        scratch_shapes=batch_scratch * 3
        + reduce_rows_scratch(units)
        + [
            pltpu.VMEM((D, columns), low),
            pltpu.VMEM((D, 3 * HD), low),
            pltpu.VMEM((D, HD), low),
            pltpu.VMEM((enc_rows, D), jnp.float32),
            pltpu.VMEM((dec_rows, D), jnp.float32),
            pltpu.VMEM((enc_rows, HD), low),
            pltpu.VMEM((enc_rows, 3 * HD), low),
            pltpu.VMEM((dec_rows, HD), low),
            pltpu.VMEM((dec_rows, 3 * HD), low),
            pltpu.VMEM((size, wanted), jnp.float32),
            pltpu.VMEM((size, wanted), jnp.float32),
            pltpu.VMEM((2, wide, 3, depth, TILE), low),
            pltpu.VMEM((2, wide, 3, depth, TILE), low),
            pltpu.VMEM((2,) + small, jnp.float32),
            pltpu.VMEM(small, jnp.float32),
            pltpu.VMEM((wide - 1,) + small, jnp.float32),
            pltpu.VMEM((rows - 1,) + small, jnp.float32),
        ]
        + [pltpu.VMEM(each, kind) for each, kind in half_shapes for _ in range(2)]
        + [
            pltpu.VMEM((H, 1, 2 * enc_rows), jnp.float32),
            pltpu.SemaphoreType.DMA((copies,)),
            pltpu.SemaphoreType.DMA((copies,)),
            pltpu.SemaphoreType.DMA((12 + wide,)),
        ],
        compiler_params=pltpu.CompilerParams(
            collective_id=7, has_side_effects=True, vmem_limit_bytes=VMEM_LIMIT
        ),
        name="last_step",
    )(*cross, *dec_sums, *enc_shares, y3, dec_attn, enc_attn, *dec_self, *enc_self, *gains)


def assemble_kernel(
    units, parts_ref, attn_ref, small_ref, enc_hot, dec_hot,
    in_ref, out_ref, gain_ref, bias_ref, win_ref, wout_ref, cin_ref, cout_ref,
):
    low = jnp.bfloat16
    wide = parts_ref.shape[1]
    place, core = lax.axis_index("wide"), lax.axis_index("section")
    pairs = 2 * wide
    row_ids = lax.broadcasted_iota(jnp.int32, (TILE, TILE), 0)
    lane_ids = lax.broadcasted_iota(jnp.int32, (TILE, TILE), 1)

    def tile_at(tile, first, columns):
        total = None
        last = min((tile + 1) * TILE, columns) - 1
        for group in range(tile * TILE // units, last // units + 1):
            half, chip, block = group % 2, group % pairs // 2, group // pairs
            shift = group * units - tile * TILE
            picks = ((row_ids + shift == lane_ids) & (row_ids < units)).astype(low)
            part = matmul(
                parts_ref[half, chip ^ place, first + block], picks
            )
            total = part if total is None else total + part
        return total

    for tile in range(in_ref.shape[2] // TILE):
        in_ref[0, :, pl.ds(tile * TILE, TILE)] = tile_at(tile, 0, in_ref.shape[2])
    for tile in range(out_ref.shape[2] // TILE):
        out_ref[0, :, pl.ds(tile * TILE, TILE)] = tile_at(tile, 2, out_ref.shape[2])
    for row in range(3):
        gain_ref[row] = small_ref[row : row + 1, 0:D]
    for section, hot in enumerate((enc_hot, dec_hot)):

        @pl.when(core == section)
        def _():
            sums = small_ref[8:16, 0 : hot.shape[1]]
            bias = lax.dot_general(
                sums, hot[...], (((1,), (1,)), ((), ())), precision=HIGHEST, preferred_element_type=jnp.float32
            )
            for head in range(H):
                bias_ref[head] = bias[head : head + 1]

    size, depth = attn_ref.shape[1], in_ref.shape[1]
    whole = jnp.concatenate([attn_ref[0], attn_ref[1, 2 * size - depth :]], axis=0)
    turned = whole.T
    start = 0
    for ref in (win_ref, wout_ref, cin_ref, cout_ref):
        ref[0] = turned[start : start + ref.shape[1]]
        start += ref.shape[1]


def assemble(rows, parts, attn_parts, small):
    wide, depth = parts.shape[1], parts.shape[3]
    shapes = [
        (1, depth, 2 * FF // rows),
        (1, depth, FF // rows),
        (3, 1, D),
        (H, 1, NB),
        (1, 3 * HD // rows, depth),
        (1, HD // rows, depth),
        (1, HD // rows, depth),
        (1, HD // rows, depth),
    ]
    return pl.pallas_call(
        lambda *refs: assemble_kernel(FF // (wide * rows * 2), *refs),
        out_shape=[jax.ShapeDtypeStruct(shape, jnp.float32) for shape in shapes],
        in_specs=[VM] * 5,
        out_specs=[VM] * len(shapes),
        compiler_params=pltpu.CompilerParams(vmem_limit_bytes=VMEM_LIMIT),
        name="assemble",
    )(
        parts,
        attn_parts,
        small,
        distance_hot(LE, True, 1 - LE),
        distance_hot(LD, False, 1 - LD),
    )


def bias_rows(source, target):
    length, span = target.shape[1], source.shape[1]
    for head in range(H):
        row = jnp.broadcast_to(source[pl.ds(head, 1), :], (length, span))
        target[head] = pltpu.roll(row, 0, 1, stride=1, stride_axis=0)[:, :length]


def distance_sums(scores, span):
    length = scores.shape[0]
    flip = (
        lax.broadcasted_iota(jnp.int32, (length, length), 0)
        + lax.broadcasted_iota(jnp.int32, (length, length), 1)
        == length - 1
    ).astype(jnp.bfloat16)
    flipped = matmul(flip, scores)
    padded = jnp.concatenate([flipped, jnp.zeros((length, span - length), jnp.float32)], axis=1)
    rolled = pltpu.roll(padded, 0, 1, stride=1, stride_axis=0)
    return jnp.sum(rolled, axis=0, keepdims=True)


def distance_hot(length, both_ways, first):
    table = bucket_table(length, both_ways)
    span = 2 * length
    hot = np.zeros((NB, span), np.float32)
    for entry in range(span):
        distance = entry + first
        if first == 0 and distance >= length:
            distance -= span
        if -length < distance < length:
            query = max(0, -distance)
            hot[table[query, query + distance], entry] = 1.0
    return jnp.asarray(hot)


def head_lanes(value, side):
    lanes = lax.broadcasted_iota(jnp.int32, value.shape, 1)
    return jnp.where((lanes < DH) == (side == 0), value, jnp.zeros_like(value))


def attend_heads(query_of, key_of, value_of, bias_of, allowed, context_ref, weights_ref):
    @pl.loop(0, H // 2)
    def _(pair):
        query, key, value = query_of(pair), key_of(pair), value_of(pair)
        total = None
        for side in range(2):
            head = 2 * pair + side
            scores = nt(head_lanes(query, side), key)
            if bias_of is not None:
                scores = scores + bias_of(head)
            scores = jnp.where(allowed, scores, NEGATIVE)
            shifted = jnp.exp(scores - jnp.max(scores, axis=-1, keepdims=True))
            weights = shifted / jnp.sum(shifted, axis=-1, keepdims=True)
            weights_ref[head] = weights
            part = matmul(weights.astype(jnp.bfloat16), head_lanes(value, side))
            total = part if total is None else total + part
        context_ref[:, pair_tile(pair, 0)] = total.astype(jnp.bfloat16)


def attend_heads_backward(query_of, key_of, value_of, weights_ref, grad_of, put, put_scores=None):
    @pl.loop(0, H // 2)
    def _(pair):
        query, key, value, grad = query_of(pair), key_of(pair), value_of(pair), grad_of(pair)
        sums = [None, None, None]
        for side in range(2):
            head = 2 * pair + side
            weights = weights_ref[head]
            own_grad = head_lanes(grad, side)
            grad_weights = nt(own_grad, value)
            inner = jnp.sum(grad_weights * weights, axis=-1, keepdims=True)
            low = (weights * (grad_weights - inner)).astype(jnp.bfloat16)
            if put_scores is not None:
                put_scores(head, low)
            parts = [
                matmul(low, head_lanes(key, side)),
                tn(low, head_lanes(query, side)),
                tn(weights.astype(jnp.bfloat16), own_grad),
            ]
            sums = [b if a is None else a + b for a, b in zip(sums, parts)]
        put(pair, *sums)


def pair_tile(pair, base):
    return pl.ds(pl.multiple_of(base + pair * TILE, TILE), TILE)


def item_numbers(lengths_ref, core, shape, axis):
    positions = lax.broadcasted_iota(jnp.int32, shape, axis)
    number, end = jnp.zeros(shape, jnp.int32), 0
    for item in range(lengths_ref.shape[1] - 1):
        end = end + lengths_ref[core, item]
        number = number + (positions >= end).astype(jnp.int32)
    return number


def weight_spec(half, width, index):
    return pl.BlockSpec((None, D, width), lambda step: (half, 0, index), memory_space=pltpu.VMEM)


W_IN = weight_spec(0, 3 * HD, 0)
W_OUT, C_IN, C_OUT = [weight_spec(1, HD, i) for i in range(3)]


def tile_of(ref, base):
    return lambda pair: ref[:, pair_tile(pair, base)]


def self_forward_rows(
    causal, x_ref, gain_ref, win_ref, wout_ref, bias_ref, lengths_ref, y_ref, low_ref, normed_ref, projected_ref, context_ref, weights_ref
):
    core = lax.axis_index("section")
    low_ref[...] = x_ref[core] if causal else x_ref[core].T
    residual = low_ref[...].astype(jnp.float32)
    normed_ref[...] = (residual * rms_rows(residual) * gain_ref[pl.ds(0, 1), :]).astype(jnp.bfloat16)
    projected_ref[...] = matmul(normed_ref[...], win_ref[...]).astype(jnp.bfloat16)
    length = low_ref.shape[0]
    allowed = item_numbers(lengths_ref, core, (length, length), 0) == item_numbers(
        lengths_ref, core, (length, length), 1
    )
    if causal:
        allowed = allowed & (
            lax.broadcasted_iota(jnp.int32, (length, length), 0)
            >= lax.broadcasted_iota(jnp.int32, (length, length), 1)
        )
    attend_heads(
        tile_of(projected_ref, 0),
        tile_of(projected_ref, HD),
        tile_of(projected_ref, 2 * HD),
        lambda head: bias_ref[head],
        allowed,
        context_ref,
        weights_ref,
    )
    y_ref[...] = residual + nt(context_ref[...], wout_ref[...])


def self_forward_kernel(
    wide, causal, x_ref, gain_ref, win_ref, wout_ref, bias_ref, lengths_ref, *refs
):
    if wide:
        blocks, dec_blocks, refs = refs[: wide - 1], refs[wide - 1 : 2 * wide - 2], refs[2 * wide - 2 :]
    y_ref, low_ref, normed_ref, projected_ref, context_ref, weights_ref = refs[:6]
    if wide:
        pieces, dec_pieces, sems = refs[6 : 5 + wide], refs[5 + wide : 4 + 2 * wide], refs[4 + 2 * wide :]
        peers = peers_of(wide)
        greet(peers + [{"rows": lax.axis_index("rows") ^ 1}])
        reshard = Reshard(blocks, pieces, 0, sems, 0, peers)
        reshard.start()
        half = dec_pieces[0].shape[0]
        mine = pl.ds(lax.axis_index("rows") % 2 * half, half)
        later = [
            remote(block.at[mine], piece, sems, 9 + v, peers[v])
            for v, (block, piece) in enumerate(zip(dec_blocks, dec_pieces))
        ]
    self_forward_rows(
        causal, x_ref, gain_ref, win_ref, wout_ref, bias_ref, lengths_ref, y_ref, low_ref, normed_ref, projected_ref, context_ref, weights_ref
    )
    if wide:
        for copy in later:
            copy.start()
        reshard.pass_on()
        reshard.finish()
        for copy in later:
            copy.wait()


def self_forward(causal, embed, gains, weight, bias, lengths, blocks=(), dec_blocks=()):
    rows = embed.shape[1 if causal else 2]
    low = jnp.bfloat16
    wide = len(blocks) + 1 if blocks else 0
    params = dict(vmem_limit_bytes=VMEM_LIMIT)
    if blocks:
        params.update(collective_id=6, has_side_effects=True)
    y, *kept = pl.pallas_call(
        lambda *refs: self_forward_kernel(wide, causal, *refs),
        out_shape=[
            jax.ShapeDtypeStruct((rows, D), jnp.float32),
            jax.ShapeDtypeStruct((rows, D), low),
            jax.ShapeDtypeStruct((rows, D), low),
            jax.ShapeDtypeStruct((rows, 3 * HD), low),
            jax.ShapeDtypeStruct((rows, HD), low),
            jax.ShapeDtypeStruct((H, rows, rows), jnp.float32),
        ]
        + [jax.ShapeDtypeStruct(each.shape, low) for each in blocks]
        + [jax.ShapeDtypeStruct((each.shape[0] // 2, *each.shape[1:]), low) for each in dec_blocks],
        in_specs=[VM, VM, W_IN, W_OUT, VM, SM] + [HBM] * (2 * len(blocks)),
        out_specs=[VM] * 6 + [HBM] * (2 * len(blocks)),
        scratch_shapes=[pltpu.SemaphoreType.DMA((12,))] * 2 if blocks else [],
        grid=(1,),
        compiler_params=pltpu.CompilerParams(**params),
        name="self_forward_%d" % rows,
    )(embed, gains, weight, weight, bias, lengths, *blocks, *dec_blocks)
    return y, kept[:5], kept[5:]


def picked(source, start, window, first, width):
    base = start // TILE * TILE
    window = min(window, source.shape[1] - base)
    lanes = lax.broadcasted_iota(jnp.int32, (window, HD), 1) - first
    rows_of = lax.broadcasted_iota(jnp.int32, (window, HD), 0) + (base - start)
    pick = ((rows_of == lanes) & (lanes >= 0) & (lanes < width)).astype(jnp.bfloat16)
    return matmul(source[:, pl.ds(base, window)], pick)


def self_backward_rows(
    g_ref,
    x_ref,
    gain_ref,
    win_ref,
    wout_ref,
    projected_ref,
    weights_ref,
    gx_ref,
    small_ref,
    context_grad,
    projected_grad,
    sums_ref,
):
    low = jnp.bfloat16
    length = x_ref.shape[0]
    context_grad[...] = matmul(g_ref[...].astype(low), wout_ref[...]).astype(low)

    def put(pair, query, key, value):
        for index, part in enumerate((query, key, value)):
            projected_grad[:, pair_tile(pair, index * HD)] = part.astype(low)

    def put_scores(head, scores):
        sums_ref[head, :, pl.ds(0, 2 * length)] = distance_sums(scores, 2 * length)

    attend_heads_backward(
        tile_of(projected_ref, 0),
        tile_of(projected_ref, HD),
        tile_of(projected_ref, 2 * HD),
        weights_ref,
        tile_of(context_grad, 0),
        put,
        put_scores,
    )
    for head in range(H):
        small_ref[pl.ds(8 + head, 1), pl.ds(0, 2 * length)] = sums_ref[head, :, pl.ds(0, 2 * length)]
    grad_normed = nt(projected_grad[...], win_ref[...])
    residual = x_ref[...].astype(jnp.float32)
    grad_residual, grad_gain = norm_pull(residual, gain_ref[pl.ds(0, 1), :], grad_normed)
    small_ref[pl.ds(0, 1), pl.ds(0, D)] = grad_gain
    gx_ref[...] = g_ref[...] + grad_residual


def self_backward_weights(g_ref, normed_ref, context_ref, projected_grad, grad_ref):
    low = jnp.bfloat16
    both = jnp.concatenate([normed_ref[...], g_ref[...].astype(low)], axis=0)
    chunks = grad_ref.shape[1] // HD
    part_in, part_out = 3 * HD // chunks, HD // chunks
    for chunk in range(chunks):
        right = jnp.concatenate(
            [
                picked(projected_grad, chunk * part_in, HD, 0, part_in),
                picked(context_ref, chunk * part_out, 2 * TILE, part_in, part_out),
            ],
            axis=0,
        ).astype(low)
        grad_ref[:, pl.ds(chunk * HD, HD)] = tn(both, right).astype(low)


def cross_forward_rows(
    x_ref, final_ref, wkey_ref, wvalue_ref, y_ref, gain_ref, wquery_ref, wout_ref, dec_lengths, enc_lengths,
    out_ref, memory_ref, kv_ref, normed_ref, query_ref, context_ref, weights_ref,
):
    low = jnp.bfloat16
    core = lax.axis_index("section")
    residual = x_ref[...]
    memory_ref[...] = (residual * rms_rows(residual) * final_ref[pl.ds(2, 1), :]).astype(low)
    kv_ref[:, pl.ds(0, HD)] = matmul(memory_ref[...], wkey_ref[...]).astype(low)
    kv_ref[:, pl.ds(HD, HD)] = matmul(memory_ref[...], wvalue_ref[...]).astype(low)
    target = y_ref[...]
    normed_ref[...] = (target * rms_rows(target) * gain_ref[pl.ds(1, 1), :]).astype(low)
    query_ref[...] = matmul(normed_ref[...], wquery_ref[...]).astype(low)
    attend_heads(
        tile_of(query_ref, 0),
        tile_of(kv_ref, 0),
        tile_of(kv_ref, HD),
        None,
        item_numbers(dec_lengths, core, (LD, LE), 0) == item_numbers(enc_lengths, core, (LD, LE), 1),
        context_ref,
        weights_ref,
    )
    out_ref[...] = target + nt(context_ref[...], wout_ref[...])


def cross_backward_rows(
    g_ref, x_ref, final_ref, wkey_ref, wvalue_ref, y_ref, gain_ref, wquery_ref, wout_ref, kv_ref, query_ref, weights_ref,
    gx_ref, gy_ref, final_out, gain_out, kv_grad, query_grad, context_grad,
):
    low = jnp.bfloat16
    grad_low = g_ref[...].astype(low)
    context_grad[...] = matmul(grad_low, wout_ref[...]).astype(low)

    def put(pair, query, key, value):
        query_grad[:, pair_tile(pair, 0)] = query.astype(low)
        kv_grad[:, pair_tile(pair, 0)] = key.astype(low)
        kv_grad[:, pair_tile(pair, HD)] = value.astype(low)

    attend_heads_backward(
        tile_of(query_ref, 0),
        tile_of(kv_ref, 0),
        tile_of(kv_ref, HD),
        weights_ref,
        tile_of(context_grad, 0),
        put,
    )
    grad_memory = nt(kv_grad[:, pl.ds(0, HD)], wkey_ref[...]) + nt(
        kv_grad[:, pl.ds(HD, HD)], wvalue_ref[...]
    )
    gx_ref[...], final_out[...] = norm_pull(x_ref[...], final_ref[pl.ds(2, 1), :], grad_memory)
    grad_residual, gain_out[...] = norm_pull(
        y_ref[...], gain_ref[pl.ds(1, 1), :], nt(query_grad[...], wquery_ref[...])
    )
    gy_ref[...] = g_ref[...] + grad_residual


def cross_weights(g_ref, kv_grad, query_grad, memory_ref, normed_ref, context_ref, grad_ref):
    low = jnp.bfloat16
    lefts = jnp.concatenate([memory_ref[...], normed_ref[...], g_ref[...].astype(low)], axis=0)
    chunks = grad_ref.shape[1] // HD
    part = HD // chunks
    for chunk in range(chunks):
        start = chunk * part
        right = jnp.concatenate(
            [
                picked(kv_grad, start, 2 * TILE, 0, part)
                + picked(kv_grad, HD + start, 2 * TILE, part, part),
                picked(query_grad, start, 2 * TILE, 2 * part, part),
                picked(context_ref, start, 2 * TILE, 3 * part, part),
            ],
            axis=0,
        ).astype(low)
        grad_ref[:, pl.ds(chunk * HD, HD)] = tn(lefts, right).astype(low)


def plain_self_forward(residual, gain_row, weight, bias_full, allowed):
    normed = to_low(rms_norm(residual, gain_row))
    projected = to_low(matmul(normed, weight[:, : 3 * HD]))
    context, weights, low_weights = attend_forward(
        projected[:, :HD], projected[:, HD : 2 * HD], projected[:, 2 * HD :], bias_full, allowed
    )
    return (
        residual + matmul(context, weight[:, 3 * HD : 4 * HD].T),
        (residual, normed, projected, context, weights, low_weights),
    )


def plain_self_backward(kept, gain_row, weight, hot, grad_out):
    residual, normed, projected, context, weights, low_weights = kept
    grad_low = to_low(grad_out)
    grad_wout = matmul(grad_low.T, context)
    grad_context = to_low(matmul(grad_low, weight[:, 3 * HD : 4 * HD]))
    grad_queries, grad_keys, grad_values, low_scores = attend_backward(
        projected[:, :HD],
        projected[:, HD : 2 * HD],
        projected[:, 2 * HD :],
        weights,
        low_weights,
        grad_context,
    )
    grad_projected = to_low(jnp.concatenate([grad_queries, grad_keys, grad_values], axis=1))
    grad_win = matmul(normed.T, grad_projected)
    grad_residual, grad_gain = plain_norm_backward(
        residual, gain_row, matmul(grad_projected, weight[:, : 3 * HD].T)
    )
    grad_bias = jnp.einsum(
        "hqk,qkb->bh", low_scores, hot.astype(jnp.bfloat16), preferred_element_type=jnp.float32
    )
    return grad_out + grad_residual, grad_gain, grad_win, grad_wout, grad_bias


def plain_reduce_attn(grad, core, wide, rows):
    depth, columns = grad.shape
    halves = plain_core_halves(grad, core, wide)
    place = lax.axis_index("wide")
    parts = [
        lax.dynamic_index_in_dim(halves, place ^ v, 0, keepdims=False) for v in range(wide)
    ]
    mine = to_low(scatter_wide(parts))
    pieces, start = [], 0
    for width in (3 * HD, HD, HD, HD):
        pieces.append(mine[:, start : start + width].reshape(mine.shape[0], rows, width // rows))
        start += width
    stacked = jnp.concatenate(pieces, axis=2).transpose(1, 0, 2)
    return lax.psum_scatter(stacked, "rows", scatter_dimension=0, tiled=True)[0]


def plain_core_halves(grad, core, wide):
    depth, columns = grad.shape
    split = to_low(grad).reshape(wide, 2, depth // wide // 2, columns)
    mine = lax.dynamic_index_in_dim(split, core, 1, keepdims=False)
    sent = lax.dynamic_index_in_dim(split, 1 - core, 1, keepdims=False)
    return mine.astype(jnp.float32) + xor_permute(sent, "section", 1).astype(jnp.float32)


def plain_both_sections(own, section):
    other = xor_permute(own, "section", 1)
    is_dec = section == 1
    return jnp.where(is_dec, other, own), jnp.where(is_dec, own, other)


def plain_norm_backward(residual, gain_row, grad_normed):
    _, norm_pull = jax.vjp(rms_norm, residual, gain_row)
    return norm_pull(grad_normed)


def plain_hidden_columns(weight):
    width = weight.shape[1] * 2 // 3
    return weight[:, :width], weight[:, width:]


def plain_ffn_hidden(blocks, weight):
    w_in, _ = plain_hidden_columns(weight)
    both = [matmul(block, w_in) for block in blocks]
    units = w_in.shape[1] // 2
    return both, [to_low(gated(part[:, :units], part[:, units:])) for part in both]


def plain_ffn_forward(residual, gain_row, weight):
    blocks = gather_wide(to_low(rms_norm(residual, gain_row)))
    both, hidden = plain_ffn_hidden(blocks, weight)
    _, w_out = plain_hidden_columns(weight)
    out = residual + scatter_wide([matmul(part, w_out.T) for part in hidden])
    return out, (residual, blocks, both, hidden)


def plain_ffn_backward(kept, gain_row, weight, grad_out, grad_blocks):
    residual, blocks, both, hidden = kept
    w_in, w_out = plain_hidden_columns(weight)
    units = w_out.shape[1]
    parts, grad_both = [], []
    for block, pre in zip(grad_blocks, both):
        _, pull = jax.vjp(gated, pre[:, :units], pre[:, units:])
        grad_gate, grad_up = pull(matmul(block, w_out))
        low = to_low(jnp.concatenate([grad_gate, grad_up], axis=1))
        grad_both.append(low)
        parts.append(matmul(low, w_in.T))
    grad_residual, grad_gain = plain_norm_backward(residual, gain_row, scatter_wide(parts))
    joined = jnp.concatenate(grad_both, axis=0)
    grad_in = matmul(jnp.concatenate(blocks, axis=0).T, joined)
    grad_wout = matmul(jnp.concatenate(grad_blocks, axis=0).T, jnp.concatenate(hidden, axis=0))
    return grad_out + grad_residual, grad_gain, (grad_in, grad_wout)


def plain_reduce_ffn(grads, core, wide, rows):
    grad_in, grad_wout = grads
    depth = grad_in.shape[0]
    both = jnp.concatenate(
        [grad_in.reshape(depth, rows, -1), grad_wout.reshape(depth, rows, -1)], axis=2
    )
    columns = both.shape[2]
    halves = plain_core_halves(both.reshape(depth, rows * columns), core, wide)
    halves = to_low(halves).reshape(wide * (depth // wide // 2), rows, columns).transpose(1, 0, 2)
    summed = lax.psum_scatter(halves, "rows", scatter_dimension=0, tiled=True)[0]
    blocks = summed.reshape(wide, depth // wide // 2, columns)
    place = lax.axis_index("wide")
    out = [lax.dynamic_index_in_dim(blocks, place, 0, keepdims=False)]
    for v in range(1, wide):
        block = lax.dynamic_index_in_dim(blocks, place ^ v, 0, keepdims=False)
        out.append(xor_permute(block, "wide", v))
    return placed_rows([piece[None] for piece in out], place)


def plain_to_section(enc_half, dec_half, core):
    is_dec = core == 1
    own = jnp.where(is_dec, dec_half, enc_half)
    got = xor_permute(jnp.where(is_dec, enc_half, dec_half), "section", 1)
    low, high = jnp.where(is_dec, got, own), jnp.where(is_dec, own, got)
    return jnp.concatenate([low, high], axis=-2).astype(jnp.float32)


def plain_shards(
    enc_embed,
    dec_embed,
    out_cot,
    enc_lengths,
    dec_lengths,
    norm_gains,
    rel_bias,
    attn_in,
    attn_out,
    ffn_in,
    ffn_out,
    cross_in,
    cross_out,
):
    core = lax.axis_index("section")
    place = lax.axis_index("wide")
    wide, rows = lax.axis_size("wide"), lax.axis_size("rows")
    depth = attn_in.shape[1]
    unit = FF // (wide * rows)

    small = jnp.concatenate([norm_gains[0].reshape(-1), rel_bias[0].reshape(-1)])
    enc_small, dec_small = plain_both_sections(small, core)
    gains = [each[: 3 * D].reshape(3, D) for each in (enc_small, dec_small)]
    biases = [each[3 * D :].reshape(NB, H) for each in (enc_small, dec_small)]

    attn_shard = jnp.concatenate([attn_in[0], attn_out[0].T, cross_in[0], cross_out[0]], axis=1)
    attn_own = placed_rows(gather_wide(attn_shard), place)
    ffn_blocks = jnp.concatenate(
        [
            ffn_in[0].reshape(depth, 2 * rows, wide, unit).transpose(2, 0, 1, 3).reshape(wide, depth, -1),
            ffn_out[0].T.reshape(depth, rows, wide, unit).transpose(2, 0, 1, 3).reshape(wide, depth, -1),
        ],
        axis=2,
    )
    ffn_got = [lax.dynamic_index_in_dim(ffn_blocks, place, 0, keepdims=False)]
    for v in range(1, wide):
        block = lax.dynamic_index_in_dim(ffn_blocks, place ^ v, 0, keepdims=False)
        ffn_got.append(xor_permute(block, "wide", v))
    ffn_own = placed_rows(ffn_got, place)
    attn_enc, attn_dec = plain_both_sections(attn_own, core)
    ffn_enc, ffn_dec = plain_both_sections(ffn_own, core)
    memory_weight = attn_enc[:, 4 * HD :]
    cross_w_in, cross_w_out = attn_dec[:, 4 * HD : 5 * HD], attn_dec[:, 5 * HD :]

    def own_row(array):
        return lax.dynamic_index_in_dim(array[:, 0], core, 0, keepdims=False)

    enc_row = own_row(enc_embed).astype(jnp.float32)
    dec_row = own_row(dec_embed).astype(jnp.float32)
    cot_row = own_row(out_cot)
    enc_items = item_ids(own_row(enc_lengths), LE)
    dec_items = item_ids(own_row(dec_lengths), LD)
    enc_hot, dec_hot = one_hot(LE, True), one_hot(LD, False)
    enc_bias = jnp.einsum("qkb,bh->hqk", enc_hot, biases[0], precision=HIGHEST)
    dec_bias = jnp.einsum("qkb,bh->hqk", dec_hot, biases[1], precision=HIGHEST)
    causal = jnp.arange(LD)[:, None] >= jnp.arange(LD)[None, :]

    cot_blocks = gather_wide(cot_row)
    x1, enc_self = plain_self_forward(
        enc_row, gains[0][0], attn_enc, enc_bias, enc_items[:, None] == enc_items[None, :]
    )
    y1, dec_self = plain_self_forward(
        dec_row,
        gains[1][0],
        attn_dec,
        dec_bias,
        (dec_items[:, None] == dec_items[None, :]) & causal,
    )
    x2, enc_ffn = plain_ffn_forward(x1, gains[0][1], ffn_enc)
    memory = to_low(rms_norm(x2, gains[0][2]))
    memory_kv = to_low(matmul(memory, memory_weight))
    cross_normed = to_low(rms_norm(y1, gains[1][1]))
    queries = to_low(matmul(cross_normed, cross_w_in))
    context, weights, low_weights = attend_forward(
        queries,
        memory_kv[:, :HD],
        memory_kv[:, HD:],
        0.0,
        dec_items[:, None] == enc_items[None, :],
    )
    y2 = y1 + matmul(context, cross_w_out.T)
    y3, dec_ffn = plain_ffn_forward(y2, gains[1][2], ffn_dec)

    g2, dec_ffn_gain, dec_ffn_grads = plain_ffn_backward(
        dec_ffn, gains[1][2], ffn_dec, cot_row.astype(jnp.float32), cot_blocks
    )
    dec_ffn_share = plain_reduce_ffn(dec_ffn_grads, core, wide, rows)
    g2_low = to_low(g2)
    grad_cross_out = matmul(g2_low.T, context)
    grad_context = to_low(matmul(g2_low, cross_w_out))
    grad_queries, grad_keys, grad_values, _ = attend_backward(
        queries, memory_kv[:, :HD], memory_kv[:, HD:], weights, low_weights, grad_context
    )
    grad_query_low = to_low(grad_queries)
    grad_kv = to_low(jnp.concatenate([grad_keys, grad_values], axis=1))
    grad_x2, enc_final_gain = plain_norm_backward(x2, gains[0][2], matmul(grad_kv, memory_weight.T))
    grad_x1, enc_ffn_gain, enc_ffn_grads = plain_ffn_backward(
        enc_ffn, gains[0][1], ffn_enc, grad_x2, gather_wide(to_low(grad_x2))
    )
    enc_ffn_share = plain_reduce_ffn(enc_ffn_grads, core, wide, rows)

    grad_cross_in = matmul(cross_normed.T, grad_query_low)
    grad_memory = matmul(memory.T, grad_kv)
    from_cross, dec_cross_gain = plain_norm_backward(
        y1, gains[1][1], matmul(grad_query_low, cross_w_in.T)
    )
    grad_y, dec_self_gain, dec_win, dec_wout, dec_bias_grad = plain_self_backward(
        dec_self, gains[1][0], attn_dec, dec_hot, g2 + from_cross
    )
    dec_attn_share = plain_reduce_attn(
        jnp.concatenate([dec_win, dec_wout, grad_cross_in, grad_cross_out], axis=1),
        core,
        wide,
        rows,
    )
    grad_x, enc_self_gain, enc_win, enc_wout, enc_bias_grad = plain_self_backward(
        enc_self, gains[0][0], attn_enc, enc_hot, grad_x1
    )
    enc_attn_share = plain_reduce_attn(
        jnp.concatenate([enc_win, enc_wout, grad_memory], axis=1), core, wide, rows
    )

    small_grads = jnp.stack(
        [
            jnp.concatenate(
                [enc_self_gain, enc_ffn_gain, enc_final_gain, enc_bias_grad.reshape(-1)]
            ),
            jnp.concatenate(
                [dec_self_gain, dec_cross_gain, dec_ffn_gain, dec_bias_grad.reshape(-1)]
            ),
        ]
    )
    small_total = lax.psum(small_grads, ("section", "wide", "rows"))
    small_own = jnp.where(core == 1, small_total[1], small_total[0])

    attn_share = plain_to_section(enc_attn_share, dec_attn_share, core)
    ffn_share = plain_to_section(enc_ffn_share, dec_ffn_share, core)
    in_width = 2 * FF // rows // wide
    ffn_in_grad = (
        ffn_share[:, :, :in_width]
        .reshape(wide, depth, 2, unit)
        .transpose(1, 2, 0, 3)
        .reshape(depth, 2 * FF // rows)
    )
    ffn_out_grad = ffn_share[:, :, in_width:].transpose(0, 2, 1).reshape(FF // rows, depth)
    widths = [3 * HD // rows, HD // rows, HD // rows]
    edges = np.cumsum([0] + widths + [HD // rows])
    win, wout, cin, cout = [attn_share[:, a:b] for a, b in zip(edges[:-1], edges[1:])]

    half = D // 2

    def by_half(own):
        halves = jnp.stack([own[:, :half], own[:, half:]])
        keep = lax.dynamic_index_in_dim(halves, core, 0, keepdims=False)
        send = lax.dynamic_index_in_dim(halves, 1 - core, 0, keepdims=False)
        got = xor_permute(send, "section", 1)
        is_dec = core == 1
        return jnp.stack([jnp.where(is_dec, got, keep), jnp.where(is_dec, keep, got)])[:, None]

    return (
        by_half(to_low(y3)),
        by_half(grad_x),
        by_half(grad_y),
        small_own[: 3 * D].reshape(1, 3, D),
        small_own[3 * D :].reshape(1, NB, H),
        win[None],
        wout.T[None],
        ffn_in_grad[None],
        ffn_out_grad[None],
        cin[None],
        cout[None],
    )


def shards(
    enc_embed,
    dec_embed,
    out_cot,
    enc_lengths,
    dec_lengths,
    norm_gains,
    rel_bias,
    attn_in,
    attn_out,
    ffn_in,
    ffn_out,
    cross_in,
    cross_out,
):
    wide, rows = lax.axis_size("wide"), lax.axis_size("rows")
    enc_attn, dec_half, gains, biases, enc_blocks, dec_blocks = start_weights(
        wide, rows, attn_in, attn_out, cross_in, cross_out, ffn_in, ffn_out, jnp.swapaxes(norm_gains, 0, 1), rel_bias.transpose(2, 0, 1)
    )
    enc_lengths, dec_lengths = enc_lengths[:, 0], dec_lengths[:, 0]
    x1, enc_self, moved = self_forward(
        False,
        jnp.swapaxes(enc_embed[:, 0], 1, 2),
        gains[0],
        enc_attn,
        biases[0],
        enc_lengths,
        tuple(enc_blocks[1:]),
        tuple(dec_blocks[1:]),
    )
    enc_pieces, dec_pieces = moved[: wide - 1], moved[wide - 1 :]
    x2, *enc_ffn = ffn_forward_call(
        wide, x1, (gains[0], 1), [enc_blocks[0], *enc_pieces], 2, (dec_half, *dec_pieces)
    )
    enc_ffn, dec_attn, dec_pieces = enc_ffn[:4], enc_ffn[4], [dec_blocks[0], *dec_pieces, *enc_ffn[5:]]
    y3, g2, dec_ffn_gain, dec_ffn_grads, y1, dec_self, cross_kept = decoder_call(
        wide,
        rows,
        out_cot[:, 0],
        (gains[1], 2),
        dec_pieces,
        x2,
        gains[0],
        dec_embed[:, 0],
        biases[1],
        dec_lengths,
        enc_lengths,
        enc_attn,
        dec_attn,
        3,
    )
    (
        grad_x1,
        enc_ffn_gain,
        enc_in,
        enc_out,
        *dec_sums,
        g1,
        enc_final_gain,
        dec_cross_gain,
        kv_grad,
        query_grad,
    ) = ffn_backward_call(
        wide,
        rows,
        x1,
        (gains[0], 1),
        enc_ffn,
        5,
        dec_ffn_grads,
        (enc_attn, dec_attn, gains[1], g2, x2, y1, cross_kept[1], cross_kept[3], cross_kept[5]),
    )
    attn_parts, ffn_parts, small_own, dec_out, enc_grad, dec_grad = last_step(
        wide,
        rows,
        (g2, kv_grad, query_grad, cross_kept[0], cross_kept[2], cross_kept[4]),
        dec_sums,
        (enc_in, enc_out),
        y3,
        dec_attn,
        enc_attn,
        (g1, dec_self[0], gains[1], *dec_self[1:]),
        (grad_x1, enc_self[0], gains[0], *enc_self[1:]),
        (enc_ffn_gain, enc_final_gain, dec_cross_gain, dec_ffn_gain),
    )
    ffn_in_grad, ffn_out_grad, gain_grad, bias_grad, win, wout, cin, cout = assemble(
        rows, ffn_parts, attn_parts, small_own
    )
    return (
        dec_out[:, None],
        jnp.swapaxes(enc_grad, 1, 2)[:, None],
        dec_grad[:, None],
        gain_grad.transpose(1, 0, 2),
        bias_grad.transpose(1, 2, 0),
        jnp.swapaxes(win, 1, 2),
        wout,
        ffn_in_grad,
        jnp.swapaxes(ffn_out_grad, 1, 2),
        jnp.swapaxes(cin, 1, 2),
        jnp.swapaxes(cout, 1, 2),
    )


def solution(mesh):
    placed = (
        P(None, ("wide", "rows"), None, None),
        P(None, ("wide", "rows"), None, None),
        P(None, ("wide", "rows"), None, None),
        P(None, ("wide", "rows"), None),
        P(None, ("wide", "rows"), None),
        P("section", None, None),
        P("section", None, None),
        P("section", "wide", None),
        P("section", None, "wide"),
        P("section", "wide", None),
        P("section", None, "wide"),
        P("section", "wide", None),
        P("section", "wide", None),
    )
    wide, rows = mesh.shape["wide"], mesh.shape["rows"]
    in_tiles = D // wide % 16 == 0 and FF // (wide * rows) % 32 == 0
    return jax.shard_map(
        shards if wide == 4 and rows == 4 and in_tiles else plain_shards,
        mesh=mesh,
        in_specs=placed,
        out_specs=(
            P(None, ("wide", "rows"), None, "section"),
            P(None, ("wide", "rows"), None, "section"),
            P(None, ("wide", "rows"), None, "section"),
            P("section", None, None),
            P("section", None, None),
            P("section", "wide", "rows"),
            P("section", "rows", "wide"),
            P("section", "wide", "rows"),
            P("section", "rows", "wide"),
            P("section", "wide", "rows"),
            P("section", "wide", "rows"),
        ),
        check_vma=False,
    )
```
